128 devices in a mesh: sym: 8 (over y_hi, x), tile: 8 (over z, y_lo), occ: 2 (over core).
Axes of the slice: x: 4, y: 4 (y_hi: 2, y_lo: 2; y = y_hi * 2 + y_lo), z: 4, core: 2. Of those that a mesh axis runs over, the one named last changes fastest.
Arguments:
- irrep_dims: int32 [8], replicated, may hold values from 1 to 384, 1600 in all
- chol_vectors: bfloat16 [16, 3072, 384], P(('sym', 'occ'), 'tile'), may hold values from -0.375 to 0.375
- amplitudes: bfloat16 [8, 16, 3072, 384], P('sym', 'occ', 'tile'), may hold values from -6 to 6
Outputs:
- sigma_ladder: float32 [8, 16, 3072, 384], P('sym', 'occ', 'tile')
The draws below stay inside these ranges and needn't reach their ends.
Inputs may be any that keep to these rules, and one draw needn't show every extreme that they name: irrep_dims[h] is the number of virtual orbitals of irrep h; the entries sum to 1600 and the largest is exactly 384.
All inputs are finite; a program needn't handle non-finite values.
Results may differ from the reference program's by a relative error of at most 0.0029.
Values may be sent and summed in bfloat16 or wider, within the bound.
A program may use at most 128 MiB of HBM per device.

```python
import math
import jax
import jax.numpy as jnp
import numpy as np
from jax import lax

NIRR = 8
VMAX = 384
NVIRT = 1600
NB = 16
NPAIR = 16


def block_scale(key, extent, cuts, least, top_value):
    def one(dim, blocks):
        steps = jax.random.uniform(jax.random.fold_in(jax.random.fold_in(key, 6), dim), (blocks,), jnp.float32, least / len(cuts), top_value / len(cuts))
        return jnp.repeat(jnp.exp(steps), extent[dim] // blocks).reshape((-1,) + (1,) * (len(extent) - dim - 1))

    factor_of = one(*cuts[0])
    for cut in cuts[1:]:
        factor_of = factor_of * one(*cut)
    return factor_of


def profile(count, total, bound, slope):
    weights = [(1 << 20) // math.isqrt(rank ** slope) + 1 for rank in range(2, count + 1)]
    spare, holding = total - bound - (count - 1), [1] * (count - 1)
    while spare > 0:
        free = [i for i in range(count - 1) if holding[i] < bound]
        whole, budget = sum([weights[i] for i in free]), spare
        for i in free:
            addition = min(bound - holding[i], max(1, budget * weights[i] // whole), spare)
            holding[i] = holding[i] + addition
            spare = spare - addition
    return np.array([bound] + holding)


def uneven_parts(own_key, number_of, total, reach, skew):
    if number_of == 2:
        one = jax.random.randint(own_key, (), max(1, total - reach), min(reach, total - 1) + 1)
        return jnp.stack([one, total - one])
    lengths = jnp.asarray(profile(number_of, total, reach, skew), jnp.int32)
    pairs = (number_of - 1) // 2
    giver, sink = lengths[1:1 + 2 * pairs:2], lengths[2:2 + 2 * pairs:2]
    room = jnp.minimum(giver - 1, reach - sink)
    moved = jax.random.randint(jax.random.fold_in(own_key, 1), (pairs,), 0, 1 << 20) % (room + 1)
    lengths = lengths.at[1:1 + 2 * pairs:2].set(giver - moved).at[2:2 + 2 * pairs:2].set(sink + moved)
    return lengths[jax.random.permutation(jax.random.fold_in(own_key, 2), number_of)]


def gaussian(own_key, shape, scale, bound, pieces=(), kind=jnp.bfloat16):
    level = block_scale(own_key, shape, pieces, -0.22, 0.18) if pieces else 1.0
    entries = jax.random.normal(own_key, shape, jnp.float32) * scale * level
    return jnp.minimum(jnp.maximum(entries, -bound), bound).astype(kind)


def setup_inputs(seed: int = 0) -> dict:
    keys = jax.random.split(jax.random.key(seed), 4)
    return {
        "irrep_dims": uneven_parts(keys[0], NIRR, NVIRT, VMAX, 2).astype(jnp.int32),
        "chol_vectors": gaussian(keys[1], (NB, NIRR * VMAX, VMAX), (1.0 / (NB ** 0.25 * VMAX ** 0.5)), 0.375, ((0, 16), (1, 8))),
        "amplitudes": gaussian(keys[2], (NIRR, NPAIR, NIRR * VMAX, VMAX), 1.0, 6.0, ((0, 8), (1, 2), (2, 8))),
    }


def reference(irrep_dims, chol_vectors, amplitudes):
    row_index = jnp.arange(VMAX, dtype=jnp.int32)
    live_mask = row_index[None, :] < irrep_dims[:, None]
    vectors = chol_vectors.reshape(NB, NIRR, VMAX, VMAX)
    vec_mask = (live_mask[:, :, None] & live_mask[:, None, :]).astype(chol_vectors.dtype)
    vectors = vectors * vec_mask[None]
    blocks = amplitudes.reshape(NIRR, NPAIR, NIRR, VMAX, VMAX)

    def one_block(combined):
        sym_block = combined // NIRR
        lead_irrep = combined % NIRR
        trail_irrep = jnp.bitwise_xor(sym_block, lead_irrep)
        leading = lax.dynamic_index_in_dim(vectors, lead_irrep, 1, keepdims=False)
        trailing = lax.dynamic_index_in_dim(vectors, trail_irrep, 1, keepdims=False)
        chosen = lax.dynamic_index_in_dim(blocks, sym_block, 0, keepdims=False)
        chosen = lax.dynamic_index_in_dim(chosen, lead_irrep, 1, keepdims=False)
        row_live = lax.dynamic_index_in_dim(live_mask, lead_irrep, 0, keepdims=False)
        col_live = lax.dynamic_index_in_dim(live_mask, trail_irrep, 0, keepdims=False)
        chosen = chosen * (row_live[:, None] & col_live[None, :]).astype(amplitudes.dtype)[None]
        halfway = jnp.einsum('pac,icd->ipad', leading.astype(jnp.float32), chosen.astype(jnp.float32))
        halfway = lax.optimization_barrier(halfway.astype(jnp.bfloat16))
        return jnp.einsum('ipad,pbd->iab', halfway.astype(jnp.float32), trailing.astype(jnp.float32))

    combos = jnp.arange(NIRR * NIRR, dtype=jnp.int32)
    result = lax.map(one_block, combos)
    result = result.reshape(NIRR, NIRR, NPAIR, VMAX, VMAX).transpose(0, 2, 1, 3, 4)
    return result.reshape(NIRR, NPAIR, NIRR * VMAX, VMAX)
```

```python
import jax
import jax.numpy as jnp
from jax import lax
from jax.experimental import pallas as pl
from jax.experimental.pallas import tpu as pltpu
from jax.sharding import PartitionSpec as P

MESH = pl.DeviceIdType.MESH
V = 384
NI = 8
ORDER = (0, 1, 3, 2)
DIRECTION = {0: 1, 1: -1, 3: 1, 2: -1}
N_SEND = 50


def kernel(dims, mine, amps, out, own, par, rc, half, t1, t2, t3, tc,
           ssem, own_sem, own_d, par_sem, par_d, t1_sem, t2_sem, t3_sem, tc_sem, cross_sem, local_sem):
    sym, tile, c = lax.axis_index("sym"), lax.axis_index("tile"), lax.axis_index("occ")
    x, yhi = sym % 4, sym // 4
    x0, x1 = x % 2, x // 2
    z, ylo = tile // 2, tile % 2
    z0, z1 = z % 2, z // 2
    y = 2 * yhi + ylo

    def dev(dx=0, dy=0, dz=0, dc=0):
        xx, yy, zz = (x + 4 + dx) % 4, (y + 4 + dy) % 4, (z + 4 + dz) % 4
        return {"sym": (yy // 2) * 4 + xx, "tile": zz * 2 + yy % 2, "occ": (c + dc) % 2}

    barrier = pltpu.get_barrier_semaphore()
    for where in (dev(dx=1), dev(dx=-1), dev(dy=1), dev(dy=-1), dev(dz=1), dev(dz=-1), dev(dc=1)):
        pl.semaphore_signal(barrier, inc=1, device_id=where, device_id_type=MESH)

    keep = pltpu.make_async_copy(mine, own.at[sym, c], local_sem.at[8])
    keep.start()
    loads = [pltpu.make_async_copy(amps.at[i], rc.at[:, pl.ds(i * V, V)], local_sem.at[i]) for i in range(NI)]
    for load in loads:
        load.start()
    pl.semaphore_wait(barrier, 7)

    pending = []

    def send(src, dst, where, index, recv, cond=None):
        def go():
            pltpu.make_async_remote_copy(src, dst, ssem.at[index], recv, device_id=where, device_id_type=MESH).start()

        if cond is None:
            go()
        else:
            pl.when(cond)(go)

        def done():
            pltpu.make_async_remote_copy(src, dst, ssem.at[index], recv, device_id=where, device_id_type=MESH).wait_send()

        pending.append((cond, done))

    def arrived(dst, recv):
        pltpu.make_async_remote_copy(dst, dst, ssem.at[0], recv, device_id=dev(dc=1), device_id_type=MESH).wait_recv()

    is_x = [x == k for k in range(4)]
    hi, lo = yhi == 1, yhi == 0
    none = jnp.logical_and(x == 0, lo)
    step_a = 1 - 2 * (yhi + ylo - 2 * yhi * ylo)
    dz_a, dz_b = 1 - 2 * z0, 2 * z0 - 1

    def q_row(j, row):
        return row * 4 + (x + 4 - j) % 4

    def feed(j, src):
        q = q_row(j, yhi)
        a, b = 26 + j, 30 + j
        two = DIRECTION[j]
        send(src, t1.at[j], dev(dz=two), b, t1_sem.at[j], x1 == 0)
        send(src, par.at[q, c], dev(dy=step_a), a, par_sem.at[q], is_x[1])
        send(src, par.at[q, c], dev(dz=dz_a), a, par_sem.at[q], is_x[2] & lo)
        send(src, t1.at[j], dev(dz=dz_a), a, t1_sem.at[j], is_x[3] | (is_x[2] & hi))
        send(src, par.at[q, c], dev(dz=dz_b), b, par_sem.at[q], is_x[2] & hi)
        send(src, t2.at[j], dev(dz=dz_b), b, t2_sem.at[j], is_x[3] | (is_x[2] & lo))

    def pass_z(j):
        two = DIRECTION[j]
        q = q_row(j, yhi)

        @pl.when(x1 == 0)
        def _():
            arrived(t1.at[j], t1_sem.at[j])

        send(t1.at[j], t2.at[j], dev(dz=two), 34 + j, t2_sem.at[j], is_x[1] | (is_x[0] & lo))
        send(t1.at[j], par.at[q, c], dev(dz=two), 34 + j, par_sem.at[q], is_x[0] & hi)

    def forward_y(j):
        two = DIRECTION[j]
        q = q_row(j, yhi)
        has1 = is_x[3] | (is_x[2] & hi)
        has2 = x0 == 1

        @pl.when(has1)
        def _():
            arrived(t1.at[j], t1_sem.at[j])

        @pl.when(has2 | lo)
        def _():
            arrived(t2.at[j], t2_sem.at[j])

        send(t1.at[j], par.at[q, c], dev(dy=step_a), 38 + j, par_sem.at[q], is_x[3])
        send(t1.at[j], t3.at[j], dev(dy=two), 38 + j, t3_sem.at[j], is_x[2] & hi)
        send(t2.at[j], par.at[q, c], dev(dy=-step_a), 42 + j, par_sem.at[q], has2)
        send(t2.at[j], t3.at[j], dev(dy=two), 42 + j, t3_sem.at[j], (x0 == 0) & lo)

    def pass_y(j):
        two = DIRECTION[j]
        row = ((y + 4 - two) % 4) // 2
        q = q_row(j, row)
        active = is_x[2] | (is_x[0] & (row == 0))

        @pl.when(active)
        def _():
            arrived(t3.at[j], t3_sem.at[j])

        send(t3.at[j], par.at[q, c], dev(dy=two), 46 + j, par_sem.at[q], active)

    def share_own(q, index):
        send(own.at[q, c], own.at[q, c], dev(dc=1), index, own_d.at[q])

    def take_own(j, row, slot):
        q = q_row(j, row)
        arrived(own.at[q, c], own_sem.at[q])
        share_own(q, 10 + slot)
        return q

    def share_par(j, row, slot):
        q = q_row(j, row)

        @pl.when(jnp.logical_not(none))
        def _():
            arrived(par.at[q, c], par_sem.at[q])

        send(par.at[q, c], par.at[q, c], dev(dc=1), 18 + slot, par_d.at[q], jnp.logical_not(none))

    def first_stage(q):
        arrived(own.at[q, 1 - c], own_d.at[q])

        @pl.loop(0, NI // 2)
        def _(m):
            left = own[q].reshape(2 * V, V)
            r = jnp.dot(left, rc[:, pl.ds(pl.multiple_of(m * (2 * V), 2 * V), 2 * V)], preferred_element_type=jnp.float32)
            r = r.astype(jnp.bfloat16)
            for k in range(2):
                for p in range(2):
                    rows = pl.ds(pl.multiple_of((2 * m + k) * V, V), V)
                    half[q, rows, p * V:(p + 1) * V] = r[p * V:(p + 1) * V, k * V:(k + 1) * V]

    def second_stage(q, first=False):
        @pl.when(jnp.logical_not(none))
        def _():
            arrived(par.at[q, 1 - c], par_d.at[q])

        @pl.when(none)
        def _():
            copy = pltpu.make_async_copy(own.at[q], par.at[q], local_sem.at[9])
            copy.start()
            copy.wait()

        @pl.loop(0, NI // 2)
        def _(m):
            rows = pl.ds(pl.multiple_of(m * (2 * V), 2 * V), 2 * V)
            right = jnp.concatenate([par[q, 0], par[q, 1]], axis=1)
            r = lax.dot_general(half[q, rows, :], right, (((1,), (1,)), ((), ())), preferred_element_type=jnp.float32)
            if first:
                out[rows, :] = r
            else:
                out[rows, :] += r

    other = 1 - yhi
    send(mine, own.at[sym, c], dev(dc=1), 10, own_d.at[sym])
    send(mine, own.at[sym, c], dev(dx=1), 0, own_sem.at[sym])
    send(mine, own.at[sym, c], dev(dx=-1), 1, own_sem.at[sym])
    upper, lower = pl.ds(0, V // 2), pl.ds(V // 2, V // 2)
    send(mine.at[upper], tc.at[0], dev(dy=1), 2, tc_sem.at[0])
    send(mine.at[lower], tc.at[1], dev(dy=-1), 3, tc_sem.at[1])
    feed(0, mine)

    n_row = dims[tile]
    n_col = dims[(z1 + yhi - 2 * z1 * yhi) * 4 + (z0 + x1 - 2 * z0 * x1) * 2 + (ylo + x0 - 2 * ylo * x0)]
    live_r = jnp.where(lax.broadcasted_iota(jnp.int32, (V, V), 0) < n_row, 1.0, 0.0)
    live = jnp.where(lax.broadcasted_iota(jnp.int32, (V, V), 1) < n_col, live_r, 0.0).astype(jnp.bfloat16)
    for load in loads:
        load.wait()
    for i in range(NI):
        rc[:, i * V:(i + 1) * V] = rc[:, i * V:(i + 1) * V] * live
    keep.wait()

    first_stage(q_row(0, yhi))

    for k, step in ((0, 1), (1, -1)):
        arrived(tc.at[k], tc_sem.at[k])
        source = ((y + 4 - step) % 4) // 2
        rows = upper if k == 0 else lower
        send(tc.at[k], own.at[source * 4 + x, c, rows], dev(dy=step), 4 + k, cross_sem.at[k])

    q = take_own(1, yhi, 1)
    send(own.at[q, c], own.at[q, c], dev(dx=1), 6, own_sem.at[q])
    feed(1, own.at[q, c])
    q = take_own(3, yhi, 3)
    feed(3, own.at[q, c])
    first_stage(q_row(1, yhi))

    q = q_row(0, other)
    arrived(own.at[q, c, upper], cross_sem.at[0])
    arrived(own.at[q, c, lower], cross_sem.at[1])
    send(own.at[q, c], own.at[q, c], dev(dx=1), 7, own_sem.at[q])
    send(own.at[q, c], own.at[q, c], dev(dx=-1), 8, own_sem.at[q])
    share_own(q, 14)
    pass_z(0)
    forward_y(0)
    first_stage(q_row(3, yhi))

    q = take_own(2, yhi, 2)
    feed(2, own.at[q, c])
    pass_z(1)
    pass_z(3)
    pass_y(0)
    first_stage(q_row(2, yhi))

    forward_y(1)
    forward_y(3)
    share_par(0, yhi, 0)
    share_par(0, other, 4)
    first_stage(q_row(0, other))

    pass_z(2)
    second_stage(q_row(0, yhi), first=True)

    q = take_own(1, other, 5)
    q = take_own(3, other, 7)
    send(own.at[q, c], own.at[q, c], dev(dx=-1), 9, own_sem.at[q])
    forward_y(2)
    pass_y(1)
    pass_y(3)
    first_stage(q_row(1, other))
    share_par(1, yhi, 1)
    share_par(1, other, 5)
    second_stage(q_row(0, other))
    pass_y(2)
    take_own(2, other, 6)
    first_stage(q_row(3, other))
    share_par(3, yhi, 3)
    share_par(3, other, 7)
    second_stage(q_row(1, yhi))
    second_stage(q_row(1, other))
    share_par(2, yhi, 2)
    share_par(2, other, 6)
    first_stage(q_row(2, other))
    second_stage(q_row(3, yhi))
    second_stage(q_row(3, other))
    second_stage(q_row(2, yhi))
    second_stage(q_row(2, other))

    for cond, done in pending:
        if cond is None:
            done()
        else:
            pl.when(cond)(done)


def shards(irrep_dims, chol_vectors, amplitudes):
    bf, sem = jnp.bfloat16, pltpu.SemaphoreType.DMA
    raw = pl.pallas_call(
        kernel,
        out_shape=jax.ShapeDtypeStruct((NI * V, V), jnp.float32),
        in_specs=[
            pl.BlockSpec(memory_space=pltpu.SMEM),
            pl.BlockSpec(memory_space=pl.ANY),
            pl.BlockSpec(memory_space=pl.ANY),
        ],
        out_specs=pl.BlockSpec(memory_space=pltpu.VMEM),
        scratch_shapes=[
            pltpu.VMEM((8, 2, V, V), bf),
            pltpu.VMEM((8, 2, V, V), bf),
            pltpu.VMEM((V, NI * V), bf),
            pltpu.VMEM((8, NI * V, 2 * V), bf),
            pltpu.VMEM((4, V, V), bf),
            pltpu.VMEM((4, V, V), bf),
            pltpu.VMEM((4, V, V), bf),
            pltpu.VMEM((2, V // 2, V), bf),
            sem((N_SEND,)), sem((8,)), sem((8,)), sem((8,)), sem((8,)),
            sem((4,)), sem((4,)), sem((4,)), sem((2,)), sem((2,)), sem((10,)),
        ],
        compiler_params=pltpu.CompilerParams(
            collective_id=0, has_side_effects=True, vmem_limit_bytes=63 * 1024 * 1024
        ),
        cost_estimate=pl.CostEstimate(flops=29_000_000_000, bytes_accessed=7_500_000, transcendentals=0),
        name="ladder",
    )(irrep_dims, chol_vectors.reshape(V, V), amplitudes.reshape(NI, V, V))
    sym, tile = lax.axis_index("sym"), lax.axis_index("tile")
    row = jnp.arange(V, dtype=jnp.int32)
    live_a = row < irrep_dims[tile]
    live_b = row < irrep_dims[jnp.bitwise_xor(tile, sym)]
    live = live_a[:, None] & live_b[None, :]
    return jnp.where(live[None, None], raw.reshape(1, NI, V, V), 0.0)


def solution(mesh):
    return jax.shard_map(
        shards,
        mesh=mesh,
        in_specs=(P(), P(("sym", "occ"), "tile", None), P("sym", "occ", "tile", None)),
        out_specs=P("sym", "occ", "tile", None),
        check_vma=False,
    )
```

```python
import functools

import jax
import jax.numpy as jnp
from jax import lax
from jax.experimental import pallas as pl
from jax.experimental.pallas import tpu as pltpu
from jax.sharding import PartitionSpec as P

MESH = pl.DeviceIdType.MESH
V = 384
NI = 8
PIECES = 2
PV = V // PIECES
STEPS = 4
CROSSF, OWN, PASS_Z, FWD_Y, PASS_Y, PAR = range(6)
SEQUENCE = (
    (1, 0, 0),
    (1, 0, 2),
    (1, 0, 3),
    (1, 0, 1),
    (2, 0, 0),
    (1, 1, 0),
    (2, 1, 0),
    (1, 1, 1),
    (1, 1, 3),
    (2, 0, 3),
    (2, 0, 1),
    (2, 1, 1),
    (2, 1, 3),
    (2, 0, 2),
    (1, 1, 2),
    (2, 1, 2),
)
EVENTS = {
    0: (
        (4, ((CROSSF, 0), (CROSSF, 1), (OWN, 0, 1, 0), (OWN, 0, 3, 0), (PASS_Z, 0, 0), (PASS_Z, 0, 1), (OWN, 0, 1, 1), (OWN, 0, 3, 1), (OWN, 1, 0, 0), (OWN, 1, 0, 1), (PASS_Z, 1, 0), (PASS_Z, 3, 0), (OWN, 0, 2, 0), (OWN, 0, 2, 1), (FWD_Y, 0, 1), (PAR, 0, 0, 1), (FWD_Y, 0, 0), (PAR, 0, 0, 0),)),
        (6, ((OWN, 1, 1, 0),)),
        (8, ((PASS_Z, 1, 1), (PASS_Z, 3, 1),)),
        (9, ((PASS_Y, 0, 1), (PASS_Y, 0, 0),)),
        (10, ((OWN, 1, 1, 1),)),
        (12, ((OWN, 1, 3, 0), (FWD_Y, 1, 0), (FWD_Y, 3, 0), (PAR, 0, 1, 0), (PAR, 0, 3, 0),)),
        (15, ((PAR, 1, 0, 0), (PAR, 1, 0, 1),)),
        (16, ((OWN, 1, 2, 1), (PASS_Z, 2, 0), (PASS_Z, 2, 1),)),
        (19, ((PASS_Y, 1, 0), (PASS_Y, 3, 0),)),
        (20, ((OWN, 1, 2, 0), (FWD_Y, 1, 1), (FWD_Y, 3, 1), (PAR, 0, 1, 1), (PAR, 0, 3, 1),)),
        (25, ((FWD_Y, 2, 0), (FWD_Y, 2, 1), (PAR, 0, 2, 0), (PAR, 0, 2, 1), (PAR, 1, 3, 0), (PAR, 1, 1, 0),)),
        (28, ((OWN, 1, 3, 1), (PASS_Y, 3, 1), (PASS_Y, 1, 1),)),
        (33, ((PASS_Y, 2, 0), (PASS_Y, 2, 1),)),
        (37, ((PAR, 1, 3, 1), (PAR, 1, 1, 1),)),
        (41, ((PAR, 1, 2, 0), (PAR, 1, 2, 1),)),
    ),
    1: (
        (4, ((CROSSF, 0), (OWN, 0, 1, 0), (OWN, 0, 3, 0), (PASS_Z, 0, 0), (PASS_Z, 0, 1), (OWN, 0, 1, 1), (OWN, 0, 3, 1), (CROSSF, 1), (PASS_Z, 1, 0), (PASS_Z, 3, 0), (OWN, 0, 2, 0), (OWN, 0, 2, 1), (FWD_Y, 0, 1), (FWD_Y, 0, 0),)),
        (5, ((OWN, 1, 0, 0),)),
        (6, ((OWN, 1, 1, 0),)),
        (7, ((OWN, 1, 3, 0),)),
        (8, ((PASS_Z, 1, 1), (PASS_Z, 3, 1),)),
        (9, ((PAR, 0, 0, 1), (PAR, 1, 0, 1),)),
        (10, ((OWN, 1, 1, 1),)),
        (11, ((OWN, 1, 3, 1),)),
        (12, ((FWD_Y, 1, 0), (FWD_Y, 3, 0),)),
        (13, ((PAR, 0, 0, 0), (PAR, 1, 0, 0),)),
        (15, ((OWN, 1, 2, 0),)),
        (16, ((OWN, 1, 2, 1), (PASS_Z, 2, 0), (PASS_Z, 2, 1),)),
        (18, ((PAR, 0, 1, 0), (PAR, 1, 1, 0),)),
        (20, ((FWD_Y, 1, 1), (FWD_Y, 3, 1), (OWN, 1, 0, 1),)),
        (22, ((PAR, 0, 3, 0), (PAR, 1, 3, 0),)),
        (24, ((FWD_Y, 2, 0), (FWD_Y, 2, 1),)),
        (26, ((PAR, 0, 1, 1), (PAR, 1, 1, 1),)),
        (30, ((PAR, 1, 3, 1),)),
        (31, ((PAR, 0, 3, 1),)),
        (35, ((PAR, 0, 2, 0), (PAR, 1, 2, 0),)),
        (39, ((PAR, 0, 2, 1), (PAR, 1, 2, 1),)),
    ),
    2: (
        (4, ((CROSSF, 0), (CROSSF, 1), (OWN, 0, 1, 0), (OWN, 0, 3, 0), (FWD_Y, 0, 0), (PAR, 0, 0, 0), (OWN, 0, 1, 1), (OWN, 0, 3, 1), (PAR, 0, 0, 1), (FWD_Y, 0, 1), (OWN, 1, 0, 0), (OWN, 1, 0, 1), (OWN, 0, 2, 0), (PAR, 0, 1, 0), (FWD_Y, 1, 0), (OWN, 0, 2, 1), (PASS_Y, 0, 0), (PASS_Y, 0, 1),)),
        (6, ((FWD_Y, 3, 0), (PAR, 0, 3, 0),)),
        (7, ((OWN, 1, 3, 0),)),
        (8, ((PASS_Y, 1, 0),)),
        (9, ((PAR, 1, 0, 0),)),
        (10, ((FWD_Y, 1, 1), (PAR, 0, 1, 1),)),
        (11, ((OWN, 1, 1, 0), (OWN, 1, 3, 1),)),
        (12, ((PAR, 1, 0, 1),)),
        (13, ((PASS_Y, 3, 0),)),
        (14, ((FWD_Y, 3, 1), (PAR, 0, 3, 1),)),
        (15, ((OWN, 1, 2, 0),)),
        (16, ((PAR, 1, 1, 0),)),
        (17, ((PASS_Y, 1, 1),)),
        (18, ((FWD_Y, 2, 0), (PAR, 0, 2, 0),)),
        (20, ((OWN, 1, 2, 1), (PASS_Y, 3, 1),)),
        (21, ((PAR, 1, 3, 0),)),
        (23, ((FWD_Y, 2, 1), (PAR, 0, 2, 1),)),
        (24, ((PASS_Y, 2, 0),)),
        (25, ((PAR, 1, 1, 1),)),
        (28, ((OWN, 1, 1, 1), (PAR, 1, 3, 1),)),
        (30, ((PASS_Y, 2, 1),)),
        (33, ((PAR, 1, 2, 0),)),
        (36, ((PAR, 1, 2, 1),)),
    ),
    3: (
        (4, ((CROSSF, 0), (CROSSF, 1), (OWN, 0, 1, 0), (OWN, 0, 3, 0), (FWD_Y, 0, 0), (OWN, 0, 1, 1), (OWN, 0, 3, 1), (FWD_Y, 0, 1), (OWN, 1, 0, 0), (OWN, 1, 0, 1), (OWN, 0, 2, 0), (FWD_Y, 1, 0), (OWN, 0, 2, 1), (PAR, 1, 0, 0), (PAR, 0, 0, 0),)),
        (6, ((OWN, 1, 1, 0), (FWD_Y, 3, 0),)),
        (7, ((OWN, 1, 3, 0),)),
        (8, ((PAR, 0, 0, 1), (PAR, 1, 0, 1),)),
        (10, ((OWN, 1, 1, 1), (FWD_Y, 1, 1),)),
        (11, ((OWN, 1, 3, 1),)),
        (12, ((PAR, 0, 1, 0), (PAR, 1, 1, 0),)),
        (14, ((FWD_Y, 3, 1),)),
        (16, ((PAR, 0, 3, 0), (PAR, 1, 3, 0),)),
        (18, ((OWN, 1, 2, 0), (FWD_Y, 2, 0),)),
        (20, ((PAR, 0, 1, 1), (PAR, 1, 1, 1),)),
        (23, ((FWD_Y, 2, 1),)),
        (24, ((PAR, 0, 3, 1), (PAR, 1, 3, 1),)),
        (28, ((PAR, 0, 2, 0), (PAR, 1, 2, 0),)),
        (33, ((PAR, 0, 2, 1), (PAR, 1, 2, 1),)),
        (34, ((OWN, 1, 2, 1),)),
    ),
}


def kernel(dims, mine, amps, out, own, par, rc, half, acc, t1, t2, t3, tc,
           ssem, own_sem, own_d, par_sem, par_d, t1_sem, t2_sem, t3_sem, tc_sem, cross_sem, local_sem):
    sym, tile, c = lax.axis_index("sym"), lax.axis_index("tile"), lax.axis_index("occ")
    x, yhi = sym % 4, sym // 4
    x0, x1 = x % 2, x // 2
    z, ylo = tile // 2, tile % 2
    z0, z1 = z % 2, z // 2
    y = 2 * yhi + ylo

    def dev(dx=0, dy=0, dz=0, dc=0):
        xx, yy, zz = (x + 4 + dx) % 4, (y + 4 + dy) % 4, (z + 4 + dz) % 4
        return {"sym": (yy // 2) * 4 + xx, "tile": zz * 2 + yy % 2, "occ": (c + dc) % 2}

    step_a = 1 - 2 * (yhi + ylo - 2 * yhi * ylo)
    step_z = 1 - 2 * z0
    to = {
        "x+": dev(dx=1), "x-": dev(dx=-1), "y+": dev(dy=1), "y-": dev(dy=-1), "z+": dev(dz=1), "z-": dev(dz=-1),
        "core": dev(dc=1), "ya": dev(dy=step_a), "yb": dev(dy=-step_a), "za": dev(dz=step_z), "zb": dev(dz=-step_z),
    }
    barrier = pltpu.get_barrier_semaphore()
    for name in ("x+", "x-", "y+", "y-", "z+", "z-", "core"):
        pl.semaphore_signal(barrier, inc=1, device_id=to[name], device_id_type=MESH)

    keep = pltpu.make_async_copy(mine, own.at[sym, c], local_sem.at[8])
    keep.start()
    loads = [pltpu.make_async_copy(amps.at[i], rc.at[:, pl.ds(i * V, V)], local_sem.at[i]) for i in range(NI)]
    for load in loads:
        load.start()

    hi, lo = yhi == 1, yhi == 0
    is_x = [x == k for k in range(4)]
    none = jnp.logical_and(x == 0, lo)
    row_of = {0: yhi, 1: 1 - yhi}
    name_of = {(row, j): row_of[row] * 4 + (x + 4 - j) % 4 for row in range(2) for j in range(4)}
    row_behind = {"+": ((y + 3) % 4) // 2, "-": ((y + 1) % 4) // 2}
    name_behind = {(sign, j): row_behind[sign] * 4 + (x + 4 - j) % 4 for sign in "+-" for j in range(4)}
    from_lo = {sign: row_behind[sign] == 0 for sign in "+-"}
    piece = [pl.ds(k * PV, PV) for k in range(PIECES)]
    pl.semaphore_wait(barrier, 7)

    sent = {None: [], 0: [], 1: [], 2: [], 3: []}

    def sign_of(j, k):
        return "+" if (k + (0, 1, 1, 0)[j]) % 2 == 0 else "-"

    def send(cls, make, cond=None):
        index = len(sent[None]) if cls is None else 12 + len(sent[cls])

        def copy():
            src, dst, where, recv = make()
            return pltpu.make_async_remote_copy(
                src, dst, ssem.at[index], recv, device_id=to[where], device_id_type=MESH
            )

        if cond is None:
            copy().start()
        else:
            pl.when(cond)(lambda: copy().start())
        sent[cls].append((cond, copy))

    def arrived(dst, recv, cond=None):
        def wait():
            pltpu.make_async_remote_copy(
                dst, dst, ssem.at[0], recv, device_id=to["core"], device_id_type=MESH
            ).wait_recv()

        if cond is None:
            wait()
        else:
            pl.when(cond)(wait)

    def unit(buffer, q, k):
        return buffer.at[q, c, piece[k]]

    def feed(cls, j, k, src):
        q = name_of[0, j]
        final = lambda where: lambda: (src(), unit(par, q, k), where, par_sem.at[q, k])
        via1 = lambda where: lambda: (src(), t1.at[j, piece[k]], where, t1_sem.at[j, k])
        via2 = lambda where: lambda: (src(), t2.at[j, piece[k]], where, t2_sem.at[j, k])
        if cls in (0, 1):
            send(cls, via1("z" + sign_of(j, k)))
        if cls == 1:
            send(cls, final("ya"))
        if cls == 2:
            send(cls, final("za"), lo)
            send(cls, via1("za"), hi)
            send(cls, via2("zb"), lo)
            send(cls, final("zb"), hi)
        if cls == 3:
            send(cls, via1("za"))
            send(cls, via2("zb"))

    def event(cls, kind, *args):
        if kind == CROSSF:
            (k,) = args
            sign = "+-"[k]
            arrived(tc.at[piece[k]], tc_sem.at[k])
            send(cls, lambda: (tc.at[piece[k]], own.at[row_behind[sign] * 4 + x, c, piece[k]], "y" + sign, cross_sem.at[k]))
        if kind == OWN:
            row, j, k = args
            q = name_of[row, j]
            here = lambda: unit(own, q, k)
            arrived(here(), cross_sem.at[k] if (row, j) == (1, 0) else own_sem.at[q, k])
            if (row, j) == (1, 0) or (j == 1 and (k + row) % 2 == 0):
                send(cls, lambda: (here(), here(), "x+", own_sem.at[q, k]))
            if (row, j) == (1, 0) or (j == 3 and (k + row) % 2 == 1):
                send(cls, lambda: (here(), here(), "x-", own_sem.at[q, k]))
            if row == 0:
                feed(cls, j, k, here)
            send(cls, lambda: (here(), here(), "core", own_d.at[q, k]))
        if kind == PASS_Z:
            j, k = args
            q = name_of[0, j]
            way = "z" + sign_of(j, k)
            here = lambda: t1.at[j, piece[k]]
            arrived(here(), t1_sem.at[j, k])
            on = lambda: (here(), t2.at[j, piece[k]], way, t2_sem.at[j, k])
            if cls == 1:
                send(cls, on)
            else:
                send(cls, on, lo)
                send(cls, lambda: (here(), unit(par, q, k), way, par_sem.at[q, k]), hi)
        if kind == FWD_Y:
            j, k = args
            q = name_of[0, j]
            way = "y" + sign_of(j, k)
            here1, here2 = (lambda: t1.at[j, piece[k]]), (lambda: t2.at[j, piece[k]])
            if cls in (2, 3):
                cond = None if cls == 3 else hi
                arrived(here1(), t1_sem.at[j, k], cond)
                if cls == 3:
                    send(cls, lambda: (here1(), unit(par, q, k), "ya", par_sem.at[q, k]))
                else:
                    send(cls, lambda: (here1(), t3.at[j, piece[k]], way, t3_sem.at[j, k]), hi)
            if cls in (1, 3):
                arrived(here2(), t2_sem.at[j, k])
                send(cls, lambda: (here2(), unit(par, q, k), "yb", par_sem.at[q, k]))
            else:
                arrived(here2(), t2_sem.at[j, k], lo)
                send(cls, lambda: (here2(), t3.at[j, piece[k]], way, t3_sem.at[j, k]), lo)
        if kind == PASS_Y:
            j, k = args
            sign = sign_of(j, k)
            q = name_behind[sign, j]
            cond = None if cls == 2 else from_lo[sign]
            arrived(t3.at[j, piece[k]], t3_sem.at[j, k], cond)
            send(cls, lambda: (t3.at[j, piece[k]], unit(par, q, k), "y" + sign, par_sem.at[q, k]), cond)
        if kind == PAR:
            row, j, k = args
            q = name_of[row, j]
            here = lambda: unit(par, q, k)
            cond = hi if cls == 0 else None
            arrived(here(), par_sem.at[q, k], cond)
            send(cls, lambda: (here(), here(), "core", par_d.at[q, k]), cond)

    def events(n):
        for cls in range(4):
            todo = dict(EVENTS[cls]).get(n, ())
            if todo:
                @pl.when(is_x[cls])
                def _():
                    for entry in todo:
                        event(cls, *entry)

    def events_within(base, m):
        for k in range(1, STEPS):
            if any(base + k in dict(EVENTS[cls]) for cls in range(4)):
                pl.when(m == k)(functools.partial(events, base + k))

    def first_stage(base, row, j):
        q = name_of[row, j]
        events(base)
        for k in range(PIECES):
            arrived(own.at[q, 1 - c, piece[k]], own_d.at[q, k])

        @pl.when(none)
        def _():
            pltpu.make_async_copy(own.at[q], par.at[q], local_sem.at[9 + q]).start()

        @pl.loop(0, STEPS)
        def _(m):
            events_within(base, m)
            for t in range(3):
                cols = pl.ds(pl.multiple_of(m * (2 * V) + t * 256, 256), 256)
                r = jnp.dot(own[q].reshape(2 * V, V), rc[:, cols], preferred_element_type=jnp.float32)
                r = r.astype(jnp.bfloat16)
                for lo_col, hi_col, pair, at in (((0, 256, 0, 0),), ((0, 128, 0, 256), (128, 256, 1, 0)), ((0, 256, 1, 128),))[t]:
                    rows = pl.ds(pl.multiple_of((2 * m + pair) * V, V), V)
                    for p in range(2):
                        lanes = pl.ds(p * V + at, hi_col - lo_col)
                        half[q, rows, lanes] = r[p * V:(p + 1) * V, lo_col:hi_col]

    def second_stage(base, row, j):
        q = name_of[row, j]
        events(base)
        for k in range(PIECES):
            arrived(par.at[q, 1 - c, piece[k]], par_d.at[q, k], jnp.logical_not(none))
        start, last = base == FIRST_SUM, base == STEPS * (len(SEQUENCE) - 1)

        @pl.when(none)
        def _():
            pltpu.make_async_copy(own.at[q], par.at[q], local_sem.at[9 + q]).wait()

        @pl.loop(0, STEPS)
        def _(m):
            events_within(base, m)
            rows = pl.ds(pl.multiple_of(m * (2 * V), 2 * V), 2 * V)
            for b0, b1 in ((0, 256), (256, 384)):
                right = jnp.concatenate([par[q, 0, b0:b1], par[q, 1, b0:b1]], axis=1)
                r = lax.dot_general(half[q, rows, :], right, (((1,), (1,)), ((), ())), preferred_element_type=jnp.float32)
                if start:
                    acc[rows, b0:b1] = r
                else:
                    acc[rows, b0:b1] += r
            if last:
                pltpu.make_async_copy(acc.at[rows], out.at[rows], local_sem.at[m]).start()

    for k in range(PIECES):
        src = mine.at[piece[k]]
        home = own.at[sym, c, piece[k]]
        send(None, lambda src=src, home=home, k=k: (src, home, "core", own_d.at[sym, k]))
    for k in range(PIECES):
        src = mine.at[piece[k]]
        home = own.at[sym, c, piece[k]]
        for way in ("x+", "x-"):
            send(None, lambda src=src, home=home, k=k, way=way: (src, home, way, own_sem.at[sym, k]))
        send(None, lambda src=src, k=k: (src, tc.at[piece[k]], "y" + "+-"[k], tc_sem.at[k]))
        for cls in range(4):
            @pl.when(is_x[cls])
            def _():
                feed(cls, 0, k, lambda src=src: src)

    n_row = dims[tile]
    n_col = dims[(z1 + yhi - 2 * z1 * yhi) * 4 + (z0 + x1 - 2 * z0 * x1) * 2 + (ylo + x0 - 2 * ylo * x0)]
    live_r = jnp.where(lax.broadcasted_iota(jnp.int32, (V, V), 0) < n_row, 1.0, 0.0)
    live = jnp.where(lax.broadcasted_iota(jnp.int32, (V, V), 1) < n_col, live_r, 0.0).astype(jnp.bfloat16)
    for load in loads:
        load.wait()
    for i in range(NI):
        rc[:, i * V:(i + 1) * V] = rc[:, i * V:(i + 1) * V] * live
    keep.wait()

    for number, (stage, row, j) in enumerate(SEQUENCE):
        (first_stage if stage == 1 else second_stage)(STEPS * number, row, j)
    events(STEPS * len(SEQUENCE))

    for cls, entries in sent.items():
        def finish(entries=entries):
            for cond, copy in entries:
                if cond is None:
                    copy().wait_send()
                else:
                    pl.when(cond)(lambda copy=copy: copy().wait_send())

        if cls is None:
            finish()
        else:
            pl.when(is_x[cls])(finish)
    for m in range(STEPS):
        rows = pl.ds(m * (2 * V), 2 * V)
        pltpu.make_async_copy(acc.at[rows], out.at[rows], local_sem.at[m]).wait()


FIRST_SUM = STEPS * [stage for stage, _, _ in SEQUENCE].index(2)


def mask_kernel(dims, raw, out):
    sym, tile = lax.axis_index("sym"), lax.axis_index("tile")
    n_row, n_col = dims[tile], dims[jnp.bitwise_xor(tile, sym)]
    live = (lax.broadcasted_iota(jnp.int32, (V, V), 0) < n_row) & (lax.broadcasted_iota(jnp.int32, (V, V), 1) < n_col)
    out[0, 0] = jnp.where(live, raw[...], 0.0)


def shards(irrep_dims, chol_vectors, amplitudes):
    bf, sem = jnp.bfloat16, pltpu.SemaphoreType.DMA
    raw = pl.pallas_call(
        kernel,
        out_shape=jax.ShapeDtypeStruct((NI * V, V), jnp.float32),
        in_specs=[
            pl.BlockSpec(memory_space=pltpu.SMEM),
            pl.BlockSpec(memory_space=pl.ANY),
            pl.BlockSpec(memory_space=pl.ANY),
        ],
        out_specs=pl.BlockSpec(memory_space=pl.ANY),
        scratch_shapes=[
            pltpu.VMEM((8, 2, V, V), bf),
            pltpu.VMEM((8, 2, V, V), bf),
            pltpu.VMEM((V, NI * V), bf),
            pltpu.VMEM((8, NI * V, 2 * V), bf),
            pltpu.VMEM((NI * V, V), jnp.float32),
            pltpu.VMEM((4, V, V), bf),
            pltpu.VMEM((4, V, V), bf),
            pltpu.VMEM((4, V, V), bf),
            pltpu.VMEM((V, V), bf),
            sem((136,)), sem((8, PIECES)), sem((8, PIECES)), sem((8, PIECES)), sem((8, PIECES)),
            sem((4, PIECES)), sem((4, PIECES)), sem((4, PIECES)), sem((2,)), sem((2,)), sem((17,)),
        ],
        compiler_params=pltpu.CompilerParams(
            collective_id=0, has_side_effects=True, vmem_limit_bytes=63 * 1024 * 1024
        ),
        cost_estimate=pl.CostEstimate(flops=29_000_000_000, bytes_accessed=7_500_000, transcendentals=0),
        name="ladder",
    )(irrep_dims, chol_vectors.reshape(V, V), amplitudes.reshape(NI, V, V))
    return pl.pallas_call(
        mask_kernel,
        grid=(NI,),
        out_shape=jax.ShapeDtypeStruct((1, NI, V, V), jnp.float32),
        in_specs=[pl.BlockSpec(memory_space=pltpu.SMEM), pl.BlockSpec((V, V), lambda i: (i, 0))],
        out_specs=pl.BlockSpec((1, 1, V, V), lambda i: (0, i, 0, 0)),
        name="live",
    )(irrep_dims, raw)


def solution(mesh):
    return jax.shard_map(
        shards,
        mesh=mesh,
        in_specs=(P(), P(("sym", "occ"), "tile", None), P("sym", "occ", "tile", None)),
        out_specs=P("sym", "occ", "tile", None),
        check_vma=False,
    )
```

```python
import functools

import jax
import jax.numpy as jnp
from jax import lax
from jax.experimental import pallas as pl
from jax.experimental.pallas import tpu as pltpu
from jax.sharding import PartitionSpec as P

MESH = pl.DeviceIdType.MESH
V = 384
NI = 8
PIECES = 2
PV = V // PIECES
STEPS = 4
COLUMNS = (((0, 256, 0, 0),), ((0, 128, 0, 256), (128, 256, 1, 0)), ((0, 256, 1, 128),))
CROSSF, OWN, PASS_Z, FWD_Y, PASS_Y, PAR = range(6)
SEQUENCE = (
    (1, 0, 0),
    (1, 0, 1),
    (1, 0, 2),
    (1, 0, 3),
    (2, 0, 0),
    (1, 1, 0),
    (2, 0, 1),
    (2, 1, 0),
    (2, 0, 3),
    (2, 0, 2),
)
EVENTS = {
    0: (
        (3, ((CROSSF, 0), (OWN, 0, 1, 0), (OWN, 0, 3, 0), (PASS_Z, 0, 0),)),
        (4, ((CROSSF, 1), (PASS_Z, 0, 1), (OWN, 0, 1, 1), (OWN, 0, 3, 1), (OWN, 1, 0, 0), (PASS_Z, 1, 0),)),
        (5, ((PASS_Z, 3, 0),)),
        (6, ((OWN, 1, 0, 1),)),
        (7, ((OWN, 0, 2, 0),)),
        (8, ((OWN, 0, 2, 1), (FWD_Y, 0, 0), (PAR, 0, 0, 0), (FWD_Y, 0, 1), (PAR, 0, 0, 1),)),
        (9, ((OWN, 1, 1, 0),)),
        (10, ((PASS_Z, 1, 1), (PASS_Z, 3, 1),)),
        (12, ((OWN, 1, 1, 1), (PASS_Y, 0, 1), (PASS_Y, 0, 0),)),
        (13, ((OWN, 1, 3, 0), (FWD_Y, 1, 0), (FWD_Y, 3, 0), (PAR, 0, 1, 0), (PAR, 0, 3, 0),)),
        (17, ((OWN, 1, 2, 0), (OWN, 1, 2, 1), (PASS_Z, 2, 0), (PASS_Z, 2, 1), (PAR, 1, 0, 0), (PAR, 1, 0, 1),)),
        (20, ((FWD_Y, 1, 1), (FWD_Y, 3, 1), (PASS_Y, 1, 0), (PASS_Y, 3, 0), (PAR, 0, 1, 1), (PAR, 0, 3, 1),)),
        (24, ((FWD_Y, 2, 0), (FWD_Y, 2, 1), (PAR, 0, 2, 0), (PAR, 0, 2, 1),)),
        (25, ((PAR, 1, 3, 0), (PAR, 1, 1, 0),)),
        (27, ((OWN, 1, 3, 1), (PASS_Y, 3, 1), (PASS_Y, 1, 1),)),
        (31, ((PASS_Y, 2, 0), (PASS_Y, 2, 1),)),
        (34, ((PAR, 1, 3, 1), (PAR, 1, 1, 1),)),
        (38, ((PAR, 1, 2, 0), (PAR, 1, 2, 1),)),
    ),
    1: (
        (3, ((CROSSF, 0), (OWN, 0, 1, 0), (OWN, 0, 3, 0), (PASS_Z, 0, 0),)),
        (4, ((PASS_Z, 0, 1), (OWN, 0, 1, 1), (OWN, 0, 3, 1), (CROSSF, 1), (PASS_Z, 1, 0),)),
        (5, ((PASS_Z, 3, 0),)),
        (7, ((OWN, 0, 2, 0),)),
        (8, ((OWN, 0, 2, 1), (FWD_Y, 0, 0), (FWD_Y, 0, 1), (OWN, 1, 0, 0),)),
        (9, ((OWN, 1, 1, 0),)),
        (10, ((OWN, 1, 3, 0), (PASS_Z, 1, 1), (PASS_Z, 3, 1),)),
        (12, ((PAR, 0, 0, 0), (PAR, 1, 0, 0), (OWN, 1, 1, 1),)),
        (13, ((OWN, 1, 3, 1), (FWD_Y, 1, 0), (FWD_Y, 3, 0),)),
        (15, ((PAR, 0, 0, 1), (PAR, 1, 0, 1),)),
        (16, ((OWN, 1, 2, 0), (PASS_Z, 2, 0),)),
        (17, ((PASS_Z, 2, 1), (OWN, 1, 2, 1),)),
        (18, ((PAR, 0, 1, 0), (PAR, 1, 1, 0),)),
        (20, ((FWD_Y, 1, 1), (FWD_Y, 3, 1), (OWN, 1, 0, 1),)),
        (22, ((PAR, 0, 3, 0), (PAR, 1, 3, 0),)),
        (23, ((FWD_Y, 2, 0), (FWD_Y, 2, 1),)),
        (24, ((PAR, 0, 1, 1), (PAR, 1, 1, 1),)),
        (27, ((PAR, 0, 3, 1), (PAR, 1, 3, 1),)),
        (30, ((PAR, 0, 2, 0), (PAR, 1, 2, 0),)),
        (34, ((PAR, 0, 2, 1), (PAR, 1, 2, 1),)),
    ),
    2: (
        (3, ((CROSSF, 0), (OWN, 0, 1, 0), (OWN, 0, 3, 0), (FWD_Y, 0, 0), (PAR, 0, 0, 0),)),
        (4, ((CROSSF, 1), (OWN, 0, 1, 1), (OWN, 0, 3, 1), (PAR, 0, 0, 1), (FWD_Y, 0, 1), (OWN, 1, 0, 0),)),
        (6, ((OWN, 1, 0, 1),)),
        (7, ((OWN, 0, 2, 0), (FWD_Y, 1, 0), (PAR, 0, 1, 0),)),
        (8, ((OWN, 0, 2, 1), (PASS_Y, 0, 0), (PASS_Y, 0, 1),)),
        (9, ((FWD_Y, 3, 0), (PAR, 0, 3, 0),)),
        (10, ((OWN, 1, 3, 0),)),
        (11, ((PASS_Y, 1, 0),)),
        (12, ((FWD_Y, 1, 1), (PAR, 0, 1, 1), (PAR, 1, 0, 0),)),
        (13, ((OWN, 1, 1, 0), (OWN, 1, 3, 1),)),
        (14, ((PAR, 1, 0, 1),)),
        (15, ((FWD_Y, 3, 1), (PASS_Y, 3, 0), (PAR, 0, 3, 1),)),
        (16, ((OWN, 1, 2, 0),)),
        (17, ((OWN, 1, 2, 1),)),
        (18, ((PASS_Y, 1, 1), (PAR, 1, 1, 0),)),
        (19, ((FWD_Y, 2, 0), (PAR, 0, 2, 0),)),
        (21, ((PASS_Y, 3, 1),)),
        (22, ((FWD_Y, 2, 1), (PAR, 0, 2, 1), (PAR, 1, 3, 0),)),
        (25, ((PASS_Y, 2, 0), (PAR, 1, 1, 1),)),
        (27, ((OWN, 1, 1, 1),)),
        (28, ((PAR, 1, 3, 1),)),
        (29, ((PASS_Y, 2, 1),)),
        (31, ((PAR, 1, 2, 0),)),
        (34, ((PAR, 1, 2, 1),)),
    ),
    3: (
        (3, ((CROSSF, 0), (OWN, 0, 1, 0), (OWN, 0, 3, 0), (FWD_Y, 0, 0),)),
        (4, ((CROSSF, 1), (OWN, 0, 1, 1), (OWN, 0, 3, 1), (FWD_Y, 0, 1), (OWN, 1, 0, 0),)),
        (7, ((OWN, 0, 2, 0), (FWD_Y, 1, 0),)),
        (8, ((OWN, 0, 2, 1), (OWN, 1, 0, 1), (PAR, 0, 0, 0), (PAR, 1, 0, 0),)),
        (9, ((OWN, 1, 1, 0), (FWD_Y, 3, 0),)),
        (10, ((OWN, 1, 3, 0), (PAR, 0, 0, 1), (PAR, 1, 0, 1),)),
        (12, ((OWN, 1, 1, 1), (FWD_Y, 1, 1),)),
        (13, ((OWN, 1, 3, 1), (PAR, 0, 1, 0), (PAR, 1, 1, 0),)),
        (15, ((FWD_Y, 3, 1),)),
        (17, ((PAR, 1, 3, 0), (PAR, 0, 3, 0),)),
        (18, ((OWN, 1, 2, 0),)),
        (19, ((FWD_Y, 2, 0),)),
        (20, ((PAR, 0, 1, 1), (PAR, 1, 1, 1),)),
        (22, ((FWD_Y, 2, 1),)),
        (24, ((PAR, 1, 3, 1), (PAR, 0, 3, 1),)),
        (27, ((PAR, 0, 2, 0), (PAR, 1, 2, 0),)),
        (31, ((PAR, 1, 2, 1), (PAR, 0, 2, 1),)),
        (32, ((OWN, 1, 2, 1),)),
    ),
}


def kernel(dims, mine, amps, out, out_own, out_par, own, par, rc, half, acc, t1, t2, t3, tc,
           ssem, own_sem, own_d, par_sem, par_d, t1_sem, t2_sem, t3_sem, tc_sem, cross_sem, local_sem):
    sym, tile, c = lax.axis_index("sym"), lax.axis_index("tile"), lax.axis_index("occ")
    x, yhi = sym % 4, sym // 4
    x0, x1 = x % 2, x // 2
    z, ylo = tile // 2, tile % 2
    z0, z1 = z % 2, z // 2
    y = 2 * yhi + ylo

    def dev(dx=0, dy=0, dz=0, dc=0):
        xx, yy, zz = (x + 4 + dx) % 4, (y + 4 + dy) % 4, (z + 4 + dz) % 4
        return {"sym": (yy // 2) * 4 + xx, "tile": zz * 2 + yy % 2, "occ": (c + dc) % 2}

    step_a = 1 - 2 * (yhi + ylo - 2 * yhi * ylo)
    step_z = 1 - 2 * z0
    to = {
        "x+": dev(dx=1), "x-": dev(dx=-1), "y+": dev(dy=1), "y-": dev(dy=-1), "z+": dev(dz=1), "z-": dev(dz=-1),
        "core": dev(dc=1), "ya": dev(dy=step_a), "yb": dev(dy=-step_a), "za": dev(dz=step_z), "zb": dev(dz=-step_z),
    }
    barrier = pltpu.get_barrier_semaphore()
    for name in ("x+", "x-", "y+", "y-", "z+", "z-", "core"):
        pl.semaphore_signal(barrier, inc=1, device_id=to[name], device_id_type=MESH)

    keep = pltpu.make_async_copy(mine, own.at[sym, c], local_sem.at[8])
    keep.start()
    loads = [pltpu.make_async_copy(amps.at[i], rc.at[:, pl.ds(i * V, V)], local_sem.at[i]) for i in range(NI)]
    for load in loads:
        load.start()

    hi, lo = yhi == 1, yhi == 0
    is_x = [x == k for k in range(4)]
    none = jnp.logical_and(x == 0, lo)
    row_of = {0: yhi, 1: 1 - yhi}
    name_of = {(row, j): row_of[row] * 4 + (x + 4 - j) % 4 for row in range(2) for j in range(4)}
    row_behind = {"+": ((y + 3) % 4) // 2, "-": ((y + 1) % 4) // 2}
    name_behind = {(sign, j): row_behind[sign] * 4 + (x + 4 - j) % 4 for sign in "+-" for j in range(4)}
    from_lo = {sign: row_behind[sign] == 0 for sign in "+-"}
    piece = [pl.ds(k * PV, PV) for k in range(PIECES)]
    pl.semaphore_wait(barrier, 7)

    sent = {None: [], 0: [], 1: [], 2: [], 3: []}

    def sign_of(j, k):
        return "+" if (k + (0, 1, 1, 0)[j]) % 2 == 0 else "-"

    def send(cls, make, cond=None):
        index = len(sent[None]) if cls is None else 12 + len(sent[cls])

        def copy():
            src, dst, where, recv = make()
            return pltpu.make_async_remote_copy(
                src, dst, ssem.at[index], recv, device_id=to[where], device_id_type=MESH
            )

        if cond is None:
            copy().start()
        else:
            pl.when(cond)(lambda: copy().start())
        sent[cls].append((cond, copy))

    def arrived(dst, recv, cond=None):
        def wait():
            pltpu.make_async_remote_copy(
                dst, dst, ssem.at[0], recv, device_id=to["core"], device_id_type=MESH
            ).wait_recv()

        if cond is None:
            wait()
        else:
            pl.when(cond)(wait)

    def unit(buffer, q, k):
        return buffer.at[q, c, piece[k]]

    def feed(cls, j, k, src):
        q = name_of[0, j]
        final = lambda where: lambda: (src(), unit(par, q, k), where, par_sem.at[q, k])
        via1 = lambda where: lambda: (src(), t1.at[j, piece[k]], where, t1_sem.at[j, k])
        via2 = lambda where: lambda: (src(), t2.at[j, piece[k]], where, t2_sem.at[j, k])
        if cls in (0, 1):
            send(cls, via1("z" + sign_of(j, k)))
        if cls == 1:
            send(cls, final("ya"))
        if cls == 2:
            send(cls, final("za"), lo)
            send(cls, via1("za"), hi)
            send(cls, via2("zb"), lo)
            send(cls, final("zb"), hi)
        if cls == 3:
            send(cls, via1("za"))
            send(cls, via2("zb"))

    def event(cls, kind, *args):
        if kind == CROSSF:
            (k,) = args
            sign = "+-"[k]
            arrived(tc.at[piece[k]], tc_sem.at[k])
            send(cls, lambda: (tc.at[piece[k]], own.at[row_behind[sign] * 4 + x, c, piece[k]], "y" + sign, cross_sem.at[k]))
        if kind == OWN:
            row, j, k = args
            q = name_of[row, j]
            here = lambda: unit(own, q, k)
            arrived(here(), cross_sem.at[k] if (row, j) == (1, 0) else own_sem.at[q, k])
            if (row, j) == (1, 0) or (j == 1 and (k + row) % 2 == 0):
                send(cls, lambda: (here(), here(), "x+", own_sem.at[q, k]))
            if (row, j) == (1, 0) or (j == 3 and (k + row) % 2 == 1):
                send(cls, lambda: (here(), here(), "x-", own_sem.at[q, k]))
            if row == 0:
                feed(cls, j, k, here)
            send(cls, lambda: (here(), here(), "core", own_d.at[q, k]))
        if kind == PASS_Z:
            j, k = args
            q = name_of[0, j]
            way = "z" + sign_of(j, k)
            here = lambda: t1.at[j, piece[k]]
            arrived(here(), t1_sem.at[j, k])
            on = lambda: (here(), t2.at[j, piece[k]], way, t2_sem.at[j, k])
            if cls == 1:
                send(cls, on)
            else:
                send(cls, on, lo)
                send(cls, lambda: (here(), unit(par, q, k), way, par_sem.at[q, k]), hi)
        if kind == FWD_Y:
            j, k = args
            q = name_of[0, j]
            way = "y" + sign_of(j, k)
            here1, here2 = (lambda: t1.at[j, piece[k]]), (lambda: t2.at[j, piece[k]])
            if cls in (2, 3):
                cond = None if cls == 3 else hi
                arrived(here1(), t1_sem.at[j, k], cond)
                if cls == 3:
                    send(cls, lambda: (here1(), unit(par, q, k), "ya", par_sem.at[q, k]))
                else:
                    send(cls, lambda: (here1(), t3.at[j, piece[k]], way, t3_sem.at[j, k]), hi)
            if cls in (1, 3):
                arrived(here2(), t2_sem.at[j, k])
                send(cls, lambda: (here2(), unit(par, q, k), "yb", par_sem.at[q, k]))
            else:
                arrived(here2(), t2_sem.at[j, k], lo)
                send(cls, lambda: (here2(), t3.at[j, piece[k]], way, t3_sem.at[j, k]), lo)
        if kind == PASS_Y:
            j, k = args
            sign = sign_of(j, k)
            q = name_behind[sign, j]
            cond = None if cls == 2 else from_lo[sign]
            arrived(t3.at[j, piece[k]], t3_sem.at[j, k], cond)
            send(cls, lambda: (t3.at[j, piece[k]], unit(par, q, k), "y" + sign, par_sem.at[q, k]), cond)
        if kind == PAR:
            row, j, k = args
            q = name_of[row, j]
            here = lambda: unit(par, q, k)
            cond = hi if cls == 0 else None
            arrived(here(), par_sem.at[q, k], cond)
            send(cls, lambda: (here(), here(), "core", par_d.at[q, k]), cond)

    def events(n):
        for cls in range(4):
            todo = dict(EVENTS[cls]).get(n, ())
            if todo:
                @pl.when(is_x[cls])
                def _():
                    for entry in todo:
                        event(cls, *entry)

    def events_within(base, m):
        for k in range(1, STEPS):
            if any(base + k in dict(EVENTS[cls]) for cls in range(4)):
                pl.when(m == k)(functools.partial(events, base + k))

    def first_stage(base, row, j):
        q = name_of[row, j]
        events(base)
        for k in range(PIECES):
            arrived(own.at[q, 1 - c, piece[k]], own_d.at[q, k])

        @pl.when(none)
        def _():
            pltpu.make_async_copy(own.at[q], par.at[q], local_sem.at[9 + q]).start()

        @pl.loop(0, STEPS)
        def _(m):
            events_within(base, m)
            for t in range(3):
                cols = pl.ds(pl.multiple_of(m * (2 * V) + t * 256, 256), 256)
                r = jnp.dot(own[q].reshape(2 * V, V), rc[:, cols], preferred_element_type=jnp.float32)
                r = r.astype(jnp.bfloat16)
                for lo_col, hi_col, pair, at in COLUMNS[t]:
                    rows = pl.ds(pl.multiple_of((2 * m + pair) * V, V), V)
                    for p in range(2):
                        lanes = pl.ds(p * V + at, hi_col - lo_col)
                        half[q, rows, lanes] = r[p * V:(p + 1) * V, lo_col:hi_col]

    def second_stage(base, row, j):
        q = name_of[row, j]
        events(base)
        for k in range(PIECES):
            arrived(par.at[q, 1 - c, piece[k]], par_d.at[q, k], jnp.logical_not(none))
        start, last = base == FIRST_SUM, base == STEPS * (len(SEQUENCE) - 1)

        @pl.when(none)
        def _():
            pltpu.make_async_copy(own.at[q], par.at[q], local_sem.at[9 + q]).wait()

        @pl.loop(0, STEPS)
        def _(m):
            events_within(base, m)
            rows = pl.ds(pl.multiple_of(m * (2 * V), 2 * V), 2 * V)
            for b0, b1 in ((0, 256), (256, 384)):
                right = jnp.concatenate([par[q, 0, b0:b1], par[q, 1, b0:b1]], axis=1)
                r = lax.dot_general(half[q, rows, :], right, (((1,), (1,)), ((), ())), preferred_element_type=jnp.float32)
                if start:
                    acc[rows, b0:b1] = r
                else:
                    acc[rows, b0:b1] += r
            if last:
                pltpu.make_async_copy(acc.at[rows], out.at[rows], local_sem.at[m]).start()

    for k in range(PIECES):
        src = mine.at[piece[k]]
        home = own.at[sym, c, piece[k]]
        send(None, lambda src=src, home=home, k=k: (src, home, "core", own_d.at[sym, k]))
    for k in range(PIECES):
        src = mine.at[piece[k]]
        home = own.at[sym, c, piece[k]]
        for way in ("x+", "x-"):
            send(None, lambda src=src, home=home, k=k, way=way: (src, home, way, own_sem.at[sym, k]))
        send(None, lambda src=src, k=k: (src, tc.at[piece[k]], "y" + "+-"[k], tc_sem.at[k]))
        for cls in range(4):
            @pl.when(is_x[cls])
            def _():
                feed(cls, 0, k, lambda src=src: src)

    n_row = dims[tile]
    n_col = dims[(z1 + yhi - 2 * z1 * yhi) * 4 + (z0 + x1 - 2 * z0 * x1) * 2 + (ylo + x0 - 2 * ylo * x0)]
    live_r = jnp.where(lax.broadcasted_iota(jnp.int32, (V, V), 0) < n_row, 1.0, 0.0)
    live = jnp.where(lax.broadcasted_iota(jnp.int32, (V, V), 1) < n_col, live_r, 0.0).astype(jnp.bfloat16)
    for load in loads:
        load.wait()
    for i in range(NI):
        rc[:, i * V:(i + 1) * V] = rc[:, i * V:(i + 1) * V] * live
    keep.wait()

    for number, (stage, row, j) in enumerate(SEQUENCE):
        (first_stage if stage == 1 else second_stage)(STEPS * number, row, j)
    events(STEPS * len(SEQUENCE))

    leaving = []
    for r, (row, j) in enumerate(REST):
        q = name_of[row, j]
        for k in range(PIECES):
            arrived(own.at[q, 1 - c, piece[k]], own_d.at[q, k])
        for k in range(PIECES):
            arrived(par.at[q, 1 - c, piece[k]], par_d.at[q, k], jnp.logical_not(none))
        leaving.append(pltpu.make_async_copy(own.at[q], out_own.at[r], local_sem.at[17 + 2 * r]))
        leaving[-1].start()
        leaving.append(pltpu.make_async_copy(par.at[q], out_par.at[r], local_sem.at[18 + 2 * r]))

        @pl.when(none)
        def _():
            pltpu.make_async_copy(own.at[q], out_par.at[r], local_sem.at[18 + 2 * r]).start()

        @pl.when(jnp.logical_not(none))
        def _():
            leaving[-1].start()

    for cls, entries in sent.items():
        def finish(entries=entries):
            for cond, copy in entries:
                if cond is None:
                    copy().wait_send()
                else:
                    pl.when(cond)(lambda copy=copy: copy().wait_send())

        if cls is None:
            finish()
        else:
            pl.when(is_x[cls])(finish)
    for m in range(STEPS):
        rows = pl.ds(m * (2 * V), 2 * V)
        pltpu.make_async_copy(acc.at[rows], out.at[rows], local_sem.at[m]).wait()
    for copy in leaving:
        copy.wait()


REST = tuple((row, j) for j in (0, 1, 3, 2) for row in range(2) if (1, row, j) not in SEQUENCE)
FIRST_SUM = STEPS * [stage for stage, _, _ in SEQUENCE].index(2)


def rest_kernel(dims, own, par, amps, raw, out, rc, half):
    sym, tile = lax.axis_index("sym"), lax.axis_index("tile")
    n_row, n_col = dims[tile], dims[jnp.bitwise_xor(tile, sym)]
    live = (lax.broadcasted_iota(jnp.int32, (V, V), 0) < n_row) & (lax.broadcasted_iota(jnp.int32, (V, V), 1) < n_col)
    live_b = jnp.where(live, 1.0, 0.0).astype(jnp.bfloat16)
    for i in range(2):
        rc[:, i * V:(i + 1) * V] = amps[i] * live_b
    n = len(REST)
    for t in range(3):
        r = jnp.dot(own[...].reshape(n * 2 * V, V), rc[:, t * 256:(t + 1) * 256], preferred_element_type=jnp.float32)
        r = r.astype(jnp.bfloat16)
        for lo_col, hi_col, pair, at in COLUMNS[t]:
            for p in range(2 * n):
                lanes = pl.ds(p * V + at, hi_col - lo_col)
                half[pair * V:(pair + 1) * V, lanes] = r[p * V:(p + 1) * V, lo_col:hi_col]
    for b0, b1 in ((0, 256), (256, 384)):
        right = jnp.concatenate([par[r, p, b0:b1] for r in range(n) for p in range(2)], axis=1)
        r = lax.dot_general(half[...], right, (((1,), (1,)), ((), ())), preferred_element_type=jnp.float32)
        r = r + raw[:, b0:b1]
        for i in range(2):
            out[0, i, :, b0:b1] = jnp.where(live[:, b0:b1], r[i * V:(i + 1) * V], 0.0)


def shards(irrep_dims, chol_vectors, amplitudes):
    bf, sem = jnp.bfloat16, pltpu.SemaphoreType.DMA
    n = len(REST)
    own, chol, amps = (n, 2, V, V), chol_vectors.reshape(V, V), amplitudes.reshape(NI, V, V)
    raw, rest_own, rest_par = pl.pallas_call(
        kernel,
        out_shape=[jax.ShapeDtypeStruct((NI * V, V), jnp.float32), jax.ShapeDtypeStruct(own, bf), jax.ShapeDtypeStruct(own, bf)],
        in_specs=[
            pl.BlockSpec(memory_space=pltpu.SMEM),
            pl.BlockSpec(memory_space=pl.ANY),
            pl.BlockSpec(memory_space=pl.ANY),
        ],
        out_specs=[pl.BlockSpec(memory_space=pl.ANY)] * 3,
        scratch_shapes=[
            pltpu.VMEM((8, 2, V, V), bf),
            pltpu.VMEM((8, 2, V, V), bf),
            pltpu.VMEM((V, NI * V), bf),
            pltpu.VMEM((8, NI * V, 2 * V), bf),
            pltpu.VMEM((NI * V, V), jnp.float32),
            pltpu.VMEM((4, V, V), bf),
            pltpu.VMEM((4, V, V), bf),
            pltpu.VMEM((4, V, V), bf),
            pltpu.VMEM((V, V), bf),
            sem((136,)), sem((8, PIECES)), sem((8, PIECES)), sem((8, PIECES)), sem((8, PIECES)),
            sem((4, PIECES)), sem((4, PIECES)), sem((4, PIECES)), sem((2,)), sem((2,)), sem((17 + 2 * n,)),
        ],
        compiler_params=pltpu.CompilerParams(
            collective_id=0, has_side_effects=True, vmem_limit_bytes=63 * 1024 * 1024
        ),
        cost_estimate=pl.CostEstimate(flops=29_000_000_000, bytes_accessed=7_500_000, transcendentals=0),
        name="ladder",
    )(irrep_dims, chol, amps)
    whole = pl.BlockSpec(own, lambda m: (0, 0, 0, 0), pipeline_mode=pl.Buffered(1))
    return pl.pallas_call(
        rest_kernel,
        grid=(STEPS,),
        out_shape=jax.ShapeDtypeStruct((1, NI, V, V), jnp.float32),
        in_specs=[
            pl.BlockSpec(memory_space=pltpu.SMEM),
            whole,
            whole,
            pl.BlockSpec((2, V, V), lambda m: (m, 0, 0)),
            pl.BlockSpec((2 * V, V), lambda m: (m, 0)),
        ],
        out_specs=pl.BlockSpec((1, 2, V, V), lambda m: (0, m, 0, 0)),
        scratch_shapes=[pltpu.VMEM((V, 2 * V), bf), pltpu.VMEM((2 * V, n * 2 * V), bf)],
        compiler_params=pltpu.CompilerParams(vmem_limit_bytes=60 * 1024 * 1024),
        name="rest",
    )(irrep_dims, rest_own, rest_par, amps, raw)


def solution(mesh):
    return jax.shard_map(
        shards,
        mesh=mesh,
        in_specs=(P(), P(("sym", "occ"), "tile", None), P("sym", "occ", "tile", None)),
        out_specs=P("sym", "occ", "tile", None),
        check_vma=False,
    )
```

```python
import functools

import jax
import jax.numpy as jnp
from jax import lax
from jax.experimental import pallas as pl
from jax.experimental.pallas import tpu as pltpu
from jax.sharding import PartitionSpec as P

MESH = pl.DeviceIdType.MESH
V = 384
NI = 8
PIECES = 2
PV = V // PIECES
STEPS = {1: 12, 2: 4}
HALF = NI * V // 2
CROSSF, OWN, PASS_Z, FWD_Y, PASS_Y, PAR = range(6)
SEQUENCE = ((1, 1), (1, 1), (1, 2), (2, 1), (1, 2), (2, 1), (2, 1), (2, 1), (2, 1), (2, 1))
UNITS = (
    (((0, 0), (0, 0), (0, 0), (0, 0), (0, 0), (0, 0), (0, 0), (0, 0)),),
    (((0, 1), (0, 1), (0, 1), (0, 1), (0, 1), (0, 1), (0, 1), (0, 1)),),
    (((0, 3), (0, 3), (0, 3), (0, 3), (0, 3), (0, 3), (0, 3), (0, 3)), ((1, 0), (0, 2), (1, 0), (1, 0), (1, 0), (0, 2), (1, 0), (1, 0)),),
    (((0, 0), (0, 0), (0, 0), (0, 0), (0, 0), (0, 0), (0, 0), (0, 0)),),
    (((0, 2), (1, 1), (0, 2), (0, 2), (0, 2), (1, 0), (0, 2), (0, 2)), ((1, 1), (1, 3), (1, 3), (1, 1), (1, 1), (1, 1), (1, 1), (1, 1)),),
    (((1, 0), (0, 1), (1, 0), (1, 0), (1, 0), (1, 0), (1, 0), (1, 0)),),
    (((0, 1), (1, 1), (0, 1), (0, 1), (0, 1), (0, 1), (0, 1), (0, 1)),),
    (((1, 1), (0, 3), (0, 3), (1, 1), (0, 3), (1, 1), (1, 1), (1, 1)),),
    (((0, 3), (1, 3), (1, 3), (0, 3), (0, 2), (0, 3), (0, 3), (0, 3)),),
    (((0, 2), (0, 2), (0, 2), (0, 2), (1, 1), (0, 2), (0, 2), (0, 2)),),
)
EVENTS = (
    (
        (10, ((CROSSF, 0), (CROSSF, 1), (OWN, 0, 1, 0), (OWN, 0, 3, 0), (PASS_Z, 0, 0), (PASS_Z, 0, 1),)),
        (12, ((OWN, 0, 1, 1), (OWN, 0, 3, 1),)),
        (13, ((OWN, 1, 0, 0), (OWN, 1, 0, 1), (PASS_Z, 1, 0), (PASS_Z, 3, 0),)),
        (19, ((OWN, 0, 2, 0),)),
        (22, ((OWN, 0, 2, 1),)),
        (23, ((FWD_Y, 0, 0), (FWD_Y, 0, 1),)),
        (28, ((OWN, 1, 1, 0),)),
        (30, ((PASS_Z, 3, 1),)),
        (31, ((PASS_Z, 1, 1),)),
        (33, ((PASS_Y, 0, 1), (PASS_Y, 0, 0),)),
        (35, ((OWN, 1, 1, 1),)),
        (37, ((OWN, 1, 3, 0), (FWD_Y, 1, 0), (FWD_Y, 3, 0),)),
        (42, ((OWN, 1, 2, 1), (PASS_Z, 2, 0), (PASS_Z, 2, 1),)),
        (45, ((PASS_Y, 1, 0), (PASS_Y, 3, 0),)),
        (49, ((OWN, 1, 2, 0), (FWD_Y, 1, 1), (FWD_Y, 3, 1),)),
        (55, ((FWD_Y, 2, 0), (FWD_Y, 2, 1),)),
        (56, ((PASS_Y, 1, 1),)),
        (57, ((PASS_Y, 3, 1),)),
        (59, ((OWN, 1, 3, 1),)),
        (62, ((PASS_Y, 2, 0), (PASS_Y, 2, 1),)),
    ),
    (
        (10, ((CROSSF, 0), (OWN, 0, 1, 0), (OWN, 0, 3, 0), (PASS_Z, 0, 0), (PASS_Z, 0, 1),)),
        (12, ((PAR, 0, 0, 0), (OWN, 0, 1, 1), (PAR, 1, 0, 0), (OWN, 0, 3, 1), (CROSSF, 1),)),
        (13, ((PASS_Z, 1, 0), (PASS_Z, 3, 0),)),
        (19, ((OWN, 0, 2, 0),)),
        (20, ((PAR, 0, 0, 1), (PAR, 1, 0, 1),)),
        (22, ((OWN, 0, 2, 1),)),
        (23, ((FWD_Y, 0, 0), (FWD_Y, 0, 1),)),
        (26, ((OWN, 1, 0, 0), (OWN, 1, 1, 0),)),
        (28, ((OWN, 1, 3, 0), (PASS_Z, 3, 1),)),
        (29, ((PASS_Z, 1, 1),)),
        (32, ((OWN, 1, 1, 1), (PAR, 0, 1, 0),)),
        (33, ((PAR, 1, 1, 0),)),
        (34, ((OWN, 1, 3, 1),)),
        (35, ((FWD_Y, 1, 0), (FWD_Y, 3, 0),)),
        (38, ((PAR, 0, 3, 0), (PAR, 1, 3, 0),)),
        (40, ((OWN, 1, 2, 0), (OWN, 1, 2, 1), (PASS_Z, 2, 0), (PASS_Z, 2, 1),)),
        (44, ((PAR, 0, 1, 1), (PAR, 1, 1, 1),)),
        (47, ((FWD_Y, 3, 1), (FWD_Y, 1, 1),)),
        (51, ((PAR, 0, 3, 1), (OWN, 1, 0, 1), (PAR, 1, 3, 1),)),
        (53, ((FWD_Y, 2, 0), (FWD_Y, 2, 1),)),
        (56, ((PAR, 0, 2, 0), (PAR, 1, 2, 0),)),
        (61, ((PAR, 0, 2, 1), (PAR, 1, 2, 1),)),
    ),
    (
        (10, ((CROSSF, 0), (CROSSF, 1), (OWN, 0, 1, 0), (OWN, 0, 3, 0), (FWD_Y, 0, 0), (PAR, 0, 0, 0),)),
        (12, ((OWN, 0, 1, 1), (PAR, 0, 0, 1), (OWN, 0, 3, 1), (FWD_Y, 0, 1),)),
        (13, ((OWN, 1, 0, 0), (OWN, 1, 0, 1),)),
        (19, ((OWN, 0, 2, 0), (FWD_Y, 1, 0), (PAR, 0, 1, 0),)),
        (22, ((OWN, 0, 2, 1),)),
        (23, ((PASS_Y, 0, 0), (PASS_Y, 0, 1),)),
        (28, ((FWD_Y, 3, 0), (PAR, 0, 3, 0),)),
        (30, ((OWN, 1, 3, 0), (PASS_Y, 1, 0),)),
        (33, ((PAR, 1, 0, 0),)),
        (34, ((FWD_Y, 1, 1), (PAR, 0, 1, 1),)),
        (36, ((OWN, 1, 3, 1),)),
        (37, ((OWN, 1, 1, 0), (PAR, 1, 0, 1),)),
        (38, ((PASS_Y, 3, 0),)),
        (40, ((FWD_Y, 3, 1), (PAR, 0, 3, 1),)),
        (41, ((OWN, 1, 2, 0),)),
        (42, ((PAR, 1, 1, 0),)),
        (44, ((PASS_Y, 1, 1),)),
        (46, ((FWD_Y, 2, 0), (PAR, 0, 2, 0),)),
        (48, ((OWN, 1, 2, 1),)),
        (49, ((PASS_Y, 3, 1),)),
        (51, ((PAR, 1, 3, 0),)),
        (53, ((FWD_Y, 2, 1), (PAR, 0, 2, 1),)),
        (55, ((PASS_Y, 2, 0),)),
        (56, ((PAR, 1, 1, 1),)),
        (59, ((OWN, 1, 1, 1),)),
        (60, ((PAR, 1, 3, 1),)),
        (61, ((PASS_Y, 2, 1),)),
        (64, ((PAR, 1, 2, 0),)),
        (68, ((PAR, 1, 2, 1),)),
    ),
    (
        (10, ((CROSSF, 0), (CROSSF, 1), (OWN, 0, 1, 0), (OWN, 0, 3, 0), (FWD_Y, 0, 0),)),
        (12, ((OWN, 0, 1, 1), (OWN, 0, 3, 1), (FWD_Y, 0, 1),)),
        (13, ((OWN, 1, 0, 0), (OWN, 1, 0, 1),)),
        (19, ((OWN, 0, 2, 0), (FWD_Y, 1, 0),)),
        (22, ((OWN, 0, 2, 1),)),
        (23, ((PAR, 0, 0, 0), (PAR, 1, 0, 0),)),
        (27, ((OWN, 1, 1, 0),)),
        (28, ((FWD_Y, 3, 0),)),
        (29, ((OWN, 1, 3, 0),)),
        (30, ((PAR, 0, 0, 1), (PAR, 1, 0, 1),)),
        (34, ((OWN, 1, 1, 1), (FWD_Y, 1, 1),)),
        (36, ((OWN, 1, 3, 1),)),
        (37, ((PAR, 0, 1, 0), (PAR, 1, 1, 0),)),
        (40, ((FWD_Y, 3, 1),)),
        (41, ((PAR, 0, 3, 0), (PAR, 1, 3, 0),)),
        (44, ((OWN, 1, 2, 0),)),
        (46, ((FWD_Y, 2, 0),)),
        (48, ((PAR, 0, 1, 1), (PAR, 1, 1, 1),)),
        (53, ((FWD_Y, 2, 1),)),
        (54, ((PAR, 0, 3, 1), (PAR, 1, 3, 1),)),
        (59, ((PAR, 0, 2, 0), (PAR, 1, 2, 0),)),
        (64, ((PAR, 0, 2, 1), (PAR, 1, 2, 1),)),
        (65, ((OWN, 1, 2, 1),)),
    ),
    (
        (10, ((CROSSF, 0), (CROSSF, 1), (OWN, 0, 1, 0), (OWN, 0, 3, 0), (PASS_Z, 0, 0), (PASS_Z, 0, 1),)),
        (12, ((OWN, 0, 1, 1), (OWN, 0, 3, 1),)),
        (13, ((OWN, 1, 0, 0), (OWN, 1, 0, 1), (PASS_Z, 1, 0), (PASS_Z, 3, 0),)),
        (19, ((OWN, 0, 2, 0),)),
        (22, ((OWN, 0, 2, 1),)),
        (23, ((PAR, 0, 0, 0), (PAR, 0, 0, 1),)),
        (28, ((OWN, 1, 1, 0),)),
        (30, ((OWN, 1, 3, 0), (PASS_Z, 3, 1),)),
        (31, ((PASS_Z, 1, 1),)),
        (33, ((PASS_Y, 0, 0), (PASS_Y, 0, 1),)),
        (34, ((OWN, 1, 1, 1),)),
        (36, ((OWN, 1, 3, 1),)),
        (37, ((PAR, 0, 1, 0), (PAR, 0, 3, 0),)),
        (40, ((PAR, 1, 0, 0), (PAR, 1, 0, 1),)),
        (41, ((OWN, 1, 2, 0),)),
        (42, ((OWN, 1, 2, 1), (PASS_Z, 2, 0), (PASS_Z, 2, 1),)),
        (47, ((PASS_Y, 3, 0), (PASS_Y, 1, 0),)),
        (49, ((PAR, 0, 1, 1), (PAR, 0, 3, 1),)),
        (55, ((PAR, 0, 2, 0), (PAR, 0, 2, 1), (PAR, 1, 3, 0), (PAR, 1, 1, 0),)),
        (58, ((PASS_Y, 1, 1), (PASS_Y, 3, 1),)),
        (63, ((PASS_Y, 2, 1), (PASS_Y, 2, 0),)),
        (68, ((PAR, 1, 3, 1), (PAR, 1, 1, 1),)),
        (71, ((PAR, 1, 2, 1),)),
        (72, ((PAR, 1, 2, 0),)),
    ),
    (
        (10, ((CROSSF, 0), (CROSSF, 1), (OWN, 0, 1, 0), (OWN, 0, 3, 0), (PASS_Z, 0, 0), (PASS_Z, 0, 1),)),
        (12, ((OWN, 0, 1, 1), (OWN, 0, 3, 1),)),
        (13, ((OWN, 1, 0, 0), (PASS_Z, 1, 0), (PASS_Z, 3, 0),)),
        (19, ((OWN, 0, 2, 0),)),
        (22, ((OWN, 1, 0, 1), (OWN, 0, 2, 1),)),
        (23, ((FWD_Y, 0, 0), (FWD_Y, 0, 1),)),
        (27, ((OWN, 1, 1, 0),)),
        (29, ((OWN, 1, 3, 0), (PASS_Z, 3, 1),)),
        (30, ((PASS_Z, 1, 1),)),
        (32, ((PAR, 1, 0, 0), (PAR, 0, 0, 0),)),
        (33, ((OWN, 1, 1, 1),)),
        (35, ((OWN, 1, 3, 1),)),
        (36, ((FWD_Y, 1, 0), (FWD_Y, 3, 0), (PAR, 1, 0, 1), (PAR, 0, 0, 1),)),
        (37, ((OWN, 1, 2, 0), (OWN, 1, 2, 1), (PASS_Z, 2, 0), (PASS_Z, 2, 1),)),
        (39, ((PAR, 0, 1, 0), (PAR, 1, 1, 0),)),
        (43, ((FWD_Y, 1, 1), (FWD_Y, 3, 1),)),
        (45, ((PAR, 0, 3, 0), (PAR, 1, 3, 0),)),
        (49, ((FWD_Y, 2, 0),)),
        (50, ((FWD_Y, 2, 1),)),
        (52, ((PAR, 0, 1, 1),)),
        (57, ((PAR, 0, 3, 1), (PAR, 1, 3, 1), (PAR, 1, 1, 1),)),
        (62, ((PAR, 1, 2, 0), (PAR, 0, 2, 0),)),
        (66, ((PAR, 0, 2, 1), (PAR, 1, 2, 1),)),
    ),
    (
        (10, ((CROSSF, 0), (CROSSF, 1), (OWN, 0, 1, 0), (OWN, 0, 3, 0), (FWD_Y, 0, 0), (PAR, 0, 0, 0),)),
        (12, ((OWN, 0, 1, 1), (FWD_Y, 0, 1), (OWN, 0, 3, 1), (PAR, 0, 0, 1),)),
        (13, ((OWN, 1, 0, 0), (OWN, 1, 0, 1),)),
        (19, ((OWN, 0, 2, 0), (FWD_Y, 1, 0), (PAR, 0, 1, 0),)),
        (22, ((OWN, 0, 2, 1),)),
        (23, ((PASS_Y, 0, 0), (PASS_Y, 0, 1),)),
        (27, ((OWN, 1, 1, 0),)),
        (28, ((FWD_Y, 3, 0), (PAR, 0, 3, 0),)),
        (29, ((OWN, 1, 3, 0),)),
        (30, ((PASS_Y, 1, 0),)),
        (33, ((PAR, 1, 0, 0),)),
        (34, ((OWN, 1, 1, 1), (FWD_Y, 1, 1), (PAR, 0, 1, 1),)),
        (36, ((OWN, 1, 3, 1),)),
        (37, ((PAR, 1, 0, 1),)),
        (38, ((PASS_Y, 3, 0),)),
        (40, ((FWD_Y, 3, 1), (PAR, 0, 3, 1),)),
        (41, ((OWN, 1, 2, 0), (OWN, 1, 2, 1), (PAR, 1, 1, 0),)),
        (44, ((PASS_Y, 1, 1),)),
        (46, ((FWD_Y, 2, 0), (PAR, 0, 2, 0),)),
        (49, ((PASS_Y, 3, 1),)),
        (51, ((PAR, 1, 3, 0),)),
        (53, ((FWD_Y, 2, 1), (PAR, 0, 2, 1),)),
        (55, ((PASS_Y, 2, 0),)),
        (56, ((PAR, 1, 1, 1),)),
        (60, ((PAR, 1, 3, 1),)),
        (61, ((PASS_Y, 2, 1),)),
        (64, ((PAR, 1, 2, 0),)),
        (68, ((PAR, 1, 2, 1),)),
    ),
    (
        (10, ((CROSSF, 0), (CROSSF, 1), (OWN, 0, 1, 0), (OWN, 0, 3, 0), (FWD_Y, 0, 0),)),
        (12, ((OWN, 0, 1, 1), (OWN, 0, 3, 1), (FWD_Y, 0, 1),)),
        (13, ((OWN, 1, 0, 0), (OWN, 1, 0, 1),)),
        (19, ((OWN, 0, 2, 0), (FWD_Y, 1, 0),)),
        (22, ((OWN, 0, 2, 1),)),
        (23, ((PAR, 0, 0, 0), (PAR, 1, 0, 0),)),
        (27, ((OWN, 1, 1, 0),)),
        (28, ((FWD_Y, 3, 0),)),
        (29, ((OWN, 1, 3, 0),)),
        (30, ((PAR, 0, 0, 1), (PAR, 1, 0, 1),)),
        (34, ((OWN, 1, 1, 1), (FWD_Y, 1, 1),)),
        (36, ((OWN, 1, 3, 1),)),
        (37, ((PAR, 0, 1, 0), (PAR, 1, 1, 0),)),
        (40, ((FWD_Y, 3, 1),)),
        (41, ((OWN, 1, 2, 0), (OWN, 1, 2, 1), (PAR, 0, 3, 0), (PAR, 1, 3, 0),)),
        (46, ((FWD_Y, 2, 0),)),
        (48, ((PAR, 0, 1, 1), (PAR, 1, 1, 1),)),
        (53, ((FWD_Y, 2, 1),)),
        (54, ((PAR, 0, 3, 1), (PAR, 1, 3, 1),)),
        (59, ((PAR, 0, 2, 0), (PAR, 1, 2, 0),)),
        (64, ((PAR, 0, 2, 1), (PAR, 1, 2, 1),)),
    ),
)


def columns(t):
    first, last = t * 256, (t + 1) * 256
    cuts = [first] + [cut for cut in range(0, NI * V, V) if first < cut < last] + [last]
    return [(u - first, w - first, u // V, u % V) for u, w in zip(cuts, cuts[1:])]


def kernel(dims, mine, amps, out, out_own, out_par, own, par, rc, half, acc, t1, t2, t3, tc,
           ssem, own_sem, own_d, par_sem, par_d, t1_sem, t2_sem, t3_sem, tc_sem, cross_sem, local_sem):
    sym, tile, c = lax.axis_index("sym"), lax.axis_index("tile"), lax.axis_index("occ")
    x, yhi = sym % 4, sym // 4
    x0, x1 = x % 2, x // 2
    z, ylo = tile // 2, tile % 2
    z0, z1 = z % 2, z // 2
    y = 2 * yhi + ylo

    def dev(dx=0, dy=0, dz=0, dc=0):
        xx, yy, zz = (x + 4 + dx) % 4, (y + 4 + dy) % 4, (z + 4 + dz) % 4
        return {"sym": (yy // 2) * 4 + xx, "tile": zz * 2 + yy % 2, "occ": (c + dc) % 2}

    step_a = 1 - 2 * (yhi + ylo - 2 * yhi * ylo)
    step_z = 1 - 2 * z0
    to = {
        "x+": dev(dx=1), "x-": dev(dx=-1), "y+": dev(dy=1), "y-": dev(dy=-1), "z+": dev(dz=1), "z-": dev(dz=-1),
        "core": dev(dc=1), "ya": dev(dy=step_a), "yb": dev(dy=-step_a), "za": dev(dz=step_z), "zb": dev(dz=-step_z),
    }
    barrier = pltpu.get_barrier_semaphore()
    for name in ("x+", "x-", "y+", "y-", "z+", "z-", "core"):
        pl.semaphore_signal(barrier, inc=1, device_id=to[name], device_id_type=MESH)

    keep = pltpu.make_async_copy(mine, own.at[sym, c], local_sem.at[8])
    keep.start()
    loads = [pltpu.make_async_copy(amps.at[i], rc.at[:, pl.ds(i * V, V)], local_sem.at[i]) for i in range(NI)]
    for load in loads:
        load.start()

    is_s = [sym == k for k in range(8)]
    none = sym == 0
    row_of = {0: yhi, 1: 1 - yhi}
    name_of = {(row, j): row_of[row] * 4 + (x + 4 - j) % 4 for row in range(2) for j in range(4)}
    row_behind = {"+": ((y + 3) % 4) // 2, "-": ((y + 1) % 4) // 2}
    name_behind = {(sign, j): row_behind[sign] * 4 + (x + 4 - j) % 4 for sign in "+-" for j in range(4)}
    from_lo = {sign: row_behind[sign] == 0 for sign in "+-"}
    digit = (1 + 7 * x0) * (1 + 63 * x1) * (1 + 4095 * yhi)

    def chosen(names):
        code = sum((row * 4 + j) * 8 ** k for k, (row, j) in enumerate(names)) // digit % 8
        return (yhi + code // 4) % 2 * 4 + (x + 4 - code % 4) % 4

    piece = [pl.ds(k * PV, PV) for k in range(PIECES)]
    pl.semaphore_wait(barrier, 7)

    sent = {cls: [] for cls in (None, *range(8))}

    def sign_of(j, k):
        return "+" if (k + (0, 1, 1, 0)[j]) % 2 == 0 else "-"

    def send(cls, make, cond=None):
        index = len(sent[None]) if cls is None else 12 + len(sent[cls])

        def copy():
            src, dst, where, recv = make()
            return pltpu.make_async_remote_copy(
                src, dst, ssem.at[index], recv, device_id=to[where], device_id_type=MESH
            )

        if cond is None:
            copy().start()
        else:
            pl.when(cond)(lambda: copy().start())
        sent[cls].append((cond, copy))

    def arrived(dst, recv, cond=None):
        def wait():
            pltpu.make_async_remote_copy(
                dst, dst, ssem.at[0], recv, device_id=to["core"], device_id_type=MESH
            ).wait_recv()

        if cond is None:
            wait()
        else:
            pl.when(cond)(wait)

    def unit(buffer, q, k):
        return buffer.at[q, c, piece[k]]

    def feed(cls, j, k, src):
        at, up = cls % 4, cls // 4 == 1
        q = name_of[0, j]
        final = lambda where: lambda: (src(), unit(par, q, k), where, par_sem.at[q, k])
        via1 = lambda where: lambda: (src(), t1.at[j, piece[k]], where, t1_sem.at[j, k])
        via2 = lambda where: lambda: (src(), t2.at[j, piece[k]], where, t2_sem.at[j, k])
        if at in (0, 1):
            send(cls, via1("z" + sign_of(j, k)))
        if at == 1:
            send(cls, final("ya"))
        if at in (2, 3):
            send(cls, final("za") if at == 2 and not up else via1("za"))
            send(cls, final("zb") if at == 2 and up else via2("zb"))

    def event(cls, kind, *args):
        at, up = cls % 4, cls // 4 == 1
        if kind == CROSSF:
            (k,) = args
            sign = "+-"[k]
            arrived(tc.at[piece[k]], tc_sem.at[k])
            send(cls, lambda: (tc.at[piece[k]], own.at[row_behind[sign] * 4 + x, c, piece[k]], "y" + sign, cross_sem.at[k]))
        if kind == OWN:
            row, j, k = args
            q = name_of[row, j]
            here = lambda: unit(own, q, k)
            arrived(here(), cross_sem.at[k] if (row, j) == (1, 0) else own_sem.at[q, k])
            if (row, j) == (1, 0) or (j == 1 and (k + row) % 2 == 0):
                send(cls, lambda: (here(), here(), "x+", own_sem.at[q, k]))
            if (row, j) == (1, 0) or (j == 3 and (k + row) % 2 == 1):
                send(cls, lambda: (here(), here(), "x-", own_sem.at[q, k]))
            if row == 0:
                feed(cls, j, k, here)
            send(cls, lambda: (here(), here(), "core", own_d.at[q, k]))
        if kind == PASS_Z:
            j, k = args
            q = name_of[0, j]
            way = "z" + sign_of(j, k)
            here = lambda: t1.at[j, piece[k]]
            arrived(here(), t1_sem.at[j, k])
            if at == 0 and up:
                send(cls, lambda: (here(), unit(par, q, k), way, par_sem.at[q, k]))
            else:
                send(cls, lambda: (here(), t2.at[j, piece[k]], way, t2_sem.at[j, k]))
        if kind == FWD_Y:
            j, k = args
            q = name_of[0, j]
            way = "y" + sign_of(j, k)
            here1, here2 = (lambda: t1.at[j, piece[k]]), (lambda: t2.at[j, piece[k]])
            if at == 3 or (at == 2 and up):
                arrived(here1(), t1_sem.at[j, k])
                if at == 3:
                    send(cls, lambda: (here1(), unit(par, q, k), "ya", par_sem.at[q, k]))
                else:
                    send(cls, lambda: (here1(), t3.at[j, piece[k]], way, t3_sem.at[j, k]))
            if at in (1, 3) or not up:
                arrived(here2(), t2_sem.at[j, k])
                if at in (1, 3):
                    send(cls, lambda: (here2(), unit(par, q, k), "yb", par_sem.at[q, k]))
                else:
                    send(cls, lambda: (here2(), t3.at[j, piece[k]], way, t3_sem.at[j, k]))
        if kind == PASS_Y:
            j, k = args
            sign = sign_of(j, k)
            q = name_behind[sign, j]
            cond = None if at == 2 else from_lo[sign]
            arrived(t3.at[j, piece[k]], t3_sem.at[j, k], cond)
            send(cls, lambda: (t3.at[j, piece[k]], unit(par, q, k), "y" + sign, par_sem.at[q, k]), cond)
        if kind == PAR:
            row, j, k = args
            q = name_of[row, j]
            here = lambda: unit(par, q, k)
            arrived(here(), par_sem.at[q, k])
            send(cls, lambda: (here(), here(), "core", par_d.at[q, k]))

    def events(n):
        for cls in range(8):
            todo = dict(EVENTS[cls]).get(n, ())
            if todo:
                @pl.when(is_s[cls])
                def _():
                    for entry in todo:
                        event(cls, *entry)

    def events_within(base, m, t):
        for k in range(4):
            n = 3 * k + t
            if n and any(base + n in dict(EVENTS[cls]) for cls in range(8)):
                pl.when(m == k)(functools.partial(events, base + n))

    def first_stage(base, names):
        events(base)
        qs = [chosen(name) for name in names]
        for q in qs:
            for k in range(PIECES):
                arrived(own.at[q, 1 - c, piece[k]], own_d.at[q, k])

        @pl.when(none)
        def _():
            for q in qs:
                pltpu.make_async_copy(own.at[q], par.at[q], local_sem.at[9 + q]).start()

        @pl.loop(0, 4)
        def _(m):
            for t in range(3):
                events_within(base, m, t)
                cols = pl.ds(pl.multiple_of(m * (2 * V) + t * 256, 256), 256)
                left = [own[q].reshape(2 * V, V) for q in qs]
                left = jnp.concatenate(left, axis=0) if len(qs) > 1 else left[0]
                r = jnp.dot(left, rc[:, cols], preferred_element_type=jnp.float32).astype(jnp.bfloat16)
                for lo_col, hi_col, pair, at in columns(t):
                    rows = pl.ds(pl.multiple_of((2 * m + pair) * V, V), V)
                    for g, q in enumerate(qs):
                        for p in range(2):
                            lanes = pl.ds(p * V + at, hi_col - lo_col)
                            half[q, rows, lanes] = r[(2 * g + p) * V:(2 * g + p + 1) * V, lo_col:hi_col]

    def second_stage(base, names):
        start, last = base == BASES[FIRST_SUM], base == BASES[-2]
        events(base)
        qs = [chosen(name) for name in names]
        for q in qs:
            for k in range(PIECES):
                arrived(par.at[q, 1 - c, piece[k]], par_d.at[q, k], jnp.logical_not(none))

        @pl.when(none)
        def _():
            for q in qs:
                pltpu.make_async_copy(own.at[q], par.at[q], local_sem.at[9 + q]).wait()

        for h in range(2):
            rows = pl.ds(h * HALF, HALF)
            for n, (b0, b1) in enumerate(((0, 256), (256, 384))):
                if 2 * h + n > 0:
                    events(base + 2 * h + n)
                left = [half[q, rows, :] for q in qs]
                left = jnp.concatenate(left, axis=1) if len(qs) > 1 else left[0]
                right = jnp.concatenate([par[q, p, b0:b1] for q in qs for p in range(2)], axis=1)
                r = lax.dot_general(left, right, (((1,), (1,)), ((), ())), preferred_element_type=jnp.float32)
                if start:
                    acc[rows, b0:b1] = r
                else:
                    acc[rows, b0:b1] += r
            if last:
                pltpu.make_async_copy(acc.at[rows], out.at[rows], local_sem.at[h]).start()

    for k in range(PIECES):
        src = mine.at[piece[k]]
        home = own.at[sym, c, piece[k]]
        send(None, lambda src=src, home=home, k=k: (src, home, "core", own_d.at[sym, k]))
    for k in range(PIECES):
        src = mine.at[piece[k]]
        home = own.at[sym, c, piece[k]]
        for way in ("x+", "x-"):
            send(None, lambda src=src, home=home, k=k, way=way: (src, home, way, own_sem.at[sym, k]))
        send(None, lambda src=src, k=k: (src, tc.at[piece[k]], "y" + "+-"[k], tc_sem.at[k]))
        for cls in range(8):
            @pl.when(is_s[cls])
            def _():
                feed(cls, 0, k, lambda src=src: src)

    n_row = dims[tile]
    n_col = dims[(z1 + yhi - 2 * z1 * yhi) * 4 + (z0 + x1 - 2 * z0 * x1) * 2 + (ylo + x0 - 2 * ylo * x0)]
    live_r = jnp.where(lax.broadcasted_iota(jnp.int32, (V, V), 0) < n_row, 1.0, 0.0)
    live = jnp.where(lax.broadcasted_iota(jnp.int32, (V, V), 1) < n_col, live_r, 0.0).astype(jnp.bfloat16)
    for load in loads:
        load.wait()
    for i in range(NI):
        rc[:, i * V:(i + 1) * V] = rc[:, i * V:(i + 1) * V] * live
    keep.wait()

    for base, (stage, _), names in zip(BASES, SEQUENCE, UNITS):
        (first_stage if stage == 1 else second_stage)(base, names)
    events(BASES[-1])

    leaving = []
    for r, names in enumerate(REST):
        q = chosen(names)
        for k in range(PIECES):
            arrived(own.at[q, 1 - c, piece[k]], own_d.at[q, k])
        for k in range(PIECES):
            arrived(par.at[q, 1 - c, piece[k]], par_d.at[q, k], jnp.logical_not(none))
        leaving.append(pltpu.make_async_copy(own.at[q], out_own.at[r], local_sem.at[17 + 2 * r]))
        leaving[-1].start()
        leaving.append(pltpu.make_async_copy(par.at[q], out_par.at[r], local_sem.at[18 + 2 * r]))

        @pl.when(none)
        def _():
            pltpu.make_async_copy(own.at[q], out_par.at[r], local_sem.at[18 + 2 * r]).start()

        @pl.when(jnp.logical_not(none))
        def _():
            leaving[-1].start()

    for cls, entries in sent.items():
        def finish(entries=entries):
            for cond, copy in entries:
                if cond is None:
                    copy().wait_send()
                else:
                    pl.when(cond)(lambda copy=copy: copy().wait_send())

        if cls is None:
            finish()
        else:
            pl.when(is_s[cls])(finish)
    for h in range(2):
        rows = pl.ds(h * HALF, HALF)
        pltpu.make_async_copy(acc.at[rows], out.at[rows], local_sem.at[h]).wait()
    for copy in leaving:
        copy.wait()


FIRST_SUM = [stage for stage, _ in SEQUENCE].index(2)
BASES = [sum(STEPS[stage] for stage, _ in SEQUENCE[:n]) for n in range(len(SEQUENCE) + 1)]
ALL = [(row, j) for j in (0, 1, 3, 2) for row in range(2)]


def left_over():
    by_s = []
    for s in range(8):
        done = [names[s] for (stage, _), group in zip(SEQUENCE, UNITS) if stage == 1 for names in group]
        by_s.append([name for name in ALL if name not in done])
    return list(zip(*by_s))


REST = left_over()


def rest_kernel(dims, own_hbm, par_hbm, amps, raw, out, own, par, rc, half, acc, sems):
    sym, tile = lax.axis_index("sym"), lax.axis_index("tile")
    n, hi = len(REST), NI // 2
    get_own = pltpu.make_async_copy(own_hbm, own, sems.at[0])
    get_par = pltpu.make_async_copy(par_hbm, par, sems.at[1])
    get_amps = [pltpu.make_async_copy(amps.at[i], rc.at[:, pl.ds(i * V, V)], sems.at[2 + i]) for i in range(NI)]
    get_raw = [
        pltpu.make_async_copy(raw.at[pl.ds(h * HALF, HALF)], acc.at[pl.ds(h * HALF, HALF)], sems.at[2 + NI + h])
        for h in range(2)
    ]
    for copy in get_amps[:hi] + [get_own, get_par, get_raw[0]] + get_amps[hi:] + [get_raw[1]]:
        copy.start()
    n_row, n_col = dims[tile], dims[jnp.bitwise_xor(tile, sym)]
    live = (lax.broadcasted_iota(jnp.int32, (V, V), 0) < n_row) & (lax.broadcasted_iota(jnp.int32, (V, V), 1) < n_col)
    live_b = jnp.where(live, 1.0, 0.0).astype(jnp.bfloat16)
    puts = []
    for h in range(2):
        for i in range(h * hi, (h + 1) * hi):
            get_amps[i].wait()
            rc[:, i * V:(i + 1) * V] = rc[:, i * V:(i + 1) * V] * live_b
        if h == 0:
            get_own.wait()
        for t in range(6 * h, 6 * (h + 1)):
            left = own[...].reshape(n * 2 * V, V)
            r = jnp.dot(left, rc[:, t * 256:(t + 1) * 256], preferred_element_type=jnp.float32).astype(jnp.bfloat16)
            for lo_col, hi_col, pair, at in columns(t):
                for p in range(2 * n):
                    lanes = pl.ds(p * V + at, hi_col - lo_col)
                    half[(pair - h * hi) * V:(pair - h * hi + 1) * V, lanes] = r[p * V:(p + 1) * V, lo_col:hi_col]
        if h == 0:
            get_par.wait()
        get_raw[h].wait()
        rows = pl.ds(h * HALF, HALF)
        for b0, b1 in ((0, 256), (256, 384)):
            right = jnp.concatenate([par[r, p, b0:b1] for r in range(n) for p in range(2)], axis=1)
            r = lax.dot_general(half[...], right, (((1,), (1,)), ((), ())), preferred_element_type=jnp.float32)
            r = r + acc[rows, b0:b1]
            for i in range(hi):
                at = pl.ds((h * hi + i) * V, V)
                acc[at, b0:b1] = jnp.where(live[:, b0:b1], r[i * V:(i + 1) * V], 0.0)
            lanes = pl.ds(b0, b1 - b0)
            puts.append(pltpu.make_async_copy(acc.at[rows, lanes], out.at[rows, lanes], sems.at[4 + NI + len(puts)]))
            puts[-1].start()
    for copy in puts:
        copy.wait()


def shards(irrep_dims, chol_vectors, amplitudes):
    bf, sem = jnp.bfloat16, pltpu.SemaphoreType.DMA
    n = len(REST)
    own, chol, amps = (n, 2, V, V), chol_vectors.reshape(V, V), amplitudes.reshape(NI, V, V)
    raw, rest_own, rest_par = pl.pallas_call(
        kernel,
        out_shape=[jax.ShapeDtypeStruct((NI * V, V), jnp.float32), jax.ShapeDtypeStruct(own, bf), jax.ShapeDtypeStruct(own, bf)],
        in_specs=[
            pl.BlockSpec(memory_space=pltpu.SMEM),
            pl.BlockSpec(memory_space=pl.ANY),
            pl.BlockSpec(memory_space=pl.ANY),
        ],
        out_specs=[pl.BlockSpec(memory_space=pl.ANY)] * 3,
        scratch_shapes=[
            pltpu.VMEM((8, 2, V, V), bf),
            pltpu.VMEM((8, 2, V, V), bf),
            pltpu.VMEM((V, NI * V), bf),
            pltpu.VMEM((8, NI * V, 2 * V), bf),
            pltpu.VMEM((NI * V, V), jnp.float32),
            pltpu.VMEM((4, V, V), bf),
            pltpu.VMEM((4, V, V), bf),
            pltpu.VMEM((4, V, V), bf),
            pltpu.VMEM((V, V), bf),
            sem((136,)), sem((8, PIECES)), sem((8, PIECES)), sem((8, PIECES)), sem((8, PIECES)),
            sem((4, PIECES)), sem((4, PIECES)), sem((4, PIECES)), sem((2,)), sem((2,)), sem((17 + 2 * n,)),
        ],
        compiler_params=pltpu.CompilerParams(
            collective_id=0, has_side_effects=True, vmem_limit_bytes=63 * 1024 * 1024
        ),
        cost_estimate=pl.CostEstimate(flops=29_000_000_000, bytes_accessed=7_500_000, transcendentals=0),
        name="ladder",
    )(irrep_dims, chol, amps)
    anywhere = pl.BlockSpec(memory_space=pl.ANY)
    total = pl.pallas_call(
        rest_kernel,
        out_shape=jax.ShapeDtypeStruct((NI * V, V), jnp.float32),
        in_specs=[pl.BlockSpec(memory_space=pltpu.SMEM)] + [anywhere] * 4,
        out_specs=anywhere,
        scratch_shapes=[
            pltpu.VMEM(own, bf),
            pltpu.VMEM(own, bf),
            pltpu.VMEM((V, NI * V), bf),
            pltpu.VMEM((HALF, n * 2 * V), bf),
            pltpu.VMEM((NI * V, V), jnp.float32),
            sem((8 + NI,)),
        ],
        compiler_params=pltpu.CompilerParams(vmem_limit_bytes=60 * 1024 * 1024),
        cost_estimate=pl.CostEstimate(flops=n * 3_600_000_000, bytes_accessed=16_000_000, transcendentals=0),
        name="rest",
    )(irrep_dims, rest_own, rest_par, amps, raw)
    return total.reshape(1, NI, V, V)


def solution(mesh):
    return jax.shard_map(
        shards,
        mesh=mesh,
        in_specs=(P(), P(("sym", "occ"), "tile", None), P("sym", "occ", "tile", None)),
        out_specs=P("sym", "occ", "tile", None),
        check_vma=False,
    )
```

```python
import jax
import jax.numpy as jnp
from jax import lax
from jax.experimental import pallas as pl
from jax.experimental.pallas import tpu as pltpu
from jax.sharding import PartitionSpec as P

V = 384
NI = 8
PIECES = 2
PV = V // PIECES
CROSSF, OWN, PASS_Z, FWD_Y, PASS_Y, PAR = range(6)
SEQUENCE = (1, 1, 1, 1, 1, 1, 1, 2, 2, 2, 2, 2, 2, 2)
UNITS = (
    ((0, 0), (0, 0), (0, 0), (0, 0), (0, 0), (0, 0), (0, 0), (0, 0), (0, 0), (0, 0), (0, 0), (0, 0), (0, 0), (0, 0), (0, 0), (0, 0)),
    ((0, 1), (0, 1), (0, 1), (0, 1), (0, 1), (0, 1), (0, 1), (0, 1), (0, 1), (0, 1), (0, 1), (0, 1), (0, 1), (0, 1), (0, 1), (0, 1)),
    ((0, 3), (0, 3), (0, 3), (0, 3), (0, 3), (0, 3), (0, 3), (0, 3), (0, 3), (0, 3), (0, 3), (0, 3), (0, 3), (0, 3), (0, 3), (0, 3)),
    ((1, 0), (1, 0), (1, 0), (1, 0), (0, 2), (0, 2), (1, 0), (1, 0), (1, 0), (1, 0), (1, 0), (1, 0), (1, 0), (1, 0), (1, 0), (1, 0)),
    ((0, 2), (0, 2), (0, 2), (0, 2), (1, 1), (1, 1), (0, 2), (0, 2), (0, 2), (0, 2), (0, 2), (0, 2), (0, 2), (0, 2), (0, 2), (0, 2)),
    ((1, 1), (1, 1), (1, 1), (1, 1), (1, 3), (1, 3), (1, 1), (1, 1), (1, 3), (1, 3), (1, 1), (1, 1), (1, 1), (1, 1), (1, 1), (1, 1)),
    ((1, 2), (1, 2), (1, 3), (1, 3), (1, 2), (1, 0), (1, 3), (1, 3), (1, 2), (1, 2), (1, 3), (1, 3), (1, 3), (1, 3), (1, 3), (1, 3)),
    ((0, 0), (0, 0), (0, 0), (0, 0), (0, 0), (0, 0), (0, 0), (0, 0), (0, 0), (0, 0), (0, 0), (0, 0), (0, 0), (0, 0), (0, 0), (0, 0)),
    ((1, 0), (1, 0), (1, 0), (1, 0), (0, 1), (1, 0), (1, 0), (1, 0), (1, 0), (1, 0), (1, 0), (1, 0), (1, 0), (1, 0), (1, 0), (1, 0)),
    ((0, 1), (0, 1), (0, 1), (0, 1), (1, 1), (0, 1), (0, 1), (0, 1), (0, 1), (0, 1), (0, 1), (0, 1), (0, 1), (0, 1), (0, 1), (0, 1)),
    ((1, 1), (1, 1), (0, 3), (0, 3), (0, 3), (1, 1), (1, 1), (1, 1), (0, 3), (0, 3), (1, 1), (1, 1), (1, 1), (1, 1), (1, 1), (1, 1)),
    ((0, 3), (0, 3), (1, 3), (1, 1), (1, 3), (0, 3), (0, 3), (0, 3), (1, 3), (1, 3), (0, 3), (0, 3), (0, 3), (0, 3), (0, 3), (0, 3)),
    ((0, 2), (0, 2), (1, 1), (1, 3), (0, 2), (1, 3), (1, 3), (1, 3), (0, 2), (0, 2), (1, 3), (1, 3), (1, 3), (1, 3), (1, 3), (1, 3)),
    ((1, 2), (1, 2), (0, 2), (0, 2), (1, 2), (0, 2), (0, 2), (0, 2), (1, 2), (1, 2), (0, 2), (0, 2), (0, 2), (0, 2), (0, 2), (0, 2)),
)
EVENTS = (
    (
        (13, ((CROSSF, 0), (OWN, 0, 3, 0), (OWN, 0, 1, 0), (PASS_Z, 0, 0), (CROSSF, 1), (PASS_Z, 0, 1), (OWN, 0, 1, 1), (OWN, 0, 3, 1), (PASS_Z, 3, 0), (PASS_Z, 1, 0), (OWN, 1, 0, 0), (OWN, 1, 0, 1),)),
        (24, ((OWN, 0, 2, 0),)),
        (29, ((OWN, 0, 2, 1), (FWD_Y, 0, 0), (FWD_Y, 0, 1),)),
        (39, ((OWN, 1, 1, 0),)),
        (44, ((PASS_Z, 1, 1), (PASS_Z, 3, 1),)),
        (49, ((PASS_Y, 0, 1),)),
        (55, ((OWN, 1, 1, 1),)),
        (59, ((FWD_Y, 1, 0), (FWD_Y, 3, 0),)),
        (63, ((OWN, 1, 2, 0),)),
        (75, ((OWN, 1, 2, 1), (PASS_Z, 2, 0), (PASS_Z, 2, 1),)),
        (78, ((PASS_Y, 1, 0),)),
        (88, ((FWD_Y, 1, 1), (FWD_Y, 3, 1),)),
        (89, ((OWN, 1, 3, 0),)),
        (104, ((FWD_Y, 2, 0), (FWD_Y, 2, 1),)),
        (109, ((PASS_Y, 3, 1),)),
        (121, ((OWN, 1, 3, 1),)),
        (125, ((PASS_Y, 2, 0),)),
    ),
    (
        (13, ((CROSSF, 0), (OWN, 0, 3, 0), (OWN, 0, 1, 0), (PASS_Z, 0, 0), (CROSSF, 1), (PASS_Z, 0, 1), (OWN, 0, 1, 1), (OWN, 0, 3, 1), (PASS_Z, 3, 0), (PASS_Z, 1, 0), (OWN, 1, 0, 0), (OWN, 1, 0, 1),)),
        (24, ((OWN, 0, 2, 0),)),
        (29, ((OWN, 0, 2, 1), (FWD_Y, 0, 0), (FWD_Y, 0, 1),)),
        (39, ((OWN, 1, 1, 0),)),
        (44, ((PASS_Z, 1, 1), (PASS_Z, 3, 1),)),
        (49, ((PASS_Y, 0, 0),)),
        (55, ((OWN, 1, 1, 1),)),
        (59, ((FWD_Y, 1, 0), (FWD_Y, 3, 0),)),
        (63, ((OWN, 1, 2, 0),)),
        (75, ((OWN, 1, 2, 1), (PASS_Z, 2, 0), (PASS_Z, 2, 1),)),
        (78, ((PASS_Y, 3, 0),)),
        (88, ((FWD_Y, 1, 1), (FWD_Y, 3, 1),)),
        (89, ((OWN, 1, 3, 0),)),
        (104, ((OWN, 1, 3, 1), (FWD_Y, 2, 0), (FWD_Y, 2, 1),)),
        (109, ((PASS_Y, 1, 1),)),
        (125, ((PASS_Y, 2, 1),)),
    ),
    (
        (13, ((CROSSF, 0), (OWN, 0, 3, 0), (OWN, 0, 1, 0), (PASS_Z, 0, 0), (CROSSF, 1), (PASS_Z, 0, 1), (OWN, 0, 1, 1), (OWN, 0, 3, 1), (PASS_Z, 3, 0), (PASS_Z, 1, 0), (OWN, 1, 0, 0), (OWN, 1, 0, 1),)),
        (24, ((OWN, 0, 2, 0),)),
        (29, ((OWN, 0, 2, 1), (PAR, 0, 0, 0), (PAR, 0, 0, 1),)),
        (39, ((OWN, 1, 1, 0),)),
        (44, ((OWN, 1, 3, 0), (PASS_Z, 1, 1), (PASS_Z, 3, 1),)),
        (49, ((PASS_Y, 0, 0),)),
        (55, ((OWN, 1, 1, 1),)),
        (59, ((OWN, 1, 3, 1), (PAR, 0, 1, 0), (PAR, 0, 3, 0),)),
        (69, ((PAR, 1, 0, 0),)),
        (70, ((PAR, 1, 0, 1),)),
        (74, ((OWN, 1, 2, 0), (PASS_Z, 2, 0), (PASS_Z, 2, 1),)),
        (75, ((OWN, 1, 2, 1),)),
        (84, ((PASS_Y, 3, 0),)),
        (89, ((PAR, 0, 1, 1), (PAR, 0, 3, 1),)),
        (99, ((PAR, 1, 3, 0),)),
        (104, ((PAR, 0, 2, 1), (PAR, 1, 1, 0),)),
        (106, ((PAR, 0, 2, 0),)),
        (115, ((PASS_Y, 1, 1),)),
        (130, ((PASS_Y, 2, 1),)),
        (137, ((PAR, 1, 3, 1),)),
        (147, ((PAR, 1, 1, 1),)),
        (153, ((PAR, 1, 2, 0),)),
        (163, ((PAR, 1, 2, 1),)),
    ),
    (
        (13, ((CROSSF, 0), (OWN, 0, 3, 0), (OWN, 0, 1, 0), (PASS_Z, 0, 0), (CROSSF, 1), (PASS_Z, 0, 1), (OWN, 0, 1, 1), (OWN, 0, 3, 1), (PASS_Z, 3, 0), (PASS_Z, 1, 0), (OWN, 1, 0, 0), (OWN, 1, 0, 1),)),
        (24, ((OWN, 0, 2, 0),)),
        (29, ((OWN, 0, 2, 1), (PAR, 0, 0, 0), (PAR, 0, 0, 1),)),
        (39, ((OWN, 1, 1, 0),)),
        (44, ((OWN, 1, 3, 0), (PASS_Z, 1, 1), (PASS_Z, 3, 1),)),
        (49, ((PASS_Y, 0, 1),)),
        (55, ((OWN, 1, 1, 1),)),
        (59, ((OWN, 1, 3, 1), (PAR, 0, 1, 0), (PAR, 0, 3, 0),)),
        (69, ((PAR, 1, 0, 1),)),
        (70, ((PAR, 1, 0, 0),)),
        (74, ((OWN, 1, 2, 0), (PASS_Z, 2, 0), (PASS_Z, 2, 1),)),
        (75, ((OWN, 1, 2, 1),)),
        (84, ((PASS_Y, 1, 0),)),
        (89, ((PAR, 0, 1, 1), (PAR, 0, 3, 1),)),
        (99, ((PAR, 1, 1, 0),)),
        (104, ((PAR, 0, 2, 1), (PAR, 1, 3, 0),)),
        (106, ((PAR, 0, 2, 0),)),
        (115, ((PASS_Y, 3, 1),)),
        (130, ((PASS_Y, 2, 0),)),
        (137, ((PAR, 1, 1, 1),)),
        (147, ((PAR, 1, 3, 1),)),
        (153, ((PAR, 1, 2, 1),)),
        (163, ((PAR, 1, 2, 0),)),
    ),
    (
        (13, ((CROSSF, 0), (PASS_Z, 0, 0), (OWN, 0, 3, 0), (OWN, 0, 1, 0), (PAR, 0, 0, 0), (PASS_Z, 0, 1), (OWN, 0, 1, 1), (PAR, 1, 0, 0), (OWN, 0, 3, 1), (CROSSF, 1), (PASS_Z, 3, 0), (PASS_Z, 1, 0),)),
        (24, ((OWN, 0, 2, 0), (PAR, 0, 0, 1), (PAR, 1, 0, 1),)),
        (29, ((OWN, 0, 2, 1), (FWD_Y, 0, 0), (FWD_Y, 0, 1),)),
        (38, ((OWN, 1, 1, 0),)),
        (39, ((PAR, 0, 1, 0), (PAR, 1, 1, 0),)),
        (43, ((OWN, 1, 3, 0), (PASS_Z, 1, 1), (PASS_Z, 3, 1),)),
        (52, ((OWN, 1, 1, 1), (PAR, 1, 3, 0), (PAR, 0, 3, 0), (FWD_Y, 3, 0), (OWN, 1, 3, 1), (FWD_Y, 1, 0),)),
        (63, ((OWN, 1, 0, 0), (PAR, 0, 1, 1),)),
        (68, ((OWN, 1, 2, 0), (OWN, 1, 2, 1), (PASS_Z, 2, 0), (PASS_Z, 2, 1),)),
        (78, ((PAR, 0, 3, 1), (PAR, 1, 1, 1),)),
        (83, ((FWD_Y, 1, 1), (FWD_Y, 3, 1),)),
        (95, ((OWN, 1, 0, 1), (PAR, 1, 3, 1),)),
        (98, ((FWD_Y, 2, 0), (FWD_Y, 2, 1),)),
        (109, ((PAR, 0, 2, 0), (PAR, 1, 2, 0),)),
        (124, ((PAR, 1, 2, 1),)),
        (125, ((PAR, 0, 2, 1),)),
    ),
    (
        (13, ((CROSSF, 0), (PASS_Z, 0, 0), (OWN, 0, 3, 0), (OWN, 0, 1, 0), (PAR, 1, 0, 0), (PASS_Z, 0, 1), (OWN, 0, 1, 1), (PAR, 0, 0, 0), (OWN, 0, 3, 1), (CROSSF, 1), (PASS_Z, 3, 0), (PASS_Z, 1, 0),)),
        (24, ((OWN, 0, 2, 0), (PAR, 0, 0, 1), (PAR, 1, 0, 1),)),
        (29, ((OWN, 0, 2, 1), (FWD_Y, 0, 0), (FWD_Y, 0, 1),)),
        (38, ((OWN, 1, 1, 0),)),
        (39, ((PAR, 0, 1, 0), (PAR, 1, 1, 0),)),
        (43, ((OWN, 1, 3, 0), (PASS_Z, 1, 1), (PASS_Z, 3, 1),)),
        (52, ((OWN, 1, 1, 1), (PAR, 0, 3, 0), (PAR, 1, 3, 0), (FWD_Y, 3, 0), (OWN, 1, 3, 1), (FWD_Y, 1, 0),)),
        (63, ((OWN, 1, 0, 0), (OWN, 1, 0, 1),)),
        (68, ((OWN, 1, 2, 0), (OWN, 1, 2, 1), (PASS_Z, 2, 0), (PASS_Z, 2, 1),)),
        (78, ((PAR, 0, 1, 1), (PAR, 1, 1, 1),)),
        (83, ((FWD_Y, 1, 1), (FWD_Y, 3, 1),)),
        (93, ((PAR, 0, 3, 1),)),
        (95, ((PAR, 1, 3, 1),)),
        (98, ((FWD_Y, 2, 0), (FWD_Y, 2, 1),)),
        (109, ((PAR, 0, 2, 0), (PAR, 1, 2, 0),)),
        (124, ((PAR, 0, 2, 1),)),
        (125, ((PAR, 1, 2, 1),)),
    ),
    (
        (13, ((CROSSF, 0), (PASS_Z, 0, 0), (OWN, 0, 3, 0), (OWN, 0, 1, 0), (CROSSF, 1), (PASS_Z, 0, 1), (OWN, 0, 1, 1), (OWN, 0, 3, 1), (PASS_Z, 3, 0), (PASS_Z, 1, 0), (OWN, 1, 0, 0), (OWN, 1, 0, 1),)),
        (24, ((OWN, 0, 2, 0),)),
        (29, ((OWN, 0, 2, 1), (FWD_Y, 0, 0), (FWD_Y, 0, 1),)),
        (39, ((OWN, 1, 1, 0),)),
        (44, ((OWN, 1, 3, 0), (PASS_Z, 1, 1), (PASS_Z, 3, 1),)),
        (49, ((PAR, 0, 0, 0), (PAR, 1, 0, 0),)),
        (54, ((OWN, 1, 1, 1),)),
        (58, ((OWN, 1, 3, 1), (FWD_Y, 3, 0),)),
        (59, ((FWD_Y, 1, 0),)),
        (64, ((PAR, 0, 0, 1), (PAR, 1, 0, 1),)),
        (74, ((OWN, 1, 2, 0), (OWN, 1, 2, 1), (PASS_Z, 2, 0), (PASS_Z, 2, 1),)),
        (80, ((PAR, 0, 1, 0), (PAR, 1, 3, 0),)),
        (88, ((FWD_Y, 1, 1),)),
        (89, ((FWD_Y, 3, 1),)),
        (95, ((PAR, 0, 3, 0), (PAR, 1, 1, 0),)),
        (104, ((FWD_Y, 2, 0), (FWD_Y, 2, 1),)),
        (109, ((PAR, 1, 1, 1),)),
        (111, ((PAR, 0, 1, 1),)),
        (125, ((PAR, 0, 3, 1), (PAR, 1, 3, 1),)),
        (141, ((PAR, 0, 2, 0), (PAR, 1, 2, 0),)),
        (156, ((PAR, 0, 2, 1), (PAR, 1, 2, 1),)),
    ),
    (
        (13, ((CROSSF, 0), (PASS_Z, 0, 0), (OWN, 0, 3, 0), (OWN, 0, 1, 0), (CROSSF, 1), (PASS_Z, 0, 1), (OWN, 0, 1, 1), (OWN, 0, 3, 1), (PASS_Z, 3, 0), (PASS_Z, 1, 0), (OWN, 1, 0, 0),)),
        (24, ((OWN, 0, 2, 0),)),
        (29, ((OWN, 0, 2, 1), (OWN, 1, 0, 1), (FWD_Y, 0, 0), (FWD_Y, 0, 1),)),
        (38, ((OWN, 1, 1, 0),)),
        (43, ((OWN, 1, 3, 0), (PASS_Z, 1, 1),)),
        (44, ((PASS_Z, 3, 1),)),
        (48, ((PAR, 0, 0, 0), (PAR, 1, 0, 0),)),
        (54, ((OWN, 1, 1, 1),)),
        (58, ((OWN, 1, 3, 1), (FWD_Y, 1, 0), (FWD_Y, 3, 0),)),
        (63, ((PAR, 0, 0, 1), (PAR, 1, 0, 1),)),
        (73, ((OWN, 1, 2, 0), (PASS_Z, 2, 0), (PASS_Z, 2, 1),)),
        (74, ((OWN, 1, 2, 1),)),
        (78, ((PAR, 0, 3, 0), (PAR, 1, 3, 0),)),
        (88, ((FWD_Y, 1, 1), (FWD_Y, 3, 1),)),
        (95, ((PAR, 0, 1, 0), (PAR, 1, 1, 0),)),
        (104, ((FWD_Y, 2, 0), (FWD_Y, 2, 1),)),
        (109, ((PAR, 0, 1, 1), (PAR, 1, 1, 1),)),
        (125, ((PAR, 0, 3, 1), (PAR, 1, 3, 1),)),
        (140, ((PAR, 0, 2, 0), (PAR, 1, 2, 0),)),
        (156, ((PAR, 0, 2, 1), (PAR, 1, 2, 1),)),
    ),
    (
        (13, ((CROSSF, 0), (PAR, 0, 0, 0), (OWN, 0, 3, 0), (OWN, 0, 1, 0), (FWD_Y, 0, 0), (CROSSF, 1), (OWN, 0, 1, 1), (PAR, 0, 0, 1), (OWN, 0, 3, 1), (FWD_Y, 0, 1), (OWN, 1, 0, 0), (OWN, 1, 0, 1),)),
        (24, ((OWN, 0, 2, 0), (FWD_Y, 1, 0), (PAR, 0, 1, 0),)),
        (29, ((OWN, 0, 2, 1), (PASS_Y, 0, 0), (PASS_Y, 0, 1),)),
        (39, ((FWD_Y, 3, 0), (PAR, 0, 3, 0),)),
        (43, ((OWN, 1, 3, 0),)),
        (44, ((PASS_Y, 1, 0),)),
        (49, ((PAR, 1, 0, 0),)),
        (55, ((FWD_Y, 1, 1), (PAR, 0, 1, 1),)),
        (58, ((OWN, 1, 3, 1),)),
        (59, ((PAR, 1, 0, 1),)),
        (64, ((PASS_Y, 3, 0),)),
        (70, ((FWD_Y, 3, 1), (PAR, 0, 3, 1),)),
        (73, ((OWN, 1, 2, 0), (OWN, 1, 2, 1),)),
        (74, ((PAR, 1, 1, 0),)),
        (78, ((PASS_Y, 1, 1),)),
        (83, ((FWD_Y, 2, 0), (PAR, 0, 2, 0),)),
        (87, ((OWN, 1, 1, 0),)),
        (88, ((PASS_Y, 3, 1),)),
        (93, ((PAR, 1, 3, 0),)),
        (98, ((FWD_Y, 2, 1), (PAR, 0, 2, 1),)),
        (102, ((PASS_Y, 2, 0),)),
        (108, ((PAR, 1, 1, 1),)),
        (119, ((OWN, 1, 1, 1), (PAR, 1, 3, 1),)),
        (124, ((PASS_Y, 2, 1),)),
        (134, ((PAR, 1, 2, 0),)),
        (145, ((PAR, 1, 2, 1),)),
    ),
    (
        (13, ((CROSSF, 0), (PAR, 0, 0, 0), (OWN, 0, 3, 0), (OWN, 0, 1, 0), (FWD_Y, 0, 0), (CROSSF, 1), (OWN, 0, 1, 1), (PAR, 0, 0, 1), (OWN, 0, 3, 1), (FWD_Y, 0, 1), (OWN, 1, 0, 0), (OWN, 1, 0, 1),)),
        (24, ((OWN, 0, 2, 0), (FWD_Y, 1, 0), (PAR, 0, 1, 0),)),
        (29, ((OWN, 0, 2, 1), (PASS_Y, 0, 0), (PASS_Y, 0, 1),)),
        (39, ((FWD_Y, 3, 0), (PAR, 0, 3, 0),)),
        (43, ((OWN, 1, 3, 0),)),
        (44, ((PASS_Y, 1, 0),)),
        (49, ((PAR, 1, 0, 0),)),
        (55, ((FWD_Y, 1, 1), (PAR, 0, 1, 1),)),
        (58, ((OWN, 1, 3, 1),)),
        (59, ((PAR, 1, 0, 1),)),
        (64, ((PASS_Y, 3, 0),)),
        (70, ((FWD_Y, 3, 1), (PAR, 0, 3, 1),)),
        (73, ((OWN, 1, 2, 0), (OWN, 1, 2, 1),)),
        (74, ((PAR, 1, 1, 0),)),
        (78, ((PASS_Y, 1, 1),)),
        (83, ((FWD_Y, 2, 0), (PAR, 0, 2, 0),)),
        (87, ((OWN, 1, 1, 0),)),
        (88, ((PASS_Y, 3, 1),)),
        (93, ((PAR, 1, 3, 0),)),
        (98, ((FWD_Y, 2, 1), (PAR, 0, 2, 1),)),
        (102, ((OWN, 1, 1, 1), (PASS_Y, 2, 0),)),
        (108, ((PAR, 1, 1, 1),)),
        (119, ((PAR, 1, 3, 1),)),
        (124, ((PASS_Y, 2, 1),)),
        (134, ((PAR, 1, 2, 0),)),
        (145, ((PAR, 1, 2, 1),)),
    ),
    (
        (13, ((CROSSF, 0), (FWD_Y, 0, 0), (OWN, 0, 3, 0), (OWN, 0, 1, 0), (PAR, 0, 0, 0), (CROSSF, 1), (OWN, 0, 1, 1), (FWD_Y, 0, 1), (OWN, 0, 3, 1), (PAR, 0, 0, 1), (OWN, 1, 0, 0), (OWN, 1, 0, 1),)),
        (24, ((OWN, 0, 2, 0), (FWD_Y, 1, 0), (PAR, 0, 1, 0),)),
        (29, ((OWN, 0, 2, 1), (PASS_Y, 0, 0), (PASS_Y, 0, 1),)),
        (38, ((OWN, 1, 1, 0),)),
        (39, ((FWD_Y, 3, 0), (PAR, 0, 3, 0),)),
        (43, ((OWN, 1, 3, 0),)),
        (44, ((PASS_Y, 1, 0),)),
        (48, ((PAR, 1, 0, 0),)),
        (54, ((OWN, 1, 1, 1), (FWD_Y, 1, 1),)),
        (55, ((PAR, 0, 1, 1),)),
        (58, ((OWN, 1, 3, 1),)),
        (59, ((PAR, 1, 0, 1),)),
        (63, ((PASS_Y, 3, 0),)),
        (69, ((FWD_Y, 3, 1), (PAR, 0, 3, 1),)),
        (73, ((OWN, 1, 2, 0), (OWN, 1, 2, 1),)),
        (74, ((PAR, 1, 1, 0),)),
        (78, ((PASS_Y, 1, 1),)),
        (84, ((FWD_Y, 2, 0), (PAR, 0, 2, 0),)),
        (89, ((PASS_Y, 3, 1),)),
        (95, ((PAR, 1, 3, 0),)),
        (99, ((FWD_Y, 2, 1), (PAR, 0, 2, 1),)),
        (104, ((PASS_Y, 2, 0),)),
        (109, ((PAR, 1, 1, 1),)),
        (121, ((PAR, 1, 3, 1),)),
        (125, ((PASS_Y, 2, 1),)),
        (135, ((PAR, 1, 2, 0),)),
        (147, ((PAR, 1, 2, 1),)),
    ),
    (
        (13, ((CROSSF, 0), (FWD_Y, 0, 0), (OWN, 0, 3, 0), (OWN, 0, 1, 0), (PAR, 0, 0, 0), (CROSSF, 1), (OWN, 0, 1, 1), (FWD_Y, 0, 1), (OWN, 0, 3, 1), (PAR, 0, 0, 1), (OWN, 1, 0, 0), (OWN, 1, 0, 1),)),
        (24, ((OWN, 0, 2, 0), (FWD_Y, 1, 0), (PAR, 0, 1, 0),)),
        (29, ((OWN, 0, 2, 1), (PASS_Y, 0, 0), (PASS_Y, 0, 1),)),
        (38, ((OWN, 1, 1, 0),)),
        (39, ((FWD_Y, 3, 0), (PAR, 0, 3, 0),)),
        (43, ((OWN, 1, 3, 0),)),
        (44, ((PASS_Y, 1, 0),)),
        (48, ((PAR, 1, 0, 0),)),
        (54, ((OWN, 1, 1, 1), (FWD_Y, 1, 1),)),
        (55, ((PAR, 0, 1, 1),)),
        (58, ((OWN, 1, 3, 1),)),
        (59, ((PAR, 1, 0, 1),)),
        (63, ((PASS_Y, 3, 0),)),
        (69, ((FWD_Y, 3, 1), (PAR, 0, 3, 1),)),
        (73, ((OWN, 1, 2, 0), (OWN, 1, 2, 1),)),
        (74, ((PAR, 1, 1, 0),)),
        (78, ((PASS_Y, 1, 1),)),
        (84, ((FWD_Y, 2, 0), (PAR, 0, 2, 0),)),
        (89, ((PASS_Y, 3, 1),)),
        (95, ((PAR, 1, 3, 0),)),
        (99, ((FWD_Y, 2, 1), (PAR, 0, 2, 1),)),
        (104, ((PASS_Y, 2, 0),)),
        (109, ((PAR, 1, 1, 1),)),
        (121, ((PAR, 1, 3, 1),)),
        (125, ((PASS_Y, 2, 1),)),
        (137, ((PAR, 1, 2, 0),)),
        (147, ((PAR, 1, 2, 1),)),
    ),
    (
        (13, ((CROSSF, 0), (OWN, 0, 3, 0), (OWN, 0, 1, 0), (FWD_Y, 0, 0), (CROSSF, 1), (OWN, 0, 1, 1), (OWN, 0, 3, 1), (FWD_Y, 0, 1), (OWN, 1, 0, 0), (PAR, 0, 0, 0),)),
        (24, ((OWN, 0, 2, 0), (FWD_Y, 1, 0),)),
        (29, ((OWN, 0, 2, 1), (OWN, 1, 0, 1), (PAR, 1, 0, 0),)),
        (38, ((OWN, 1, 1, 0),)),
        (39, ((FWD_Y, 3, 0),)),
        (43, ((OWN, 1, 3, 0), (PAR, 0, 0, 1), (PAR, 1, 0, 1),)),
        (54, ((OWN, 1, 1, 1), (FWD_Y, 1, 1),)),
        (58, ((OWN, 1, 3, 1), (PAR, 0, 1, 0), (PAR, 1, 1, 0),)),
        (69, ((FWD_Y, 3, 1),)),
        (73, ((PAR, 0, 3, 0), (PAR, 1, 3, 0),)),
        (84, ((FWD_Y, 2, 0),)),
        (88, ((PAR, 0, 1, 1), (PAR, 1, 1, 1),)),
        (99, ((FWD_Y, 2, 1),)),
        (104, ((PAR, 0, 3, 1), (PAR, 1, 3, 1),)),
        (109, ((OWN, 1, 2, 0),)),
        (119, ((PAR, 0, 2, 0), (PAR, 1, 2, 0),)),
        (135, ((PAR, 0, 2, 1), (PAR, 1, 2, 1),)),
        (141, ((OWN, 1, 2, 1),)),
    ),
    (
        (13, ((CROSSF, 0), (OWN, 0, 3, 0), (OWN, 0, 1, 0), (FWD_Y, 0, 0), (CROSSF, 1), (OWN, 0, 1, 1), (OWN, 0, 3, 1), (FWD_Y, 0, 1), (OWN, 1, 0, 0), (PAR, 1, 0, 0),)),
        (24, ((OWN, 0, 2, 0), (FWD_Y, 1, 0),)),
        (29, ((OWN, 0, 2, 1), (OWN, 1, 0, 1), (PAR, 0, 0, 0),)),
        (38, ((OWN, 1, 1, 0),)),
        (39, ((FWD_Y, 3, 0),)),
        (43, ((OWN, 1, 3, 0), (PAR, 0, 0, 1), (PAR, 1, 0, 1),)),
        (54, ((OWN, 1, 1, 1), (FWD_Y, 1, 1),)),
        (58, ((OWN, 1, 3, 1), (PAR, 0, 1, 0), (PAR, 1, 1, 0),)),
        (69, ((FWD_Y, 3, 1),)),
        (73, ((PAR, 0, 3, 0), (PAR, 1, 3, 0),)),
        (84, ((FWD_Y, 2, 0),)),
        (88, ((PAR, 0, 1, 1), (PAR, 1, 1, 1),)),
        (99, ((FWD_Y, 2, 1),)),
        (104, ((PAR, 0, 3, 1), (PAR, 1, 3, 1),)),
        (109, ((OWN, 1, 2, 0),)),
        (119, ((PAR, 0, 2, 0), (PAR, 1, 2, 0),)),
        (125, ((OWN, 1, 2, 1),)),
        (135, ((PAR, 0, 2, 1), (PAR, 1, 2, 1),)),
    ),
    (
        (13, ((CROSSF, 0), (OWN, 0, 3, 0), (OWN, 0, 1, 0), (FWD_Y, 0, 0), (CROSSF, 1), (OWN, 0, 1, 1), (OWN, 0, 3, 1), (FWD_Y, 0, 1), (OWN, 1, 0, 0), (PAR, 0, 0, 0),)),
        (24, ((OWN, 0, 2, 0), (FWD_Y, 1, 0),)),
        (29, ((OWN, 0, 2, 1), (OWN, 1, 0, 1), (PAR, 1, 0, 0),)),
        (38, ((OWN, 1, 1, 0),)),
        (39, ((FWD_Y, 3, 0),)),
        (43, ((OWN, 1, 3, 0), (PAR, 1, 0, 1),)),
        (44, ((PAR, 0, 0, 1),)),
        (54, ((OWN, 1, 1, 1), (FWD_Y, 1, 1),)),
        (58, ((OWN, 1, 3, 1), (PAR, 0, 1, 0), (PAR, 1, 1, 0),)),
        (69, ((FWD_Y, 3, 1),)),
        (73, ((OWN, 1, 2, 0), (OWN, 1, 2, 1), (PAR, 0, 3, 0), (PAR, 1, 3, 0),)),
        (84, ((FWD_Y, 2, 0),)),
        (88, ((PAR, 0, 1, 1), (PAR, 1, 1, 1),)),
        (99, ((FWD_Y, 2, 1),)),
        (102, ((PAR, 1, 3, 1),)),
        (104, ((PAR, 0, 3, 1),)),
        (119, ((PAR, 0, 2, 0), (PAR, 1, 2, 0),)),
        (135, ((PAR, 0, 2, 1), (PAR, 1, 2, 1),)),
    ),
    (
        (13, ((CROSSF, 0), (OWN, 0, 3, 0), (OWN, 0, 1, 0), (FWD_Y, 0, 0), (CROSSF, 1), (OWN, 0, 1, 1), (OWN, 0, 3, 1), (FWD_Y, 0, 1), (OWN, 1, 0, 0), (PAR, 1, 0, 0),)),
        (24, ((OWN, 0, 2, 0), (FWD_Y, 1, 0),)),
        (29, ((OWN, 0, 2, 1), (OWN, 1, 0, 1), (PAR, 0, 0, 0),)),
        (38, ((OWN, 1, 1, 0),)),
        (39, ((FWD_Y, 3, 0),)),
        (43, ((OWN, 1, 3, 0), (PAR, 0, 0, 1),)),
        (44, ((PAR, 1, 0, 1),)),
        (54, ((OWN, 1, 1, 1), (FWD_Y, 1, 1),)),
        (58, ((OWN, 1, 3, 1), (PAR, 0, 1, 0), (PAR, 1, 1, 0),)),
        (69, ((FWD_Y, 3, 1),)),
        (73, ((OWN, 1, 2, 0), (OWN, 1, 2, 1), (PAR, 0, 3, 0), (PAR, 1, 3, 0),)),
        (84, ((FWD_Y, 2, 0),)),
        (88, ((PAR, 0, 1, 1), (PAR, 1, 1, 1),)),
        (99, ((FWD_Y, 2, 1),)),
        (102, ((PAR, 0, 3, 1),)),
        (104, ((PAR, 1, 3, 1),)),
        (119, ((PAR, 0, 2, 0), (PAR, 1, 2, 0),)),
        (135, ((PAR, 0, 2, 1), (PAR, 1, 2, 1),)),
    ),
)

STAGES = len(SEQUENCE)
POINTS = 13 * STAGES + 1
PAR_AT, T1_AT, T2_AT, T3_AT, TC_AT, SLOTS = 32, 64, 72, 80, 88, 90
WAYS = ("x+", "x-", "y+", "y-", "z+", "z-", "core", "ya", "yb", "za", "zb")
WAIT = 15
CLASSES = [(x, y) for x in range(4) for y in range(4)]


def sign_of(j, k):
    return "+" if (k + (0, 1, 1, 0)[j]) % 2 == 0 else "-"


def name_of(x, y, row, j):
    return (y // 2 + row) % 2 * 4 + (x + 4 - j) % 4


def row_behind(y, sign):
    return (y + 3) % 4 // 2 if sign == "+" else (y + 1) % 4 // 2


def feed(x, y, j, k, src):
    up = y // 2 == 1
    final, via1, via2 = ("par", name_of(x, y, 0, j), k), ("t1", j, k), ("t2", j, k)
    sends = []
    if x in (0, 1):
        sends.append((src, via1, "z" + sign_of(j, k)))
    if x == 1:
        sends.append((src, final, "ya"))
    if x in (2, 3):
        sends.append((src, final if x == 2 and not up else via1, "za"))
        sends.append((src, final if x == 2 and up else via2, "zb"))
    return sends


def expand(x, y, event):
    kind, args = event[0], event[1:]
    up = y // 2 == 1
    ops = []
    if kind == CROSSF:
        (k,) = args
        sign = "+-"[k]
        ops = [("tc", k), (("tc", k), ("own", row_behind(y, sign) * 4 + x, k), "y" + sign)]
    if kind == OWN:
        row, j, k = args
        here = ("own", name_of(x, y, row, j), k)
        ops = [here]
        if (row, j) == (1, 0) or (j == 1 and (k + row) % 2 == 0):
            ops.append((here, here, "x+"))
        if (row, j) == (1, 0) or (j == 3 and (k + row) % 2 == 1):
            ops.append((here, here, "x-"))
        if row == 0:
            ops += feed(x, y, j, k, here)
        ops.append((here, here, "core"))
    if kind == PASS_Z:
        j, k = args
        here = ("t1", j, k)
        there = ("par", name_of(x, y, 0, j), k) if x == 0 and up else ("t2", j, k)
        ops = [here, (here, there, "z" + sign_of(j, k))]
    if kind == FWD_Y:
        j, k = args
        final, there, way = ("par", name_of(x, y, 0, j), k), ("t3", j, k), "y" + sign_of(j, k)
        if x == 3 or (x == 2 and up):
            ops += [("t1", j, k), (("t1", j, k), final, "ya") if x == 3 else (("t1", j, k), there, way)]
        if x in (1, 3) or not up:
            ops += [("t2", j, k), (("t2", j, k), final, "yb") if x in (1, 3) else (("t2", j, k), there, way)]
    if kind == PASS_Y:
        j, k = args
        sign = sign_of(j, k)
        row = row_behind(y, sign)
        if x == 2 or row == 0:
            ops = [("t3", j, k), (("t3", j, k), ("par", row * 4 + (x + 4 - j) % 4, k), "y" + sign)]
    if kind == PAR:
        row, j, k = args
        here = ("par", name_of(x, y, row, j), k)
        ops = [here, (here, here, "core")]
    return ops


def slot(place, c):
    kind, rest = place[0], place[1:]
    if kind in ("own", "par"):
        q, k = rest
        return (PAR_AT if kind == "par" else 0) + q * 4 + c * 2 + k
    if kind == "tc":
        return TC_AT + rest[0]
    return {"t1": T1_AT, "t2": T2_AT, "t3": T3_AT}[kind] + rest[0] * 2 + rest[1]


def tables(x, y):
    per_core = []
    for c in range(2):
        ops, begins, sends, at = [], [], 0, dict(EVENTS[CLASSES.index((x, y))])
        for point in range(POINTS):
            begins.append(len(ops))
            for event in at.get(point, ()):
                for op in expand(x, y, event):
                    if isinstance(op[0], str):
                        ops.append(slot(op, c) + 2097152 * WAIT)
                    else:
                        src, dst, way = op
                        ops.append(slot(src, c) + 128 * slot(dst, c) + 16384 * sends + 2097152 * WAYS.index(way))
                        sends += 1
        per_core.append((ops, begins + [len(ops)], sends))
    return per_core


TABLES = {cls: tables(*cls) for cls in CLASSES}
MOST_OPS = max(len(ops) for cores in TABLES.values() for ops, _, _ in cores)
MOST_SENDS = max(sends for cores in TABLES.values() for _, _, sends in cores)
FIRST_SENDS = 12


def columns(t):
    first, last = t * 256, (t + 1) * 256
    cuts = [first] + [cut for cut in range(0, NI * V, V) if first < cut < last] + [last]
    return [(u - first, w - first, u // V, u % V) for u, w in zip(cuts, cuts[1:])]


def kernel(dims, mine, amps, out, out_own, out_par, buf, rc, half, acc, ops, begins, devs,
           ssem, first_sem, rsem, local_sem):
    sym, tile, c = lax.axis_index("sym"), lax.axis_index("tile"), lax.axis_index("occ")
    x, yhi = sym % 4, sym // 4
    x0, x1 = x % 2, x // 2
    z, ylo = tile // 2, tile % 2
    z0, z1 = z % 2, z // 2
    y = 2 * yhi + ylo
    none = sym == 0

    def dev(dx=0, dy=0, dz=0, dc=0):
        xx, yy, zz = (x + 4 + dx) % 4, (y + 4 + dy) % 4, (z + 4 + dz) % 4
        return ((yy // 2) * 4 + xx) * 16 + (zz * 2 + yy % 2) * 2 + (c + dc) % 2

    step_a = 1 - 2 * (yhi + ylo - 2 * yhi * ylo)
    step_z = 1 - 2 * z0
    to = {
        "x+": dev(dx=1), "x-": dev(dx=-1), "y+": dev(dy=1), "y-": dev(dy=-1), "z+": dev(dz=1), "z-": dev(dz=-1),
        "core": dev(dc=1), "ya": dev(dy=step_a), "yb": dev(dy=-step_a), "za": dev(dz=step_z), "zb": dev(dz=-step_z),
    }
    barrier = pltpu.get_barrier_semaphore()
    for way in WAYS[:7]:
        pl.semaphore_signal(barrier, inc=1, device_id=to[way], device_id_type=pl.DeviceIdType.LOGICAL)

    def own_slot(q, core, k):
        return q * 4 + core * 2 + k

    keep = []
    for k in range(PIECES):
        keep.append(pltpu.make_async_copy(mine.at[pl.ds(k * PV, PV)], buf.at[own_slot(sym, c, k)], local_sem.at[8 + k]))
        keep[-1].start()
    loads = [pltpu.make_async_copy(amps.at[i], rc.at[:, pl.ds(i * V, V)], local_sem.at[i]) for i in range(NI)]
    for load in loads:
        load.start()

    pl.semaphore_wait(barrier, 7)

    def remote(src, dst_slot, sem, where):
        return pltpu.make_async_remote_copy(
            src, buf.at[dst_slot], sem, rsem.at[dst_slot], device_id=where, device_id_type=pl.DeviceIdType.LOGICAL
        )

    def arrived(at):
        remote(buf.at[at], at, first_sem.at[0], to["core"]).wait_recv()

    firsts = []

    def first(src, place, where, cond=None):
        index = len(firsts)
        if cond is None:
            remote(src, place, first_sem.at[index], where).start()
        else:
            pl.when(cond)(lambda: remote(src, place, first_sem.at[index], where).start())
        firsts.append((src, place, cond, index))

    step_2 = {k: {"+": to["z+"], "-": to["z-"]}[sign_of(0, k)] for k in range(PIECES)}
    for k in range(PIECES):
        src = mine.at[pl.ds(k * PV, PV)]
        home = own_slot(sym, c, k)
        final, via1, via2 = PAR_AT + home, T1_AT + k, T2_AT + k
        first(src, home, to["core"])
        first(src, home, to["x+"])
        first(src, home, to["x-"])
        first(src, TC_AT + k, to["y" + "+-"[k]])
        direct_b, direct_a = x0 + 2 * (1 - x1) + (1 - yhi) == 0, x0 + 2 * (1 - x1) + yhi == 0
        where_b = x1 * to["zb"] + (1 - x1) * step_2[k]
        place_b = jnp.where(direct_b, final, x1 * via2 + (1 - x1) * via1)
        first(src, place_b, where_b)
        where_a = x1 * to["za"] + (1 - x1) * to["ya"]
        place_a = jnp.where(direct_a | (x1 == 0), final, via1)
        first(src, place_a, where_a, x > 0)

    for (at_x, at_y), cores in TABLES.items():
        @pl.when((x == at_x) & (y == at_y))
        def _():
            (ops0, begins0, _), (ops1, _, _) = cores
            for n, (op0, op1) in enumerate(zip(ops0, ops1)):
                ops[n] = op0 + (op1 - op0) * c if op0 != op1 else op0
            for n, begin in enumerate(begins0):
                begins[n] = begin
    for n, way in enumerate(WAYS):
        devs[n] = to[way]

    n_row = dims[tile]
    n_col = dims[(z1 + yhi - 2 * z1 * yhi) * 4 + (z0 + x1 - 2 * z0 * x1) * 2 + (ylo + x0 - 2 * ylo * x0)]
    live_r = jnp.where(lax.broadcasted_iota(jnp.int32, (V, V), 0) < n_row, 1.0, 0.0)
    live = jnp.where(lax.broadcasted_iota(jnp.int32, (V, V), 1) < n_col, live_r, 0.0).astype(jnp.bfloat16)
    acc[...] = jnp.zeros_like(acc)
    for load in loads:
        load.wait()
    for i in range(NI):
        rc[:, i * V:(i + 1) * V] = rc[:, i * V:(i + 1) * V] * live
    for copy in keep:
        copy.wait()

    def decoded(n):
        op = ops[n]
        src, rest = lax.rem(op, 128), lax.div(op, 128)
        dst, rest = lax.rem(rest, 128), lax.div(rest, 128)
        return src, dst, lax.rem(rest, 128), lax.div(rest, 128)

    def events(point):
        @pl.loop(begins[point], begins[point + 1])
        def _(n):
            src, dst, index, way = decoded(n)

            @pl.when(way == WAIT)
            def _():
                arrived(src)

            @pl.when(way != WAIT)
            def _():
                remote(buf.at[src], dst, ssem.at[index], devs[way]).start()

    digit = (1 + 7 * x0) * (1 + 63 * x1) * (1 + 4095 * yhi)

    def chosen(groups, n):
        code = 0
        for k, names in enumerate(groups):
            packed = [0, 0]
            for (at_x, at_y), (row, j) in zip(CLASSES, names):
                packed[at_y % 2] += (row * 4 + j) * 8 ** (at_y // 2 * 4 + at_x)
            code = code + (n == k) * 1 * (packed[0] + (packed[1] - packed[0]) * ylo)
        code = lax.rem(lax.div(code, digit), 8)
        return (yhi + code // 4) % 2 * 4 + (x + 4 - code % 4) % 4

    def unit(base, q, core):
        at = base + q * 4 + core * 2
        return buf[pl.ds(at, 2)].reshape(V, V)

    def first_stage(n, q):
        for k in range(PIECES):
            arrived(own_slot(q, 1 - c, k))

        @pl.when(none)
        def _():
            pltpu.make_async_copy(buf.at[pl.ds(q * 4, 4)], buf.at[pl.ds(PAR_AT + q * 4, 4)], local_sem.at[10 + q]).start()

        @pl.loop(0, 4)
        def _(m):
            for t in range(3):
                events(13 * n + 1 + 3 * m + t)
                cols = pl.ds(pl.multiple_of(m * (2 * V) + t * 256, 256), 256)
                left = buf[pl.ds(q * 4, 4)].reshape(2 * V, V)
                r = jnp.dot(left, rc[:, cols], preferred_element_type=jnp.float32).astype(jnp.bfloat16)
                for lo_col, hi_col, pair, at in columns(t):
                    rows = pl.ds(pl.multiple_of((2 * m + pair) * V, V), V)
                    for p in range(2):
                        half[q, rows, pl.ds(p * V + at, hi_col - lo_col)] = r[p * V:(p + 1) * V, lo_col:hi_col]

    def second_stage(n, q):
        @pl.when(none)
        def _():
            pltpu.make_async_copy(buf.at[pl.ds(q * 4, 4)], buf.at[pl.ds(PAR_AT + q * 4, 4)], local_sem.at[10 + q]).wait()

        @pl.when(jnp.logical_not(none))
        def _():
            for k in range(PIECES):
                arrived(PAR_AT + own_slot(q, 1 - c, k))

        @pl.loop(0, 4)
        def _(m):
            rows = pl.ds(pl.multiple_of(m * (2 * V), 2 * V), 2 * V)
            for t, (b0, b1) in enumerate(((0, 256), (256, 384))):
                events(13 * n + 1 + 3 * m + t)
                right = jnp.concatenate([unit(PAR_AT, q, p)[b0:b1] for p in range(2)], axis=1)
                acc[rows, b0:b1] += lax.dot_general(
                    half[q, rows, :], right, (((1,), (1,)), ((), ())), preferred_element_type=jnp.float32
                )

            @pl.when(n == STAGES - 1)
            def _():
                pltpu.make_async_copy(acc.at[rows], out.at[rows], local_sem.at[m]).start()


    @pl.loop(0, STAGES)
    def _(n):
        second = sum((n == k) * 1 for k, stage in enumerate(SEQUENCE) if stage == 2)
        q = chosen(UNITS, n)
        events(13 * n)
        pl.when(second == 0)(lambda: first_stage(n, q))
        pl.when(second == 1)(lambda: second_stage(n, q))

    events(POINTS - 1)

    leaving = []
    for r in range(len(REST)):
        q = chosen(REST, jnp.int32(r))
        for k in range(PIECES):
            arrived(own_slot(q, 1 - c, k))

        @pl.when(jnp.logical_not(none))
        def _():
            for k in range(PIECES):
                arrived(PAR_AT + own_slot(q, 1 - c, k))

        par_at = jnp.where(none, 0, PAR_AT) + q * 4
        for source, target, sem in ((q * 4, out_own.at[r], 18 + 2 * r), (par_at, out_par.at[r], 19 + 2 * r)):
            leaving.append(pltpu.make_async_copy(buf.at[pl.ds(source, 4)], target, local_sem.at[sem]))
            leaving[-1].start()

    for src, place, cond, index in firsts:
        def sent(src=src, place=place, index=index):
            remote(src, place, first_sem.at[index], to["core"]).wait_send()

        if cond is None:
            sent()
        else:
            pl.when(cond)(sent)

    @pl.loop(0, begins[POINTS])
    def _(n):
        src, dst, index, way = decoded(n)

        @pl.when(way != WAIT)
        def _():
            remote(buf.at[src], dst, ssem.at[index], devs[way]).wait_send()

    for m in range(4):
        rows = pl.ds(m * (2 * V), 2 * V)
        pltpu.make_async_copy(acc.at[rows], out.at[rows], local_sem.at[m]).wait()
    for copy in leaving:
        copy.wait()


ALL = [(row, j) for j in (0, 1, 3, 2) for row in range(2)]


def left_over():
    by_class = []
    for at in range(len(CLASSES)):
        done = [names[at] for stage, names in zip(SEQUENCE, UNITS) if stage == 1]
        by_class.append([name for name in ALL if name not in done])
    return tuple(zip(*by_class))


REST = left_over()


def rest_kernel(dims, own_hbm, par_hbm, amps, raw, out, own, par, rc, half, acc, sems):
    sym, tile = lax.axis_index("sym"), lax.axis_index("tile")
    n = len(REST)
    get_own = pltpu.make_async_copy(own_hbm, own, sems.at[0])
    get_par = pltpu.make_async_copy(par_hbm, par, sems.at[1])

    def get_amps(i):
        return pltpu.make_async_copy(amps.at[i], rc.at[i], sems.at[2 + i])

    def get_raw(m):
        rows = pl.ds(m * 2 * V, 2 * V)
        return pltpu.make_async_copy(raw.at[rows], acc.at[rows], sems.at[2 + NI + m])

    def put(m):
        rows = pl.ds(m * 2 * V, 2 * V)
        return pltpu.make_async_copy(acc.at[rows], out.at[rows], sems.at[6 + NI + m])

    get_own.start()
    get_amps(0).start()
    get_amps(1).start()
    get_par.start()
    get_raw(0).start()
    for i in range(2, NI):
        get_amps(i).start()
    for m in range(1, 4):
        get_raw(m).start()
    n_row, n_col = dims[tile], dims[jnp.bitwise_xor(tile, sym)]
    live = (lax.broadcasted_iota(jnp.int32, (V, V), 0) < n_row) & (lax.broadcasted_iota(jnp.int32, (V, V), 1) < n_col)
    live_f = jnp.where(live, 1.0, 0.0)
    live_b = live_f.astype(jnp.bfloat16)
    get_own.wait()

    @pl.loop(0, 4)
    def _(m):
        for i in range(2):
            get_amps(2 * m + i).wait()
        both = jnp.concatenate([rc[2 * m] * live_b, rc[2 * m + 1] * live_b], axis=1)
        for t in range(3):
            left = own[...].reshape(n * 2 * V, V)
            r = jnp.dot(left, both[:, t * 256:(t + 1) * 256], preferred_element_type=jnp.float32).astype(jnp.bfloat16)
            for lo_col, hi_col, pair, at in columns(t):
                for p in range(2 * n):
                    lanes = pl.ds(p * V + at, hi_col - lo_col)
                    half[pair * V:(pair + 1) * V, lanes] = r[p * V:(p + 1) * V, lo_col:hi_col]
        pl.when(m == 0)(get_par.wait)
        get_raw(m).wait()
        for b0, b1 in ((0, 256), (256, 384)):
            right = [par[r, pl.ds(2 * p, 2)].reshape(V, V)[b0:b1] for r in range(n) for p in range(2)]
            r = lax.dot_general(
                half[...], jnp.concatenate(right, axis=1), (((1,), (1,)), ((), ())), preferred_element_type=jnp.float32
            )
            for i in range(2):
                at = pl.ds(pl.multiple_of((2 * m + i) * V, V), V)
                acc[at, b0:b1] = jnp.where(live[:, b0:b1], acc[at, b0:b1] + r[i * V:(i + 1) * V], 0.0)
        put(m).start()

    for m in range(4):
        put(m).wait()


def shards(irrep_dims, chol_vectors, amplitudes):
    bf, sem = jnp.bfloat16, pltpu.SemaphoreType.DMA
    n = len(REST)
    own, chol, amps = (n, 4, PV, V), chol_vectors.reshape(V, V), amplitudes.reshape(NI, V, V)
    anywhere = pl.BlockSpec(memory_space=pl.ANY)
    raw, rest_own, rest_par = pl.pallas_call(
        kernel,
        out_shape=[
            jax.ShapeDtypeStruct((NI * V, V), jnp.float32),
            jax.ShapeDtypeStruct(own, bf),
            jax.ShapeDtypeStruct(own, bf),
        ],
        in_specs=[pl.BlockSpec(memory_space=pltpu.SMEM), anywhere, anywhere],
        out_specs=[anywhere] * 3,
        scratch_shapes=[
            pltpu.VMEM((SLOTS, PV, V), bf),
            pltpu.VMEM((V, NI * V), bf),
            pltpu.VMEM((8, NI * V, 2 * V), bf),
            pltpu.VMEM((NI * V, V), jnp.float32),
            pltpu.SMEM((MOST_OPS,), jnp.int32),
            pltpu.SMEM((POINTS + 1,), jnp.int32),
            pltpu.SMEM((len(WAYS),), jnp.int32),
            sem((MOST_SENDS,)), sem((FIRST_SENDS,)), sem((SLOTS,)), sem((18 + 2 * n,)),
        ],
        compiler_params=pltpu.CompilerParams(
            collective_id=0, has_side_effects=True, vmem_limit_bytes=63 * 1024 * 1024
        ),
        cost_estimate=pl.CostEstimate(flops=(8 - n) * 3_600_000_000, bytes_accessed=12_000_000, transcendentals=0),
        name="ladder",
    )(irrep_dims, chol, amps)
    total = pl.pallas_call(
        rest_kernel,
        out_shape=jax.ShapeDtypeStruct((NI * V, V), jnp.float32),
        in_specs=[pl.BlockSpec(memory_space=pltpu.SMEM)] + [anywhere] * 4,
        out_specs=anywhere,
        scratch_shapes=[
            pltpu.VMEM(own, bf),
            pltpu.VMEM(own, bf),
            pltpu.VMEM((NI, V, V), bf),
            pltpu.VMEM((2 * V, n * 2 * V), bf),
            pltpu.VMEM((NI * V, V), jnp.float32),
            sem((10 + NI,)),
        ],
        compiler_params=pltpu.CompilerParams(vmem_limit_bytes=60 * 1024 * 1024),
        cost_estimate=pl.CostEstimate(flops=n * 3_600_000_000, bytes_accessed=16_000_000, transcendentals=0),
        name="rest",
    )(irrep_dims, rest_own, rest_par, amps, raw)
    return total.reshape(1, NI, V, V)


def solution(mesh):
    return jax.shard_map(
        shards,
        mesh=mesh,
        in_specs=(P(), P(("sym", "occ"), "tile", None), P("sym", "occ", "tile", None)),
        out_specs=P("sym", "occ", "tile", None),
        check_vma=False,
    )
```

```python
import jax
import jax.numpy as jnp
from jax import lax
from jax.experimental import pallas as pl
from jax.experimental.pallas import tpu as pltpu
from jax.sharding import PartitionSpec as P

V = 384
NI = 8
PIECES = 2
PV = V // PIECES
HALF = NI * V // 2
CROSSF, OWN, PASS_Z, FWD_Y, PASS_Y, PAR = range(6)
PARTS = 2
SEQUENCE = (1, 1, 1, 1, 1, 1, 2, 2, 2, 2, 2, 2)
UNITS = (
    ((0, 0), (0, 0), (0, 0), (0, 0), (0, 0), (0, 0), (0, 0), (0, 0), (0, 0), (0, 0), (0, 0), (0, 0), (0, 0), (0, 0), (0, 0), (0, 0)),
    ((0, 1), (0, 1), (0, 1), (0, 1), (0, 1), (0, 1), (0, 1), (0, 1), (0, 1), (0, 1), (0, 1), (0, 1), (0, 1), (0, 1), (0, 1), (0, 1)),
    ((0, 3), (0, 3), (0, 3), (0, 3), (0, 3), (0, 3), (0, 3), (0, 3), (0, 3), (0, 3), (0, 3), (0, 3), (0, 3), (0, 3), (0, 3), (0, 3)),
    ((1, 0), (1, 0), (1, 0), (1, 0), (0, 2), (0, 2), (1, 0), (1, 0), (1, 0), (1, 0), (1, 0), (1, 0), (1, 0), (1, 0), (1, 0), (1, 0)),
    ((0, 2), (0, 2), (0, 2), (0, 2), (1, 1), (1, 0), (0, 2), (0, 2), (0, 2), (0, 2), (0, 2), (0, 2), (0, 2), (0, 2), (0, 2), (0, 2)),
    ((1, 1), (1, 1), (1, 1), (1, 1), (1, 3), (1, 1), (1, 1), (1, 1), (1, 3), (1, 3), (1, 1), (1, 1), (1, 1), (1, 1), (1, 1), (1, 1)),
    ((0, 0), (0, 0), (0, 0), (0, 0), (0, 0), (0, 0), (0, 0), (0, 0), (0, 0), (0, 0), (0, 0), (0, 0), (0, 0), (0, 0), (0, 0), (0, 0)),
    ((1, 0), (1, 0), (1, 0), (1, 0), (0, 1), (1, 0), (1, 0), (1, 0), (1, 0), (1, 0), (1, 0), (1, 0), (1, 0), (1, 0), (1, 0), (1, 0)),
    ((0, 1), (0, 1), (0, 1), (0, 1), (1, 1), (0, 1), (1, 1), (1, 1), (0, 1), (0, 1), (0, 1), (0, 1), (0, 1), (0, 1), (0, 1), (0, 1)),
    ((1, 1), (1, 1), (0, 3), (0, 3), (0, 3), (1, 1), (0, 1), (0, 1), (0, 3), (0, 3), (1, 1), (1, 1), (1, 1), (1, 1), (1, 1), (1, 1)),
    ((0, 3), (0, 3), (0, 2), (0, 2), (1, 3), (0, 3), (0, 3), (0, 3), (1, 3), (1, 3), (0, 3), (0, 3), (0, 3), (0, 3), (0, 3), (0, 3)),
    ((0, 2), (0, 2), (1, 1), (1, 1), (0, 2), (0, 2), (0, 2), (0, 2), (0, 2), (0, 2), (0, 2), (0, 2), (0, 2), (0, 2), (0, 2), (0, 2)),
)
EVENTS = (
    (
        (2, ((CROSSF, 0), (CROSSF, 1), (OWN, 0, 1, 0), (OWN, 0, 3, 0), (PASS_Z, 0, 0), (PASS_Z, 0, 1), (OWN, 0, 1, 1), (OWN, 0, 3, 1),)),
        (3, ((OWN, 1, 0, 0), (OWN, 1, 0, 1), (PASS_Z, 1, 0), (PASS_Z, 3, 0),)),
        (4, ((OWN, 0, 2, 0), (OWN, 0, 2, 1),)),
        (5, ((FWD_Y, 0, 0), (FWD_Y, 0, 1),)),
        (6, ((OWN, 1, 1, 0),)),
        (7, ((PASS_Z, 1, 1), (PASS_Z, 3, 1),)),
        (8, ((OWN, 1, 1, 1), (PASS_Y, 0, 1),)),
        (9, ((OWN, 1, 3, 0), (FWD_Y, 1, 0), (FWD_Y, 3, 0),)),
        (11, ((OWN, 1, 2, 0), (OWN, 1, 2, 1), (PASS_Z, 2, 0), (PASS_Z, 2, 1),)),
        (12, ((PASS_Y, 1, 0),)),
        (13, ((FWD_Y, 1, 1), (FWD_Y, 3, 1),)),
        (15, ((FWD_Y, 2, 0), (FWD_Y, 2, 1),)),
        (16, ((PASS_Y, 3, 1),)),
        (18, ((OWN, 1, 3, 1),)),
        (19, ((PASS_Y, 2, 0),)),
    ),
    (
        (2, ((CROSSF, 0), (CROSSF, 1), (OWN, 0, 1, 0), (OWN, 0, 3, 0), (PASS_Z, 0, 0), (PASS_Z, 0, 1), (OWN, 0, 1, 1), (OWN, 0, 3, 1),)),
        (3, ((OWN, 1, 0, 0), (OWN, 1, 0, 1), (PASS_Z, 1, 0), (PASS_Z, 3, 0),)),
        (4, ((OWN, 0, 2, 0), (OWN, 0, 2, 1),)),
        (5, ((FWD_Y, 0, 0), (FWD_Y, 0, 1),)),
        (6, ((OWN, 1, 1, 0),)),
        (7, ((PASS_Z, 1, 1), (PASS_Z, 3, 1),)),
        (8, ((OWN, 1, 1, 1), (PASS_Y, 0, 0),)),
        (9, ((OWN, 1, 3, 0), (FWD_Y, 1, 0), (FWD_Y, 3, 0),)),
        (11, ((OWN, 1, 3, 1), (OWN, 1, 2, 1), (PASS_Z, 2, 0), (PASS_Z, 2, 1),)),
        (12, ((PASS_Y, 3, 0),)),
        (13, ((OWN, 1, 2, 0), (FWD_Y, 1, 1), (FWD_Y, 3, 1),)),
        (15, ((FWD_Y, 2, 0), (FWD_Y, 2, 1),)),
        (16, ((PASS_Y, 1, 1),)),
        (18, ((PASS_Y, 2, 1),)),
    ),
    (
        (2, ((CROSSF, 0), (CROSSF, 1), (OWN, 0, 1, 0), (OWN, 0, 3, 0), (PASS_Z, 0, 0), (PASS_Z, 0, 1), (OWN, 0, 1, 1), (OWN, 0, 3, 1),)),
        (3, ((OWN, 1, 0, 0), (OWN, 1, 0, 1), (PASS_Z, 1, 0), (PASS_Z, 3, 0),)),
        (4, ((OWN, 0, 2, 0), (OWN, 0, 2, 1),)),
        (5, ((PAR, 0, 0, 0), (PAR, 0, 0, 1),)),
        (6, ((OWN, 1, 1, 0),)),
        (7, ((OWN, 1, 3, 0), (PASS_Z, 1, 1), (PASS_Z, 3, 1),)),
        (8, ((OWN, 1, 1, 1), (PASS_Y, 0, 0),)),
        (9, ((OWN, 1, 3, 1), (PAR, 0, 1, 0), (PAR, 0, 3, 0),)),
        (11, ((OWN, 1, 2, 0), (OWN, 1, 2, 1), (PASS_Z, 2, 0), (PASS_Z, 2, 1), (PAR, 1, 0, 0), (PAR, 1, 0, 1),)),
        (13, ((PASS_Y, 3, 0), (PAR, 0, 1, 1), (PAR, 0, 3, 1),)),
        (15, ((PAR, 0, 2, 0), (PAR, 0, 2, 1), (PAR, 1, 3, 0),)),
        (16, ((PAR, 1, 1, 0),)),
        (18, ((PASS_Y, 1, 1),)),
        (20, ((PASS_Y, 2, 1),)),
        (21, ((PAR, 1, 3, 1),)),
        (22, ((PAR, 1, 1, 1),)),
        (23, ((PAR, 1, 2, 0), (PAR, 1, 2, 1),)),
    ),
    (
        (2, ((CROSSF, 0), (CROSSF, 1), (OWN, 0, 1, 0), (OWN, 0, 3, 0), (PASS_Z, 0, 0), (PASS_Z, 0, 1), (OWN, 0, 1, 1), (OWN, 0, 3, 1),)),
        (3, ((OWN, 1, 0, 0), (OWN, 1, 0, 1), (PASS_Z, 1, 0), (PASS_Z, 3, 0),)),
        (4, ((OWN, 0, 2, 0), (OWN, 0, 2, 1),)),
        (5, ((PAR, 0, 0, 0), (PAR, 0, 0, 1),)),
        (6, ((OWN, 1, 1, 0),)),
        (7, ((OWN, 1, 3, 0), (PASS_Z, 1, 1), (PASS_Z, 3, 1),)),
        (8, ((OWN, 1, 1, 1), (PASS_Y, 0, 1),)),
        (9, ((OWN, 1, 3, 1), (PAR, 0, 1, 0), (PAR, 0, 3, 0),)),
        (11, ((OWN, 1, 2, 0), (OWN, 1, 2, 1), (PASS_Z, 2, 0), (PASS_Z, 2, 1), (PAR, 1, 0, 0), (PAR, 1, 0, 1),)),
        (13, ((PASS_Y, 1, 0), (PAR, 0, 1, 1), (PAR, 0, 3, 1),)),
        (15, ((PAR, 0, 2, 0), (PAR, 0, 2, 1), (PAR, 1, 1, 0),)),
        (16, ((PAR, 1, 3, 0),)),
        (18, ((PASS_Y, 3, 1),)),
        (20, ((PASS_Y, 2, 0),)),
        (21, ((PAR, 1, 1, 1),)),
        (22, ((PAR, 1, 3, 1),)),
        (23, ((PAR, 1, 2, 1),)),
        (24, ((PAR, 1, 2, 0),)),
    ),
    (
        (2, ((CROSSF, 0), (OWN, 0, 1, 0), (OWN, 0, 3, 0), (PASS_Z, 0, 0), (PASS_Z, 0, 1), (PAR, 0, 0, 0), (OWN, 0, 1, 1), (PAR, 1, 0, 0), (OWN, 0, 3, 1), (CROSSF, 1),)),
        (3, ((PASS_Z, 1, 0), (PASS_Z, 3, 0),)),
        (4, ((OWN, 0, 2, 0), (PAR, 0, 0, 1), (PAR, 1, 0, 1),)),
        (5, ((OWN, 0, 2, 1), (FWD_Y, 0, 0), (FWD_Y, 0, 1),)),
        (6, ((OWN, 1, 0, 0), (OWN, 1, 1, 0), (PAR, 0, 1, 0),)),
        (7, ((OWN, 1, 3, 0), (PASS_Z, 1, 1), (PASS_Z, 3, 1),)),
        (8, ((OWN, 1, 1, 1), (PAR, 0, 3, 0), (PAR, 1, 1, 0), (OWN, 1, 3, 1), (FWD_Y, 1, 0), (FWD_Y, 3, 0),)),
        (9, ((PAR, 0, 1, 1), (PAR, 1, 3, 0),)),
        (10, ((OWN, 1, 2, 0), (OWN, 1, 2, 1), (PASS_Z, 2, 0), (PASS_Z, 2, 1),)),
        (11, ((PAR, 1, 1, 1),)),
        (12, ((FWD_Y, 1, 1), (FWD_Y, 3, 1), (PAR, 0, 3, 1),)),
        (14, ((OWN, 1, 0, 1), (FWD_Y, 2, 0), (PAR, 1, 3, 1),)),
        (15, ((FWD_Y, 2, 1),)),
        (16, ((PAR, 0, 2, 0), (PAR, 1, 2, 0),)),
        (18, ((PAR, 0, 2, 1), (PAR, 1, 2, 1),)),
    ),
    (
        (2, ((CROSSF, 0), (OWN, 0, 1, 0), (OWN, 0, 3, 0), (PASS_Z, 0, 0), (PASS_Z, 0, 1), (PAR, 1, 0, 0), (OWN, 0, 1, 1), (PAR, 0, 0, 0), (OWN, 0, 3, 1), (CROSSF, 1),)),
        (3, ((PASS_Z, 1, 0), (PASS_Z, 3, 0),)),
        (4, ((OWN, 0, 2, 0), (PAR, 0, 0, 1), (PAR, 1, 0, 1),)),
        (5, ((OWN, 0, 2, 1), (FWD_Y, 0, 0), (FWD_Y, 0, 1),)),
        (6, ((OWN, 1, 0, 0), (OWN, 1, 0, 1), (OWN, 1, 1, 0),)),
        (7, ((OWN, 1, 3, 0), (PASS_Z, 1, 1), (PASS_Z, 3, 1),)),
        (8, ((OWN, 1, 1, 1), (PAR, 0, 1, 0), (PAR, 1, 1, 0),)),
        (9, ((OWN, 1, 3, 1), (FWD_Y, 1, 0), (FWD_Y, 3, 0),)),
        (10, ((PAR, 0, 3, 0), (PAR, 1, 3, 0),)),
        (11, ((OWN, 1, 2, 0), (OWN, 1, 2, 1), (PASS_Z, 2, 0), (PASS_Z, 2, 1),)),
        (12, ((PAR, 0, 1, 1), (PAR, 1, 1, 1),)),
        (13, ((FWD_Y, 1, 1), (FWD_Y, 3, 1),)),
        (14, ((PAR, 0, 3, 1), (PAR, 1, 3, 1),)),
        (15, ((FWD_Y, 2, 0), (FWD_Y, 2, 1),)),
        (16, ((PAR, 0, 2, 0), (PAR, 1, 2, 0),)),
        (19, ((PAR, 0, 2, 1), (PAR, 1, 2, 1),)),
    ),
    (
        (2, ((CROSSF, 0), (CROSSF, 1), (OWN, 0, 1, 0), (OWN, 0, 3, 0), (PASS_Z, 0, 0), (PASS_Z, 0, 1), (OWN, 0, 1, 1), (OWN, 0, 3, 1),)),
        (3, ((OWN, 1, 0, 0), (OWN, 1, 0, 1), (PASS_Z, 1, 0), (PASS_Z, 3, 0),)),
        (4, ((OWN, 0, 2, 0), (OWN, 0, 2, 1),)),
        (5, ((FWD_Y, 0, 0), (FWD_Y, 0, 1),)),
        (6, ((OWN, 1, 1, 0), (OWN, 1, 3, 0),)),
        (7, ((PASS_Z, 1, 1), (PASS_Z, 3, 1),)),
        (8, ((OWN, 1, 1, 1), (PAR, 0, 0, 0), (PAR, 1, 0, 0),)),
        (9, ((OWN, 1, 3, 1), (FWD_Y, 1, 0), (FWD_Y, 3, 0),)),
        (10, ((PAR, 0, 0, 1), (PAR, 1, 0, 1),)),
        (11, ((OWN, 1, 2, 0), (OWN, 1, 2, 1), (PASS_Z, 2, 0), (PASS_Z, 2, 1),)),
        (12, ((PAR, 0, 1, 0), (PAR, 1, 1, 0),)),
        (13, ((FWD_Y, 1, 1), (FWD_Y, 3, 1),)),
        (14, ((PAR, 1, 3, 0),)),
        (15, ((FWD_Y, 2, 0), (FWD_Y, 2, 1), (PAR, 0, 3, 0),)),
        (16, ((PAR, 1, 1, 1), (PAR, 0, 1, 1),)),
        (18, ((PAR, 0, 3, 1), (PAR, 1, 3, 1),)),
        (20, ((PAR, 0, 2, 0), (PAR, 1, 2, 0),)),
        (22, ((PAR, 0, 2, 1), (PAR, 1, 2, 1),)),
    ),
    (
        (2, ((CROSSF, 0), (CROSSF, 1), (OWN, 0, 1, 0), (OWN, 0, 3, 0), (PASS_Z, 0, 0), (PASS_Z, 0, 1), (OWN, 0, 1, 1), (OWN, 0, 3, 1),)),
        (3, ((OWN, 1, 0, 0), (PASS_Z, 1, 0), (PASS_Z, 3, 0),)),
        (4, ((OWN, 0, 2, 0), (OWN, 0, 2, 1),)),
        (5, ((OWN, 1, 0, 1), (FWD_Y, 0, 0), (FWD_Y, 0, 1),)),
        (6, ((OWN, 1, 1, 0), (OWN, 1, 3, 0),)),
        (7, ((PASS_Z, 1, 1), (PASS_Z, 3, 1),)),
        (8, ((OWN, 1, 1, 1), (PAR, 0, 0, 0), (PAR, 1, 0, 0),)),
        (9, ((OWN, 1, 3, 1), (FWD_Y, 1, 0), (FWD_Y, 3, 0),)),
        (10, ((PAR, 0, 0, 1), (PAR, 1, 0, 1),)),
        (11, ((OWN, 1, 2, 0), (OWN, 1, 2, 1), (PASS_Z, 2, 0), (PASS_Z, 2, 1),)),
        (12, ((PAR, 0, 1, 0), (PAR, 1, 1, 0),)),
        (13, ((FWD_Y, 1, 1), (FWD_Y, 3, 1),)),
        (14, ((PAR, 1, 3, 0),)),
        (15, ((FWD_Y, 2, 0), (FWD_Y, 2, 1), (PAR, 0, 3, 0),)),
        (16, ((PAR, 1, 1, 1), (PAR, 0, 1, 1),)),
        (18, ((PAR, 0, 3, 1), (PAR, 1, 3, 1),)),
        (20, ((PAR, 0, 2, 0), (PAR, 1, 2, 0),)),
        (22, ((PAR, 0, 2, 1), (PAR, 1, 2, 1),)),
    ),
    (
        (2, ((CROSSF, 0), (CROSSF, 1), (OWN, 0, 1, 0), (OWN, 0, 3, 0), (FWD_Y, 0, 0), (PAR, 0, 0, 0), (OWN, 0, 1, 1), (PAR, 0, 0, 1), (OWN, 0, 3, 1), (FWD_Y, 0, 1),)),
        (3, ((OWN, 1, 0, 0), (OWN, 1, 0, 1),)),
        (4, ((OWN, 0, 2, 0), (OWN, 0, 2, 1), (FWD_Y, 1, 0), (PAR, 0, 1, 0),)),
        (5, ((PASS_Y, 0, 0), (PASS_Y, 0, 1),)),
        (6, ((OWN, 1, 3, 0), (FWD_Y, 3, 0), (PAR, 0, 3, 0),)),
        (7, ((PASS_Y, 1, 0),)),
        (8, ((FWD_Y, 1, 1), (PAR, 0, 1, 1), (PAR, 1, 0, 0),)),
        (9, ((OWN, 1, 1, 0), (OWN, 1, 3, 1), (PAR, 1, 0, 1),)),
        (10, ((FWD_Y, 3, 1), (PASS_Y, 3, 0), (PAR, 0, 3, 1),)),
        (11, ((OWN, 1, 2, 0), (OWN, 1, 2, 1), (PAR, 1, 1, 0),)),
        (12, ((FWD_Y, 2, 0), (PASS_Y, 1, 1), (PAR, 0, 2, 0),)),
        (14, ((FWD_Y, 2, 1), (PASS_Y, 3, 1), (PAR, 0, 2, 1),)),
        (15, ((PAR, 1, 3, 0),)),
        (16, ((PASS_Y, 2, 0),)),
        (17, ((PAR, 1, 1, 1),)),
        (18, ((OWN, 1, 1, 1), (PAR, 1, 3, 1),)),
        (19, ((PASS_Y, 2, 1),)),
        (20, ((PAR, 1, 2, 0),)),
        (22, ((PAR, 1, 2, 1),)),
    ),
    (
        (2, ((CROSSF, 0), (CROSSF, 1), (OWN, 0, 1, 0), (OWN, 0, 3, 0), (FWD_Y, 0, 0), (PAR, 0, 0, 0), (OWN, 0, 1, 1), (PAR, 0, 0, 1), (OWN, 0, 3, 1), (FWD_Y, 0, 1),)),
        (3, ((OWN, 1, 0, 0), (OWN, 1, 0, 1),)),
        (4, ((OWN, 0, 2, 0), (OWN, 0, 2, 1), (FWD_Y, 1, 0), (PAR, 0, 1, 0),)),
        (5, ((PASS_Y, 0, 0), (PASS_Y, 0, 1),)),
        (6, ((OWN, 1, 3, 0), (FWD_Y, 3, 0), (PAR, 0, 3, 0),)),
        (7, ((PASS_Y, 1, 0),)),
        (8, ((FWD_Y, 1, 1), (PAR, 0, 1, 1), (PAR, 1, 0, 0),)),
        (9, ((OWN, 1, 1, 0), (OWN, 1, 3, 1), (PAR, 1, 0, 1),)),
        (10, ((FWD_Y, 3, 1), (PASS_Y, 3, 0), (PAR, 0, 3, 1),)),
        (11, ((OWN, 1, 1, 1), (OWN, 1, 2, 0), (PAR, 1, 1, 0),)),
        (12, ((FWD_Y, 2, 0), (PASS_Y, 1, 1), (PAR, 0, 2, 0),)),
        (13, ((OWN, 1, 2, 1),)),
        (14, ((FWD_Y, 2, 1), (PASS_Y, 3, 1), (PAR, 0, 2, 1),)),
        (15, ((PAR, 1, 3, 0),)),
        (16, ((PASS_Y, 2, 0),)),
        (17, ((PAR, 1, 1, 1),)),
        (18, ((PAR, 1, 3, 1),)),
        (19, ((PASS_Y, 2, 1),)),
        (20, ((PAR, 1, 2, 0),)),
        (22, ((PAR, 1, 2, 1),)),
    ),
    (
        (2, ((CROSSF, 0), (CROSSF, 1), (OWN, 0, 1, 0), (OWN, 0, 3, 0), (FWD_Y, 0, 0), (PAR, 0, 0, 0), (OWN, 0, 1, 1), (FWD_Y, 0, 1), (OWN, 0, 3, 1), (PAR, 0, 0, 1),)),
        (3, ((OWN, 1, 0, 0), (OWN, 1, 0, 1),)),
        (4, ((OWN, 0, 2, 0), (OWN, 0, 2, 1), (FWD_Y, 1, 0), (PAR, 0, 1, 0),)),
        (5, ((PASS_Y, 0, 0), (PASS_Y, 0, 1),)),
        (6, ((OWN, 1, 1, 0), (OWN, 1, 3, 0), (FWD_Y, 3, 0), (PAR, 0, 3, 0),)),
        (7, ((PASS_Y, 1, 0),)),
        (8, ((OWN, 1, 1, 1), (FWD_Y, 1, 1), (PAR, 0, 1, 1), (PAR, 1, 0, 0),)),
        (9, ((OWN, 1, 3, 1), (PAR, 1, 0, 1),)),
        (10, ((FWD_Y, 3, 1), (PASS_Y, 3, 0), (PAR, 0, 3, 1),)),
        (11, ((OWN, 1, 2, 0), (OWN, 1, 2, 1), (PAR, 1, 1, 0),)),
        (12, ((FWD_Y, 2, 0), (PASS_Y, 1, 1), (PAR, 0, 2, 0),)),
        (13, ((PASS_Y, 3, 1),)),
        (14, ((FWD_Y, 2, 1), (PAR, 0, 2, 1),)),
        (15, ((PAR, 1, 3, 0),)),
        (16, ((PASS_Y, 2, 0),)),
        (17, ((PAR, 1, 1, 1),)),
        (18, ((PAR, 1, 3, 1),)),
        (19, ((PASS_Y, 2, 1),)),
        (20, ((PAR, 1, 2, 0),)),
        (22, ((PAR, 1, 2, 1),)),
    ),
    (
        (2, ((CROSSF, 0), (CROSSF, 1), (OWN, 0, 1, 0), (OWN, 0, 3, 0), (FWD_Y, 0, 0), (PAR, 0, 0, 0), (OWN, 0, 1, 1), (FWD_Y, 0, 1), (OWN, 0, 3, 1), (PAR, 0, 0, 1),)),
        (3, ((OWN, 1, 0, 0), (OWN, 1, 0, 1),)),
        (4, ((OWN, 0, 2, 0), (OWN, 0, 2, 1), (FWD_Y, 1, 0), (PAR, 0, 1, 0),)),
        (5, ((PASS_Y, 0, 0), (PASS_Y, 0, 1),)),
        (6, ((OWN, 1, 1, 0), (OWN, 1, 3, 0), (FWD_Y, 3, 0), (PAR, 0, 3, 0),)),
        (7, ((PASS_Y, 1, 0),)),
        (8, ((OWN, 1, 1, 1), (FWD_Y, 1, 1), (PAR, 0, 1, 1), (PAR, 1, 0, 0),)),
        (9, ((OWN, 1, 3, 1), (PAR, 1, 0, 1),)),
        (10, ((FWD_Y, 3, 1), (PASS_Y, 3, 0), (PAR, 0, 3, 1),)),
        (11, ((OWN, 1, 2, 0), (OWN, 1, 2, 1), (PAR, 1, 1, 0),)),
        (12, ((FWD_Y, 2, 0), (PASS_Y, 1, 1), (PAR, 0, 2, 0),)),
        (13, ((PASS_Y, 3, 1),)),
        (14, ((FWD_Y, 2, 1), (PAR, 0, 2, 1),)),
        (15, ((PAR, 1, 3, 0),)),
        (16, ((PASS_Y, 2, 0),)),
        (17, ((PAR, 1, 1, 1),)),
        (18, ((PAR, 1, 3, 1),)),
        (19, ((PASS_Y, 2, 1),)),
        (20, ((PAR, 1, 2, 0),)),
        (22, ((PAR, 1, 2, 1),)),
    ),
    (
        (2, ((CROSSF, 0), (CROSSF, 1), (OWN, 0, 1, 0), (OWN, 0, 3, 0), (FWD_Y, 0, 0), (OWN, 0, 1, 1), (OWN, 0, 3, 1), (FWD_Y, 0, 1),)),
        (3, ((OWN, 1, 0, 0), (OWN, 1, 0, 1),)),
        (4, ((OWN, 0, 2, 0), (OWN, 0, 2, 1), (FWD_Y, 1, 0),)),
        (5, ((PAR, 0, 0, 0), (PAR, 1, 0, 0),)),
        (6, ((OWN, 1, 1, 0), (OWN, 1, 3, 0), (FWD_Y, 3, 0),)),
        (7, ((PAR, 0, 0, 1), (PAR, 1, 0, 1),)),
        (8, ((OWN, 1, 1, 1), (FWD_Y, 1, 1),)),
        (9, ((OWN, 1, 3, 1), (PAR, 0, 1, 0), (PAR, 1, 1, 0),)),
        (10, ((FWD_Y, 3, 1),)),
        (11, ((PAR, 0, 3, 0), (PAR, 1, 3, 0),)),
        (12, ((OWN, 1, 2, 0), (FWD_Y, 2, 0),)),
        (13, ((PAR, 0, 1, 1), (PAR, 1, 1, 1),)),
        (14, ((FWD_Y, 2, 1),)),
        (15, ((PAR, 0, 3, 1), (PAR, 1, 3, 1),)),
        (17, ((PAR, 0, 2, 0), (PAR, 1, 2, 0),)),
        (19, ((PAR, 0, 2, 1), (PAR, 1, 2, 1),)),
        (21, ((OWN, 1, 2, 1),)),
    ),
    (
        (2, ((CROSSF, 0), (CROSSF, 1), (OWN, 0, 1, 0), (OWN, 0, 3, 0), (FWD_Y, 0, 0), (OWN, 0, 1, 1), (OWN, 0, 3, 1), (FWD_Y, 0, 1),)),
        (3, ((OWN, 1, 0, 0), (OWN, 1, 0, 1),)),
        (4, ((OWN, 0, 2, 0), (OWN, 0, 2, 1), (FWD_Y, 1, 0),)),
        (5, ((PAR, 0, 0, 0), (PAR, 1, 0, 0),)),
        (6, ((OWN, 1, 1, 0), (OWN, 1, 3, 0), (FWD_Y, 3, 0),)),
        (7, ((PAR, 0, 0, 1), (PAR, 1, 0, 1),)),
        (8, ((OWN, 1, 1, 1), (FWD_Y, 1, 1),)),
        (9, ((OWN, 1, 3, 1), (PAR, 0, 1, 0), (PAR, 1, 1, 0),)),
        (10, ((FWD_Y, 3, 1),)),
        (11, ((PAR, 0, 3, 0), (PAR, 1, 3, 0),)),
        (12, ((OWN, 1, 2, 0), (FWD_Y, 2, 0),)),
        (13, ((PAR, 0, 1, 1), (PAR, 1, 1, 1),)),
        (14, ((OWN, 1, 2, 1), (FWD_Y, 2, 1),)),
        (15, ((PAR, 0, 3, 1), (PAR, 1, 3, 1),)),
        (17, ((PAR, 0, 2, 0), (PAR, 1, 2, 0),)),
        (19, ((PAR, 0, 2, 1), (PAR, 1, 2, 1),)),
    ),
    (
        (2, ((CROSSF, 0), (CROSSF, 1), (OWN, 0, 1, 0), (OWN, 0, 3, 0), (FWD_Y, 0, 0), (OWN, 0, 1, 1), (OWN, 0, 3, 1), (FWD_Y, 0, 1),)),
        (3, ((OWN, 1, 0, 0), (OWN, 1, 0, 1),)),
        (4, ((OWN, 0, 2, 0), (OWN, 0, 2, 1), (FWD_Y, 1, 0),)),
        (5, ((PAR, 0, 0, 0), (PAR, 1, 0, 0),)),
        (6, ((OWN, 1, 1, 0), (OWN, 1, 3, 0), (FWD_Y, 3, 0),)),
        (7, ((PAR, 0, 0, 1), (PAR, 1, 0, 1),)),
        (8, ((OWN, 1, 1, 1), (FWD_Y, 1, 1),)),
        (9, ((OWN, 1, 3, 1), (PAR, 0, 1, 0), (PAR, 1, 1, 0),)),
        (10, ((FWD_Y, 3, 1),)),
        (11, ((OWN, 1, 2, 0), (OWN, 1, 2, 1), (PAR, 0, 3, 0), (PAR, 1, 3, 0),)),
        (12, ((FWD_Y, 2, 0),)),
        (13, ((PAR, 0, 1, 1), (PAR, 1, 1, 1),)),
        (14, ((FWD_Y, 2, 1),)),
        (15, ((PAR, 0, 3, 1), (PAR, 1, 3, 1),)),
        (17, ((PAR, 0, 2, 0), (PAR, 1, 2, 0),)),
        (19, ((PAR, 0, 2, 1), (PAR, 1, 2, 1),)),
    ),
    (
        (2, ((CROSSF, 0), (CROSSF, 1), (OWN, 0, 1, 0), (OWN, 0, 3, 0), (FWD_Y, 0, 0), (OWN, 0, 1, 1), (OWN, 0, 3, 1), (FWD_Y, 0, 1),)),
        (3, ((OWN, 1, 0, 0), (OWN, 1, 0, 1),)),
        (4, ((OWN, 0, 2, 0), (OWN, 0, 2, 1), (FWD_Y, 1, 0),)),
        (5, ((PAR, 0, 0, 0), (PAR, 1, 0, 0),)),
        (6, ((OWN, 1, 1, 0), (OWN, 1, 3, 0), (FWD_Y, 3, 0),)),
        (7, ((PAR, 0, 0, 1), (PAR, 1, 0, 1),)),
        (8, ((OWN, 1, 1, 1), (FWD_Y, 1, 1),)),
        (9, ((OWN, 1, 3, 1), (PAR, 0, 1, 0), (PAR, 1, 1, 0),)),
        (10, ((FWD_Y, 3, 1),)),
        (11, ((OWN, 1, 2, 0), (OWN, 1, 2, 1), (PAR, 0, 3, 0), (PAR, 1, 3, 0),)),
        (12, ((FWD_Y, 2, 0),)),
        (13, ((PAR, 0, 1, 1), (PAR, 1, 1, 1),)),
        (14, ((FWD_Y, 2, 1),)),
        (15, ((PAR, 0, 3, 1), (PAR, 1, 3, 1),)),
        (17, ((PAR, 0, 2, 0), (PAR, 1, 2, 0),)),
        (19, ((PAR, 0, 2, 1), (PAR, 1, 2, 1),)),
    ),
)

STAGES = len(SEQUENCE)
POINTS = PARTS * STAGES + 1
PAR_AT, T1_AT, T2_AT, T3_AT, TC_AT, SLOTS = 32, 64, 72, 80, 88, 90
WAYS = ("x+", "x-", "y+", "y-", "z+", "z-", "core", "ya", "yb", "za", "zb")
WAIT = 15
CLASSES = [(x, y) for x in range(4) for y in range(4)]


def sign_of(j, k):
    return "+" if (k + (0, 1, 1, 0)[j]) % 2 == 0 else "-"


def name_of(x, y, row, j):
    return (y // 2 + row) % 2 * 4 + (x + 4 - j) % 4


def row_behind(y, sign):
    return (y + 3) % 4 // 2 if sign == "+" else (y + 1) % 4 // 2


def feed(x, y, j, k, src):
    up = y // 2 == 1
    final, via1, via2 = ("par", name_of(x, y, 0, j), k), ("t1", j, k), ("t2", j, k)
    sends = []
    if x in (0, 1):
        sends.append((src, via1, "z" + sign_of(j, k)))
    if x == 1:
        sends.append((src, final, "ya"))
    if x in (2, 3):
        sends.append((src, final if x == 2 and not up else via1, "za"))
        sends.append((src, final if x == 2 and up else via2, "zb"))
    return sends


def expand(x, y, event):
    kind, args = event[0], event[1:]
    up = y // 2 == 1
    ops = []
    if kind == CROSSF:
        (k,) = args
        sign = "+-"[k]
        ops = [("tc", k), (("tc", k), ("own", row_behind(y, sign) * 4 + x, k), "y" + sign)]
    if kind == OWN:
        row, j, k = args
        here = ("own", name_of(x, y, row, j), k)
        ops = [here]
        if (row, j) == (1, 0) or (j == 1 and (k + row) % 2 == 0):
            ops.append((here, here, "x+"))
        if (row, j) == (1, 0) or (j == 3 and (k + row) % 2 == 1):
            ops.append((here, here, "x-"))
        if row == 0:
            ops += feed(x, y, j, k, here)
        ops.append((here, here, "core"))
    if kind == PASS_Z:
        j, k = args
        here = ("t1", j, k)
        there = ("par", name_of(x, y, 0, j), k) if x == 0 and up else ("t2", j, k)
        ops = [here, (here, there, "z" + sign_of(j, k))]
    if kind == FWD_Y:
        j, k = args
        final, there, way = ("par", name_of(x, y, 0, j), k), ("t3", j, k), "y" + sign_of(j, k)
        if x == 3 or (x == 2 and up):
            ops += [("t1", j, k), (("t1", j, k), final, "ya") if x == 3 else (("t1", j, k), there, way)]
        if x in (1, 3) or not up:
            ops += [("t2", j, k), (("t2", j, k), final, "yb") if x in (1, 3) else (("t2", j, k), there, way)]
    if kind == PASS_Y:
        j, k = args
        sign = sign_of(j, k)
        row = row_behind(y, sign)
        if x == 2 or row == 0:
            ops = [("t3", j, k), (("t3", j, k), ("par", row * 4 + (x + 4 - j) % 4, k), "y" + sign)]
    if kind == PAR:
        row, j, k = args
        here = ("par", name_of(x, y, row, j), k)
        ops = [here, (here, here, "core")]
    return ops


def slot(place, c):
    kind, rest = place[0], place[1:]
    if kind in ("own", "par"):
        q, k = rest
        return (PAR_AT if kind == "par" else 0) + q * 4 + c * 2 + k
    if kind == "tc":
        return TC_AT + rest[0]
    return {"t1": T1_AT, "t2": T2_AT, "t3": T3_AT}[kind] + rest[0] * 2 + rest[1]


def tables(x, y):
    per_core = []
    for c in range(2):
        ops, begins, sends, at = [], [], 0, dict(EVENTS[CLASSES.index((x, y))])
        for point in range(POINTS):
            begins.append(len(ops))
            for event in at.get(point, ()):
                for op in expand(x, y, event):
                    if isinstance(op[0], str):
                        ops.append(slot(op, c) + 2097152 * WAIT)
                    else:
                        src, dst, way = op
                        ops.append(slot(src, c) + 128 * slot(dst, c) + 16384 * sends + 2097152 * WAYS.index(way))
                        sends += 1
        per_core.append((ops, begins + [len(ops)], sends))
    return per_core


TABLES = {cls: tables(*cls) for cls in CLASSES}
MOST_OPS = max(len(ops) for cores in TABLES.values() for ops, _, _ in cores)
MOST_SENDS = max(sends for cores in TABLES.values() for _, _, sends in cores)
FIRST_SENDS = 12


def columns(t):
    first, last = t * 256, (t + 1) * 256
    cuts = [first] + [cut for cut in range(0, NI * V, V) if first < cut < last] + [last]
    return [(u - first, w - first, u // V, u % V) for u, w in zip(cuts, cuts[1:])]


def kernel(dims, mine, amps, out, out_own, out_par, buf, rc, half, acc, ops, begins, devs,
           ssem, first_sem, rsem, local_sem):
    sym, tile, c = lax.axis_index("sym"), lax.axis_index("tile"), lax.axis_index("occ")
    x, yhi = sym % 4, sym // 4
    x0, x1 = x % 2, x // 2
    z, ylo = tile // 2, tile % 2
    z0, z1 = z % 2, z // 2
    y = 2 * yhi + ylo
    none = sym == 0

    def dev(dx=0, dy=0, dz=0, dc=0):
        xx, yy, zz = (x + 4 + dx) % 4, (y + 4 + dy) % 4, (z + 4 + dz) % 4
        return ((yy // 2) * 4 + xx) * 16 + (zz * 2 + yy % 2) * 2 + (c + dc) % 2

    step_a = 1 - 2 * (yhi + ylo - 2 * yhi * ylo)
    step_z = 1 - 2 * z0
    to = {
        "x+": dev(dx=1), "x-": dev(dx=-1), "y+": dev(dy=1), "y-": dev(dy=-1), "z+": dev(dz=1), "z-": dev(dz=-1),
        "core": dev(dc=1), "ya": dev(dy=step_a), "yb": dev(dy=-step_a), "za": dev(dz=step_z), "zb": dev(dz=-step_z),
    }
    barrier = pltpu.get_barrier_semaphore()
    for way in WAYS[:7]:
        pl.semaphore_signal(barrier, inc=1, device_id=to[way], device_id_type=pl.DeviceIdType.LOGICAL)

    def own_slot(q, core, k):
        return q * 4 + core * 2 + k

    keep = []
    for k in range(PIECES):
        keep.append(pltpu.make_async_copy(mine.at[pl.ds(k * PV, PV)], buf.at[own_slot(sym, c, k)], local_sem.at[8 + k]))
        keep[-1].start()
    loads = [pltpu.make_async_copy(amps.at[i], rc.at[:, pl.ds(i * V, V)], local_sem.at[i]) for i in range(NI)]
    for load in loads:
        load.start()

    pl.semaphore_wait(barrier, 7)

    def remote(src, dst_slot, sem, where):
        return pltpu.make_async_remote_copy(
            src, buf.at[dst_slot], sem, rsem.at[dst_slot], device_id=where, device_id_type=pl.DeviceIdType.LOGICAL
        )

    def arrived(at):
        remote(buf.at[at], at, first_sem.at[0], to["core"]).wait_recv()

    firsts = []

    def first(src, place, where, cond=None):
        index = len(firsts)
        if cond is None:
            remote(src, place, first_sem.at[index], where).start()
        else:
            pl.when(cond)(lambda: remote(src, place, first_sem.at[index], where).start())
        firsts.append((src, place, cond, index))

    step_2 = {k: {"+": to["z+"], "-": to["z-"]}[sign_of(0, k)] for k in range(PIECES)}
    for k in range(PIECES):
        src = mine.at[pl.ds(k * PV, PV)]
        home = own_slot(sym, c, k)
        final, via1, via2 = PAR_AT + home, T1_AT + k, T2_AT + k
        first(src, home, to["core"])
        first(src, home, to["x+"])
        first(src, home, to["x-"])
        first(src, TC_AT + k, to["y" + "+-"[k]])
        direct_b, direct_a = x0 + 2 * (1 - x1) + (1 - yhi) == 0, x0 + 2 * (1 - x1) + yhi == 0
        where_b = x1 * to["zb"] + (1 - x1) * step_2[k]
        place_b = jnp.where(direct_b, final, x1 * via2 + (1 - x1) * via1)
        first(src, place_b, where_b)
        where_a = x1 * to["za"] + (1 - x1) * to["ya"]
        place_a = jnp.where(direct_a | (x1 == 0), final, via1)
        first(src, place_a, where_a, x > 0)

    for (at_x, at_y), cores in TABLES.items():
        @pl.when((x == at_x) & (y == at_y))
        def _():
            (ops0, begins0, _), (ops1, _, _) = cores
            for n, (op0, op1) in enumerate(zip(ops0, ops1)):
                ops[n] = op0 + (op1 - op0) * c if op0 != op1 else op0
            for n, begin in enumerate(begins0):
                begins[n] = begin
    for n, way in enumerate(WAYS):
        devs[n] = to[way]

    n_row = dims[tile]
    n_col = dims[(z1 + yhi - 2 * z1 * yhi) * 4 + (z0 + x1 - 2 * z0 * x1) * 2 + (ylo + x0 - 2 * ylo * x0)]
    live_r = jnp.where(lax.broadcasted_iota(jnp.int32, (V, V), 0) < n_row, 1.0, 0.0)
    live = jnp.where(lax.broadcasted_iota(jnp.int32, (V, V), 1) < n_col, live_r, 0.0).astype(jnp.bfloat16)
    acc[...] = jnp.zeros_like(acc)
    for load in loads:
        load.wait()
    for i in range(NI):
        rc[:, i * V:(i + 1) * V] = rc[:, i * V:(i + 1) * V] * live
    for copy in keep:
        copy.wait()

    def decoded(n):
        op = ops[n]
        src, rest = lax.rem(op, 128), lax.div(op, 128)
        dst, rest = lax.rem(rest, 128), lax.div(rest, 128)
        return src, dst, lax.rem(rest, 128), lax.div(rest, 128)

    def events(point):
        @pl.loop(begins[point], begins[point + 1])
        def _(n):
            src, dst, index, way = decoded(n)

            @pl.when(way == WAIT)
            def _():
                arrived(src)

            @pl.when(way != WAIT)
            def _():
                remote(buf.at[src], dst, ssem.at[index], devs[way]).start()

    digit = (1 + 7 * x0) * (1 + 63 * x1) * (1 + 4095 * yhi)

    def chosen(groups, n):
        code = 0
        for k, names in enumerate(groups):
            packed = [0, 0]
            for (at_x, at_y), (row, j) in zip(CLASSES, names):
                packed[at_y % 2] += (row * 4 + j) * 8 ** (at_y // 2 * 4 + at_x)
            code = code + (n == k) * 1 * (packed[0] + (packed[1] - packed[0]) * ylo)
        code = lax.rem(lax.div(code, digit), 8)
        return (yhi + code // 4) % 2 * 4 + (x + 4 - code % 4) % 4

    def unit(base, q, core):
        at = base + q * 4 + core * 2
        return buf[pl.ds(at, 2)].reshape(V, V)

    def first_stage(n, q):
        for k in range(PIECES):
            arrived(own_slot(q, 1 - c, k))

        @pl.when(none)
        def _():
            pltpu.make_async_copy(buf.at[pl.ds(q * 4, 4)], buf.at[pl.ds(PAR_AT + q * 4, 4)], local_sem.at[10 + q]).start()

        for h in range(PARTS):
            if h:
                events(PARTS * n + h)
            for t in range(h * 12 // PARTS, (h + 1) * 12 // PARTS):
                left = buf[pl.ds(q * 4, 4)].reshape(2 * V, V)
                r = jnp.dot(left, rc[:, t * 256:(t + 1) * 256], preferred_element_type=jnp.float32).astype(jnp.bfloat16)
                for lo_col, hi_col, pair, at in columns(t):
                    for p in range(2):
                        lanes = pl.ds(p * V + at, hi_col - lo_col)
                        half[q, pair * V:(pair + 1) * V, lanes] = r[p * V:(p + 1) * V, lo_col:hi_col]

    def second_stage(n, q):
        @pl.when(none)
        def _():
            pltpu.make_async_copy(buf.at[pl.ds(q * 4, 4)], buf.at[pl.ds(PAR_AT + q * 4, 4)], local_sem.at[10 + q]).wait()

        @pl.when(jnp.logical_not(none))
        def _():
            for k in range(PIECES):
                arrived(PAR_AT + own_slot(q, 1 - c, k))

        for h in range(2):
            if h and PARTS > 1:
                events(PARTS * n + h)
            rows = pl.ds(h * HALF, HALF)
            for b0, b1 in ((0, 256), (256, 384)):
                right = jnp.concatenate([unit(PAR_AT, q, p)[b0:b1] for p in range(2)], axis=1)
                acc[rows, b0:b1] += lax.dot_general(
                    half[q, rows, :], right, (((1,), (1,)), ((), ())), preferred_element_type=jnp.float32
                )

    @pl.loop(0, STAGES)
    def _(n):
        second = sum((n == k) * 1 for k, stage in enumerate(SEQUENCE) if stage == 2)
        q = chosen(UNITS, n)
        events(PARTS * n)
        pl.when(second == 0)(lambda: first_stage(n, q))
        pl.when(second == 1)(lambda: second_stage(n, q))

    for h in range(2):
        rows = pl.ds(h * HALF, HALF)
        pltpu.make_async_copy(acc.at[rows], out.at[rows], local_sem.at[h]).start()
    events(POINTS - 1)

    leaving = []
    for r in range(len(REST)):
        q = chosen(REST, jnp.int32(r))
        for k in range(PIECES):
            arrived(own_slot(q, 1 - c, k))

        @pl.when(jnp.logical_not(none))
        def _():
            for k in range(PIECES):
                arrived(PAR_AT + own_slot(q, 1 - c, k))

        par_at = jnp.where(none, 0, PAR_AT) + q * 4
        for source, target, sem in ((q * 4, out_own.at[r], 18 + 2 * r), (par_at, out_par.at[r], 19 + 2 * r)):
            leaving.append(pltpu.make_async_copy(buf.at[pl.ds(source, 4)], target, local_sem.at[sem]))
            leaving[-1].start()

    for src, place, cond, index in firsts:
        def sent(src=src, place=place, index=index):
            remote(src, place, first_sem.at[index], to["core"]).wait_send()

        if cond is None:
            sent()
        else:
            pl.when(cond)(sent)

    @pl.loop(0, begins[POINTS])
    def _(n):
        src, dst, index, way = decoded(n)

        @pl.when(way != WAIT)
        def _():
            remote(buf.at[src], dst, ssem.at[index], devs[way]).wait_send()

    for h in range(2):
        rows = pl.ds(h * HALF, HALF)
        pltpu.make_async_copy(acc.at[rows], out.at[rows], local_sem.at[h]).wait()
    for copy in leaving:
        copy.wait()


ALL = [(row, j) for j in (0, 1, 3, 2) for row in range(2)]


def left_over():
    by_class = []
    for at in range(len(CLASSES)):
        done = [names[at] for stage, names in zip(SEQUENCE, UNITS) if stage == 1]
        by_class.append([name for name in ALL if name not in done])
    return tuple(zip(*by_class))


REST = left_over()


def rest_kernel(dims, own_hbm, par_hbm, amps, raw, out, own, par, rc, half, acc, sems):
    sym, tile = lax.axis_index("sym"), lax.axis_index("tile")
    n, hi = len(REST), NI // 2
    get_own = pltpu.make_async_copy(own_hbm, own, sems.at[0])
    get_par = pltpu.make_async_copy(par_hbm, par, sems.at[1])
    get_amps = [pltpu.make_async_copy(amps.at[i], rc.at[:, pl.ds(i * V, V)], sems.at[2 + i]) for i in range(NI)]
    get_raw = [
        pltpu.make_async_copy(raw.at[pl.ds(h * HALF, HALF)], acc.at[pl.ds(h * HALF, HALF)], sems.at[2 + NI + h])
        for h in range(2)
    ]
    for copy in get_amps[:hi] + [get_own, get_par, get_raw[0]] + get_amps[hi:] + [get_raw[1]]:
        copy.start()
    n_row, n_col = dims[tile], dims[jnp.bitwise_xor(tile, sym)]
    live = (lax.broadcasted_iota(jnp.int32, (V, V), 0) < n_row) & (lax.broadcasted_iota(jnp.int32, (V, V), 1) < n_col)
    live_b = jnp.where(live, 1.0, 0.0).astype(jnp.bfloat16)
    puts = []
    for h in range(2):
        for i in range(h * hi, (h + 1) * hi):
            get_amps[i].wait()
            rc[:, i * V:(i + 1) * V] = rc[:, i * V:(i + 1) * V] * live_b
        if h == 0:
            get_own.wait()
        for t in range(6 * h, 6 * (h + 1)):
            left = own[...].reshape(n * 2 * V, V)
            r = jnp.dot(left, rc[:, t * 256:(t + 1) * 256], preferred_element_type=jnp.float32).astype(jnp.bfloat16)
            for lo_col, hi_col, pair, at in columns(t):
                for p in range(2 * n):
                    lanes = pl.ds(p * V + at, hi_col - lo_col)
                    half[(pair - h * hi) * V:(pair - h * hi + 1) * V, lanes] = r[p * V:(p + 1) * V, lo_col:hi_col]
        if h == 0:
            get_par.wait()
        get_raw[h].wait()
        rows = pl.ds(h * HALF, HALF)
        for b0, b1 in ((0, 256), (256, 384)):
            right = [par[r, pl.ds(2 * p, 2)].reshape(V, V)[b0:b1] for r in range(n) for p in range(2)]
            right = jnp.concatenate(right, axis=1)
            r = lax.dot_general(half[...], right, (((1,), (1,)), ((), ())), preferred_element_type=jnp.float32)
            r = r + acc[rows, b0:b1]
            for i in range(hi):
                at = pl.ds((h * hi + i) * V, V)
                acc[at, b0:b1] = jnp.where(live[:, b0:b1], r[i * V:(i + 1) * V], 0.0)
            lanes = pl.ds(b0, b1 - b0)
            puts.append(pltpu.make_async_copy(acc.at[rows, lanes], out.at[rows, lanes], sems.at[4 + NI + len(puts)]))
            puts[-1].start()
    for copy in puts:
        copy.wait()


def shards(irrep_dims, chol_vectors, amplitudes):
    bf, sem = jnp.bfloat16, pltpu.SemaphoreType.DMA
    n = len(REST)
    own, chol, amps = (n, 4, PV, V), chol_vectors.reshape(V, V), amplitudes.reshape(NI, V, V)
    anywhere = pl.BlockSpec(memory_space=pl.ANY)
    raw, rest_own, rest_par = pl.pallas_call(
        kernel,
        out_shape=[
            jax.ShapeDtypeStruct((NI * V, V), jnp.float32),
            jax.ShapeDtypeStruct(own, bf),
            jax.ShapeDtypeStruct(own, bf),
        ],
        in_specs=[pl.BlockSpec(memory_space=pltpu.SMEM), anywhere, anywhere],
        out_specs=[anywhere] * 3,
        scratch_shapes=[
            pltpu.VMEM((SLOTS, PV, V), bf),
            pltpu.VMEM((V, NI * V), bf),
            pltpu.VMEM((8, NI * V, 2 * V), bf),
            pltpu.VMEM((NI * V, V), jnp.float32),
            pltpu.SMEM((MOST_OPS,), jnp.int32),
            pltpu.SMEM((POINTS + 1,), jnp.int32),
            pltpu.SMEM((len(WAYS),), jnp.int32),
            sem((MOST_SENDS,)), sem((FIRST_SENDS,)), sem((SLOTS,)), sem((18 + 2 * n,)),
        ],
        compiler_params=pltpu.CompilerParams(
            collective_id=0, has_side_effects=True, vmem_limit_bytes=63 * 1024 * 1024
        ),
        cost_estimate=pl.CostEstimate(flops=(8 - n) * 3_600_000_000, bytes_accessed=12_000_000, transcendentals=0),
        name="ladder",
    )(irrep_dims, chol, amps)
    total = pl.pallas_call(
        rest_kernel,
        out_shape=jax.ShapeDtypeStruct((NI * V, V), jnp.float32),
        in_specs=[pl.BlockSpec(memory_space=pltpu.SMEM)] + [anywhere] * 4,
        out_specs=anywhere,
        scratch_shapes=[
            pltpu.VMEM(own, bf),
            pltpu.VMEM(own, bf),
            pltpu.VMEM((V, NI * V), bf),
            pltpu.VMEM((HALF, n * 2 * V), bf),
            pltpu.VMEM((NI * V, V), jnp.float32),
            sem((8 + NI,)),
        ],
        compiler_params=pltpu.CompilerParams(vmem_limit_bytes=60 * 1024 * 1024),
        cost_estimate=pl.CostEstimate(flops=n * 3_600_000_000, bytes_accessed=16_000_000, transcendentals=0),
        name="rest",
    )(irrep_dims, rest_own, rest_par, amps, raw)
    return total.reshape(1, NI, V, V)


def solution(mesh):
    return jax.shard_map(
        shards,
        mesh=mesh,
        in_specs=(P(), P(("sym", "occ"), "tile", None), P("sym", "occ", "tile", None)),
        out_specs=P("sym", "occ", "tile", None),
        check_vma=False,
    )
```

```python
import jax
import jax.numpy as jnp
from jax import lax
from jax.experimental import pallas as pl
from jax.experimental.pallas import tpu as pltpu
from jax.sharding import PartitionSpec as P

V = 384
NI = 8
PIECES = 2
PV = V // PIECES
HALF = NI * V // 2
CROSSF, OWN, PASS_Z, FWD_Y, PASS_Y, PAR = range(6)
PARTS = 1
SEQUENCE = (1, 1, 1, 1, 1, 1, 1, 2, 2, 2, 2, 2, 2, 1, 2, 2)
UNITS = (
    ((0, 0), (0, 0), (0, 0), (0, 0), (0, 0), (0, 0), (0, 0), (0, 0), (0, 0), (0, 0), (0, 0), (0, 0), (0, 0), (0, 0), (0, 0), (0, 0)),
    ((0, 1), (0, 1), (0, 1), (0, 1), (0, 1), (0, 1), (0, 1), (0, 1), (0, 1), (0, 1), (0, 1), (0, 1), (0, 1), (0, 1), (0, 1), (0, 1)),
    ((0, 3), (0, 3), (0, 3), (0, 3), (0, 3), (0, 3), (0, 3), (0, 3), (0, 3), (0, 3), (0, 3), (0, 3), (0, 3), (0, 3), (0, 3), (0, 3)),
    ((1, 0), (1, 0), (1, 0), (1, 0), (0, 2), (0, 2), (1, 0), (0, 2), (1, 0), (1, 0), (1, 0), (1, 0), (0, 2), (0, 2), (0, 2), (0, 2)),
    ((0, 2), (0, 2), (0, 2), (0, 2), (1, 1), (1, 1), (0, 2), (1, 0), (0, 2), (0, 2), (0, 2), (0, 2), (1, 0), (1, 0), (1, 0), (1, 0)),
    ((1, 1), (1, 1), (1, 1), (1, 1), (1, 3), (1, 3), (1, 1), (1, 1), (1, 3), (1, 3), (1, 1), (1, 1), (1, 1), (1, 1), (1, 1), (1, 1)),
    ((1, 2), (1, 2), (1, 3), (1, 3), (1, 2), (1, 0), (1, 3), (1, 3), (1, 2), (1, 2), (1, 3), (1, 3), (1, 3), (1, 3), (1, 3), (1, 3)),
    ((0, 0), (0, 0), (0, 0), (0, 0), (0, 0), (0, 0), (0, 0), (0, 0), (0, 0), (0, 0), (0, 0), (0, 0), (0, 0), (0, 0), (0, 0), (0, 0)),
    ((1, 0), (1, 0), (0, 1), (0, 1), (0, 1), (1, 0), (1, 0), (1, 0), (1, 0), (1, 0), (1, 0), (1, 0), (1, 0), (1, 0), (1, 0), (1, 0)),
    ((0, 1), (0, 1), (1, 0), (1, 0), (1, 1), (0, 1), (1, 1), (0, 1), (0, 1), (0, 1), (0, 1), (0, 1), (0, 1), (0, 1), (0, 1), (0, 1)),
    ((1, 1), (1, 1), (0, 3), (0, 3), (0, 3), (1, 1), (0, 1), (1, 1), (0, 3), (0, 3), (0, 3), (0, 3), (1, 1), (1, 1), (1, 1), (1, 1)),
    ((0, 3), (0, 3), (0, 2), (0, 2), (1, 3), (0, 3), (0, 3), (0, 3), (1, 3), (1, 3), (1, 1), (1, 1), (0, 3), (0, 3), (0, 3), (0, 3)),
    ((0, 2), (0, 2), (1, 3), (1, 1), (0, 2), (1, 3), (1, 3), (1, 3), (0, 2), (0, 2), (1, 3), (1, 3), (1, 3), (1, 3), (1, 3), (1, 3)),
    ((1, 3), (1, 3), (1, 2), (1, 2), (1, 0), (1, 2), (1, 2), (1, 2), (1, 1), (1, 1), (1, 2), (1, 2), (1, 2), (1, 2), (1, 2), (1, 2)),
    ((1, 3), (1, 3), (1, 1), (1, 3), (1, 0), (0, 2), (0, 2), (0, 2), (1, 1), (1, 1), (0, 2), (0, 2), (0, 2), (0, 2), (0, 2), (0, 2)),
    ((1, 2), (1, 2), (1, 2), (1, 2), (1, 2), (1, 2), (1, 2), (1, 2), (1, 2), (1, 2), (1, 2), (1, 2), (1, 2), (1, 2), (1, 2), (1, 2)),
)
EVENTS = (
    (
        (1, ((CROSSF, 0), (OWN, 0, 1, 0), (OWN, 0, 3, 0), (PASS_Z, 0, 0), (CROSSF, 1), (PASS_Z, 0, 1), (OWN, 0, 1, 1), (OWN, 0, 3, 1), (PASS_Z, 1, 0), (PASS_Z, 3, 0), (OWN, 1, 0, 0), (OWN, 1, 0, 1),)),
        (2, ((OWN, 0, 2, 0),)),
        (3, ((OWN, 0, 2, 1), (FWD_Y, 0, 0), (FWD_Y, 0, 1),)),
        (4, ((OWN, 1, 1, 0), (PASS_Z, 1, 1), (PASS_Z, 3, 1),)),
        (5, ((OWN, 1, 1, 1), (FWD_Y, 1, 0), (FWD_Y, 3, 0), (PASS_Y, 0, 1), (OWN, 1, 2, 0),)),
        (6, ((OWN, 1, 2, 1), (PASS_Z, 2, 0), (PASS_Z, 2, 1), (PASS_Y, 1, 0),)),
        (7, ((OWN, 1, 3, 0), (FWD_Y, 1, 1), (FWD_Y, 3, 1),)),
        (8, ((FWD_Y, 2, 0), (FWD_Y, 2, 1),)),
        (9, ((PASS_Y, 3, 1),)),
        (10, ((OWN, 1, 3, 1), (PASS_Y, 2, 0),)),
    ),
    (
        (1, ((CROSSF, 0), (OWN, 0, 1, 0), (OWN, 0, 3, 0), (PASS_Z, 0, 0), (CROSSF, 1), (PASS_Z, 0, 1), (OWN, 0, 1, 1), (OWN, 0, 3, 1), (PASS_Z, 1, 0), (PASS_Z, 3, 0), (OWN, 1, 0, 0), (OWN, 1, 0, 1),)),
        (2, ((OWN, 0, 2, 0),)),
        (3, ((OWN, 0, 2, 1), (FWD_Y, 0, 0), (FWD_Y, 0, 1),)),
        (4, ((OWN, 1, 1, 0), (PASS_Z, 1, 1), (PASS_Z, 3, 1),)),
        (5, ((OWN, 1, 1, 1), (FWD_Y, 1, 0), (FWD_Y, 3, 0), (PASS_Y, 0, 0), (OWN, 1, 2, 0),)),
        (6, ((OWN, 1, 2, 1), (PASS_Z, 2, 0), (PASS_Z, 2, 1), (PASS_Y, 3, 0),)),
        (7, ((OWN, 1, 3, 0), (FWD_Y, 1, 1), (FWD_Y, 3, 1),)),
        (8, ((OWN, 1, 3, 1), (FWD_Y, 2, 0), (FWD_Y, 2, 1),)),
        (9, ((PASS_Y, 1, 1),)),
        (10, ((PASS_Y, 2, 1),)),
    ),
    (
        (1, ((CROSSF, 0), (OWN, 0, 1, 0), (OWN, 0, 3, 0), (PASS_Z, 0, 0), (CROSSF, 1), (PASS_Z, 0, 1), (OWN, 0, 1, 1), (OWN, 0, 3, 1), (PASS_Z, 1, 0), (PASS_Z, 3, 0), (OWN, 1, 0, 0), (OWN, 1, 0, 1),)),
        (2, ((OWN, 0, 2, 0),)),
        (3, ((OWN, 0, 2, 1), (PAR, 0, 0, 0), (PAR, 0, 0, 1),)),
        (4, ((OWN, 1, 1, 0), (OWN, 1, 3, 0), (PASS_Z, 1, 1), (PASS_Z, 3, 1),)),
        (5, ((OWN, 1, 1, 1), (OWN, 1, 3, 1), (PASS_Y, 0, 0), (PAR, 0, 1, 0), (PAR, 0, 3, 0),)),
        (6, ((OWN, 1, 2, 0), (OWN, 1, 2, 1), (PASS_Z, 2, 0), (PASS_Z, 2, 1),)),
        (7, ((PASS_Y, 3, 0), (PAR, 0, 1, 1), (PAR, 0, 3, 1), (PAR, 1, 0, 1),)),
        (8, ((PAR, 1, 0, 0),)),
        (9, ((PAR, 0, 2, 0), (PAR, 0, 2, 1), (PAR, 1, 1, 0), (PAR, 1, 3, 0),)),
        (10, ((PASS_Y, 1, 1),)),
        (12, ((PASS_Y, 2, 1), (PAR, 1, 3, 1),)),
        (13, ((PAR, 1, 1, 1),)),
        (14, ((PAR, 1, 2, 0), (PAR, 1, 2, 1),)),
    ),
    (
        (1, ((CROSSF, 0), (OWN, 0, 1, 0), (OWN, 0, 3, 0), (PASS_Z, 0, 0), (CROSSF, 1), (PASS_Z, 0, 1), (OWN, 0, 1, 1), (OWN, 0, 3, 1), (PASS_Z, 1, 0), (PASS_Z, 3, 0), (OWN, 1, 0, 0), (OWN, 1, 0, 1),)),
        (2, ((OWN, 0, 2, 0),)),
        (3, ((OWN, 0, 2, 1), (PAR, 0, 0, 0), (PAR, 0, 0, 1),)),
        (4, ((OWN, 1, 1, 0), (OWN, 1, 3, 0), (PASS_Z, 1, 1), (PASS_Z, 3, 1),)),
        (5, ((OWN, 1, 1, 1), (OWN, 1, 3, 1), (PASS_Y, 0, 1), (PAR, 0, 1, 0), (PAR, 0, 3, 0),)),
        (6, ((OWN, 1, 2, 0), (OWN, 1, 2, 1), (PASS_Z, 2, 0), (PASS_Z, 2, 1),)),
        (7, ((PASS_Y, 1, 0), (PAR, 0, 1, 1), (PAR, 0, 3, 1), (PAR, 1, 0, 0),)),
        (8, ((PAR, 1, 0, 1),)),
        (9, ((PAR, 0, 2, 0), (PAR, 0, 2, 1), (PAR, 1, 1, 0), (PAR, 1, 3, 0),)),
        (10, ((PASS_Y, 3, 1),)),
        (12, ((PASS_Y, 2, 0), (PAR, 1, 1, 1),)),
        (13, ((PAR, 1, 3, 1),)),
        (14, ((PAR, 1, 2, 0), (PAR, 1, 2, 1),)),
    ),
    (
        (1, ((CROSSF, 0), (PASS_Z, 0, 0), (OWN, 0, 1, 0), (OWN, 0, 3, 0), (PAR, 0, 0, 0), (PASS_Z, 0, 1), (OWN, 0, 1, 1), (PAR, 1, 0, 0), (OWN, 0, 3, 1), (CROSSF, 1), (PASS_Z, 1, 0), (PASS_Z, 3, 0),)),
        (2, ((OWN, 0, 2, 0), (PAR, 0, 0, 1), (PAR, 1, 0, 1),)),
        (3, ((OWN, 0, 2, 1), (FWD_Y, 0, 0), (FWD_Y, 0, 1), (OWN, 1, 1, 0), (PAR, 1, 1, 0), (PAR, 0, 1, 0), (PASS_Z, 1, 1), (PASS_Z, 3, 1), (OWN, 1, 3, 0),)),
        (4, ((OWN, 1, 1, 1), (PAR, 0, 3, 0), (PAR, 1, 3, 0), (FWD_Y, 1, 0), (FWD_Y, 3, 0), (OWN, 1, 3, 1),)),
        (5, ((OWN, 1, 0, 0), (PAR, 0, 1, 1),)),
        (6, ((OWN, 1, 2, 0), (PAR, 0, 3, 1), (OWN, 1, 2, 1), (PASS_Z, 2, 0), (PASS_Z, 2, 1), (PAR, 1, 1, 1), (FWD_Y, 1, 1), (FWD_Y, 3, 1),)),
        (7, ((OWN, 1, 0, 1), (PAR, 1, 3, 1),)),
        (8, ((FWD_Y, 2, 0), (FWD_Y, 2, 1), (PAR, 0, 2, 0), (PAR, 1, 2, 0),)),
        (10, ((PAR, 0, 2, 1), (PAR, 1, 2, 1),)),
    ),
    (
        (1, ((CROSSF, 0), (PASS_Z, 0, 0), (OWN, 0, 1, 0), (OWN, 0, 3, 0), (PAR, 1, 0, 0), (PASS_Z, 0, 1), (OWN, 0, 1, 1), (PAR, 0, 0, 0), (OWN, 0, 3, 1), (CROSSF, 1), (PASS_Z, 1, 0), (PASS_Z, 3, 0),)),
        (2, ((OWN, 0, 2, 0), (PAR, 0, 0, 1), (PAR, 1, 0, 1),)),
        (3, ((OWN, 0, 2, 1), (FWD_Y, 0, 0), (FWD_Y, 0, 1), (OWN, 1, 1, 0), (PAR, 0, 1, 0), (PAR, 1, 1, 0), (PASS_Z, 1, 1), (PASS_Z, 3, 1), (OWN, 1, 3, 0),)),
        (4, ((OWN, 1, 1, 1), (PAR, 0, 3, 0), (PAR, 1, 3, 0), (FWD_Y, 1, 0), (FWD_Y, 3, 0), (OWN, 1, 3, 1),)),
        (5, ((OWN, 1, 0, 0), (OWN, 1, 0, 1),)),
        (6, ((OWN, 1, 2, 0), (OWN, 1, 2, 1), (PASS_Z, 2, 0), (PASS_Z, 2, 1), (PAR, 0, 1, 1), (PAR, 1, 1, 1),)),
        (7, ((FWD_Y, 1, 1), (FWD_Y, 3, 1),)),
        (8, ((FWD_Y, 2, 0), (FWD_Y, 2, 1), (PAR, 0, 3, 1), (PAR, 1, 3, 1),)),
        (9, ((PAR, 0, 2, 0), (PAR, 1, 2, 0),)),
        (10, ((PAR, 0, 2, 1), (PAR, 1, 2, 1),)),
    ),
    (
        (1, ((CROSSF, 0), (PASS_Z, 0, 0), (OWN, 0, 1, 0), (OWN, 0, 3, 0), (CROSSF, 1), (PASS_Z, 0, 1), (OWN, 0, 1, 1), (OWN, 0, 3, 1), (PASS_Z, 1, 0), (PASS_Z, 3, 0), (OWN, 1, 0, 0), (OWN, 1, 0, 1),)),
        (2, ((OWN, 0, 2, 0),)),
        (3, ((OWN, 0, 2, 1), (FWD_Y, 0, 0), (FWD_Y, 0, 1),)),
        (4, ((OWN, 1, 1, 0), (OWN, 1, 3, 0), (PASS_Z, 1, 1), (PASS_Z, 3, 1),)),
        (5, ((OWN, 1, 1, 1), (OWN, 1, 3, 1), (FWD_Y, 1, 0), (FWD_Y, 3, 0), (PAR, 0, 0, 0), (PAR, 1, 0, 0),)),
        (6, ((OWN, 1, 2, 0), (PASS_Z, 2, 0), (PASS_Z, 2, 1), (PAR, 0, 0, 1), (PAR, 1, 0, 1),)),
        (7, ((OWN, 1, 2, 1), (FWD_Y, 1, 1), (FWD_Y, 3, 1), (PAR, 0, 1, 0), (PAR, 1, 1, 0),)),
        (8, ((FWD_Y, 2, 0), (FWD_Y, 2, 1), (PAR, 0, 3, 0), (PAR, 1, 3, 0),)),
        (9, ((PAR, 1, 1, 1), (PAR, 0, 1, 1),)),
        (10, ((PAR, 0, 3, 1), (PAR, 1, 3, 1),)),
        (12, ((PAR, 0, 2, 0), (PAR, 1, 2, 0),)),
        (13, ((PAR, 0, 2, 1), (PAR, 1, 2, 1),)),
    ),
    (
        (1, ((CROSSF, 0), (PASS_Z, 0, 0), (OWN, 0, 1, 0), (OWN, 0, 3, 0), (CROSSF, 1), (PASS_Z, 0, 1), (OWN, 0, 1, 1), (OWN, 0, 3, 1), (PASS_Z, 1, 0), (PASS_Z, 3, 0), (OWN, 1, 0, 0),)),
        (2, ((OWN, 0, 2, 0),)),
        (3, ((OWN, 0, 2, 1), (OWN, 1, 0, 1), (FWD_Y, 0, 0), (FWD_Y, 0, 1), (OWN, 1, 1, 0), (PASS_Z, 1, 1), (PASS_Z, 3, 1), (OWN, 1, 3, 0),)),
        (4, ((OWN, 1, 1, 1),)),
        (5, ((OWN, 1, 3, 1), (FWD_Y, 1, 0), (FWD_Y, 3, 0), (PAR, 0, 0, 0), (PAR, 1, 0, 0),)),
        (6, ((OWN, 1, 2, 0), (PASS_Z, 2, 0), (PASS_Z, 2, 1), (PAR, 0, 0, 1), (PAR, 1, 0, 1),)),
        (7, ((OWN, 1, 2, 1), (FWD_Y, 1, 1), (FWD_Y, 3, 1), (PAR, 0, 1, 0), (PAR, 1, 1, 0),)),
        (8, ((FWD_Y, 2, 0), (FWD_Y, 2, 1), (PAR, 0, 3, 0), (PAR, 1, 3, 0),)),
        (9, ((PAR, 0, 1, 1), (PAR, 1, 1, 1),)),
        (10, ((PAR, 0, 3, 1), (PAR, 1, 3, 1),)),
        (12, ((PAR, 0, 2, 0), (PAR, 1, 2, 0),)),
        (13, ((PAR, 0, 2, 1), (PAR, 1, 2, 1),)),
    ),
    (
        (1, ((CROSSF, 0), (PAR, 0, 0, 0), (OWN, 0, 1, 0), (OWN, 0, 3, 0), (FWD_Y, 0, 0), (CROSSF, 1), (OWN, 0, 1, 1), (PAR, 0, 0, 1), (OWN, 0, 3, 1), (FWD_Y, 0, 1), (OWN, 1, 0, 0), (OWN, 1, 0, 1),)),
        (2, ((OWN, 0, 2, 0), (FWD_Y, 1, 0), (PAR, 0, 1, 0),)),
        (3, ((OWN, 0, 2, 1), (PASS_Y, 0, 0), (PASS_Y, 0, 1),)),
        (4, ((OWN, 1, 3, 0), (FWD_Y, 3, 0), (PASS_Y, 1, 0), (PAR, 0, 3, 0),)),
        (5, ((OWN, 1, 3, 1), (FWD_Y, 1, 1), (PAR, 0, 1, 1), (PAR, 1, 0, 0), (PAR, 1, 0, 1),)),
        (6, ((OWN, 1, 2, 0), (OWN, 1, 2, 1), (FWD_Y, 3, 1), (PASS_Y, 3, 0), (PAR, 0, 3, 1), (PAR, 1, 1, 0), (PAR, 0, 2, 0), (FWD_Y, 2, 0),)),
        (7, ((OWN, 1, 1, 0), (PASS_Y, 1, 1),)),
        (8, ((FWD_Y, 2, 1), (PASS_Y, 3, 1), (PAR, 0, 2, 1), (PAR, 1, 3, 0),)),
        (9, ((PASS_Y, 2, 0), (PAR, 1, 1, 1),)),
        (10, ((OWN, 1, 1, 1), (PASS_Y, 2, 1), (PAR, 1, 3, 1),)),
        (11, ((PAR, 1, 2, 0),)),
        (13, ((PAR, 1, 2, 1),)),
    ),
    (
        (1, ((CROSSF, 0), (PAR, 0, 0, 0), (OWN, 0, 1, 0), (OWN, 0, 3, 0), (FWD_Y, 0, 0), (CROSSF, 1), (OWN, 0, 1, 1), (PAR, 0, 0, 1), (OWN, 0, 3, 1), (FWD_Y, 0, 1), (OWN, 1, 0, 0), (OWN, 1, 0, 1),)),
        (2, ((OWN, 0, 2, 0), (FWD_Y, 1, 0), (PAR, 0, 1, 0),)),
        (3, ((OWN, 0, 2, 1), (PASS_Y, 0, 0), (PASS_Y, 0, 1),)),
        (4, ((OWN, 1, 3, 0), (FWD_Y, 3, 0), (PASS_Y, 1, 0), (PAR, 0, 3, 0),)),
        (5, ((OWN, 1, 3, 1), (FWD_Y, 1, 1), (PAR, 0, 1, 1), (PAR, 1, 0, 0), (PAR, 1, 0, 1),)),
        (6, ((OWN, 1, 2, 0), (OWN, 1, 2, 1), (FWD_Y, 3, 1), (PASS_Y, 3, 0), (PAR, 0, 3, 1), (PAR, 1, 1, 0), (PAR, 0, 2, 0), (FWD_Y, 2, 0),)),
        (7, ((OWN, 1, 1, 0), (PASS_Y, 1, 1),)),
        (8, ((OWN, 1, 1, 1), (FWD_Y, 2, 1), (PASS_Y, 3, 1), (PAR, 0, 2, 1), (PAR, 1, 3, 0),)),
        (9, ((PASS_Y, 2, 0), (PAR, 1, 1, 1),)),
        (10, ((PASS_Y, 2, 1), (PAR, 1, 3, 1),)),
        (11, ((PAR, 1, 2, 0),)),
        (12, ((PAR, 1, 2, 1),)),
    ),
    (
        (1, ((CROSSF, 0), (FWD_Y, 0, 0), (OWN, 0, 1, 0), (OWN, 0, 3, 0), (PAR, 0, 0, 0), (CROSSF, 1), (OWN, 0, 1, 1), (FWD_Y, 0, 1), (OWN, 0, 3, 1), (PAR, 0, 0, 1), (OWN, 1, 0, 0), (OWN, 1, 0, 1),)),
        (2, ((OWN, 0, 2, 0), (FWD_Y, 1, 0), (PAR, 0, 1, 0),)),
        (3, ((OWN, 0, 2, 1), (PASS_Y, 0, 0), (PASS_Y, 0, 1),)),
        (4, ((OWN, 1, 1, 0), (OWN, 1, 3, 0), (FWD_Y, 3, 0), (PASS_Y, 1, 0), (PAR, 0, 3, 0),)),
        (5, ((OWN, 1, 1, 1), (OWN, 1, 3, 1), (FWD_Y, 1, 1), (PAR, 0, 1, 1), (PAR, 1, 0, 0), (PAR, 1, 0, 1),)),
        (6, ((OWN, 1, 2, 0), (FWD_Y, 3, 1), (PASS_Y, 3, 0), (PAR, 0, 3, 1), (PAR, 1, 1, 0),)),
        (7, ((OWN, 1, 2, 1), (FWD_Y, 2, 0), (PASS_Y, 1, 1), (PAR, 0, 2, 0),)),
        (8, ((FWD_Y, 2, 1), (PASS_Y, 3, 1), (PAR, 0, 2, 1), (PAR, 1, 3, 0),)),
        (9, ((PASS_Y, 2, 0),)),
        (10, ((PAR, 1, 1, 1),)),
        (11, ((PASS_Y, 2, 1), (PAR, 1, 3, 1),)),
        (12, ((PAR, 1, 2, 0),)),
        (13, ((PAR, 1, 2, 1),)),
    ),
    (
        (1, ((CROSSF, 0), (FWD_Y, 0, 0), (OWN, 0, 1, 0), (OWN, 0, 3, 0), (PAR, 0, 0, 0), (CROSSF, 1), (OWN, 0, 1, 1), (FWD_Y, 0, 1), (OWN, 0, 3, 1), (PAR, 0, 0, 1), (OWN, 1, 0, 0), (OWN, 1, 0, 1),)),
        (2, ((OWN, 0, 2, 0), (FWD_Y, 1, 0), (PAR, 0, 1, 0),)),
        (3, ((OWN, 0, 2, 1), (PASS_Y, 0, 0), (PASS_Y, 0, 1),)),
        (4, ((OWN, 1, 1, 0), (OWN, 1, 3, 0), (FWD_Y, 3, 0), (PASS_Y, 1, 0), (PAR, 0, 3, 0),)),
        (5, ((OWN, 1, 1, 1), (OWN, 1, 3, 1), (FWD_Y, 1, 1), (PAR, 0, 1, 1), (PAR, 1, 0, 0), (PAR, 1, 0, 1),)),
        (6, ((OWN, 1, 2, 0), (OWN, 1, 2, 1), (FWD_Y, 3, 1), (PASS_Y, 3, 0), (PAR, 0, 3, 1), (PAR, 1, 1, 0),)),
        (7, ((FWD_Y, 2, 0), (PASS_Y, 1, 1), (PAR, 0, 2, 0),)),
        (8, ((FWD_Y, 2, 1), (PASS_Y, 3, 1), (PAR, 0, 2, 1), (PAR, 1, 3, 0),)),
        (9, ((PASS_Y, 2, 0),)),
        (10, ((PAR, 1, 1, 1),)),
        (11, ((PASS_Y, 2, 1), (PAR, 1, 3, 1),)),
        (12, ((PAR, 1, 2, 0),)),
        (13, ((PAR, 1, 2, 1),)),
    ),
    (
        (1, ((CROSSF, 0), (OWN, 0, 1, 0), (OWN, 0, 3, 0), (FWD_Y, 0, 0), (CROSSF, 1), (OWN, 0, 1, 1), (OWN, 0, 3, 1), (FWD_Y, 0, 1), (OWN, 1, 0, 0), (PAR, 0, 0, 0),)),
        (2, ((OWN, 0, 2, 0), (FWD_Y, 1, 0),)),
        (3, ((OWN, 0, 2, 1), (OWN, 1, 0, 1), (OWN, 1, 1, 0), (PAR, 1, 0, 0), (FWD_Y, 3, 0), (PAR, 1, 0, 1), (OWN, 1, 3, 0),)),
        (4, ((OWN, 1, 1, 1), (FWD_Y, 1, 1), (PAR, 0, 0, 1),)),
        (5, ((OWN, 1, 3, 1), (PAR, 0, 1, 0), (PAR, 1, 1, 0),)),
        (6, ((FWD_Y, 3, 1), (PAR, 0, 3, 0), (PAR, 1, 3, 0),)),
        (7, ((FWD_Y, 2, 0), (PAR, 0, 1, 1), (PAR, 1, 1, 1),)),
        (8, ((FWD_Y, 2, 1), (PAR, 1, 3, 1),)),
        (9, ((OWN, 1, 2, 0), (PAR, 0, 3, 1),)),
        (10, ((PAR, 0, 2, 0), (PAR, 1, 2, 0),)),
        (11, ((PAR, 0, 2, 1), (PAR, 1, 2, 1),)),
        (13, ((OWN, 1, 2, 1),)),
    ),
    (
        (1, ((CROSSF, 0), (OWN, 0, 1, 0), (OWN, 0, 3, 0), (FWD_Y, 0, 0), (CROSSF, 1), (OWN, 0, 1, 1), (OWN, 0, 3, 1), (FWD_Y, 0, 1), (OWN, 1, 0, 0), (PAR, 1, 0, 0),)),
        (2, ((OWN, 0, 2, 0), (FWD_Y, 1, 0),)),
        (3, ((OWN, 0, 2, 1), (OWN, 1, 0, 1), (OWN, 1, 1, 0), (PAR, 0, 0, 0), (FWD_Y, 3, 0), (PAR, 0, 0, 1), (OWN, 1, 3, 0),)),
        (4, ((OWN, 1, 1, 1), (FWD_Y, 1, 1), (PAR, 1, 0, 1),)),
        (5, ((OWN, 1, 3, 1), (PAR, 0, 1, 0), (PAR, 1, 1, 0),)),
        (6, ((FWD_Y, 3, 1), (PAR, 0, 3, 0), (PAR, 1, 3, 0),)),
        (7, ((FWD_Y, 2, 0), (PAR, 0, 1, 1), (PAR, 1, 1, 1),)),
        (8, ((FWD_Y, 2, 1), (PAR, 0, 3, 1),)),
        (9, ((OWN, 1, 2, 0), (PAR, 1, 3, 1),)),
        (10, ((PAR, 0, 2, 0), (PAR, 1, 2, 0),)),
        (11, ((OWN, 1, 2, 1), (PAR, 0, 2, 1), (PAR, 1, 2, 1),)),
    ),
    (
        (1, ((CROSSF, 0), (OWN, 0, 1, 0), (OWN, 0, 3, 0), (FWD_Y, 0, 0), (CROSSF, 1), (OWN, 0, 1, 1), (OWN, 0, 3, 1), (FWD_Y, 0, 1), (OWN, 1, 0, 0), (PAR, 0, 0, 0),)),
        (2, ((OWN, 0, 2, 0), (FWD_Y, 1, 0),)),
        (3, ((OWN, 0, 2, 1), (OWN, 1, 0, 1), (OWN, 1, 1, 0), (PAR, 1, 0, 0), (FWD_Y, 3, 0), (PAR, 1, 0, 1), (OWN, 1, 3, 0),)),
        (4, ((OWN, 1, 1, 1), (FWD_Y, 1, 1), (PAR, 0, 0, 1),)),
        (5, ((OWN, 1, 3, 1), (PAR, 0, 1, 0), (PAR, 1, 1, 0),)),
        (6, ((OWN, 1, 2, 0), (FWD_Y, 3, 1), (PAR, 0, 3, 0), (PAR, 1, 3, 0),)),
        (7, ((OWN, 1, 2, 1), (FWD_Y, 2, 0), (PAR, 0, 1, 1), (PAR, 1, 1, 1),)),
        (8, ((FWD_Y, 2, 1), (PAR, 0, 3, 1), (PAR, 1, 3, 1),)),
        (10, ((PAR, 0, 2, 0), (PAR, 1, 2, 0),)),
        (11, ((PAR, 0, 2, 1), (PAR, 1, 2, 1),)),
    ),
    (
        (1, ((CROSSF, 0), (OWN, 0, 1, 0), (OWN, 0, 3, 0), (FWD_Y, 0, 0), (CROSSF, 1), (OWN, 0, 1, 1), (OWN, 0, 3, 1), (FWD_Y, 0, 1), (OWN, 1, 0, 0), (PAR, 1, 0, 0),)),
        (2, ((OWN, 0, 2, 0), (FWD_Y, 1, 0),)),
        (3, ((OWN, 0, 2, 1), (OWN, 1, 0, 1), (OWN, 1, 1, 0), (PAR, 0, 0, 0), (FWD_Y, 3, 0), (PAR, 0, 0, 1), (OWN, 1, 3, 0),)),
        (4, ((OWN, 1, 1, 1), (FWD_Y, 1, 1), (PAR, 1, 0, 1),)),
        (5, ((OWN, 1, 3, 1), (PAR, 0, 1, 0), (PAR, 1, 1, 0),)),
        (6, ((OWN, 1, 2, 0), (FWD_Y, 3, 1), (PAR, 0, 3, 0), (PAR, 1, 3, 0),)),
        (7, ((OWN, 1, 2, 1), (FWD_Y, 2, 0), (PAR, 0, 1, 1), (PAR, 1, 1, 1),)),
        (8, ((FWD_Y, 2, 1), (PAR, 0, 3, 1), (PAR, 1, 3, 1),)),
        (10, ((PAR, 0, 2, 0), (PAR, 1, 2, 0),)),
        (11, ((PAR, 0, 2, 1), (PAR, 1, 2, 1),)),
    ),
)

STAGES = len(SEQUENCE)
POINTS = PARTS * STAGES + 1
PAR_AT, T1_AT, T2_AT, T3_AT, TC_AT, SLOTS = 32, 64, 72, 80, 88, 90
WAYS = ("x+", "x-", "y+", "y-", "z+", "z-", "core", "ya", "yb", "za", "zb")
WAIT = 15
CLASSES = [(x, y) for x in range(4) for y in range(4)]


def sign_of(j, k):
    return "+" if (k + (0, 1, 1, 0)[j]) % 2 == 0 else "-"


def name_of(x, y, row, j):
    return (y // 2 + row) % 2 * 4 + (x + 4 - j) % 4


def row_behind(y, sign):
    return (y + 3) % 4 // 2 if sign == "+" else (y + 1) % 4 // 2


def feed(x, y, j, k, src):
    up = y // 2 == 1
    final, via1, via2 = ("par", name_of(x, y, 0, j), k), ("t1", j, k), ("t2", j, k)
    sends = []
    if x in (0, 1):
        sends.append((src, via1, "z" + sign_of(j, k)))
    if x == 1:
        sends.append((src, final, "ya"))
    if x in (2, 3):
        sends.append((src, final if x == 2 and not up else via1, "za"))
        sends.append((src, final if x == 2 and up else via2, "zb"))
    return sends


def expand(x, y, event):
    kind, args = event[0], event[1:]
    up = y // 2 == 1
    ops = []
    if kind == CROSSF:
        (k,) = args
        sign = "+-"[k]
        ops = [("tc", k), (("tc", k), ("own", row_behind(y, sign) * 4 + x, k), "y" + sign)]
    if kind == OWN:
        row, j, k = args
        here = ("own", name_of(x, y, row, j), k)
        ops = [here]
        if (row, j) == (1, 0) or (j == 1 and (k + row) % 2 == 0):
            ops.append((here, here, "x+"))
        if (row, j) == (1, 0) or (j == 3 and (k + row) % 2 == 1):
            ops.append((here, here, "x-"))
        if row == 0:
            ops += feed(x, y, j, k, here)
        ops.append((here, here, "core"))
    if kind == PASS_Z:
        j, k = args
        here = ("t1", j, k)
        there = ("par", name_of(x, y, 0, j), k) if x == 0 and up else ("t2", j, k)
        ops = [here, (here, there, "z" + sign_of(j, k))]
    if kind == FWD_Y:
        j, k = args
        final, there, way = ("par", name_of(x, y, 0, j), k), ("t3", j, k), "y" + sign_of(j, k)
        if x == 3 or (x == 2 and up):
            ops += [("t1", j, k), (("t1", j, k), final, "ya") if x == 3 else (("t1", j, k), there, way)]
        if x in (1, 3) or not up:
            ops += [("t2", j, k), (("t2", j, k), final, "yb") if x in (1, 3) else (("t2", j, k), there, way)]
    if kind == PASS_Y:
        j, k = args
        sign = sign_of(j, k)
        row = row_behind(y, sign)
        if x == 2 or row == 0:
            ops = [("t3", j, k), (("t3", j, k), ("par", row * 4 + (x + 4 - j) % 4, k), "y" + sign)]
    if kind == PAR:
        row, j, k = args
        here = ("par", name_of(x, y, row, j), k)
        ops = [here, (here, here, "core")]
    return ops


def slot(place, c):
    kind, rest = place[0], place[1:]
    if kind in ("own", "par"):
        q, k = rest
        return (PAR_AT if kind == "par" else 0) + q * 4 + c * 2 + k
    if kind == "tc":
        return TC_AT + rest[0]
    return {"t1": T1_AT, "t2": T2_AT, "t3": T3_AT}[kind] + rest[0] * 2 + rest[1]


def tables(x, y):
    per_core = []
    for c in range(2):
        ops, begins, sends, at = [], [], 0, dict(EVENTS[CLASSES.index((x, y))])
        for point in range(POINTS):
            begins.append(len(ops))
            for event in at.get(point, ()):
                for op in expand(x, y, event):
                    if isinstance(op[0], str):
                        ops.append(slot(op, c) + 2097152 * WAIT)
                    else:
                        src, dst, way = op
                        ops.append(slot(src, c) + 128 * slot(dst, c) + 16384 * sends + 2097152 * WAYS.index(way))
                        sends += 1
        per_core.append((ops, begins + [len(ops)], sends))
    return per_core


TABLES = {cls: tables(*cls) for cls in CLASSES}
MOST_OPS = max(len(ops) for cores in TABLES.values() for ops, _, _ in cores)
MOST_SENDS = max(sends for cores in TABLES.values() for _, _, sends in cores)
FIRST_SENDS = 12


def columns(t):
    first, last = t * 256, (t + 1) * 256
    cuts = [first] + [cut for cut in range(0, NI * V, V) if first < cut < last] + [last]
    return [(u - first, w - first, u // V, u % V) for u, w in zip(cuts, cuts[1:])]


def kernel(dims, mine, amps, out, buf, rc, half, acc, ops, begins, devs,
           ssem, first_sem, rsem, local_sem):
    sym, tile, c = lax.axis_index("sym"), lax.axis_index("tile"), lax.axis_index("occ")
    x, yhi = sym % 4, sym // 4
    x0, x1 = x % 2, x // 2
    z, ylo = tile // 2, tile % 2
    z0, z1 = z % 2, z // 2
    y = 2 * yhi + ylo
    none = sym == 0

    def dev(dx=0, dy=0, dz=0, dc=0):
        xx, yy, zz = (x + 4 + dx) % 4, (y + 4 + dy) % 4, (z + 4 + dz) % 4
        return ((yy // 2) * 4 + xx) * 16 + (zz * 2 + yy % 2) * 2 + (c + dc) % 2

    step_a = 1 - 2 * (yhi + ylo - 2 * yhi * ylo)
    step_z = 1 - 2 * z0
    to = {
        "x+": dev(dx=1), "x-": dev(dx=-1), "y+": dev(dy=1), "y-": dev(dy=-1), "z+": dev(dz=1), "z-": dev(dz=-1),
        "core": dev(dc=1), "ya": dev(dy=step_a), "yb": dev(dy=-step_a), "za": dev(dz=step_z), "zb": dev(dz=-step_z),
    }
    barrier = pltpu.get_barrier_semaphore()
    for way in WAYS[:7]:
        pl.semaphore_signal(barrier, inc=1, device_id=to[way], device_id_type=pl.DeviceIdType.LOGICAL)

    def own_slot(q, core, k):
        return q * 4 + core * 2 + k

    keep = []
    for k in range(PIECES):
        keep.append(pltpu.make_async_copy(mine.at[pl.ds(k * PV, PV)], buf.at[own_slot(sym, c, k)], local_sem.at[8 + k]))
        keep[-1].start()
    loads = [pltpu.make_async_copy(amps.at[i], rc.at[:, pl.ds(i * V, V)], local_sem.at[i]) for i in range(NI)]
    for load in loads:
        load.start()

    pl.semaphore_wait(barrier, 7)

    def remote(src, dst_slot, sem, where):
        return pltpu.make_async_remote_copy(
            src, buf.at[dst_slot], sem, rsem.at[dst_slot], device_id=where, device_id_type=pl.DeviceIdType.LOGICAL
        )

    def arrived(at):
        remote(buf.at[at], at, first_sem.at[0], to["core"]).wait_recv()

    firsts = []

    def first(src, place, where, cond=None):
        index = len(firsts)
        if cond is None:
            remote(src, place, first_sem.at[index], where).start()
        else:
            pl.when(cond)(lambda: remote(src, place, first_sem.at[index], where).start())
        firsts.append((src, place, cond, index))

    step_2 = {k: {"+": to["z+"], "-": to["z-"]}[sign_of(0, k)] for k in range(PIECES)}
    for k in range(PIECES):
        src = mine.at[pl.ds(k * PV, PV)]
        home = own_slot(sym, c, k)
        final, via1, via2 = PAR_AT + home, T1_AT + k, T2_AT + k
        first(src, home, to["core"])
        first(src, home, to["x+"])
        first(src, home, to["x-"])
        first(src, TC_AT + k, to["y" + "+-"[k]])
        direct_b, direct_a = x0 + 2 * (1 - x1) + (1 - yhi) == 0, x0 + 2 * (1 - x1) + yhi == 0
        where_b = x1 * to["zb"] + (1 - x1) * step_2[k]
        place_b = jnp.where(direct_b, final, x1 * via2 + (1 - x1) * via1)
        first(src, place_b, where_b)
        where_a = x1 * to["za"] + (1 - x1) * to["ya"]
        place_a = jnp.where(direct_a | (x1 == 0), final, via1)
        first(src, place_a, where_a, x > 0)

    for (at_x, at_y), cores in TABLES.items():
        @pl.when((x == at_x) & (y == at_y))
        def _():
            (ops0, begins0, _), (ops1, _, _) = cores
            for n, (op0, op1) in enumerate(zip(ops0, ops1)):
                ops[n] = op0 + (op1 - op0) * c if op0 != op1 else op0
            for n, begin in enumerate(begins0):
                begins[n] = begin
    for n, way in enumerate(WAYS):
        devs[n] = to[way]

    n_row = dims[tile]
    n_col = dims[(z1 + yhi - 2 * z1 * yhi) * 4 + (z0 + x1 - 2 * z0 * x1) * 2 + (ylo + x0 - 2 * ylo * x0)]
    alive = (lax.broadcasted_iota(jnp.int32, (V, V), 0) < n_row) & (lax.broadcasted_iota(jnp.int32, (V, V), 1) < n_col)
    live = jnp.where(alive, 1.0, 0.0).astype(jnp.bfloat16)
    acc[...] = jnp.zeros_like(acc)
    for load in loads:
        load.wait()
    for i in range(NI):
        rc[:, i * V:(i + 1) * V] = rc[:, i * V:(i + 1) * V] * live
    for copy in keep:
        copy.wait()

    def decoded(n):
        op = ops[n]
        src, rest = lax.rem(op, 128), lax.div(op, 128)
        dst, rest = lax.rem(rest, 128), lax.div(rest, 128)
        return src, dst, lax.rem(rest, 128), lax.div(rest, 128)

    def events(point):
        @pl.loop(begins[point], begins[point + 1])
        def _(n):
            src, dst, index, way = decoded(n)

            @pl.when(way == WAIT)
            def _():
                arrived(src)

            @pl.when(way != WAIT)
            def _():
                remote(buf.at[src], dst, ssem.at[index], devs[way]).start()

    digit = (1 + 7 * x0) * (1 + 63 * x1) * (1 + 4095 * yhi)

    def chosen(groups, n):
        code = 0
        for k, names in enumerate(groups):
            packed = [0, 0]
            for (at_x, at_y), (row, j) in zip(CLASSES, names):
                packed[at_y % 2] += (row * 4 + j) * 8 ** (at_y // 2 * 4 + at_x)
            code = code + (n == k) * 1 * (packed[0] + (packed[1] - packed[0]) * ylo)
        code = lax.rem(lax.div(code, digit), 8)
        return (yhi + code // 4) % 2 * 4 + (x + 4 - code % 4) % 4

    def unit(base, q, core):
        at = base + q * 4 + core * 2
        return buf[pl.ds(at, 2)].reshape(V, V)

    def first_stage(n, q):
        for k in range(PIECES):
            arrived(own_slot(q, 1 - c, k))

        @pl.when(none)
        def _():
            pltpu.make_async_copy(buf.at[pl.ds(q * 4, 4)], buf.at[pl.ds(PAR_AT + q * 4, 4)], local_sem.at[10 + q]).start()

        for h in range(PARTS):
            if h:
                events(PARTS * n + h)
            for t in range(h * 12 // PARTS, (h + 1) * 12 // PARTS):
                left = buf[pl.ds(q * 4, 4)].reshape(2 * V, V)
                r = jnp.dot(left, rc[:, t * 256:(t + 1) * 256], preferred_element_type=jnp.float32).astype(jnp.bfloat16)
                for lo_col, hi_col, pair, at in columns(t):
                    for p in range(2):
                        lanes = pl.ds(p * V + at, hi_col - lo_col)
                        half[q, pair * V:(pair + 1) * V, lanes] = r[p * V:(p + 1) * V, lo_col:hi_col]

    def second_stage(n, q):
        @pl.when(none)
        def _():
            pltpu.make_async_copy(buf.at[pl.ds(q * 4, 4)], buf.at[pl.ds(PAR_AT + q * 4, 4)], local_sem.at[10 + q]).wait()

        @pl.when(jnp.logical_not(none))
        def _():
            for k in range(PIECES):
                arrived(PAR_AT + own_slot(q, 1 - c, k))

        for h in range(2):
            if h and PARTS > 1:
                events(PARTS * n + h)
            rows = pl.ds(h * HALF, HALF)
            for b0, b1 in ((0, 256), (256, 384)):
                right = jnp.concatenate([unit(PAR_AT, q, p)[b0:b1] for p in range(2)], axis=1)
                acc[rows, b0:b1] += lax.dot_general(
                    half[q, rows, :], right, (((1,), (1,)), ((), ())), preferred_element_type=jnp.float32
                )

    @pl.loop(0, STAGES)
    def _(n):
        second = sum((n == k) * 1 for k, stage in enumerate(SEQUENCE) if stage == 2)
        q = chosen(UNITS, n)
        events(PARTS * n)
        pl.when(second == 0)(lambda: first_stage(n, q))
        pl.when(second == 1)(lambda: second_stage(n, q))

    for i in range(NI):
        rows = pl.ds(i * V, V)
        acc[rows, :] = jnp.where(alive, acc[rows, :], 0.0)
        pltpu.make_async_copy(acc.at[rows], out.at[rows], local_sem.at[i]).start()
    events(POINTS - 1)

    for src, place, cond, index in firsts:
        def sent(src=src, place=place, index=index):
            remote(src, place, first_sem.at[index], to["core"]).wait_send()

        if cond is None:
            sent()
        else:
            pl.when(cond)(sent)

    @pl.loop(0, begins[POINTS])
    def _(n):
        src, dst, index, way = decoded(n)

        @pl.when(way != WAIT)
        def _():
            remote(buf.at[src], dst, ssem.at[index], devs[way]).wait_send()

    for i in range(NI):
        rows = pl.ds(i * V, V)
        pltpu.make_async_copy(acc.at[rows], out.at[rows], local_sem.at[i]).wait()


def shards(irrep_dims, chol_vectors, amplitudes):
    bf, sem = jnp.bfloat16, pltpu.SemaphoreType.DMA
    raw = pl.pallas_call(
        kernel,
        out_shape=jax.ShapeDtypeStruct((NI * V, V), jnp.float32),
        in_specs=[
            pl.BlockSpec(memory_space=pltpu.SMEM),
            pl.BlockSpec(memory_space=pl.ANY),
            pl.BlockSpec(memory_space=pl.ANY),
        ],
        out_specs=pl.BlockSpec(memory_space=pl.ANY),
        scratch_shapes=[
            pltpu.VMEM((SLOTS, PV, V), bf),
            pltpu.VMEM((V, NI * V), bf),
            pltpu.VMEM((8, NI * V, 2 * V), bf),
            pltpu.VMEM((NI * V, V), jnp.float32),
            pltpu.SMEM((MOST_OPS,), jnp.int32),
            pltpu.SMEM((POINTS + 1,), jnp.int32),
            pltpu.SMEM((len(WAYS),), jnp.int32),
            sem((MOST_SENDS,)), sem((FIRST_SENDS,)), sem((SLOTS,)), sem((18,)),
        ],
        compiler_params=pltpu.CompilerParams(
            collective_id=0, has_side_effects=True, vmem_limit_bytes=63 * 1024 * 1024
        ),
        cost_estimate=pl.CostEstimate(flops=29_000_000_000, bytes_accessed=12_000_000, transcendentals=0),
        name="ladder",
    )(irrep_dims, chol_vectors.reshape(V, V), amplitudes.reshape(NI, V, V))
    return raw.reshape(1, NI, V, V)


def solution(mesh):
    return jax.shard_map(
        shards,
        mesh=mesh,
        in_specs=(P(), P(("sym", "occ"), "tile", None), P("sym", "occ", "tile", None)),
        out_specs=P("sym", "occ", "tile", None),
        check_vma=False,
    )
```

```python
import jax
import jax.numpy as jnp
from jax import lax
from jax.experimental import pallas as pl
from jax.experimental.pallas import tpu as pltpu
from jax.sharding import PartitionSpec as P

V = 384
NI = 8
PIECES = 2
PV = V // PIECES
HALF = NI * V // 2
CROSSF, OWN, PASS_Z, FWD_Y, PASS_Y, PAR = range(6)
PARTS = {1: 2, 2: 1}
SEQUENCE = (1, 1, 1, 1, 1, 2, 1, 2, 1, 2, 2, 2, 2, 2)
UNITS = (
    (
        ((0, 0, 0), (0, 0, 0), (0, 0, 0), (0, 0, 0), (0, 0, 0), (0, 0, 0), (0, 0, 0), (0, 0, 0), (0, 0, 0), (0, 0, 0), (0, 0, 0), (0, 0, 0), (0, 0, 0), (0, 0, 0), (0, 0, 0), (0, 0, 0)),
        ((0, 1, 0), (0, 1, 0), (0, 1, 0), (0, 1, 0), (0, 1, 0), (0, 1, 0), (0, 1, 0), (0, 1, 0), (0, 1, 0), (0, 1, 0), (0, 1, 0), (0, 1, 0), (0, 1, 0), (0, 1, 0), (0, 1, 0), (0, 1, 0)),
        ((0, 1, 1), (0, 1, 1), (0, 1, 1), (0, 1, 1), (0, 1, 1), (0, 1, 1), (0, 1, 1), (0, 1, 1), (0, 1, 1), (0, 1, 1), (0, 1, 1), (0, 1, 1), (0, 1, 1), (0, 1, 1), (0, 1, 1), (0, 1, 1)),
        ((1, 0, 0), (1, 0, 0), (1, 0, 0), (1, 0, 0), (0, 2, 0), (0, 2, 0), (1, 0, 0), (1, 0, 0), (1, 0, 0), (1, 0, 0), (1, 0, 0), (1, 0, 0), (1, 0, 0), (1, 0, 0), (1, 0, 0), (1, 0, 0)),
        ((0, 2, 0), (0, 2, 0), (0, 2, 0), (0, 2, 0), (1, 0, 0), (1, 0, 0), (0, 2, 0), (1, 0, 1), (0, 2, 0), (0, 2, 0), (0, 2, 0), (0, 2, 0), (0, 2, 0), (0, 2, 0), (0, 2, 0), (0, 2, 0)),
        ((0, 0, 0), (0, 0, 0), (0, 0, 0), (0, 0, 0), (0, 0, 0), (0, 0, 0), (1, 0, 0), (1, 0, 0), (0, 0, 0), (0, 0, 0), (0, 0, 0), (0, 0, 0), (0, 0, 0), (0, 0, 0), (0, 0, 0), (0, 0, 0)),
        ((1, 1, 0), (1, 1, 0), (1, 1, 0), (1, 1, 0), (1, 3, 0), (1, 1, 0), (1, 1, 0), (1, 1, 0), (1, 3, 0), (1, 3, 0), (1, 1, 0), (1, 1, 0), (1, 1, 0), (1, 1, 0), (1, 1, 0), (1, 1, 0)),
        ((1, 0, 0), (1, 0, 0), (1, 0, 0), (1, 0, 0), (0, 1, 0), (1, 0, 0), (0, 0, 0), (0, 0, 0), (1, 0, 0), (1, 0, 0), (1, 0, 0), (1, 0, 0), (1, 0, 0), (1, 0, 0), (1, 0, 0), (1, 0, 0)),
        ((1, 3, 0), (1, 3, 0), (1, 1, 1), (1, 1, 1), (1, 0, 1), (1, 1, 1), (1, 1, 1), (1, 1, 1), (1, 1, 0), (1, 1, 0), (1, 1, 1), (1, 1, 1), (1, 1, 1), (1, 1, 1), (1, 1, 1), (1, 1, 1)),
        ((0, 1, 0), (0, 1, 0), (0, 1, 0), (0, 1, 0), (1, 0, 0), (0, 1, 0), (0, 1, 0), (0, 1, 0), (0, 1, 0), (0, 1, 0), (0, 1, 0), (0, 1, 0), (0, 1, 0), (0, 1, 0), (0, 1, 0), (0, 1, 0)),
        ((1, 1, 0), (1, 1, 0), (0, 3, 0), (0, 3, 0), (1, 1, 0), (1, 1, 0), (1, 1, 0), (1, 1, 0), (1, 1, 0), (1, 1, 0), (1, 1, 0), (1, 1, 0), (1, 1, 0), (1, 1, 0), (1, 1, 0), (1, 1, 0)),
        ((0, 3, 0), (0, 3, 0), (0, 2, 0), (0, 2, 0), (0, 3, 0), (0, 3, 0), (0, 3, 0), (0, 3, 0), (0, 3, 0), (0, 3, 0), (0, 3, 0), (0, 3, 0), (0, 3, 0), (0, 3, 0), (0, 3, 0), (0, 3, 0)),
        ((1, 3, 0), (1, 3, 0), (1, 3, 0), (1, 1, 0), (1, 3, 0), (1, 3, 0), (1, 3, 0), (1, 3, 0), (1, 3, 0), (1, 3, 0), (1, 3, 0), (1, 3, 0), (1, 3, 0), (1, 3, 0), (1, 3, 0), (1, 3, 0)),
        ((0, 2, 0), (0, 2, 0), (1, 1, 0), (1, 3, 0), (0, 2, 0), (0, 2, 0), (0, 2, 0), (0, 2, 0), (0, 2, 0), (0, 2, 0), (0, 2, 0), (0, 2, 0), (0, 2, 0), (0, 2, 0), (0, 2, 0), (0, 2, 0)),
    ),
    (
        ((0, 0, 1), (0, 0, 1), (0, 0, 1), (0, 0, 1), (0, 0, 1), (0, 0, 1), (0, 0, 1), (0, 0, 1), (0, 0, 1), (0, 0, 1), (0, 0, 1), (0, 0, 1), (0, 0, 1), (0, 0, 1), (0, 0, 1), (0, 0, 1)),
        ((0, 3, 0), (0, 3, 0), (0, 3, 0), (0, 3, 0), (0, 3, 0), (0, 3, 0), (0, 3, 0), (0, 3, 0), (0, 3, 0), (0, 3, 0), (0, 3, 0), (0, 3, 0), (0, 3, 0), (0, 3, 0), (0, 3, 0), (0, 3, 0)),
        ((0, 3, 1), (0, 3, 1), (0, 3, 1), (0, 3, 1), (0, 3, 1), (0, 3, 1), (0, 3, 1), (0, 3, 1), (0, 3, 1), (0, 3, 1), (0, 3, 1), (0, 3, 1), (0, 3, 1), (0, 3, 1), (0, 3, 1), (0, 3, 1)),
        ((1, 0, 1), (1, 0, 1), (1, 0, 1), (1, 0, 1), (0, 2, 1), (0, 2, 1), (1, 0, 1), (0, 2, 0), (1, 0, 1), (1, 0, 1), (1, 0, 1), (1, 0, 1), (1, 0, 1), (1, 0, 1), (1, 0, 1), (1, 0, 1)),
        ((0, 2, 1), (0, 2, 1), (0, 2, 1), (0, 2, 1), (1, 1, 0), (1, 0, 1), (0, 2, 1), (0, 2, 1), (0, 2, 1), (0, 2, 1), (0, 2, 1), (0, 2, 1), (0, 2, 1), (0, 2, 1), (0, 2, 1), (0, 2, 1)),
        ((0, 0, 0), (0, 0, 0), (0, 0, 0), (0, 0, 0), (0, 0, 0), (0, 0, 0), (1, 0, 0), (1, 0, 0), (0, 0, 0), (0, 0, 0), (0, 0, 0), (0, 0, 0), (0, 0, 0), (0, 0, 0), (0, 0, 0), (0, 0, 0)),
        ((1, 1, 1), (1, 1, 1), (1, 3, 0), (1, 3, 0), (1, 1, 1), (1, 3, 0), (1, 3, 0), (1, 3, 0), (1, 3, 1), (1, 3, 1), (1, 3, 0), (1, 3, 0), (1, 3, 0), (1, 3, 0), (1, 3, 0), (1, 3, 0)),
        ((1, 0, 0), (1, 0, 0), (1, 0, 0), (1, 0, 0), (0, 1, 0), (1, 0, 0), (0, 0, 0), (0, 0, 0), (1, 0, 0), (1, 0, 0), (1, 0, 0), (1, 0, 0), (1, 0, 0), (1, 0, 0), (1, 0, 0), (1, 0, 0)),
        ((1, 3, 1), (1, 3, 1), (1, 3, 1), (1, 3, 1), (1, 3, 1), (1, 3, 1), (1, 3, 1), (1, 3, 1), (1, 1, 1), (1, 1, 1), (1, 3, 1), (1, 3, 1), (1, 3, 1), (1, 3, 1), (1, 3, 1), (1, 3, 1)),
        ((0, 1, 0), (0, 1, 0), (0, 1, 0), (0, 1, 0), (1, 0, 0), (0, 1, 0), (0, 1, 0), (0, 1, 0), (0, 1, 0), (0, 1, 0), (0, 1, 0), (0, 1, 0), (0, 1, 0), (0, 1, 0), (0, 1, 0), (0, 1, 0)),
        ((1, 1, 0), (1, 1, 0), (0, 3, 0), (0, 3, 0), (1, 1, 0), (1, 1, 0), (1, 1, 0), (1, 1, 0), (1, 1, 0), (1, 1, 0), (1, 1, 0), (1, 1, 0), (1, 1, 0), (1, 1, 0), (1, 1, 0), (1, 1, 0)),
        ((0, 3, 0), (0, 3, 0), (0, 2, 0), (0, 2, 0), (0, 3, 0), (0, 3, 0), (0, 3, 0), (0, 3, 0), (0, 3, 0), (0, 3, 0), (0, 3, 0), (0, 3, 0), (0, 3, 0), (0, 3, 0), (0, 3, 0), (0, 3, 0)),
        ((1, 3, 0), (1, 3, 0), (1, 3, 0), (1, 1, 0), (1, 3, 0), (1, 3, 0), (1, 3, 0), (1, 3, 0), (1, 3, 0), (1, 3, 0), (1, 3, 0), (1, 3, 0), (1, 3, 0), (1, 3, 0), (1, 3, 0), (1, 3, 0)),
        ((0, 2, 0), (0, 2, 0), (1, 1, 0), (1, 3, 0), (0, 2, 0), (0, 2, 0), (0, 2, 0), (0, 2, 0), (0, 2, 0), (0, 2, 0), (0, 2, 0), (0, 2, 0), (0, 2, 0), (0, 2, 0), (0, 2, 0), (0, 2, 0)),
    ),
)
EVENTS = (
    (
        (2, ((CROSSF, 0), (CROSSF, 1), (OWN, 0, 1, 0), (OWN, 0, 3, 0), (PASS_Z, 0, 0), (PASS_Z, 0, 1),)),
        (3, ((OWN, 0, 1, 1), (OWN, 0, 3, 1),)),
        (4, ((OWN, 1, 0, 0), (OWN, 1, 0, 1), (PASS_Z, 1, 0), (PASS_Z, 3, 0),)),
        (5, ((OWN, 0, 2, 0),)),
        (6, ((OWN, 0, 2, 1), (FWD_Y, 0, 0), (FWD_Y, 0, 1),)),
        (8, ((OWN, 1, 1, 0), (PASS_Z, 1, 1), (PASS_Z, 3, 1),)),
        (9, ((PASS_Y, 0, 1),)),
        (10, ((OWN, 1, 1, 1),)),
        (11, ((OWN, 1, 3, 0), (FWD_Y, 1, 0), (FWD_Y, 3, 0),)),
        (12, ((OWN, 1, 2, 1), (PASS_Z, 2, 0), (PASS_Z, 2, 1),)),
        (13, ((OWN, 1, 2, 0),)),
        (14, ((FWD_Y, 1, 1), (FWD_Y, 3, 1), (PASS_Y, 1, 0), (OWN, 1, 3, 1),)),
        (15, ((FWD_Y, 2, 0), (FWD_Y, 2, 1),)),
        (17, ((PASS_Y, 3, 1),)),
        (18, ((PASS_Y, 2, 0),)),
    ),
    (
        (2, ((CROSSF, 0), (CROSSF, 1), (OWN, 0, 1, 0), (OWN, 0, 3, 0), (PASS_Z, 0, 0), (PASS_Z, 0, 1),)),
        (3, ((OWN, 0, 1, 1), (OWN, 0, 3, 1),)),
        (4, ((OWN, 1, 0, 0), (OWN, 1, 0, 1), (PASS_Z, 1, 0), (PASS_Z, 3, 0),)),
        (5, ((OWN, 0, 2, 0),)),
        (6, ((OWN, 0, 2, 1), (FWD_Y, 0, 0), (FWD_Y, 0, 1),)),
        (8, ((OWN, 1, 1, 0), (PASS_Z, 1, 1), (PASS_Z, 3, 1),)),
        (9, ((PASS_Y, 0, 0),)),
        (10, ((OWN, 1, 1, 1),)),
        (11, ((OWN, 1, 3, 0), (FWD_Y, 1, 0), (FWD_Y, 3, 0),)),
        (12, ((OWN, 1, 2, 1), (PASS_Z, 2, 0), (PASS_Z, 2, 1),)),
        (13, ((OWN, 1, 3, 1),)),
        (14, ((OWN, 1, 2, 0), (FWD_Y, 1, 1), (FWD_Y, 3, 1), (PASS_Y, 3, 0),)),
        (16, ((FWD_Y, 2, 0), (FWD_Y, 2, 1),)),
        (17, ((PASS_Y, 1, 1),)),
        (18, ((PASS_Y, 2, 1),)),
    ),
    (
        (2, ((CROSSF, 0), (CROSSF, 1), (OWN, 0, 1, 0), (OWN, 0, 3, 0), (PASS_Z, 0, 0), (PASS_Z, 0, 1),)),
        (3, ((OWN, 0, 1, 1), (OWN, 0, 3, 1),)),
        (4, ((OWN, 1, 0, 0), (OWN, 1, 0, 1), (PASS_Z, 1, 0), (PASS_Z, 3, 0),)),
        (5, ((OWN, 0, 2, 0),)),
        (6, ((OWN, 0, 2, 1), (PAR, 0, 0, 0), (PAR, 0, 0, 1),)),
        (8, ((OWN, 1, 1, 0), (OWN, 1, 3, 0), (PASS_Z, 1, 1), (PASS_Z, 3, 1),)),
        (9, ((PASS_Y, 0, 0),)),
        (10, ((OWN, 1, 1, 1),)),
        (11, ((OWN, 1, 3, 1), (PAR, 0, 1, 0), (PAR, 0, 3, 0),)),
        (12, ((OWN, 1, 2, 0), (OWN, 1, 2, 1), (PASS_Z, 2, 0), (PASS_Z, 2, 1), (PAR, 1, 0, 0), (PAR, 1, 0, 1),)),
        (13, ((PAR, 0, 3, 1), (PAR, 0, 1, 1),)),
        (14, ((PASS_Y, 3, 0),)),
        (15, ((PAR, 0, 2, 0), (PAR, 0, 2, 1),)),
        (17, ((PASS_Y, 1, 1), (PAR, 1, 1, 0),)),
        (18, ((PAR, 1, 3, 0),)),
        (19, ((PASS_Y, 2, 1), (PAR, 1, 3, 1),)),
        (20, ((PAR, 1, 1, 1), (PAR, 1, 2, 0),)),
        (21, ((PAR, 1, 2, 1),)),
    ),
    (
        (2, ((CROSSF, 0), (CROSSF, 1), (OWN, 0, 1, 0), (OWN, 0, 3, 0), (PASS_Z, 0, 0), (PASS_Z, 0, 1),)),
        (3, ((OWN, 0, 1, 1), (OWN, 0, 3, 1),)),
        (4, ((OWN, 1, 0, 0), (OWN, 1, 0, 1), (PASS_Z, 1, 0), (PASS_Z, 3, 0),)),
        (5, ((OWN, 0, 2, 0),)),
        (6, ((OWN, 0, 2, 1), (PAR, 0, 0, 0), (PAR, 0, 0, 1),)),
        (8, ((OWN, 1, 1, 0), (OWN, 1, 3, 0), (PASS_Z, 1, 1), (PASS_Z, 3, 1),)),
        (9, ((PASS_Y, 0, 1),)),
        (10, ((OWN, 1, 1, 1),)),
        (11, ((OWN, 1, 3, 1), (PAR, 0, 1, 0), (PAR, 0, 3, 0),)),
        (12, ((OWN, 1, 2, 0), (OWN, 1, 2, 1), (PASS_Z, 2, 0), (PASS_Z, 2, 1), (PAR, 1, 0, 0), (PAR, 1, 0, 1),)),
        (13, ((PAR, 0, 3, 1), (PAR, 0, 1, 1),)),
        (14, ((PASS_Y, 1, 0),)),
        (15, ((PAR, 0, 2, 0), (PAR, 0, 2, 1),)),
        (17, ((PASS_Y, 3, 1), (PAR, 1, 3, 0),)),
        (18, ((PAR, 1, 1, 0),)),
        (19, ((PASS_Y, 2, 0), (PAR, 1, 1, 1),)),
        (20, ((PAR, 1, 3, 1), (PAR, 1, 2, 1),)),
        (21, ((PAR, 1, 2, 0),)),
    ),
    (
        (2, ((CROSSF, 0), (OWN, 0, 1, 0), (OWN, 0, 3, 0), (PASS_Z, 0, 0), (PASS_Z, 0, 1), (PAR, 0, 0, 0),)),
        (3, ((CROSSF, 1), (OWN, 0, 1, 1), (OWN, 0, 3, 1), (PAR, 1, 0, 0),)),
        (4, ((PASS_Z, 1, 0), (PASS_Z, 3, 0),)),
        (5, ((OWN, 0, 2, 0), (PAR, 0, 0, 1), (PAR, 1, 0, 1),)),
        (6, ((OWN, 0, 2, 1), (FWD_Y, 0, 0), (FWD_Y, 0, 1),)),
        (7, ((OWN, 1, 0, 0), (OWN, 1, 1, 0), (PAR, 0, 1, 0),)),
        (8, ((OWN, 1, 3, 0), (PASS_Z, 1, 1), (PASS_Z, 3, 1),)),
        (9, ((OWN, 1, 1, 1), (PAR, 0, 3, 0), (PAR, 1, 1, 0),)),
        (10, ((OWN, 1, 3, 1), (FWD_Y, 1, 0), (FWD_Y, 3, 0),)),
        (11, ((OWN, 1, 0, 1), (OWN, 1, 2, 0), (PASS_Z, 2, 0), (PASS_Z, 2, 1), (PAR, 1, 3, 0),)),
        (12, ((OWN, 1, 2, 1), (PAR, 0, 1, 1), (PAR, 1, 1, 1),)),
        (13, ((FWD_Y, 1, 1), (FWD_Y, 3, 1),)),
        (14, ((FWD_Y, 2, 0), (PAR, 0, 3, 1), (PAR, 1, 3, 1),)),
        (15, ((FWD_Y, 2, 1),)),
        (16, ((PAR, 0, 2, 0), (PAR, 1, 2, 0),)),
        (17, ((PAR, 0, 2, 1), (PAR, 1, 2, 1),)),
    ),
    (
        (2, ((CROSSF, 0), (OWN, 0, 1, 0), (OWN, 0, 3, 0), (PASS_Z, 0, 0), (PASS_Z, 0, 1), (PAR, 1, 0, 0),)),
        (3, ((CROSSF, 1), (OWN, 0, 1, 1), (OWN, 0, 3, 1), (PAR, 0, 0, 0),)),
        (4, ((PASS_Z, 1, 0), (PASS_Z, 3, 0),)),
        (5, ((OWN, 0, 2, 0), (PAR, 0, 0, 1), (PAR, 1, 0, 1),)),
        (6, ((OWN, 0, 2, 1), (FWD_Y, 0, 0), (FWD_Y, 0, 1),)),
        (7, ((OWN, 1, 0, 0), (OWN, 1, 0, 1), (OWN, 1, 1, 0),)),
        (8, ((OWN, 1, 3, 0), (PASS_Z, 1, 1), (PASS_Z, 3, 1),)),
        (9, ((OWN, 1, 1, 1), (PAR, 0, 1, 0), (PAR, 1, 1, 0),)),
        (10, ((OWN, 1, 3, 1), (FWD_Y, 1, 0), (FWD_Y, 3, 0),)),
        (11, ((OWN, 1, 2, 0), (OWN, 1, 2, 1), (PASS_Z, 2, 0), (PASS_Z, 2, 1), (PAR, 0, 3, 0), (PAR, 1, 3, 0),)),
        (12, ((PAR, 0, 1, 1), (PAR, 1, 1, 1),)),
        (13, ((FWD_Y, 1, 1), (FWD_Y, 3, 1),)),
        (14, ((FWD_Y, 2, 0), (FWD_Y, 2, 1), (PAR, 0, 3, 1), (PAR, 1, 3, 1),)),
        (16, ((PAR, 0, 2, 0), (PAR, 1, 2, 0),)),
        (17, ((PAR, 0, 2, 1), (PAR, 1, 2, 1),)),
    ),
    (
        (2, ((CROSSF, 0), (CROSSF, 1), (OWN, 0, 1, 0), (OWN, 0, 3, 0), (PASS_Z, 0, 0), (PASS_Z, 0, 1),)),
        (3, ((OWN, 0, 1, 1), (OWN, 0, 3, 1),)),
        (4, ((OWN, 1, 0, 0), (OWN, 1, 0, 1), (PASS_Z, 1, 0), (PASS_Z, 3, 0),)),
        (5, ((OWN, 0, 2, 0),)),
        (6, ((OWN, 0, 2, 1), (FWD_Y, 0, 0), (FWD_Y, 0, 1),)),
        (7, ((OWN, 1, 1, 0),)),
        (8, ((OWN, 1, 3, 0), (PASS_Z, 1, 1), (PASS_Z, 3, 1),)),
        (9, ((OWN, 1, 1, 1), (PAR, 0, 0, 0), (PAR, 1, 0, 0),)),
        (10, ((OWN, 1, 3, 1), (FWD_Y, 1, 0), (FWD_Y, 3, 0), (PAR, 1, 0, 1), (PAR, 0, 0, 1),)),
        (11, ((OWN, 1, 2, 0), (OWN, 1, 2, 1), (PASS_Z, 2, 0), (PASS_Z, 2, 1), (PAR, 0, 1, 0),)),
        (12, ((FWD_Y, 1, 1), (FWD_Y, 3, 1), (PAR, 1, 1, 0),)),
        (13, ((PAR, 0, 3, 0),)),
        (14, ((FWD_Y, 2, 0), (FWD_Y, 2, 1), (PAR, 1, 3, 0),)),
        (15, ((PAR, 0, 1, 1), (PAR, 1, 1, 1),)),
        (17, ((PAR, 0, 3, 1), (PAR, 1, 3, 1),)),
        (18, ((PAR, 0, 2, 0), (PAR, 1, 2, 0),)),
        (19, ((PAR, 0, 2, 1),)),
        (20, ((PAR, 1, 2, 1),)),
    ),
    (
        (2, ((CROSSF, 0), (CROSSF, 1), (OWN, 0, 1, 0), (OWN, 0, 3, 0), (PASS_Z, 0, 0), (PASS_Z, 0, 1),)),
        (3, ((OWN, 0, 1, 1), (OWN, 0, 3, 1),)),
        (4, ((OWN, 1, 0, 0), (PASS_Z, 1, 0), (PASS_Z, 3, 0),)),
        (5, ((OWN, 0, 2, 0),)),
        (6, ((OWN, 0, 2, 1), (OWN, 1, 0, 1), (FWD_Y, 0, 0), (FWD_Y, 0, 1),)),
        (7, ((OWN, 1, 1, 0),)),
        (8, ((OWN, 1, 3, 0), (PASS_Z, 1, 1), (PASS_Z, 3, 1),)),
        (9, ((OWN, 1, 1, 1), (PAR, 0, 0, 0), (PAR, 1, 0, 0),)),
        (10, ((OWN, 1, 3, 1), (FWD_Y, 1, 0), (FWD_Y, 3, 0), (PAR, 1, 0, 1), (PAR, 0, 0, 1),)),
        (11, ((OWN, 1, 2, 0), (OWN, 1, 2, 1), (PASS_Z, 2, 0), (PASS_Z, 2, 1), (PAR, 0, 1, 0),)),
        (12, ((FWD_Y, 1, 1), (FWD_Y, 3, 1), (PAR, 1, 1, 0),)),
        (13, ((PAR, 0, 3, 0),)),
        (14, ((FWD_Y, 2, 0), (FWD_Y, 2, 1), (PAR, 1, 3, 0),)),
        (15, ((PAR, 0, 1, 1), (PAR, 1, 1, 1),)),
        (17, ((PAR, 0, 3, 1), (PAR, 1, 3, 1),)),
        (18, ((PAR, 0, 2, 0), (PAR, 1, 2, 0),)),
        (19, ((PAR, 0, 2, 1),)),
        (20, ((PAR, 1, 2, 1),)),
    ),
    (
        (2, ((CROSSF, 0), (CROSSF, 1), (OWN, 0, 1, 0), (OWN, 0, 3, 0), (FWD_Y, 0, 0), (PAR, 0, 0, 0),)),
        (3, ((OWN, 0, 1, 1), (OWN, 0, 3, 1), (FWD_Y, 0, 1), (PAR, 0, 0, 1),)),
        (4, ((OWN, 1, 0, 0), (OWN, 1, 0, 1),)),
        (5, ((OWN, 0, 2, 0), (FWD_Y, 1, 0), (PAR, 0, 1, 0),)),
        (6, ((OWN, 0, 2, 1), (PASS_Y, 0, 0), (PASS_Y, 0, 1),)),
        (7, ((FWD_Y, 3, 0), (PAR, 0, 3, 0),)),
        (8, ((OWN, 1, 3, 0), (PASS_Y, 1, 0),)),
        (9, ((FWD_Y, 1, 1), (PAR, 0, 1, 1), (PAR, 1, 0, 0),)),
        (10, ((OWN, 1, 3, 1), (PAR, 1, 0, 1),)),
        (11, ((OWN, 1, 1, 0), (FWD_Y, 3, 1), (PASS_Y, 3, 0), (PAR, 0, 3, 1),)),
        (12, ((OWN, 1, 2, 0), (OWN, 1, 2, 1), (PAR, 1, 1, 0),)),
        (13, ((FWD_Y, 2, 0), (PASS_Y, 1, 1), (PAR, 0, 2, 0),)),
        (14, ((OWN, 1, 1, 1), (FWD_Y, 2, 1), (PASS_Y, 3, 1), (PAR, 0, 2, 1), (PAR, 1, 3, 0),)),
        (15, ((PASS_Y, 2, 0),)),
        (16, ((PAR, 1, 1, 1),)),
        (17, ((PASS_Y, 2, 1), (PAR, 1, 3, 1),)),
        (18, ((PAR, 1, 2, 0),)),
        (20, ((PAR, 1, 2, 1),)),
    ),
    (
        (2, ((CROSSF, 0), (CROSSF, 1), (OWN, 0, 1, 0), (OWN, 0, 3, 0), (FWD_Y, 0, 0), (PAR, 0, 0, 0),)),
        (3, ((OWN, 0, 1, 1), (OWN, 0, 3, 1), (FWD_Y, 0, 1), (PAR, 0, 0, 1),)),
        (4, ((OWN, 1, 0, 0), (OWN, 1, 0, 1),)),
        (5, ((OWN, 0, 2, 0), (FWD_Y, 1, 0), (PAR, 0, 1, 0),)),
        (6, ((OWN, 0, 2, 1), (PASS_Y, 0, 0), (PASS_Y, 0, 1),)),
        (7, ((FWD_Y, 3, 0), (PAR, 0, 3, 0),)),
        (8, ((OWN, 1, 3, 0), (PASS_Y, 1, 0),)),
        (9, ((FWD_Y, 1, 1), (PAR, 0, 1, 1), (PAR, 1, 0, 0),)),
        (10, ((OWN, 1, 3, 1), (PAR, 1, 0, 1),)),
        (11, ((OWN, 1, 1, 0), (FWD_Y, 3, 1), (PASS_Y, 3, 0), (PAR, 0, 3, 1),)),
        (12, ((OWN, 1, 1, 1), (OWN, 1, 2, 0), (PAR, 1, 1, 0),)),
        (13, ((FWD_Y, 2, 0), (PASS_Y, 1, 1), (PAR, 0, 2, 0),)),
        (14, ((OWN, 1, 2, 1), (FWD_Y, 2, 1), (PASS_Y, 3, 1), (PAR, 0, 2, 1), (PAR, 1, 3, 0),)),
        (16, ((PASS_Y, 2, 0), (PAR, 1, 1, 1),)),
        (17, ((PAR, 1, 3, 1),)),
        (18, ((PASS_Y, 2, 1),)),
        (19, ((PAR, 1, 2, 0),)),
        (20, ((PAR, 1, 2, 1),)),
    ),
    (
        (2, ((CROSSF, 0), (CROSSF, 1), (OWN, 0, 1, 0), (OWN, 0, 3, 0), (FWD_Y, 0, 0), (PAR, 0, 0, 0),)),
        (3, ((OWN, 0, 1, 1), (OWN, 0, 3, 1), (FWD_Y, 0, 1), (PAR, 0, 0, 1),)),
        (4, ((OWN, 1, 0, 0), (OWN, 1, 0, 1),)),
        (5, ((OWN, 0, 2, 0), (FWD_Y, 1, 0), (PAR, 0, 1, 0),)),
        (6, ((OWN, 0, 2, 1), (PASS_Y, 0, 0), (PASS_Y, 0, 1),)),
        (7, ((OWN, 1, 1, 0), (FWD_Y, 3, 0), (PAR, 0, 3, 0),)),
        (8, ((OWN, 1, 3, 0), (PASS_Y, 1, 0),)),
        (9, ((OWN, 1, 1, 1), (FWD_Y, 1, 1), (PAR, 0, 1, 1), (PAR, 1, 0, 0),)),
        (10, ((OWN, 1, 3, 1), (PAR, 1, 0, 1),)),
        (11, ((OWN, 1, 2, 1), (FWD_Y, 3, 1), (PASS_Y, 3, 0), (PAR, 0, 3, 1),)),
        (12, ((OWN, 1, 2, 0), (PAR, 1, 1, 0),)),
        (13, ((FWD_Y, 2, 0), (PASS_Y, 1, 1), (PAR, 0, 2, 0),)),
        (14, ((FWD_Y, 2, 1), (PASS_Y, 3, 1), (PAR, 0, 2, 1), (PAR, 1, 3, 0),)),
        (16, ((PASS_Y, 2, 0), (PAR, 1, 1, 1),)),
        (17, ((PAR, 1, 3, 1),)),
        (18, ((PASS_Y, 2, 1),)),
        (19, ((PAR, 1, 2, 0),)),
        (20, ((PAR, 1, 2, 1),)),
    ),
    (
        (2, ((CROSSF, 0), (CROSSF, 1), (OWN, 0, 1, 0), (OWN, 0, 3, 0), (FWD_Y, 0, 0), (PAR, 0, 0, 0),)),
        (3, ((OWN, 0, 1, 1), (OWN, 0, 3, 1), (FWD_Y, 0, 1), (PAR, 0, 0, 1),)),
        (4, ((OWN, 1, 0, 0), (OWN, 1, 0, 1),)),
        (5, ((OWN, 0, 2, 0), (FWD_Y, 1, 0), (PAR, 0, 1, 0),)),
        (6, ((OWN, 0, 2, 1), (PASS_Y, 0, 0), (PASS_Y, 0, 1),)),
        (7, ((OWN, 1, 1, 0), (FWD_Y, 3, 0), (PAR, 0, 3, 0),)),
        (8, ((OWN, 1, 3, 0), (PASS_Y, 1, 0),)),
        (9, ((OWN, 1, 1, 1), (FWD_Y, 1, 1), (PAR, 0, 1, 1), (PAR, 1, 0, 0),)),
        (10, ((OWN, 1, 3, 1), (PAR, 1, 0, 1),)),
        (11, ((OWN, 1, 2, 1), (FWD_Y, 3, 1), (PASS_Y, 3, 0), (PAR, 0, 3, 1),)),
        (12, ((OWN, 1, 2, 0), (PAR, 1, 1, 0),)),
        (13, ((FWD_Y, 2, 0), (PASS_Y, 1, 1), (PAR, 0, 2, 0),)),
        (14, ((FWD_Y, 2, 1), (PASS_Y, 3, 1), (PAR, 0, 2, 1), (PAR, 1, 3, 0),)),
        (16, ((PASS_Y, 2, 0), (PAR, 1, 1, 1),)),
        (17, ((PAR, 1, 3, 1),)),
        (18, ((PASS_Y, 2, 1),)),
        (19, ((PAR, 1, 2, 0),)),
        (20, ((PAR, 1, 2, 1),)),
    ),
    (
        (2, ((CROSSF, 0), (CROSSF, 1), (OWN, 0, 1, 0), (OWN, 0, 3, 0), (FWD_Y, 0, 0),)),
        (3, ((OWN, 0, 1, 1), (OWN, 0, 3, 1), (FWD_Y, 0, 1),)),
        (4, ((OWN, 1, 0, 0), (OWN, 1, 0, 1),)),
        (5, ((OWN, 0, 2, 0), (FWD_Y, 1, 0),)),
        (6, ((OWN, 0, 2, 1), (PAR, 0, 0, 0), (PAR, 1, 0, 0),)),
        (7, ((OWN, 1, 1, 0), (FWD_Y, 3, 0),)),
        (8, ((OWN, 1, 3, 0), (PAR, 0, 0, 1), (PAR, 1, 0, 1),)),
        (9, ((OWN, 1, 1, 1), (FWD_Y, 1, 1),)),
        (10, ((OWN, 1, 3, 1), (PAR, 0, 1, 0), (PAR, 1, 1, 0),)),
        (11, ((FWD_Y, 3, 1),)),
        (12, ((PAR, 0, 3, 0), (PAR, 1, 3, 0),)),
        (13, ((FWD_Y, 2, 0),)),
        (14, ((OWN, 1, 2, 0), (FWD_Y, 2, 1), (PAR, 0, 1, 1), (PAR, 1, 1, 1),)),
        (15, ((PAR, 0, 3, 1), (PAR, 1, 3, 1),)),
        (17, ((OWN, 1, 2, 1), (PAR, 0, 2, 0), (PAR, 1, 2, 0),)),
        (18, ((PAR, 0, 2, 1), (PAR, 1, 2, 1),)),
    ),
    (
        (2, ((CROSSF, 0), (CROSSF, 1), (OWN, 0, 1, 0), (OWN, 0, 3, 0), (FWD_Y, 0, 0),)),
        (3, ((OWN, 0, 1, 1), (OWN, 0, 3, 1), (FWD_Y, 0, 1),)),
        (4, ((OWN, 1, 0, 0), (OWN, 1, 0, 1),)),
        (5, ((OWN, 0, 2, 0), (FWD_Y, 1, 0),)),
        (6, ((OWN, 0, 2, 1), (PAR, 0, 0, 0), (PAR, 1, 0, 0),)),
        (7, ((OWN, 1, 1, 0), (FWD_Y, 3, 0),)),
        (8, ((OWN, 1, 3, 0), (PAR, 0, 0, 1), (PAR, 1, 0, 1),)),
        (9, ((OWN, 1, 1, 1), (FWD_Y, 1, 1),)),
        (10, ((OWN, 1, 3, 1), (PAR, 0, 1, 0), (PAR, 1, 1, 0),)),
        (11, ((FWD_Y, 3, 1),)),
        (12, ((PAR, 0, 3, 0), (PAR, 1, 3, 0),)),
        (13, ((FWD_Y, 2, 0),)),
        (14, ((OWN, 1, 2, 0), (FWD_Y, 2, 1), (PAR, 0, 1, 1), (PAR, 1, 1, 1),)),
        (15, ((OWN, 1, 2, 1), (PAR, 0, 3, 1), (PAR, 1, 3, 1),)),
        (17, ((PAR, 0, 2, 0), (PAR, 1, 2, 0),)),
        (18, ((PAR, 0, 2, 1), (PAR, 1, 2, 1),)),
    ),
    (
        (2, ((CROSSF, 0), (CROSSF, 1), (OWN, 0, 1, 0), (OWN, 0, 3, 0), (FWD_Y, 0, 0),)),
        (3, ((OWN, 0, 1, 1), (OWN, 0, 3, 1), (FWD_Y, 0, 1),)),
        (4, ((OWN, 1, 0, 0), (OWN, 1, 0, 1),)),
        (5, ((OWN, 0, 2, 0), (FWD_Y, 1, 0),)),
        (6, ((OWN, 0, 2, 1), (PAR, 0, 0, 0), (PAR, 1, 0, 0),)),
        (7, ((OWN, 1, 1, 0), (FWD_Y, 3, 0),)),
        (8, ((OWN, 1, 3, 0), (PAR, 0, 0, 1), (PAR, 1, 0, 1),)),
        (9, ((OWN, 1, 1, 1), (FWD_Y, 1, 1),)),
        (10, ((OWN, 1, 3, 1), (PAR, 0, 1, 0), (PAR, 1, 1, 0),)),
        (11, ((OWN, 1, 2, 1), (FWD_Y, 3, 1),)),
        (12, ((OWN, 1, 2, 0), (PAR, 0, 3, 0), (PAR, 1, 3, 0),)),
        (13, ((FWD_Y, 2, 0),)),
        (14, ((FWD_Y, 2, 1), (PAR, 0, 1, 1), (PAR, 1, 1, 1),)),
        (15, ((PAR, 0, 3, 1), (PAR, 1, 3, 1),)),
        (17, ((PAR, 0, 2, 0), (PAR, 1, 2, 0),)),
        (18, ((PAR, 0, 2, 1), (PAR, 1, 2, 1),)),
    ),
    (
        (2, ((CROSSF, 0), (CROSSF, 1), (OWN, 0, 1, 0), (OWN, 0, 3, 0), (FWD_Y, 0, 0),)),
        (3, ((OWN, 0, 1, 1), (OWN, 0, 3, 1), (FWD_Y, 0, 1),)),
        (4, ((OWN, 1, 0, 0), (OWN, 1, 0, 1),)),
        (5, ((OWN, 0, 2, 0), (FWD_Y, 1, 0),)),
        (6, ((OWN, 0, 2, 1), (PAR, 0, 0, 0), (PAR, 1, 0, 0),)),
        (7, ((OWN, 1, 1, 0), (FWD_Y, 3, 0),)),
        (8, ((OWN, 1, 3, 0), (PAR, 0, 0, 1), (PAR, 1, 0, 1),)),
        (9, ((OWN, 1, 1, 1), (FWD_Y, 1, 1),)),
        (10, ((OWN, 1, 3, 1), (PAR, 0, 1, 0), (PAR, 1, 1, 0),)),
        (11, ((OWN, 1, 2, 1), (FWD_Y, 3, 1),)),
        (12, ((OWN, 1, 2, 0), (PAR, 0, 3, 0), (PAR, 1, 3, 0),)),
        (13, ((FWD_Y, 2, 0),)),
        (14, ((FWD_Y, 2, 1), (PAR, 0, 1, 1), (PAR, 1, 1, 1),)),
        (15, ((PAR, 0, 3, 1), (PAR, 1, 3, 1),)),
        (17, ((PAR, 0, 2, 0), (PAR, 1, 2, 0),)),
        (18, ((PAR, 0, 2, 1), (PAR, 1, 2, 1),)),
    ),
)

STAGES = len(SEQUENCE)
BASES = [sum(PARTS[stage] for stage in SEQUENCE[:n]) for n in range(STAGES + 1)]
POINTS = BASES[-1] + 1
PAR_AT, T1_AT, T2_AT, T3_AT, TC_AT, SLOTS = 32, 64, 72, 80, 88, 90
WAYS = ("x+", "x-", "y+", "y-", "z+", "z-", "core", "ya", "yb", "za", "zb")
WAIT = 15
CLASSES = [(x, y) for x in range(4) for y in range(4)]


def sign_of(j, k):
    return "+" if (k + (0, 1, 1, 0)[j]) % 2 == 0 else "-"


def name_of(x, y, row, j):
    return (y // 2 + row) % 2 * 4 + (x + 4 - j) % 4


def row_behind(y, sign):
    return (y + 3) % 4 // 2 if sign == "+" else (y + 1) % 4 // 2


def feed(x, y, j, k, src):
    up = y // 2 == 1
    final, via1, via2 = ("par", name_of(x, y, 0, j), k), ("t1", j, k), ("t2", j, k)
    sends = []
    if x in (0, 1):
        sends.append((src, via1, "z" + sign_of(j, k)))
    if x == 1:
        sends.append((src, final, "ya"))
    if x in (2, 3):
        sends.append((src, final if x == 2 and not up else via1, "za"))
        sends.append((src, final if x == 2 and up else via2, "zb"))
    return sends


def expand(x, y, event):
    kind, args = event[0], event[1:]
    up = y // 2 == 1
    ops = []
    if kind == CROSSF:
        (k,) = args
        sign = "+-"[k]
        ops = [("tc", k), (("tc", k), ("own", row_behind(y, sign) * 4 + x, k), "y" + sign)]
    if kind == OWN:
        row, j, k = args
        here = ("own", name_of(x, y, row, j), k)
        ops = [here]
        if (row, j) == (1, 0) or (j == 1 and (k + row) % 2 == 0):
            ops.append((here, here, "x+"))
        if (row, j) == (1, 0) or (j == 3 and (k + row) % 2 == 1):
            ops.append((here, here, "x-"))
        if row == 0:
            ops += feed(x, y, j, k, here)
        ops.append((here, here, "core"))
    if kind == PASS_Z:
        j, k = args
        here = ("t1", j, k)
        there = ("par", name_of(x, y, 0, j), k) if x == 0 and up else ("t2", j, k)
        ops = [here, (here, there, "z" + sign_of(j, k))]
    if kind == FWD_Y:
        j, k = args
        final, there, way = ("par", name_of(x, y, 0, j), k), ("t3", j, k), "y" + sign_of(j, k)
        if x == 3 or (x == 2 and up):
            ops += [("t1", j, k), (("t1", j, k), final, "ya") if x == 3 else (("t1", j, k), there, way)]
        if x in (1, 3) or not up:
            ops += [("t2", j, k), (("t2", j, k), final, "yb") if x in (1, 3) else (("t2", j, k), there, way)]
    if kind == PASS_Y:
        j, k = args
        sign = sign_of(j, k)
        row = row_behind(y, sign)
        if x == 2 or row == 0:
            ops = [("t3", j, k), (("t3", j, k), ("par", row * 4 + (x + 4 - j) % 4, k), "y" + sign)]
    if kind == PAR:
        row, j, k = args
        here = ("par", name_of(x, y, row, j), k)
        ops = [here, (here, here, "core")]
    return ops


def slot(place, c):
    kind, rest = place[0], place[1:]
    if kind in ("own", "par"):
        q, k = rest
        return (PAR_AT if kind == "par" else 0) + q * 4 + c * 2 + k
    if kind == "tc":
        return TC_AT + rest[0]
    return {"t1": T1_AT, "t2": T2_AT, "t3": T3_AT}[kind] + rest[0] * 2 + rest[1]


def tables(x, y):
    per_core = []
    for c in range(2):
        ops, begins, sends, at = [], [], 0, dict(EVENTS[CLASSES.index((x, y))])
        for point in range(POINTS):
            begins.append(len(ops))
            for event in at.get(point, ()):
                for op in expand(x, y, event):
                    if isinstance(op[0], str):
                        ops.append(slot(op, c) + 2097152 * WAIT)
                    else:
                        src, dst, way = op
                        ops.append(slot(src, c) + 128 * slot(dst, c) + 16384 * sends + 2097152 * WAYS.index(way))
                        sends += 1
        per_core.append((ops, begins + [len(ops)], sends))
    return per_core


TABLES = {cls: tables(*cls) for cls in CLASSES}
MOST_OPS = max(len(ops) for cores in TABLES.values() for ops, _, _ in cores)
MOST_SENDS = max(sends for cores in TABLES.values() for _, _, sends in cores)
FIRST_SENDS = 12


def columns(t):
    first, last = t * 256, (t + 1) * 256
    cuts = [first] + [cut for cut in range(0, NI * V, V) if first < cut < last] + [last]
    return [(u - first, w - first, u // V, u % V) for u, w in zip(cuts, cuts[1:])]


def kernel(dims, mine, amps, out, out_own, out_par, buf, rc, half, acc, ops, begins, devs,
           ssem, first_sem, rsem, local_sem):
    sym, tile, c = lax.axis_index("sym"), lax.axis_index("tile"), lax.axis_index("occ")
    x, yhi = sym % 4, sym // 4
    x0, x1 = x % 2, x // 2
    z, ylo = tile // 2, tile % 2
    z0, z1 = z % 2, z // 2
    y = 2 * yhi + ylo
    none = sym == 0

    def dev(dx=0, dy=0, dz=0, dc=0):
        xx, yy, zz = (x + 4 + dx) % 4, (y + 4 + dy) % 4, (z + 4 + dz) % 4
        return ((yy // 2) * 4 + xx) * 16 + (zz * 2 + yy % 2) * 2 + (c + dc) % 2

    step_a = 1 - 2 * (yhi + ylo - 2 * yhi * ylo)
    step_z = 1 - 2 * z0
    to = {
        "x+": dev(dx=1), "x-": dev(dx=-1), "y+": dev(dy=1), "y-": dev(dy=-1), "z+": dev(dz=1), "z-": dev(dz=-1),
        "core": dev(dc=1), "ya": dev(dy=step_a), "yb": dev(dy=-step_a), "za": dev(dz=step_z), "zb": dev(dz=-step_z),
    }
    barrier = pltpu.get_barrier_semaphore()
    for way in WAYS[:7]:
        pl.semaphore_signal(barrier, inc=1, device_id=to[way], device_id_type=pl.DeviceIdType.LOGICAL)

    def own_slot(q, core, k):
        return q * 4 + core * 2 + k

    keep = []
    for k in range(PIECES):
        keep.append(pltpu.make_async_copy(mine.at[pl.ds(k * PV, PV)], buf.at[own_slot(sym, c, k)], local_sem.at[8 + k]))
        keep[-1].start()
    loads = [pltpu.make_async_copy(amps.at[i], rc.at[:, pl.ds(i * V, V)], local_sem.at[i]) for i in range(NI)]
    for load in loads:
        load.start()

    pl.semaphore_wait(barrier, 7)

    def remote(src, dst_slot, sem, where):
        return pltpu.make_async_remote_copy(
            src, buf.at[dst_slot], sem, rsem.at[dst_slot], device_id=where, device_id_type=pl.DeviceIdType.LOGICAL
        )

    def arrived(at):
        remote(buf.at[at], at, first_sem.at[0], to["core"]).wait_recv()

    firsts = []

    def first(src, place, where, cond=None):
        index = len(firsts)
        if cond is None:
            remote(src, place, first_sem.at[index], where).start()
        else:
            pl.when(cond)(lambda: remote(src, place, first_sem.at[index], where).start())
        firsts.append((src, place, cond, index))

    step_2 = {k: {"+": to["z+"], "-": to["z-"]}[sign_of(0, k)] for k in range(PIECES)}
    for k in range(PIECES):
        src = mine.at[pl.ds(k * PV, PV)]
        home = own_slot(sym, c, k)
        final, via1, via2 = PAR_AT + home, T1_AT + k, T2_AT + k
        first(src, home, to["core"])
        first(src, home, to["x+"])
        first(src, home, to["x-"])
        first(src, TC_AT + k, to["y" + "+-"[k]])
        direct_b, direct_a = x0 + 2 * (1 - x1) + (1 - yhi) == 0, x0 + 2 * (1 - x1) + yhi == 0
        where_b = x1 * to["zb"] + (1 - x1) * step_2[k]
        place_b = jnp.where(direct_b, final, x1 * via2 + (1 - x1) * via1)
        first(src, place_b, where_b)
        where_a = x1 * to["za"] + (1 - x1) * to["ya"]
        place_a = jnp.where(direct_a | (x1 == 0), final, via1)
        first(src, place_a, where_a, x > 0)

    for (at_x, at_y), cores in TABLES.items():
        @pl.when((x == at_x) & (y == at_y))
        def _():
            (ops0, begins0, _), (ops1, _, _) = cores
            for n, (op0, op1) in enumerate(zip(ops0, ops1)):
                ops[n] = op0 + (op1 - op0) * c if op0 != op1 else op0
            for n, begin in enumerate(begins0):
                begins[n] = begin
    for n, way in enumerate(WAYS):
        devs[n] = to[way]

    n_row = dims[tile]
    n_col = dims[(z1 + yhi - 2 * z1 * yhi) * 4 + (z0 + x1 - 2 * z0 * x1) * 2 + (ylo + x0 - 2 * ylo * x0)]
    live_r = jnp.where(lax.broadcasted_iota(jnp.int32, (V, V), 0) < n_row, 1.0, 0.0)
    live = jnp.where(lax.broadcasted_iota(jnp.int32, (V, V), 1) < n_col, live_r, 0.0).astype(jnp.bfloat16)
    acc[...] = jnp.zeros_like(acc)
    for load in loads:
        load.wait()
    for i in range(NI):
        rc[:, i * V:(i + 1) * V] = rc[:, i * V:(i + 1) * V] * live
    for copy in keep:
        copy.wait()

    def decoded(n):
        op = ops[n]
        src, rest = lax.rem(op, 128), lax.div(op, 128)
        dst, rest = lax.rem(rest, 128), lax.div(rest, 128)
        return src, dst, lax.rem(rest, 128), lax.div(rest, 128)

    def events(point):
        @pl.loop(begins[point], begins[point + 1])
        def _(n):
            src, dst, index, way = decoded(n)

            @pl.when(way == WAIT)
            def _():
                arrived(src)

            @pl.when(way != WAIT)
            def _():
                remote(buf.at[src], dst, ssem.at[index], devs[way]).start()

    digit = (1 + 15 * x0) * (1 + 255 * x1)

    def chosen(groups, n):
        code = 0
        for number, names in enumerate(groups):
            of_y = [0] * 4
            for (at_x, at_y), (row, j, k) in zip(CLASSES, names):
                of_y[at_y] += (row * 8 + j * 2 + k) * 16 ** at_x
            value = of_y[0]
            if len(set(of_y)) > 1:
                value = value + (of_y[1] - of_y[0]) * ylo + (of_y[2] - of_y[0]) * yhi
                value = value + (of_y[3] - of_y[2] - of_y[1] + of_y[0]) * (yhi * ylo)
            code = code + (n == number) * 1 * value
        code = lax.rem(lax.div(code, digit), 16)
        return (yhi + code // 8) % 2 * 4 + (x + 4 - code // 2 % 4) % 4, code % 2

    def base_of(n):
        return sum((n == number) * base for number, base in enumerate(BASES[:-1]) if base)

    par_base = PAR_AT * (1 - (sym == 0) * 1)

    def unit(base, q, core):
        at = base + q * 4 + core * 2
        return buf[pl.ds(at, 2)].reshape(V, V)

    def first_stage(base, halves):
        for q, k in halves:
            arrived(own_slot(q, 1 - c, k))
        for h in range(PARTS[1]):
            if h:
                events(base + h)
            for t in range(h * 12 // PARTS[1], (h + 1) * 12 // PARTS[1]):
                left = jnp.concatenate([buf[q * 4 + 2 * p + k] for q, k in halves for p in range(2)], axis=0)
                r = jnp.dot(left, rc[:, t * 256:(t + 1) * 256], preferred_element_type=jnp.float32).astype(jnp.bfloat16)
                for lo_col, hi_col, pair, at in columns(t):
                    for number, (q, k) in enumerate(halves):
                        rows = pl.ds(pl.multiple_of(pair * V + k * PV, PV), PV)
                        for p in range(2):
                            lanes = pl.ds(p * V + at, hi_col - lo_col)
                            first = (2 * number + p) * PV
                            half[q, rows, lanes] = r[first:first + PV, lo_col:hi_col]

    def second_stage(base, q):
        @pl.when(jnp.logical_not(none))
        def _():
            for k in range(PIECES):
                arrived(PAR_AT + own_slot(q, 1 - c, k))

        for h in range(2):
            if h and PARTS[2] > 1:
                events(base + h)
            rows = pl.ds(h * HALF, HALF)
            for b0, b1 in ((0, 256), (256, 384)):
                right = jnp.concatenate([unit(par_base, q, p)[b0:b1] for p in range(2)], axis=1)
                acc[rows, b0:b1] += lax.dot_general(
                    half[q, rows, :], right, (((1,), (1,)), ((), ())), preferred_element_type=jnp.float32
                )

    @pl.loop(0, STAGES)
    def _(n):
        second = sum((n == k) * 1 for k, stage in enumerate(SEQUENCE) if stage == 2)
        halves = [chosen(group, n) for group in UNITS]
        base = base_of(n)
        events(base)
        pl.when(second == 0)(lambda: first_stage(base, halves))
        pl.when(second == 1)(lambda: second_stage(base, halves[0][0]))

    for h in range(2):
        rows = pl.ds(h * HALF, HALF)
        pltpu.make_async_copy(acc.at[rows], out.at[rows], local_sem.at[h]).start()
    events(POINTS - 1)

    leaving = []
    for r in range(len(REST)):
        q, _ = chosen(REST, jnp.int32(r))
        for k in range(PIECES):
            arrived(own_slot(q, 1 - c, k))

        @pl.when(jnp.logical_not(none))
        def _():
            for k in range(PIECES):
                arrived(PAR_AT + own_slot(q, 1 - c, k))

        par_at = par_base + q * 4
        for source, target, sem in ((q * 4, out_own.at[r], 18 + 2 * r), (par_at, out_par.at[r], 19 + 2 * r)):
            leaving.append(pltpu.make_async_copy(buf.at[pl.ds(source, 4)], target, local_sem.at[sem - 8]))
            leaving[-1].start()

    for src, place, cond, index in firsts:
        def sent(src=src, place=place, index=index):
            remote(src, place, first_sem.at[index], to["core"]).wait_send()

        if cond is None:
            sent()
        else:
            pl.when(cond)(sent)

    @pl.loop(0, begins[POINTS])
    def _(n):
        src, dst, index, way = decoded(n)

        @pl.when(way != WAIT)
        def _():
            remote(buf.at[src], dst, ssem.at[index], devs[way]).wait_send()

    for h in range(2):
        rows = pl.ds(h * HALF, HALF)
        pltpu.make_async_copy(acc.at[rows], out.at[rows], local_sem.at[h]).wait()
    for copy in leaving:
        copy.wait()


ALL = [(row, j) for j in (0, 1, 3, 2) for row in range(2)]


def left_over():
    by_class = []
    for at in range(len(CLASSES)):
        done = [names[at][:2] for group in UNITS for stage, names in zip(SEQUENCE, group) if stage == 1]
        by_class.append([name + (0,) for name in ALL if name not in done])
    return tuple(zip(*by_class))


REST = left_over()


def rest_kernel(dims, own_hbm, par_hbm, amps, raw, out, own, par, rc, half, acc, sems):
    sym, tile = lax.axis_index("sym"), lax.axis_index("tile")
    n, hi = len(REST), NI // 2
    get_own = pltpu.make_async_copy(own_hbm, own, sems.at[0])
    get_par = pltpu.make_async_copy(par_hbm, par, sems.at[1])
    get_amps = [pltpu.make_async_copy(amps.at[i], rc.at[:, pl.ds(i * V, V)], sems.at[2 + i]) for i in range(NI)]
    get_raw = [
        pltpu.make_async_copy(raw.at[pl.ds(h * HALF, HALF)], acc.at[pl.ds(h * HALF, HALF)], sems.at[2 + NI + h])
        for h in range(2)
    ]
    for copy in get_amps[:hi] + [get_own, get_par, get_raw[0]] + get_amps[hi:] + [get_raw[1]]:
        copy.start()
    n_row, n_col = dims[tile], dims[jnp.bitwise_xor(tile, sym)]
    live = (lax.broadcasted_iota(jnp.int32, (V, V), 0) < n_row) & (lax.broadcasted_iota(jnp.int32, (V, V), 1) < n_col)
    live_b = jnp.where(live, 1.0, 0.0).astype(jnp.bfloat16)
    puts = []
    for h in range(2):
        for i in range(h * hi, (h + 1) * hi):
            get_amps[i].wait()
            rc[:, i * V:(i + 1) * V] = rc[:, i * V:(i + 1) * V] * live_b
        if h == 0:
            get_own.wait()
        for t in range(6 * h, 6 * (h + 1)):
            left = own[...].reshape(n * 2 * V, V)
            r = jnp.dot(left, rc[:, t * 256:(t + 1) * 256], preferred_element_type=jnp.float32).astype(jnp.bfloat16)
            for lo_col, hi_col, pair, at in columns(t):
                for p in range(2 * n):
                    lanes = pl.ds(p * V + at, hi_col - lo_col)
                    half[(pair - h * hi) * V:(pair - h * hi + 1) * V, lanes] = r[p * V:(p + 1) * V, lo_col:hi_col]
        if h == 0:
            get_par.wait()
        get_raw[h].wait()
        rows = pl.ds(h * HALF, HALF)
        for b0, b1 in ((0, 256), (256, 384)):
            right = [par[r, pl.ds(2 * p, 2)].reshape(V, V)[b0:b1] for r in range(n) for p in range(2)]
            right = jnp.concatenate(right, axis=1)
            r = lax.dot_general(half[...], right, (((1,), (1,)), ((), ())), preferred_element_type=jnp.float32)
            r = r + acc[rows, b0:b1]
            for i in range(hi):
                at = pl.ds((h * hi + i) * V, V)
                acc[at, b0:b1] = jnp.where(live[:, b0:b1], r[i * V:(i + 1) * V], 0.0)
            lanes = pl.ds(b0, b1 - b0)
            puts.append(pltpu.make_async_copy(acc.at[rows, lanes], out.at[rows, lanes], sems.at[4 + NI + len(puts)]))
            puts[-1].start()
    for copy in puts:
        copy.wait()


def shards(irrep_dims, chol_vectors, amplitudes):
    bf, sem = jnp.bfloat16, pltpu.SemaphoreType.DMA
    n = len(REST)
    own, chol, amps = (n, 4, PV, V), chol_vectors.reshape(V, V), amplitudes.reshape(NI, V, V)
    anywhere = pl.BlockSpec(memory_space=pl.ANY)
    raw, rest_own, rest_par = pl.pallas_call(
        kernel,
        out_shape=[
            jax.ShapeDtypeStruct((NI * V, V), jnp.float32),
            jax.ShapeDtypeStruct(own, bf),
            jax.ShapeDtypeStruct(own, bf),
        ],
        in_specs=[pl.BlockSpec(memory_space=pltpu.SMEM), anywhere, anywhere],
        out_specs=[anywhere] * 3,
        scratch_shapes=[
            pltpu.VMEM((SLOTS, PV, V), bf),
            pltpu.VMEM((V, NI * V), bf),
            pltpu.VMEM((8, NI * V, 2 * V), bf),
            pltpu.VMEM((NI * V, V), jnp.float32),
            pltpu.SMEM((MOST_OPS,), jnp.int32),
            pltpu.SMEM((POINTS + 1,), jnp.int32),
            pltpu.SMEM((len(WAYS),), jnp.int32),
            sem((MOST_SENDS,)), sem((FIRST_SENDS,)), sem((SLOTS,)), sem((10 + 2 * n,)),
        ],
        compiler_params=pltpu.CompilerParams(
            collective_id=0, has_side_effects=True, vmem_limit_bytes=63 * 1024 * 1024
        ),
        cost_estimate=pl.CostEstimate(flops=(8 - n) * 3_600_000_000, bytes_accessed=12_000_000, transcendentals=0),
        name="ladder",
    )(irrep_dims, chol, amps)
    total = pl.pallas_call(
        rest_kernel,
        out_shape=jax.ShapeDtypeStruct((NI * V, V), jnp.float32),
        in_specs=[pl.BlockSpec(memory_space=pltpu.SMEM)] + [anywhere] * 4,
        out_specs=anywhere,
        scratch_shapes=[
            pltpu.VMEM(own, bf),
            pltpu.VMEM(own, bf),
            pltpu.VMEM((V, NI * V), bf),
            pltpu.VMEM((HALF, n * 2 * V), bf),
            pltpu.VMEM((NI * V, V), jnp.float32),
            sem((8 + NI,)),
        ],
        compiler_params=pltpu.CompilerParams(vmem_limit_bytes=60 * 1024 * 1024),
        cost_estimate=pl.CostEstimate(flops=n * 3_600_000_000, bytes_accessed=16_000_000, transcendentals=0),
        name="rest",
    )(irrep_dims, rest_own, rest_par, amps, raw)
    return total.reshape(1, NI, V, V)


def solution(mesh):
    return jax.shard_map(
        shards,
        mesh=mesh,
        in_specs=(P(), P(("sym", "occ"), "tile", None), P("sym", "occ", "tile", None)),
        out_specs=P("sym", "occ", "tile", None),
        check_vma=False,
    )
```

```python
import jax
import jax.numpy as jnp
from jax import lax
from jax.experimental import pallas as pl
from jax.experimental.pallas import tpu as pltpu
from jax.sharding import PartitionSpec as P

V = 384
NI = 8
PIECES = 2
PV = V // PIECES
HALF = NI * V // 2
CROSSF, OWN, PASS_Z, FWD_Y, PASS_Y, PAR = range(6)
PARTS = {1: 2, 2: 1, 3: 1}
SEQUENCE = (1, 1, 1, 1, 1, 1, 2, 2, 1, 2, 2, 2, 2, 2)
UNITS = (
    (
        ((0, 0, 0), (0, 0, 0), (0, 0, 0), (0, 0, 0), (0, 0, 0), (0, 0, 0), (0, 0, 0), (0, 0, 0), (0, 0, 0), (0, 0, 0), (0, 0, 0), (0, 0, 0), (0, 0, 0), (0, 0, 0), (0, 0, 0), (0, 0, 0)),
        ((0, 3, 0), (0, 3, 0), (0, 3, 0), (0, 3, 0), (0, 3, 0), (0, 3, 0), (0, 3, 0), (0, 3, 0), (0, 3, 0), (0, 3, 0), (0, 3, 0), (0, 3, 0), (0, 3, 0), (0, 3, 0), (0, 3, 0), (0, 3, 0)),
        ((0, 3, 1), (0, 3, 1), (0, 3, 1), (0, 3, 1), (0, 3, 1), (0, 3, 1), (0, 3, 1), (0, 3, 1), (0, 3, 1), (0, 3, 1), (0, 3, 1), (0, 3, 1), (0, 3, 1), (0, 3, 1), (0, 3, 1), (0, 3, 1)),
        ((1, 0, 0), (1, 0, 0), (1, 0, 0), (1, 0, 0), (0, 2, 0), (0, 2, 0), (1, 0, 0), (1, 0, 0), (1, 0, 0), (1, 0, 0), (1, 0, 0), (1, 0, 0), (1, 0, 0), (1, 0, 0), (1, 0, 0), (1, 0, 0)),
        ((0, 2, 0), (0, 2, 0), (0, 2, 0), (0, 2, 0), (1, 0, 0), (1, 0, 0), (0, 2, 0), (0, 2, 1), (0, 2, 0), (0, 2, 0), (0, 2, 0), (0, 2, 0), (0, 2, 1), (0, 2, 1), (0, 2, 1), (0, 2, 1)),
        ((1, 1, 1), (1, 1, 1), (1, 3, 0), (1, 3, 0), (1, 1, 1), (1, 1, 1), (1, 3, 0), (1, 3, 0), (1, 3, 0), (1, 3, 0), (1, 3, 0), (1, 3, 0), (1, 3, 0), (1, 3, 0), (1, 3, 0), (1, 3, 0)),
        ((0, 3, 0), (0, 3, 0), (0, 0, 0), (0, 0, 0), (0, 0, 0), (0, 0, 0), (1, 0, 0), (1, 0, 0), (0, 3, 0), (0, 3, 0), (0, 3, 0), (0, 3, 0), (1, 0, 0), (1, 0, 0), (1, 0, 0), (1, 0, 0)),
        ((1, 0, 0), (1, 0, 0), (0, 1, 0), (0, 1, 0), (1, 1, 0), (1, 1, 0), (0, 0, 0), (0, 0, 0), (1, 0, 0), (1, 0, 0), (1, 0, 0), (1, 0, 0), (0, 0, 0), (0, 0, 0), (0, 0, 0), (0, 0, 0)),
        ((1, 3, 1), (1, 3, 1), (1, 3, 1), (1, 3, 1), (1, 3, 1), (1, 3, 1), (1, 3, 1), (1, 3, 1), (1, 3, 1), (1, 3, 1), (1, 3, 1), (1, 3, 1), (1, 3, 1), (1, 3, 1), (1, 3, 1), (1, 3, 1)),
        ((0, 2, 0), (0, 2, 0), (0, 3, 0), (0, 3, 0), (0, 3, 0), (0, 3, 0), (0, 1, 0), (0, 1, 0), (0, 2, 0), (0, 2, 0), (0, 2, 0), (0, 2, 0), (0, 3, 0), (0, 3, 0), (0, 3, 0), (0, 3, 0)),
        ((1, 1, 0), (1, 1, 0), (1, 0, 0), (1, 0, 0), (1, 0, 0), (1, 0, 0), (1, 1, 0), (1, 1, 0), (1, 1, 0), (1, 1, 0), (1, 1, 0), (1, 1, 0), (1, 1, 0), (1, 1, 0), (1, 1, 0), (1, 1, 0)),
        ((1, 3, 0), (1, 3, 0), (0, 2, 0), (0, 2, 0), (0, 2, 0), (0, 2, 0), (0, 3, 0), (0, 3, 0), (1, 3, 0), (1, 3, 0), (1, 3, 0), (1, 3, 0), (0, 2, 0), (0, 2, 0), (0, 2, 0), (0, 2, 0)),
        ((0, 1, 0), (0, 1, 0), (1, 3, 0), (1, 1, 0), (1, 3, 0), (1, 3, 0), (1, 3, 0), (1, 3, 0), (0, 1, 0), (0, 1, 0), (0, 1, 0), (0, 1, 0), (1, 3, 0), (1, 3, 0), (1, 3, 0), (1, 3, 0)),
        ((0, 0, 0), (0, 0, 0), (1, 1, 0), (1, 3, 0), (0, 1, 0), (0, 1, 0), (0, 2, 0), (0, 2, 0), (0, 0, 0), (0, 0, 0), (0, 0, 0), (0, 0, 0), (0, 1, 0), (0, 1, 0), (0, 1, 0), (0, 1, 0)),
    ),
    (
        ((0, 0, 1), (0, 0, 1), (0, 0, 1), (0, 0, 1), (0, 0, 1), (0, 0, 1), (0, 0, 1), (0, 0, 1), (0, 0, 1), (0, 0, 1), (0, 0, 1), (0, 0, 1), (0, 0, 1), (0, 0, 1), (0, 0, 1), (0, 0, 1)),
        ((0, 1, 0), (0, 1, 0), (0, 1, 0), (0, 1, 0), (0, 1, 0), (0, 1, 0), (0, 1, 0), (0, 1, 0), (0, 1, 0), (0, 1, 0), (0, 1, 0), (0, 1, 0), (0, 1, 0), (0, 1, 0), (0, 1, 0), (0, 1, 0)),
        ((0, 1, 1), (0, 1, 1), (0, 1, 1), (0, 1, 1), (0, 1, 1), (0, 1, 1), (0, 1, 1), (0, 1, 1), (0, 1, 1), (0, 1, 1), (0, 1, 1), (0, 1, 1), (0, 1, 1), (0, 1, 1), (0, 1, 1), (0, 1, 1)),
        ((1, 0, 1), (1, 0, 1), (1, 0, 1), (1, 0, 1), (0, 2, 1), (0, 2, 1), (1, 0, 1), (0, 2, 0), (1, 0, 1), (1, 0, 1), (1, 0, 1), (1, 0, 1), (0, 2, 0), (0, 2, 0), (0, 2, 0), (0, 2, 0)),
        ((0, 2, 1), (0, 2, 1), (0, 2, 1), (0, 2, 1), (1, 1, 0), (1, 1, 0), (0, 2, 1), (1, 0, 1), (0, 2, 1), (0, 2, 1), (0, 2, 1), (0, 2, 1), (1, 0, 1), (1, 0, 1), (1, 0, 1), (1, 0, 1)),
        ((1, 1, 0), (1, 1, 0), (1, 1, 0), (1, 1, 0), (1, 3, 0), (1, 3, 0), (1, 1, 0), (1, 1, 0), (1, 1, 0), (1, 1, 0), (1, 1, 0), (1, 1, 0), (1, 1, 0), (1, 1, 0), (1, 1, 0), (1, 1, 0)),
        ((0, 3, 0), (0, 3, 0), (0, 0, 0), (0, 0, 0), (0, 0, 0), (0, 0, 0), (1, 0, 0), (1, 0, 0), (0, 3, 0), (0, 3, 0), (0, 3, 0), (0, 3, 0), (1, 0, 0), (1, 0, 0), (1, 0, 0), (1, 0, 0)),
        ((1, 0, 0), (1, 0, 0), (0, 1, 0), (0, 1, 0), (1, 1, 0), (1, 1, 0), (0, 0, 0), (0, 0, 0), (1, 0, 0), (1, 0, 0), (1, 0, 0), (1, 0, 0), (0, 0, 0), (0, 0, 0), (0, 0, 0), (0, 0, 0)),
        ((1, 3, 0), (1, 3, 0), (1, 1, 1), (1, 1, 1), (1, 0, 1), (1, 0, 1), (1, 1, 1), (1, 1, 1), (1, 1, 1), (1, 1, 1), (1, 1, 1), (1, 1, 1), (1, 1, 1), (1, 1, 1), (1, 1, 1), (1, 1, 1)),
        ((0, 2, 0), (0, 2, 0), (0, 3, 0), (0, 3, 0), (0, 3, 0), (0, 3, 0), (0, 1, 0), (0, 1, 0), (0, 2, 0), (0, 2, 0), (0, 2, 0), (0, 2, 0), (0, 3, 0), (0, 3, 0), (0, 3, 0), (0, 3, 0)),
        ((1, 1, 0), (1, 1, 0), (1, 0, 0), (1, 0, 0), (1, 0, 0), (1, 0, 0), (1, 1, 0), (1, 1, 0), (1, 1, 0), (1, 1, 0), (1, 1, 0), (1, 1, 0), (1, 1, 0), (1, 1, 0), (1, 1, 0), (1, 1, 0)),
        ((1, 3, 0), (1, 3, 0), (0, 2, 0), (0, 2, 0), (0, 2, 0), (0, 2, 0), (0, 3, 0), (0, 3, 0), (1, 3, 0), (1, 3, 0), (1, 3, 0), (1, 3, 0), (0, 2, 0), (0, 2, 0), (0, 2, 0), (0, 2, 0)),
        ((0, 1, 0), (0, 1, 0), (1, 3, 0), (1, 1, 0), (1, 3, 0), (1, 3, 0), (1, 3, 0), (1, 3, 0), (0, 1, 0), (0, 1, 0), (0, 1, 0), (0, 1, 0), (1, 3, 0), (1, 3, 0), (1, 3, 0), (1, 3, 0)),
        ((0, 0, 0), (0, 0, 0), (1, 1, 0), (1, 3, 0), (0, 1, 0), (0, 1, 0), (0, 2, 0), (0, 2, 0), (0, 0, 0), (0, 0, 0), (0, 0, 0), (0, 0, 0), (0, 1, 0), (0, 1, 0), (0, 1, 0), (0, 1, 0)),
    ),
)
EVENTS = (
    (
        (2, ((CROSSF, 0), (CROSSF, 1), (PASS_Z, 0, 1), (OWN, 0, 1, 0), (OWN, 0, 3, 0), (PASS_Z, 0, 0),)),
        (3, ((OWN, 0, 1, 1), (OWN, 0, 3, 1),)),
        (4, ((OWN, 1, 0, 0), (OWN, 1, 0, 1), (PASS_Z, 1, 0), (PASS_Z, 3, 0),)),
        (5, ((OWN, 0, 2, 0), (OWN, 0, 2, 1), (FWD_Y, 0, 0), (FWD_Y, 0, 1),)),
        (6, ((OWN, 1, 1, 0), (PASS_Z, 1, 1), (PASS_Z, 3, 1),)),
        (7, ((OWN, 1, 1, 1), (OWN, 1, 3, 0), (FWD_Y, 1, 0), (FWD_Y, 3, 0), (PASS_Y, 0, 1),)),
        (8, ((PASS_Z, 2, 0),)),
        (9, ((OWN, 1, 2, 0), (PASS_Z, 2, 1),)),
        (10, ((OWN, 1, 3, 1), (OWN, 1, 2, 1), (FWD_Y, 1, 1), (FWD_Y, 3, 1), (PASS_Y, 1, 0),)),
        (11, ((FWD_Y, 2, 0), (FWD_Y, 2, 1),)),
        (12, ((PASS_Y, 3, 1),)),
        (14, ((PASS_Y, 2, 0),)),
    ),
    (
        (2, ((CROSSF, 0), (CROSSF, 1), (PASS_Z, 0, 1), (OWN, 0, 1, 0), (OWN, 0, 3, 0), (PASS_Z, 0, 0),)),
        (3, ((OWN, 0, 1, 1), (OWN, 0, 3, 1),)),
        (4, ((OWN, 1, 0, 0), (OWN, 1, 0, 1), (PASS_Z, 1, 0), (PASS_Z, 3, 0),)),
        (5, ((OWN, 0, 2, 0), (OWN, 0, 2, 1), (FWD_Y, 0, 0), (FWD_Y, 0, 1),)),
        (6, ((OWN, 1, 1, 0), (PASS_Z, 1, 1), (PASS_Z, 3, 1),)),
        (7, ((OWN, 1, 1, 1), (OWN, 1, 3, 0), (FWD_Y, 1, 0), (FWD_Y, 3, 0), (PASS_Y, 0, 0),)),
        (8, ((PASS_Z, 2, 0),)),
        (9, ((OWN, 1, 2, 0), (PASS_Z, 2, 1),)),
        (10, ((OWN, 1, 3, 1), (OWN, 1, 2, 1), (FWD_Y, 1, 1), (FWD_Y, 3, 1), (PASS_Y, 3, 0),)),
        (11, ((FWD_Y, 2, 0), (FWD_Y, 2, 1),)),
        (12, ((PASS_Y, 1, 1),)),
        (14, ((PASS_Y, 2, 1),)),
    ),
    (
        (2, ((CROSSF, 0), (CROSSF, 1), (PASS_Z, 0, 1), (OWN, 0, 1, 0), (OWN, 0, 3, 0), (PASS_Z, 0, 0),)),
        (3, ((OWN, 0, 1, 1), (OWN, 0, 3, 1),)),
        (4, ((OWN, 1, 0, 0), (OWN, 1, 0, 1), (PASS_Z, 1, 0), (PASS_Z, 3, 0),)),
        (5, ((OWN, 0, 2, 0), (OWN, 0, 2, 1), (PAR, 0, 0, 0), (PAR, 0, 0, 1),)),
        (6, ((OWN, 1, 1, 0), (OWN, 1, 3, 0), (PASS_Z, 1, 1), (PASS_Z, 3, 1),)),
        (7, ((OWN, 1, 1, 1), (OWN, 1, 3, 1), (PASS_Y, 0, 0), (PAR, 0, 1, 0), (PAR, 0, 3, 0),)),
        (9, ((OWN, 1, 2, 0), (PASS_Z, 2, 0), (PASS_Z, 2, 1),)),
        (10, ((OWN, 1, 2, 1), (PASS_Y, 3, 0), (PAR, 0, 1, 1), (PAR, 0, 3, 1), (PAR, 1, 0, 1), (PAR, 1, 0, 0),)),
        (11, ((PAR, 0, 2, 0), (PAR, 0, 2, 1),)),
        (12, ((PASS_Y, 1, 1), (PAR, 1, 1, 0),)),
        (14, ((PAR, 1, 3, 0), (PAR, 1, 3, 1),)),
        (15, ((PASS_Y, 2, 1),)),
        (16, ((PAR, 1, 1, 1),)),
        (17, ((PAR, 1, 2, 0), (PAR, 1, 2, 1),)),
    ),
    (
        (2, ((CROSSF, 0), (CROSSF, 1), (PASS_Z, 0, 1), (OWN, 0, 1, 0), (OWN, 0, 3, 0), (PASS_Z, 0, 0),)),
        (3, ((OWN, 0, 1, 1), (OWN, 0, 3, 1),)),
        (4, ((OWN, 1, 0, 0), (OWN, 1, 0, 1), (PASS_Z, 1, 0), (PASS_Z, 3, 0),)),
        (5, ((OWN, 0, 2, 0), (OWN, 0, 2, 1), (PAR, 0, 0, 0), (PAR, 0, 0, 1),)),
        (6, ((OWN, 1, 1, 0), (OWN, 1, 3, 0), (PASS_Z, 1, 1), (PASS_Z, 3, 1),)),
        (7, ((OWN, 1, 1, 1), (OWN, 1, 3, 1), (PASS_Y, 0, 1), (PAR, 0, 1, 0), (PAR, 0, 3, 0),)),
        (9, ((OWN, 1, 2, 0), (PASS_Z, 2, 0), (PASS_Z, 2, 1),)),
        (10, ((OWN, 1, 2, 1), (PASS_Y, 1, 0), (PAR, 0, 1, 1), (PAR, 0, 3, 1), (PAR, 1, 0, 0), (PAR, 1, 0, 1),)),
        (11, ((PAR, 0, 2, 0), (PAR, 0, 2, 1),)),
        (12, ((PASS_Y, 3, 1), (PAR, 1, 3, 0),)),
        (14, ((PAR, 1, 1, 0), (PAR, 1, 1, 1),)),
        (15, ((PASS_Y, 2, 0),)),
        (16, ((PAR, 1, 3, 1),)),
        (17, ((PAR, 1, 2, 0), (PAR, 1, 2, 1),)),
    ),
    (
        (2, ((CROSSF, 0), (PASS_Z, 0, 1), (OWN, 0, 1, 0), (OWN, 0, 3, 0), (PASS_Z, 0, 0), (PAR, 0, 0, 0),)),
        (3, ((CROSSF, 1), (OWN, 0, 1, 1), (OWN, 0, 3, 1), (PAR, 1, 0, 0),)),
        (4, ((PASS_Z, 1, 0), (PASS_Z, 3, 0),)),
        (5, ((OWN, 0, 2, 0), (OWN, 0, 2, 1), (FWD_Y, 0, 0), (FWD_Y, 0, 1), (PAR, 0, 0, 1), (PAR, 1, 0, 1), (OWN, 1, 1, 0), (OWN, 1, 0, 0), (PAR, 0, 1, 0),)),
        (6, ((OWN, 1, 1, 1), (OWN, 1, 3, 0), (PASS_Z, 1, 1), (PASS_Z, 3, 1), (PAR, 0, 3, 0), (PAR, 1, 1, 0),)),
        (7, ((OWN, 1, 0, 1), (OWN, 1, 3, 1), (FWD_Y, 1, 0), (FWD_Y, 3, 0), (PAR, 1, 3, 0),)),
        (8, ((OWN, 1, 2, 0), (PASS_Z, 2, 0), (PASS_Z, 2, 1),)),
        (9, ((OWN, 1, 2, 1), (PAR, 0, 1, 1), (PAR, 1, 1, 1),)),
        (10, ((FWD_Y, 1, 1), (FWD_Y, 3, 1), (PAR, 0, 3, 1), (PAR, 1, 3, 1),)),
        (11, ((FWD_Y, 2, 0), (FWD_Y, 2, 1), (PAR, 0, 2, 0), (PAR, 1, 2, 0),)),
        (13, ((PAR, 0, 2, 1), (PAR, 1, 2, 1),)),
    ),
    (
        (2, ((CROSSF, 0), (PASS_Z, 0, 1), (OWN, 0, 1, 0), (OWN, 0, 3, 0), (PASS_Z, 0, 0), (PAR, 1, 0, 0),)),
        (3, ((CROSSF, 1), (OWN, 0, 1, 1), (OWN, 0, 3, 1), (PAR, 0, 0, 0),)),
        (4, ((PASS_Z, 1, 0), (PASS_Z, 3, 0),)),
        (5, ((OWN, 0, 2, 0), (OWN, 0, 2, 1), (FWD_Y, 0, 0), (FWD_Y, 0, 1), (PAR, 0, 0, 1), (PAR, 1, 0, 1), (OWN, 1, 1, 0), (OWN, 1, 0, 0), (PAR, 1, 1, 0),)),
        (6, ((OWN, 1, 1, 1), (OWN, 1, 3, 0), (PASS_Z, 1, 1), (PASS_Z, 3, 1), (PAR, 0, 1, 0), (PAR, 1, 3, 0),)),
        (7, ((OWN, 1, 0, 1), (OWN, 1, 3, 1), (FWD_Y, 1, 0), (FWD_Y, 3, 0), (PAR, 0, 3, 0),)),
        (8, ((OWN, 1, 2, 0), (PASS_Z, 2, 0), (PASS_Z, 2, 1),)),
        (9, ((OWN, 1, 2, 1), (PAR, 0, 1, 1), (PAR, 1, 1, 1),)),
        (10, ((FWD_Y, 1, 1), (FWD_Y, 3, 1), (PAR, 0, 3, 1), (PAR, 1, 3, 1),)),
        (11, ((FWD_Y, 2, 0), (FWD_Y, 2, 1), (PAR, 0, 2, 0), (PAR, 1, 2, 0),)),
        (13, ((PAR, 0, 2, 1), (PAR, 1, 2, 1),)),
    ),
    (
        (2, ((CROSSF, 0), (CROSSF, 1), (PASS_Z, 0, 1), (OWN, 0, 1, 0), (OWN, 0, 3, 0), (PASS_Z, 0, 0),)),
        (3, ((OWN, 0, 1, 1), (OWN, 0, 3, 1),)),
        (4, ((OWN, 1, 0, 0), (OWN, 1, 0, 1), (PASS_Z, 1, 0), (PASS_Z, 3, 0),)),
        (5, ((OWN, 0, 2, 0), (OWN, 0, 2, 1), (FWD_Y, 0, 0), (FWD_Y, 0, 1),)),
        (6, ((OWN, 1, 1, 0), (OWN, 1, 3, 0), (PASS_Z, 1, 1), (PASS_Z, 3, 1),)),
        (7, ((OWN, 1, 1, 1), (OWN, 1, 3, 1), (FWD_Y, 1, 0), (FWD_Y, 3, 0), (PAR, 0, 0, 0), (PAR, 1, 0, 0),)),
        (8, ((PAR, 0, 0, 1), (PAR, 1, 0, 1),)),
        (9, ((OWN, 1, 2, 0), (PASS_Z, 2, 0), (PASS_Z, 2, 1),)),
        (10, ((OWN, 1, 2, 1), (FWD_Y, 1, 1), (FWD_Y, 3, 1), (PAR, 0, 1, 0), (PAR, 1, 1, 0),)),
        (11, ((FWD_Y, 2, 0), (FWD_Y, 2, 1), (PAR, 0, 3, 0), (PAR, 1, 3, 0),)),
        (12, ((PAR, 0, 1, 1),)),
        (13, ((PAR, 1, 1, 1),)),
        (14, ((PAR, 0, 3, 1), (PAR, 1, 3, 1),)),
        (15, ((PAR, 0, 2, 0),)),
        (16, ((PAR, 0, 2, 1), (PAR, 1, 2, 0),)),
        (17, ((PAR, 1, 2, 1),)),
    ),
    (
        (2, ((CROSSF, 0), (CROSSF, 1), (PASS_Z, 0, 1), (OWN, 0, 1, 0), (OWN, 0, 3, 0), (PASS_Z, 0, 0),)),
        (3, ((OWN, 0, 1, 1), (OWN, 0, 3, 1),)),
        (4, ((OWN, 1, 0, 0), (PASS_Z, 1, 0), (PASS_Z, 3, 0),)),
        (5, ((OWN, 0, 2, 0), (OWN, 0, 2, 1), (OWN, 1, 0, 1), (FWD_Y, 0, 0), (FWD_Y, 0, 1), (OWN, 1, 1, 0),)),
        (6, ((OWN, 1, 3, 0), (PASS_Z, 1, 1), (PASS_Z, 3, 1),)),
        (7, ((OWN, 1, 1, 1), (OWN, 1, 3, 1), (FWD_Y, 1, 0), (FWD_Y, 3, 0), (PAR, 0, 0, 0), (PAR, 1, 0, 0),)),
        (8, ((PASS_Z, 2, 0), (PASS_Z, 2, 1), (PAR, 0, 0, 1), (PAR, 1, 0, 1),)),
        (9, ((OWN, 1, 2, 0), (OWN, 1, 2, 1),)),
        (10, ((FWD_Y, 1, 1), (FWD_Y, 3, 1), (PAR, 0, 1, 0), (PAR, 1, 1, 0),)),
        (11, ((FWD_Y, 2, 0), (FWD_Y, 2, 1), (PAR, 0, 3, 0), (PAR, 1, 3, 0),)),
        (12, ((PAR, 0, 1, 1),)),
        (13, ((PAR, 1, 1, 1),)),
        (14, ((PAR, 0, 3, 1), (PAR, 1, 3, 1),)),
        (15, ((PAR, 0, 2, 0), (PAR, 1, 2, 0),)),
        (16, ((PAR, 0, 2, 1),)),
        (17, ((PAR, 1, 2, 1),)),
    ),
    (
        (2, ((CROSSF, 0), (CROSSF, 1), (OWN, 0, 1, 0), (OWN, 0, 3, 0), (FWD_Y, 0, 0), (PAR, 0, 0, 0),)),
        (3, ((OWN, 0, 1, 1), (OWN, 0, 3, 1), (FWD_Y, 0, 1), (PAR, 0, 0, 1),)),
        (4, ((OWN, 1, 0, 0), (OWN, 1, 0, 1),)),
        (5, ((OWN, 0, 2, 0), (OWN, 0, 2, 1), (FWD_Y, 1, 0), (PASS_Y, 0, 0), (PASS_Y, 0, 1), (PAR, 0, 1, 0),)),
        (6, ((OWN, 1, 3, 0), (FWD_Y, 3, 0), (PAR, 0, 3, 0),)),
        (7, ((OWN, 1, 1, 0), (OWN, 1, 3, 1), (FWD_Y, 1, 1), (PASS_Y, 1, 0), (PAR, 0, 1, 1), (PAR, 1, 0, 0), (PAR, 0, 3, 1), (FWD_Y, 3, 1),)),
        (8, ((OWN, 1, 2, 0), (OWN, 1, 2, 1), (PASS_Y, 3, 0), (PAR, 1, 0, 1),)),
        (9, ((FWD_Y, 2, 0), (PAR, 0, 2, 0),)),
        (10, ((OWN, 1, 1, 1), (PASS_Y, 1, 1), (PAR, 0, 2, 1), (PAR, 1, 1, 0),)),
        (11, ((FWD_Y, 2, 1), (PASS_Y, 3, 1), (PAR, 1, 3, 0),)),
        (12, ((PASS_Y, 2, 0), (PAR, 1, 1, 1),)),
        (14, ((PASS_Y, 2, 1), (PAR, 1, 3, 1),)),
        (15, ((PAR, 1, 2, 0),)),
        (16, ((PAR, 1, 2, 1),)),
    ),
    (
        (2, ((CROSSF, 0), (CROSSF, 1), (OWN, 0, 1, 0), (OWN, 0, 3, 0), (FWD_Y, 0, 0), (PAR, 0, 0, 0),)),
        (3, ((OWN, 0, 1, 1), (OWN, 0, 3, 1), (FWD_Y, 0, 1), (PAR, 0, 0, 1),)),
        (4, ((OWN, 1, 0, 0), (OWN, 1, 0, 1),)),
        (5, ((OWN, 0, 2, 0), (OWN, 0, 2, 1), (FWD_Y, 1, 0), (PASS_Y, 0, 0), (PASS_Y, 0, 1), (PAR, 0, 1, 0),)),
        (6, ((OWN, 1, 3, 0), (FWD_Y, 3, 0), (PAR, 0, 3, 0),)),
        (7, ((OWN, 1, 1, 0), (OWN, 1, 3, 1), (FWD_Y, 1, 1), (PASS_Y, 1, 0), (PAR, 0, 1, 1), (PAR, 1, 0, 0), (PAR, 0, 3, 1), (FWD_Y, 3, 1),)),
        (8, ((OWN, 1, 2, 0), (OWN, 1, 2, 1), (PASS_Y, 3, 0), (PAR, 1, 0, 1),)),
        (9, ((FWD_Y, 2, 0), (PAR, 0, 2, 0),)),
        (10, ((OWN, 1, 1, 1), (PASS_Y, 1, 1), (PAR, 0, 2, 1), (PAR, 1, 1, 0),)),
        (11, ((FWD_Y, 2, 1), (PASS_Y, 3, 1), (PAR, 1, 3, 0),)),
        (12, ((PASS_Y, 2, 0), (PAR, 1, 1, 1),)),
        (14, ((PASS_Y, 2, 1), (PAR, 1, 3, 1),)),
        (15, ((PAR, 1, 2, 0),)),
        (16, ((PAR, 1, 2, 1),)),
    ),
    (
        (2, ((CROSSF, 0), (CROSSF, 1), (OWN, 0, 1, 0), (OWN, 0, 3, 0), (FWD_Y, 0, 0), (PAR, 0, 0, 0),)),
        (3, ((OWN, 0, 1, 1), (OWN, 0, 3, 1), (FWD_Y, 0, 1), (PAR, 0, 0, 1),)),
        (4, ((OWN, 1, 0, 0), (OWN, 1, 0, 1),)),
        (5, ((OWN, 0, 2, 0), (OWN, 0, 2, 1), (FWD_Y, 1, 0), (PASS_Y, 0, 0), (PASS_Y, 0, 1), (PAR, 0, 1, 0),)),
        (6, ((OWN, 1, 1, 0), (OWN, 1, 3, 0), (FWD_Y, 3, 0), (PAR, 0, 3, 0),)),
        (7, ((OWN, 1, 1, 1), (OWN, 1, 3, 1), (FWD_Y, 1, 1), (PASS_Y, 1, 0), (PAR, 0, 1, 1), (PAR, 1, 0, 0),)),
        (8, ((FWD_Y, 3, 1), (PASS_Y, 3, 0), (PAR, 0, 3, 1), (PAR, 1, 0, 1),)),
        (9, ((OWN, 1, 2, 0),)),
        (10, ((OWN, 1, 2, 1), (FWD_Y, 2, 0), (PASS_Y, 1, 1), (PAR, 0, 2, 0), (PAR, 1, 1, 0),)),
        (11, ((FWD_Y, 2, 1), (PASS_Y, 3, 1), (PAR, 0, 2, 1), (PAR, 1, 3, 0),)),
        (12, ((PASS_Y, 2, 0),)),
        (13, ((PAR, 1, 1, 1),)),
        (14, ((PASS_Y, 2, 1), (PAR, 1, 3, 1),)),
        (15, ((PAR, 1, 2, 0),)),
        (16, ((PAR, 1, 2, 1),)),
    ),
    (
        (2, ((CROSSF, 0), (CROSSF, 1), (OWN, 0, 1, 0), (OWN, 0, 3, 0), (FWD_Y, 0, 0), (PAR, 0, 0, 0),)),
        (3, ((OWN, 0, 1, 1), (OWN, 0, 3, 1), (FWD_Y, 0, 1), (PAR, 0, 0, 1),)),
        (4, ((OWN, 1, 0, 0), (OWN, 1, 0, 1),)),
        (5, ((OWN, 0, 2, 0), (OWN, 0, 2, 1), (FWD_Y, 1, 0), (PASS_Y, 0, 0), (PASS_Y, 0, 1), (PAR, 0, 1, 0),)),
        (6, ((OWN, 1, 1, 0), (OWN, 1, 3, 0), (FWD_Y, 3, 0), (PAR, 0, 3, 0),)),
        (7, ((OWN, 1, 1, 1), (OWN, 1, 3, 1), (FWD_Y, 1, 1), (PASS_Y, 1, 0), (PAR, 0, 1, 1), (PAR, 1, 0, 0),)),
        (8, ((FWD_Y, 3, 1), (PASS_Y, 3, 0), (PAR, 0, 3, 1), (PAR, 1, 0, 1),)),
        (9, ((OWN, 1, 2, 0),)),
        (10, ((OWN, 1, 2, 1), (FWD_Y, 2, 0), (PASS_Y, 1, 1), (PAR, 0, 2, 0), (PAR, 1, 1, 0),)),
        (11, ((FWD_Y, 2, 1), (PASS_Y, 3, 1), (PAR, 0, 2, 1), (PAR, 1, 3, 0),)),
        (12, ((PASS_Y, 2, 0), (PAR, 1, 1, 1),)),
        (14, ((PASS_Y, 2, 1), (PAR, 1, 3, 1),)),
        (15, ((PAR, 1, 2, 0),)),
        (16, ((PAR, 1, 2, 1),)),
    ),
    (
        (2, ((CROSSF, 0), (CROSSF, 1), (OWN, 0, 1, 0), (OWN, 0, 3, 0), (FWD_Y, 0, 0),)),
        (3, ((OWN, 0, 1, 1), (OWN, 0, 3, 1), (FWD_Y, 0, 1),)),
        (4, ((OWN, 1, 0, 0), (PAR, 0, 0, 0),)),
        (5, ((OWN, 0, 2, 0), (OWN, 0, 2, 1), (OWN, 1, 0, 1), (FWD_Y, 1, 0), (PAR, 1, 0, 0), (FWD_Y, 3, 0), (OWN, 1, 1, 0),)),
        (6, ((OWN, 1, 3, 0), (PAR, 0, 0, 1), (PAR, 1, 0, 1),)),
        (7, ((OWN, 1, 1, 1), (OWN, 1, 3, 1), (FWD_Y, 1, 1), (PAR, 0, 1, 0), (PAR, 1, 1, 0),)),
        (8, ((FWD_Y, 3, 1), (PAR, 1, 3, 0),)),
        (9, ((OWN, 1, 2, 0), (FWD_Y, 2, 0), (PAR, 0, 3, 0),)),
        (10, ((PAR, 0, 1, 1), (PAR, 1, 1, 1),)),
        (11, ((FWD_Y, 2, 1), (PAR, 0, 3, 1), (PAR, 1, 3, 1),)),
        (12, ((OWN, 1, 2, 1), (PAR, 1, 2, 0),)),
        (13, ((PAR, 0, 2, 0),)),
        (14, ((PAR, 0, 2, 1), (PAR, 1, 2, 1),)),
    ),
    (
        (2, ((CROSSF, 0), (CROSSF, 1), (OWN, 0, 1, 0), (OWN, 0, 3, 0), (FWD_Y, 0, 0),)),
        (3, ((OWN, 0, 1, 1), (OWN, 0, 3, 1), (FWD_Y, 0, 1),)),
        (4, ((OWN, 1, 0, 0), (PAR, 1, 0, 0),)),
        (5, ((OWN, 0, 2, 0), (OWN, 0, 2, 1), (OWN, 1, 0, 1), (FWD_Y, 1, 0), (PAR, 0, 0, 0), (FWD_Y, 3, 0), (OWN, 1, 1, 0),)),
        (6, ((OWN, 1, 3, 0), (PAR, 0, 0, 1), (PAR, 1, 0, 1),)),
        (7, ((OWN, 1, 1, 1), (OWN, 1, 3, 1), (FWD_Y, 1, 1), (PAR, 0, 1, 0), (PAR, 1, 1, 0),)),
        (8, ((FWD_Y, 3, 1), (PAR, 0, 3, 0),)),
        (9, ((OWN, 1, 2, 0), (FWD_Y, 2, 0), (PAR, 1, 3, 0),)),
        (10, ((PAR, 0, 1, 1), (PAR, 1, 1, 1),)),
        (11, ((FWD_Y, 2, 1), (PAR, 0, 3, 1), (PAR, 1, 3, 1),)),
        (12, ((OWN, 1, 2, 1), (PAR, 0, 2, 0),)),
        (13, ((PAR, 1, 2, 0),)),
        (14, ((PAR, 0, 2, 1), (PAR, 1, 2, 1),)),
    ),
    (
        (2, ((CROSSF, 0), (CROSSF, 1), (OWN, 0, 1, 0), (OWN, 0, 3, 0), (FWD_Y, 0, 0),)),
        (3, ((OWN, 0, 1, 1), (OWN, 0, 3, 1), (FWD_Y, 0, 1),)),
        (4, ((OWN, 1, 0, 0), (PAR, 0, 0, 0),)),
        (5, ((OWN, 0, 2, 0), (OWN, 0, 2, 1), (OWN, 1, 0, 1), (FWD_Y, 1, 0), (PAR, 1, 0, 0), (FWD_Y, 3, 0), (OWN, 1, 1, 0),)),
        (6, ((OWN, 1, 3, 0), (PAR, 0, 0, 1), (PAR, 1, 0, 1),)),
        (7, ((OWN, 1, 1, 1), (OWN, 1, 3, 1), (FWD_Y, 1, 1), (PAR, 0, 1, 0), (PAR, 1, 1, 0),)),
        (8, ((OWN, 1, 2, 0), (FWD_Y, 3, 1), (PAR, 1, 3, 0),)),
        (9, ((OWN, 1, 2, 1), (FWD_Y, 2, 0), (PAR, 0, 3, 0),)),
        (10, ((PAR, 0, 1, 1), (PAR, 1, 1, 1),)),
        (11, ((FWD_Y, 2, 1), (PAR, 0, 3, 1), (PAR, 1, 3, 1),)),
        (12, ((PAR, 1, 2, 0),)),
        (13, ((PAR, 0, 2, 0),)),
        (14, ((PAR, 0, 2, 1), (PAR, 1, 2, 1),)),
    ),
    (
        (2, ((CROSSF, 0), (CROSSF, 1), (OWN, 0, 1, 0), (OWN, 0, 3, 0), (FWD_Y, 0, 0),)),
        (3, ((OWN, 0, 1, 1), (OWN, 0, 3, 1), (FWD_Y, 0, 1),)),
        (4, ((OWN, 1, 0, 0), (PAR, 1, 0, 0),)),
        (5, ((OWN, 0, 2, 0), (OWN, 0, 2, 1), (OWN, 1, 0, 1), (FWD_Y, 1, 0), (PAR, 0, 0, 0), (FWD_Y, 3, 0), (OWN, 1, 1, 0),)),
        (6, ((OWN, 1, 3, 0), (PAR, 0, 0, 1), (PAR, 1, 0, 1),)),
        (7, ((OWN, 1, 1, 1), (OWN, 1, 3, 1), (FWD_Y, 1, 1), (PAR, 0, 1, 0), (PAR, 1, 1, 0),)),
        (8, ((OWN, 1, 2, 0), (FWD_Y, 3, 1), (PAR, 0, 3, 0),)),
        (9, ((OWN, 1, 2, 1), (FWD_Y, 2, 0), (PAR, 1, 3, 0),)),
        (10, ((PAR, 0, 1, 1), (PAR, 1, 1, 1),)),
        (11, ((FWD_Y, 2, 1), (PAR, 0, 3, 1), (PAR, 1, 3, 1),)),
        (12, ((PAR, 0, 2, 0),)),
        (13, ((PAR, 1, 2, 0),)),
        (14, ((PAR, 0, 2, 1), (PAR, 1, 2, 1),)),
    ),
)

STAGES = len(SEQUENCE)
BASES = [sum(PARTS[stage] for stage in SEQUENCE[:n]) for n in range(STAGES + 1)]
POINTS = BASES[-1] + 1
PAR_AT, T1_AT, T2_AT, T3_AT, TC_AT, SLOTS = 32, 64, 72, 80, 88, 90
WAYS = ("x+", "x-", "y+", "y-", "z+", "z-", "core", "ya", "yb", "za", "zb")
WAIT = 15
CLASSES = [(x, y) for x in range(4) for y in range(4)]


def sign_of(j, k):
    return "+" if (k + (0, 1, 1, 0)[j]) % 2 == 0 else "-"


def name_of(x, y, row, j):
    return (y // 2 + row) % 2 * 4 + (x + 4 - j) % 4


def row_behind(y, sign):
    return (y + 3) % 4 // 2 if sign == "+" else (y + 1) % 4 // 2


def feed(x, y, j, k, src):
    up = y // 2 == 1
    final, via1, via2 = ("par", name_of(x, y, 0, j), k), ("t1", j, k), ("t2", j, k)
    sends = []
    if x in (0, 1):
        sends.append((src, via1, "z" + sign_of(j, k)))
    if x == 1:
        sends.append((src, final, "ya"))
    if x in (2, 3):
        sends.append((src, final if x == 2 and not up else via1, "za"))
        sends.append((src, final if x == 2 and up else via2, "zb"))
    return sends


def expand(x, y, event):
    kind, args = event[0], event[1:]
    up = y // 2 == 1
    ops = []
    if kind == CROSSF:
        (k,) = args
        sign = "+-"[k]
        ops = [("tc", k), (("tc", k), ("own", row_behind(y, sign) * 4 + x, k), "y" + sign)]
    if kind == OWN:
        row, j, k = args
        here = ("own", name_of(x, y, row, j), k)
        ops = [here]
        if (row, j) == (1, 0) or (j == 1 and (k + row) % 2 == 0):
            ops.append((here, here, "x+"))
        if (row, j) == (1, 0) or (j == 3 and (k + row) % 2 == 1):
            ops.append((here, here, "x-"))
        if row == 0:
            ops += feed(x, y, j, k, here)
        ops.append((here, here, "core"))
    if kind == PASS_Z:
        j, k = args
        here = ("t1", j, k)
        there = ("par", name_of(x, y, 0, j), k) if x == 0 and up else ("t2", j, k)
        ops = [here, (here, there, "z" + sign_of(j, k))]
    if kind == FWD_Y:
        j, k = args
        final, there, way = ("par", name_of(x, y, 0, j), k), ("t3", j, k), "y" + sign_of(j, k)
        if x == 3 or (x == 2 and up):
            ops += [("t1", j, k), (("t1", j, k), final, "ya") if x == 3 else (("t1", j, k), there, way)]
        if x in (1, 3) or not up:
            ops += [("t2", j, k), (("t2", j, k), final, "yb") if x in (1, 3) else (("t2", j, k), there, way)]
    if kind == PASS_Y:
        j, k = args
        sign = sign_of(j, k)
        row = row_behind(y, sign)
        if x == 2 or row == 0:
            ops = [("t3", j, k), (("t3", j, k), ("par", row * 4 + (x + 4 - j) % 4, k), "y" + sign)]
    if kind == PAR:
        row, j, k = args
        here = ("par", name_of(x, y, row, j), k)
        ops = [here, (here, here, "core")]
    return ops


def slot(place, c):
    kind, rest = place[0], place[1:]
    if kind in ("own", "par"):
        q, k = rest
        return (PAR_AT if kind == "par" else 0) + q * 4 + c * 2 + k
    if kind == "tc":
        return TC_AT + rest[0]
    return {"t1": T1_AT, "t2": T2_AT, "t3": T3_AT}[kind] + rest[0] * 2 + rest[1]


def tables(x, y):
    per_core = []
    for c in range(2):
        ops, begins, sends, at = [], [], 0, dict(EVENTS[CLASSES.index((x, y))])
        for point in range(POINTS):
            begins.append(len(ops))
            for event in at.get(point, ()):
                for op in expand(x, y, event):
                    if isinstance(op[0], str):
                        ops.append(slot(op, c) + 2097152 * WAIT)
                    else:
                        src, dst, way = op
                        ops.append(slot(src, c) + 128 * slot(dst, c) + 16384 * sends + 2097152 * WAYS.index(way))
                        sends += 1
        per_core.append((ops, begins + [len(ops), sends], sends))
    return per_core


TABLES = {cls: tables(*cls) for cls in CLASSES}
MOST_OPS = max(len(ops) for cores in TABLES.values() for ops, _, _ in cores)
MOST_SENDS = max(sends for cores in TABLES.values() for _, _, sends in cores)
FIRST_SENDS = 12


def columns(t):
    first, last = t * 256, (t + 1) * 256
    cuts = [first] + [cut for cut in range(0, NI * V, V) if first < cut < last] + [last]
    return [(u - first, w - first, u // V, u % V) for u, w in zip(cuts, cuts[1:])]


def kernel(dims, mine, amps, out, out_own, out_par, buf, rc, half, acc, ops, begins, devs,
           ssem, first_sem, rsem, local_sem):
    sym, tile, c = lax.axis_index("sym"), lax.axis_index("tile"), lax.axis_index("occ")
    x, yhi = sym % 4, sym // 4
    x0, x1 = x % 2, x // 2
    z, ylo = tile // 2, tile % 2
    z0, z1 = z % 2, z // 2
    y = 2 * yhi + ylo
    none = sym == 0

    def dev(dx=0, dy=0, dz=0, dc=0):
        xx, yy, zz = (x + 4 + dx) % 4, (y + 4 + dy) % 4, (z + 4 + dz) % 4
        return ((yy // 2) * 4 + xx) * 16 + (zz * 2 + yy % 2) * 2 + (c + dc) % 2

    step_a = 1 - 2 * (yhi + ylo - 2 * yhi * ylo)
    step_z = 1 - 2 * z0
    to = {
        "x+": dev(dx=1), "x-": dev(dx=-1), "y+": dev(dy=1), "y-": dev(dy=-1), "z+": dev(dz=1), "z-": dev(dz=-1),
        "core": dev(dc=1), "ya": dev(dy=step_a), "yb": dev(dy=-step_a), "za": dev(dz=step_z), "zb": dev(dz=-step_z),
    }
    barrier = pltpu.get_barrier_semaphore()
    for way in WAYS[:7]:
        pl.semaphore_signal(barrier, inc=1, device_id=to[way], device_id_type=pl.DeviceIdType.LOGICAL)

    def own_slot(q, core, k):
        return q * 4 + core * 2 + k

    keep = []
    for k in range(PIECES):
        keep.append(pltpu.make_async_copy(mine.at[pl.ds(k * PV, PV)], buf.at[own_slot(sym, c, k)], local_sem.at[8 + k]))
        keep[-1].start()
    loads = [pltpu.make_async_copy(amps.at[i], rc.at[:, pl.ds(i * V, V)], local_sem.at[i]) for i in range(NI)]
    for load in loads:
        load.start()

    pl.semaphore_wait(barrier, 7)

    def remote(src, dst_slot, sem, where):
        return pltpu.make_async_remote_copy(
            src, buf.at[dst_slot], sem, rsem.at[dst_slot], device_id=where, device_id_type=pl.DeviceIdType.LOGICAL
        )

    def arrived(at):
        remote(buf.at[at], at, first_sem.at[0], to["core"]).wait_recv()

    firsts = []

    def first(src, place, where, cond=None):
        index = len(firsts)
        if cond is None:
            remote(src, place, first_sem.at[index], where).start()
        else:
            pl.when(cond)(lambda: remote(src, place, first_sem.at[index], where).start())
        firsts.append((src, place, cond, index))

    step_2 = {k: {"+": to["z+"], "-": to["z-"]}[sign_of(0, k)] for k in range(PIECES)}
    for k in range(PIECES):
        src = mine.at[pl.ds(k * PV, PV)]
        home = own_slot(sym, c, k)
        final, via1, via2 = PAR_AT + home, T1_AT + k, T2_AT + k
        first(src, home, to["core"])
        first(src, home, to["x+"])
        first(src, home, to["x-"])
        first(src, TC_AT + k, to["y" + "+-"[k]])
        direct_b, direct_a = x0 + 2 * (1 - x1) + (1 - yhi) == 0, x0 + 2 * (1 - x1) + yhi == 0
        where_b = x1 * to["zb"] + (1 - x1) * step_2[k]
        place_b = jnp.where(direct_b, final, x1 * via2 + (1 - x1) * via1)
        first(src, place_b, where_b)
        where_a = x1 * to["za"] + (1 - x1) * to["ya"]
        place_a = jnp.where(direct_a | (x1 == 0), final, via1)
        first(src, place_a, where_a, x > 0)

    for (at_x, at_y), cores in TABLES.items():
        @pl.when((x == at_x) & (y == at_y))
        def _():
            (ops0, begins0, _), (ops1, _, _) = cores
            for n, (op0, op1) in enumerate(zip(ops0, ops1)):
                ops[n] = op0 + (op1 - op0) * c if op0 != op1 else op0
            for n, begin in enumerate(begins0):
                begins[n] = begin
    for n, way in enumerate(WAYS):
        devs[n] = to[way]

    n_row = dims[tile]
    n_col = dims[(z1 + yhi - 2 * z1 * yhi) * 4 + (z0 + x1 - 2 * z0 * x1) * 2 + (ylo + x0 - 2 * ylo * x0)]
    live_r = jnp.where(lax.broadcasted_iota(jnp.int32, (V, V), 0) < n_row, 1.0, 0.0)
    live = jnp.where(lax.broadcasted_iota(jnp.int32, (V, V), 1) < n_col, live_r, 0.0).astype(jnp.bfloat16)
    acc[...] = jnp.zeros_like(acc)
    for load in loads:
        load.wait()
    for i in range(NI):
        rc[:, i * V:(i + 1) * V] = rc[:, i * V:(i + 1) * V] * live
    for copy in keep:
        copy.wait()

    def decoded(n):
        op = ops[n]
        src, rest = lax.rem(op, 128), lax.div(op, 128)
        dst, rest = lax.rem(rest, 128), lax.div(rest, 128)
        return src, dst, lax.rem(rest, 128), lax.div(rest, 128)

    def events(point):
        @pl.loop(begins[point], begins[point + 1])
        def _(n):
            src, dst, index, way = decoded(n)

            @pl.when(way == WAIT)
            def _():
                arrived(src)

            @pl.when(way != WAIT)
            def _():
                remote(buf.at[src], dst, ssem.at[index], devs[way]).start()

    digit = (1 + 15 * x0) * (1 + 255 * x1)

    def chosen(groups, n):
        code = 0
        for number, names in enumerate(groups):
            of_y = [0] * 4
            for (at_x, at_y), (row, j, k) in zip(CLASSES, names):
                of_y[at_y] += (row * 8 + j * 2 + k) * 16 ** at_x
            value = of_y[0]
            if len(set(of_y)) > 1:
                value = value + (of_y[1] - of_y[0]) * ylo + (of_y[2] - of_y[0]) * yhi
                value = value + (of_y[3] - of_y[2] - of_y[1] + of_y[0]) * (yhi * ylo)
            code = code + (n == number) * 1 * value
        code = lax.rem(lax.div(code, digit), 16)
        return (yhi + code // 8) % 2 * 4 + (x + 4 - code // 2 % 4) % 4, code % 2

    def base_of(n):
        return sum((n == number) * base for number, base in enumerate(BASES[:-1]) if base)

    par_base = PAR_AT * (1 - (sym == 0) * 1)

    def unit(base, q, core):
        at = base + q * 4 + core * 2
        return buf[pl.ds(at, 2)].reshape(V, V)

    def first_stage(base, halves, parts):
        for q, k in halves:
            arrived(own_slot(q, 1 - c, k))
        for h in range(parts):
            if h:
                events(base + h)
            for t in range(h * 12 // parts, (h + 1) * 12 // parts):
                left = jnp.concatenate([buf[q * 4 + 2 * p + k] for q, k in halves for p in range(2)], axis=0)
                r = jnp.dot(left, rc[:, t * 256:(t + 1) * 256], preferred_element_type=jnp.float32).astype(jnp.bfloat16)
                for lo_col, hi_col, pair, at in columns(t):
                    for number, (q, k) in enumerate(halves):
                        rows = pl.ds(pl.multiple_of(pair * V + k * PV, PV), PV)
                        for p in range(2):
                            lanes = pl.ds(p * V + at, hi_col - lo_col)
                            first = (2 * number + p) * PV
                            half[q, rows, lanes] = r[first:first + PV, lo_col:hi_col]

    def second_stage(base, q):
        @pl.when(jnp.logical_not(none))
        def _():
            for k in range(PIECES):
                arrived(PAR_AT + own_slot(q, 1 - c, k))

        for h in range(2):
            if h and PARTS[2] > 1:
                events(base + h)
            rows = pl.ds(h * HALF, HALF)
            for b0, b1 in ((0, 256), (256, 384)):
                right = jnp.concatenate([unit(par_base, q, p)[b0:b1] for p in range(2)], axis=1)
                acc[rows, b0:b1] += lax.dot_general(
                    half[q, rows, :], right, (((1,), (1,)), ((), ())), preferred_element_type=jnp.float32
                )

    @pl.loop(0, STAGES)
    def _(n):
        kind = sum((n == k) * 1 * stage for k, stage in enumerate(SEQUENCE))
        halves = [chosen(group, n) for group in UNITS]
        base = base_of(n)
        events(base)
        for stage in set(SEQUENCE) - {2}:
            pl.when(kind == stage)(lambda stage=stage: first_stage(base, halves, PARTS[stage]))
        pl.when(kind == 2)(lambda: second_stage(base, halves[0][0]))

    for h in range(2):
        rows = pl.ds(h * HALF, HALF)
        pltpu.make_async_copy(acc.at[rows], out.at[rows], local_sem.at[h]).start()
    events(POINTS - 1)

    leaving = []
    for r in range(len(REST)):
        q, _ = chosen(REST, jnp.int32(r))
        for k in range(PIECES):
            arrived(own_slot(q, 1 - c, k))

        @pl.when(jnp.logical_not(none))
        def _():
            for k in range(PIECES):
                arrived(PAR_AT + own_slot(q, 1 - c, k))

        par_at = par_base + q * 4
        for source, target, sem in ((q * 4, out_own.at[r], 18 + 2 * r), (par_at, out_par.at[r], 19 + 2 * r)):
            leaving.append(pltpu.make_async_copy(buf.at[pl.ds(source, 4)], target, local_sem.at[sem - 8]))
            leaving[-1].start()

    for src, place, cond, index in firsts:
        def sent(src=src, place=place, index=index):
            remote(src, place, first_sem.at[index], to["core"]).wait_send()

        if cond is None:
            sent()
        else:
            pl.when(cond)(sent)

    @pl.loop(0, begins[POINTS + 1])
    def _(n):
        remote(buf.at[0], 0, ssem.at[n], to["core"]).wait_send()

    for h in range(2):
        rows = pl.ds(h * HALF, HALF)
        pltpu.make_async_copy(acc.at[rows], out.at[rows], local_sem.at[h]).wait()
    for copy in leaving:
        copy.wait()


ALL = [(row, j) for j in (0, 1, 3, 2) for row in range(2)]


def left_over():
    by_class = []
    for at in range(len(CLASSES)):
        done = [names[at][:2] for group in UNITS for stage, names in zip(SEQUENCE, group) if stage != 2]
        by_class.append([name + (0,) for name in ALL if name not in done])
    return tuple(zip(*by_class))


REST = left_over()


def rest_kernel(dims, own_hbm, par_hbm, amps, raw, out, own, par, rc, half, acc, sems):
    sym, tile = lax.axis_index("sym"), lax.axis_index("tile")
    n, hi = len(REST), NI // 2
    get_own = pltpu.make_async_copy(own_hbm, own, sems.at[0])
    get_par = pltpu.make_async_copy(par_hbm, par, sems.at[1])
    get_amps = [pltpu.make_async_copy(amps.at[i], rc.at[:, pl.ds(i * V, V)], sems.at[2 + i]) for i in range(NI)]
    get_raw = [
        pltpu.make_async_copy(raw.at[pl.ds(h * HALF, HALF)], acc.at[pl.ds(h * HALF, HALF)], sems.at[2 + NI + h])
        for h in range(2)
    ]
    for copy in get_amps[:hi] + [get_own, get_par, get_raw[0]] + get_amps[hi:] + [get_raw[1]]:
        copy.start()
    n_row, n_col = dims[tile], dims[jnp.bitwise_xor(tile, sym)]
    live = (lax.broadcasted_iota(jnp.int32, (V, V), 0) < n_row) & (lax.broadcasted_iota(jnp.int32, (V, V), 1) < n_col)
    live_b = jnp.where(live, 1.0, 0.0).astype(jnp.bfloat16)
    puts = []
    for h in range(2):
        for i in range(h * hi, (h + 1) * hi):
            get_amps[i].wait()
            rc[:, i * V:(i + 1) * V] = rc[:, i * V:(i + 1) * V] * live_b
        if h == 0:
            get_own.wait()
        for t in range(6 * h, 6 * (h + 1)):
            left = own[...].reshape(n * 2 * V, V)
            r = jnp.dot(left, rc[:, t * 256:(t + 1) * 256], preferred_element_type=jnp.float32).astype(jnp.bfloat16)
            for lo_col, hi_col, pair, at in columns(t):
                for p in range(2 * n):
                    lanes = pl.ds(p * V + at, hi_col - lo_col)
                    half[(pair - h * hi) * V:(pair - h * hi + 1) * V, lanes] = r[p * V:(p + 1) * V, lo_col:hi_col]
        if h == 0:
            get_par.wait()
        get_raw[h].wait()
        rows = pl.ds(h * HALF, HALF)
        for b0, b1 in ((0, 256), (256, 384)):
            right = [par[r, pl.ds(2 * p, 2)].reshape(V, V)[b0:b1] for r in range(n) for p in range(2)]
            right = jnp.concatenate(right, axis=1)
            r = lax.dot_general(half[...], right, (((1,), (1,)), ((), ())), preferred_element_type=jnp.float32)
            r = r + acc[rows, b0:b1]
            for i in range(hi):
                at = pl.ds((h * hi + i) * V, V)
                acc[at, b0:b1] = jnp.where(live[:, b0:b1], r[i * V:(i + 1) * V], 0.0)
            lanes = pl.ds(b0, b1 - b0)
            puts.append(pltpu.make_async_copy(acc.at[rows, lanes], out.at[rows, lanes], sems.at[4 + NI + len(puts)]))
            puts[-1].start()
    for copy in puts:
        copy.wait()


def shards(irrep_dims, chol_vectors, amplitudes):
    bf, sem = jnp.bfloat16, pltpu.SemaphoreType.DMA
    n = len(REST)
    own, chol, amps = (n, 4, PV, V), chol_vectors.reshape(V, V), amplitudes.reshape(NI, V, V)
    anywhere = pl.BlockSpec(memory_space=pl.ANY)
    raw, rest_own, rest_par = pl.pallas_call(
        kernel,
        out_shape=[
            jax.ShapeDtypeStruct((NI * V, V), jnp.float32),
            jax.ShapeDtypeStruct(own, bf),
            jax.ShapeDtypeStruct(own, bf),
        ],
        in_specs=[pl.BlockSpec(memory_space=pltpu.SMEM), anywhere, anywhere],
        out_specs=[anywhere] * 3,
        scratch_shapes=[
            pltpu.VMEM((SLOTS, PV, V), bf),
            pltpu.VMEM((V, NI * V), bf),
            pltpu.VMEM((8, NI * V, 2 * V), bf),
            pltpu.VMEM((NI * V, V), jnp.float32),
            pltpu.SMEM((MOST_OPS,), jnp.int32),
            pltpu.SMEM((POINTS + 2,), jnp.int32),
            pltpu.SMEM((len(WAYS),), jnp.int32),
            sem((MOST_SENDS,)), sem((FIRST_SENDS,)), sem((SLOTS,)), sem((10 + 2 * n,)),
        ],
        compiler_params=pltpu.CompilerParams(
            collective_id=0, has_side_effects=True, vmem_limit_bytes=63 * 1024 * 1024
        ),
        cost_estimate=pl.CostEstimate(flops=(8 - n) * 3_600_000_000, bytes_accessed=12_000_000, transcendentals=0),
        name="ladder",
    )(irrep_dims, chol, amps)
    total = pl.pallas_call(
        rest_kernel,
        out_shape=jax.ShapeDtypeStruct((NI * V, V), jnp.float32),
        in_specs=[pl.BlockSpec(memory_space=pltpu.SMEM)] + [anywhere] * 4,
        out_specs=anywhere,
        scratch_shapes=[
            pltpu.VMEM(own, bf),
            pltpu.VMEM(own, bf),
            pltpu.VMEM((V, NI * V), bf),
            pltpu.VMEM((HALF, n * 2 * V), bf),
            pltpu.VMEM((NI * V, V), jnp.float32),
            sem((8 + NI,)),
        ],
        compiler_params=pltpu.CompilerParams(vmem_limit_bytes=60 * 1024 * 1024),
        cost_estimate=pl.CostEstimate(flops=n * 3_600_000_000, bytes_accessed=16_000_000, transcendentals=0),
        name="rest",
    )(irrep_dims, rest_own, rest_par, amps, raw)
    return total.reshape(1, NI, V, V)


def solution(mesh):
    return jax.shard_map(
        shards,
        mesh=mesh,
        in_specs=(P(), P(("sym", "occ"), "tile", None), P("sym", "occ", "tile", None)),
        out_specs=P("sym", "occ", "tile", None),
        check_vma=False,
    )
```

```python
import jax
import jax.numpy as jnp
from jax import lax
from jax.experimental import pallas as pl
from jax.experimental.pallas import tpu as pltpu
from jax.sharding import PartitionSpec as P

V = 384
NI = 8
PIECES = 2
PV = V // PIECES
HALF = NI * V // 2
CROSSF, OWN, PASS_Z, FWD_Y, PASS_Y, PAR = range(6)
PARTS = {1: 2, 2: 1}
SEQUENCE = (1, 1, 1, 1, 1, 2, 1, 2, 1, 2, 2, 2, 2, 2)
UNITS = (
    (
        ((0, 0, 0), (0, 0, 0), (0, 0, 0), (0, 0, 0), (0, 0, 0), (0, 0, 0), (0, 0, 0), (0, 0, 0), (0, 0, 0), (0, 0, 0), (0, 0, 0), (0, 0, 0), (0, 0, 0), (0, 0, 0), (0, 0, 0), (0, 0, 0)),
        ((0, 1, 0), (0, 1, 0), (0, 1, 0), (0, 1, 0), (0, 1, 0), (0, 1, 0), (0, 1, 0), (0, 1, 0), (0, 1, 0), (0, 1, 0), (0, 1, 0), (0, 1, 0), (0, 1, 0), (0, 1, 0), (0, 1, 0), (0, 1, 0)),
        ((0, 1, 1), (0, 1, 1), (0, 1, 1), (0, 1, 1), (0, 1, 1), (0, 1, 1), (0, 1, 1), (0, 1, 1), (0, 1, 1), (0, 1, 1), (0, 1, 1), (0, 1, 1), (0, 1, 1), (0, 1, 1), (0, 1, 1), (0, 1, 1)),
        ((1, 0, 0), (1, 0, 0), (1, 0, 0), (1, 0, 0), (0, 2, 0), (0, 2, 0), (1, 0, 0), (1, 0, 0), (1, 0, 0), (1, 0, 0), (1, 0, 0), (1, 0, 0), (1, 0, 0), (1, 0, 0), (1, 0, 0), (1, 0, 0)),
        ((0, 2, 0), (0, 2, 0), (0, 2, 0), (0, 2, 0), (1, 0, 0), (1, 0, 0), (0, 2, 0), (1, 0, 1), (0, 2, 0), (0, 2, 0), (0, 2, 0), (0, 2, 0), (0, 2, 0), (0, 2, 0), (0, 2, 0), (0, 2, 0)),
        ((0, 0, 0), (0, 0, 0), (0, 0, 0), (0, 0, 0), (0, 0, 0), (0, 0, 0), (1, 0, 0), (1, 0, 0), (0, 0, 0), (0, 0, 0), (0, 0, 0), (0, 0, 0), (0, 0, 0), (0, 0, 0), (0, 0, 0), (0, 0, 0)),
        ((1, 1, 0), (1, 1, 0), (1, 1, 0), (1, 1, 0), (1, 3, 0), (1, 1, 0), (1, 1, 0), (1, 1, 0), (1, 3, 0), (1, 3, 0), (1, 1, 0), (1, 1, 0), (1, 1, 0), (1, 1, 0), (1, 1, 0), (1, 1, 0)),
        ((1, 0, 0), (1, 0, 0), (1, 0, 0), (1, 0, 0), (0, 1, 0), (1, 0, 0), (0, 0, 0), (0, 0, 0), (1, 0, 0), (1, 0, 0), (1, 0, 0), (1, 0, 0), (1, 0, 0), (1, 0, 0), (1, 0, 0), (1, 0, 0)),
        ((1, 3, 0), (1, 3, 0), (1, 1, 1), (1, 1, 1), (1, 0, 1), (1, 1, 1), (1, 1, 1), (1, 1, 1), (1, 1, 0), (1, 1, 0), (1, 1, 1), (1, 1, 1), (1, 1, 1), (1, 1, 1), (1, 1, 1), (1, 1, 1)),
        ((0, 1, 0), (0, 1, 0), (0, 1, 0), (0, 1, 0), (1, 0, 0), (0, 1, 0), (0, 1, 0), (0, 1, 0), (0, 1, 0), (0, 1, 0), (0, 1, 0), (0, 1, 0), (0, 1, 0), (0, 1, 0), (0, 1, 0), (0, 1, 0)),
        ((1, 1, 0), (1, 1, 0), (0, 3, 0), (0, 3, 0), (1, 1, 0), (1, 1, 0), (1, 1, 0), (1, 1, 0), (1, 1, 0), (1, 1, 0), (1, 1, 0), (1, 1, 0), (1, 1, 0), (1, 1, 0), (1, 1, 0), (1, 1, 0)),
        ((0, 3, 0), (0, 3, 0), (0, 2, 0), (0, 2, 0), (0, 3, 0), (0, 3, 0), (0, 3, 0), (0, 3, 0), (0, 3, 0), (0, 3, 0), (0, 3, 0), (0, 3, 0), (0, 3, 0), (0, 3, 0), (0, 3, 0), (0, 3, 0)),
        ((1, 3, 0), (1, 3, 0), (1, 3, 0), (1, 1, 0), (1, 3, 0), (1, 3, 0), (1, 3, 0), (1, 3, 0), (1, 3, 0), (1, 3, 0), (1, 3, 0), (1, 3, 0), (1, 3, 0), (1, 3, 0), (1, 3, 0), (1, 3, 0)),
        ((0, 2, 0), (0, 2, 0), (1, 1, 0), (1, 3, 0), (0, 2, 0), (0, 2, 0), (0, 2, 0), (0, 2, 0), (0, 2, 0), (0, 2, 0), (0, 2, 0), (0, 2, 0), (0, 2, 0), (0, 2, 0), (0, 2, 0), (0, 2, 0)),
    ),
    (
        ((0, 0, 1), (0, 0, 1), (0, 0, 1), (0, 0, 1), (0, 0, 1), (0, 0, 1), (0, 0, 1), (0, 0, 1), (0, 0, 1), (0, 0, 1), (0, 0, 1), (0, 0, 1), (0, 0, 1), (0, 0, 1), (0, 0, 1), (0, 0, 1)),
        ((0, 3, 0), (0, 3, 0), (0, 3, 0), (0, 3, 0), (0, 3, 0), (0, 3, 0), (0, 3, 0), (0, 3, 0), (0, 3, 0), (0, 3, 0), (0, 3, 0), (0, 3, 0), (0, 3, 0), (0, 3, 0), (0, 3, 0), (0, 3, 0)),
        ((0, 3, 1), (0, 3, 1), (0, 3, 1), (0, 3, 1), (0, 3, 1), (0, 3, 1), (0, 3, 1), (0, 3, 1), (0, 3, 1), (0, 3, 1), (0, 3, 1), (0, 3, 1), (0, 3, 1), (0, 3, 1), (0, 3, 1), (0, 3, 1)),
        ((1, 0, 1), (1, 0, 1), (1, 0, 1), (1, 0, 1), (0, 2, 1), (0, 2, 1), (1, 0, 1), (0, 2, 0), (1, 0, 1), (1, 0, 1), (1, 0, 1), (1, 0, 1), (1, 0, 1), (1, 0, 1), (1, 0, 1), (1, 0, 1)),
        ((0, 2, 1), (0, 2, 1), (0, 2, 1), (0, 2, 1), (1, 1, 0), (1, 0, 1), (0, 2, 1), (0, 2, 1), (0, 2, 1), (0, 2, 1), (0, 2, 1), (0, 2, 1), (0, 2, 1), (0, 2, 1), (0, 2, 1), (0, 2, 1)),
        ((0, 0, 0), (0, 0, 0), (0, 0, 0), (0, 0, 0), (0, 0, 0), (0, 0, 0), (1, 0, 0), (1, 0, 0), (0, 0, 0), (0, 0, 0), (0, 0, 0), (0, 0, 0), (0, 0, 0), (0, 0, 0), (0, 0, 0), (0, 0, 0)),
        ((1, 1, 1), (1, 1, 1), (1, 3, 0), (1, 3, 0), (1, 1, 1), (1, 3, 0), (1, 3, 0), (1, 3, 0), (1, 3, 1), (1, 3, 1), (1, 3, 0), (1, 3, 0), (1, 3, 0), (1, 3, 0), (1, 3, 0), (1, 3, 0)),
        ((1, 0, 0), (1, 0, 0), (1, 0, 0), (1, 0, 0), (0, 1, 0), (1, 0, 0), (0, 0, 0), (0, 0, 0), (1, 0, 0), (1, 0, 0), (1, 0, 0), (1, 0, 0), (1, 0, 0), (1, 0, 0), (1, 0, 0), (1, 0, 0)),
        ((1, 3, 1), (1, 3, 1), (1, 3, 1), (1, 3, 1), (1, 3, 1), (1, 3, 1), (1, 3, 1), (1, 3, 1), (1, 1, 1), (1, 1, 1), (1, 3, 1), (1, 3, 1), (1, 3, 1), (1, 3, 1), (1, 3, 1), (1, 3, 1)),
        ((0, 1, 0), (0, 1, 0), (0, 1, 0), (0, 1, 0), (1, 0, 0), (0, 1, 0), (0, 1, 0), (0, 1, 0), (0, 1, 0), (0, 1, 0), (0, 1, 0), (0, 1, 0), (0, 1, 0), (0, 1, 0), (0, 1, 0), (0, 1, 0)),
        ((1, 1, 0), (1, 1, 0), (0, 3, 0), (0, 3, 0), (1, 1, 0), (1, 1, 0), (1, 1, 0), (1, 1, 0), (1, 1, 0), (1, 1, 0), (1, 1, 0), (1, 1, 0), (1, 1, 0), (1, 1, 0), (1, 1, 0), (1, 1, 0)),
        ((0, 3, 0), (0, 3, 0), (0, 2, 0), (0, 2, 0), (0, 3, 0), (0, 3, 0), (0, 3, 0), (0, 3, 0), (0, 3, 0), (0, 3, 0), (0, 3, 0), (0, 3, 0), (0, 3, 0), (0, 3, 0), (0, 3, 0), (0, 3, 0)),
        ((1, 3, 0), (1, 3, 0), (1, 3, 0), (1, 1, 0), (1, 3, 0), (1, 3, 0), (1, 3, 0), (1, 3, 0), (1, 3, 0), (1, 3, 0), (1, 3, 0), (1, 3, 0), (1, 3, 0), (1, 3, 0), (1, 3, 0), (1, 3, 0)),
        ((0, 2, 0), (0, 2, 0), (1, 1, 0), (1, 3, 0), (0, 2, 0), (0, 2, 0), (0, 2, 0), (0, 2, 0), (0, 2, 0), (0, 2, 0), (0, 2, 0), (0, 2, 0), (0, 2, 0), (0, 2, 0), (0, 2, 0), (0, 2, 0)),
    ),
)
EVENTS = (
    (
        (2, ((CROSSF, 0), (CROSSF, 1), (OWN, 0, 1, 0), (OWN, 0, 3, 0), (PASS_Z, 0, 0), (PASS_Z, 0, 1),)),
        (3, ((OWN, 0, 1, 1), (OWN, 0, 3, 1),)),
        (4, ((OWN, 1, 0, 0), (OWN, 1, 0, 1), (PASS_Z, 1, 0), (PASS_Z, 3, 0),)),
        (5, ((OWN, 0, 2, 0),)),
        (6, ((OWN, 0, 2, 1), (FWD_Y, 0, 0), (FWD_Y, 0, 1),)),
        (8, ((OWN, 1, 1, 0), (PASS_Z, 1, 1), (PASS_Z, 3, 1),)),
        (9, ((PASS_Y, 0, 1),)),
        (10, ((OWN, 1, 1, 1),)),
        (11, ((OWN, 1, 3, 0), (FWD_Y, 1, 0), (FWD_Y, 3, 0),)),
        (12, ((OWN, 1, 2, 1), (PASS_Z, 2, 0), (PASS_Z, 2, 1),)),
        (13, ((OWN, 1, 2, 0),)),
        (14, ((FWD_Y, 1, 1), (FWD_Y, 3, 1), (PASS_Y, 1, 0), (OWN, 1, 3, 1),)),
        (15, ((FWD_Y, 2, 0), (FWD_Y, 2, 1),)),
        (17, ((PASS_Y, 3, 1),)),
        (18, ((PASS_Y, 2, 0),)),
    ),
    (
        (2, ((CROSSF, 0), (CROSSF, 1), (OWN, 0, 1, 0), (OWN, 0, 3, 0), (PASS_Z, 0, 0), (PASS_Z, 0, 1),)),
        (3, ((OWN, 0, 1, 1), (OWN, 0, 3, 1),)),
        (4, ((OWN, 1, 0, 0), (OWN, 1, 0, 1), (PASS_Z, 1, 0), (PASS_Z, 3, 0),)),
        (5, ((OWN, 0, 2, 0),)),
        (6, ((OWN, 0, 2, 1), (FWD_Y, 0, 0), (FWD_Y, 0, 1),)),
        (8, ((OWN, 1, 1, 0), (PASS_Z, 1, 1), (PASS_Z, 3, 1),)),
        (9, ((PASS_Y, 0, 0),)),
        (10, ((OWN, 1, 1, 1),)),
        (11, ((OWN, 1, 3, 0), (FWD_Y, 1, 0), (FWD_Y, 3, 0),)),
        (12, ((OWN, 1, 2, 1), (PASS_Z, 2, 0), (PASS_Z, 2, 1),)),
        (13, ((OWN, 1, 3, 1),)),
        (14, ((OWN, 1, 2, 0), (FWD_Y, 1, 1), (FWD_Y, 3, 1), (PASS_Y, 3, 0),)),
        (16, ((FWD_Y, 2, 0), (FWD_Y, 2, 1),)),
        (17, ((PASS_Y, 1, 1),)),
        (18, ((PASS_Y, 2, 1),)),
    ),
    (
        (2, ((CROSSF, 0), (CROSSF, 1), (OWN, 0, 1, 0), (OWN, 0, 3, 0), (PASS_Z, 0, 0), (PASS_Z, 0, 1),)),
        (3, ((OWN, 0, 1, 1), (OWN, 0, 3, 1),)),
        (4, ((OWN, 1, 0, 0), (OWN, 1, 0, 1), (PASS_Z, 1, 0), (PASS_Z, 3, 0),)),
        (5, ((OWN, 0, 2, 0),)),
        (6, ((OWN, 0, 2, 1), (PAR, 0, 0, 0), (PAR, 0, 0, 1),)),
        (8, ((OWN, 1, 1, 0), (OWN, 1, 3, 0), (PASS_Z, 1, 1), (PASS_Z, 3, 1),)),
        (9, ((PASS_Y, 0, 0),)),
        (10, ((OWN, 1, 1, 1),)),
        (11, ((OWN, 1, 3, 1), (PAR, 0, 1, 0), (PAR, 0, 3, 0),)),
        (12, ((OWN, 1, 2, 0), (OWN, 1, 2, 1), (PASS_Z, 2, 0), (PASS_Z, 2, 1), (PAR, 1, 0, 0), (PAR, 1, 0, 1),)),
        (13, ((PAR, 0, 3, 1), (PAR, 0, 1, 1),)),
        (14, ((PASS_Y, 3, 0),)),
        (15, ((PAR, 0, 2, 0), (PAR, 0, 2, 1),)),
        (17, ((PASS_Y, 1, 1), (PAR, 1, 1, 0),)),
        (18, ((PAR, 1, 3, 0),)),
        (19, ((PASS_Y, 2, 1), (PAR, 1, 3, 1),)),
        (20, ((PAR, 1, 1, 1), (PAR, 1, 2, 0),)),
        (21, ((PAR, 1, 2, 1),)),
    ),
    (
        (2, ((CROSSF, 0), (CROSSF, 1), (OWN, 0, 1, 0), (OWN, 0, 3, 0), (PASS_Z, 0, 0), (PASS_Z, 0, 1),)),
        (3, ((OWN, 0, 1, 1), (OWN, 0, 3, 1),)),
        (4, ((OWN, 1, 0, 0), (OWN, 1, 0, 1), (PASS_Z, 1, 0), (PASS_Z, 3, 0),)),
        (5, ((OWN, 0, 2, 0),)),
        (6, ((OWN, 0, 2, 1), (PAR, 0, 0, 0), (PAR, 0, 0, 1),)),
        (8, ((OWN, 1, 1, 0), (OWN, 1, 3, 0), (PASS_Z, 1, 1), (PASS_Z, 3, 1),)),
        (9, ((PASS_Y, 0, 1),)),
        (10, ((OWN, 1, 1, 1),)),
        (11, ((OWN, 1, 3, 1), (PAR, 0, 1, 0), (PAR, 0, 3, 0),)),
        (12, ((OWN, 1, 2, 0), (OWN, 1, 2, 1), (PASS_Z, 2, 0), (PASS_Z, 2, 1), (PAR, 1, 0, 0), (PAR, 1, 0, 1),)),
        (13, ((PAR, 0, 3, 1), (PAR, 0, 1, 1),)),
        (14, ((PASS_Y, 1, 0),)),
        (15, ((PAR, 0, 2, 0), (PAR, 0, 2, 1),)),
        (17, ((PASS_Y, 3, 1), (PAR, 1, 3, 0),)),
        (18, ((PAR, 1, 1, 0),)),
        (19, ((PASS_Y, 2, 0), (PAR, 1, 1, 1),)),
        (20, ((PAR, 1, 3, 1), (PAR, 1, 2, 1),)),
        (21, ((PAR, 1, 2, 0),)),
    ),
    (
        (2, ((CROSSF, 0), (OWN, 0, 1, 0), (OWN, 0, 3, 0), (PASS_Z, 0, 0), (PASS_Z, 0, 1), (PAR, 0, 0, 0),)),
        (3, ((CROSSF, 1), (OWN, 0, 1, 1), (OWN, 0, 3, 1), (PAR, 1, 0, 0),)),
        (4, ((PASS_Z, 1, 0), (PASS_Z, 3, 0),)),
        (5, ((OWN, 0, 2, 0), (PAR, 0, 0, 1), (PAR, 1, 0, 1),)),
        (6, ((OWN, 0, 2, 1), (FWD_Y, 0, 0), (FWD_Y, 0, 1),)),
        (7, ((OWN, 1, 0, 0), (OWN, 1, 1, 0), (PAR, 0, 1, 0),)),
        (8, ((OWN, 1, 3, 0), (PASS_Z, 1, 1), (PASS_Z, 3, 1),)),
        (9, ((OWN, 1, 1, 1), (PAR, 0, 3, 0), (PAR, 1, 1, 0),)),
        (10, ((OWN, 1, 3, 1), (FWD_Y, 1, 0), (FWD_Y, 3, 0),)),
        (11, ((OWN, 1, 0, 1), (OWN, 1, 2, 0), (PASS_Z, 2, 0), (PASS_Z, 2, 1), (PAR, 1, 3, 0),)),
        (12, ((OWN, 1, 2, 1), (PAR, 0, 1, 1), (PAR, 1, 1, 1),)),
        (13, ((FWD_Y, 1, 1), (FWD_Y, 3, 1),)),
        (14, ((FWD_Y, 2, 0), (PAR, 0, 3, 1), (PAR, 1, 3, 1),)),
        (15, ((FWD_Y, 2, 1),)),
        (16, ((PAR, 0, 2, 0), (PAR, 1, 2, 0),)),
        (17, ((PAR, 0, 2, 1), (PAR, 1, 2, 1),)),
    ),
    (
        (2, ((CROSSF, 0), (OWN, 0, 1, 0), (OWN, 0, 3, 0), (PASS_Z, 0, 0), (PASS_Z, 0, 1), (PAR, 1, 0, 0),)),
        (3, ((CROSSF, 1), (OWN, 0, 1, 1), (OWN, 0, 3, 1), (PAR, 0, 0, 0),)),
        (4, ((PASS_Z, 1, 0), (PASS_Z, 3, 0),)),
        (5, ((OWN, 0, 2, 0), (PAR, 0, 0, 1), (PAR, 1, 0, 1),)),
        (6, ((OWN, 0, 2, 1), (FWD_Y, 0, 0), (FWD_Y, 0, 1),)),
        (7, ((OWN, 1, 0, 0), (OWN, 1, 0, 1), (OWN, 1, 1, 0),)),
        (8, ((OWN, 1, 3, 0), (PASS_Z, 1, 1), (PASS_Z, 3, 1),)),
        (9, ((OWN, 1, 1, 1), (PAR, 0, 1, 0), (PAR, 1, 1, 0),)),
        (10, ((OWN, 1, 3, 1), (FWD_Y, 1, 0), (FWD_Y, 3, 0),)),
        (11, ((OWN, 1, 2, 0), (OWN, 1, 2, 1), (PASS_Z, 2, 0), (PASS_Z, 2, 1), (PAR, 0, 3, 0), (PAR, 1, 3, 0),)),
        (12, ((PAR, 0, 1, 1), (PAR, 1, 1, 1),)),
        (13, ((FWD_Y, 1, 1), (FWD_Y, 3, 1),)),
        (14, ((FWD_Y, 2, 0), (FWD_Y, 2, 1), (PAR, 0, 3, 1), (PAR, 1, 3, 1),)),
        (16, ((PAR, 0, 2, 0), (PAR, 1, 2, 0),)),
        (17, ((PAR, 0, 2, 1), (PAR, 1, 2, 1),)),
    ),
    (
        (2, ((CROSSF, 0), (CROSSF, 1), (OWN, 0, 1, 0), (OWN, 0, 3, 0), (PASS_Z, 0, 0), (PASS_Z, 0, 1),)),
        (3, ((OWN, 0, 1, 1), (OWN, 0, 3, 1),)),
        (4, ((OWN, 1, 0, 0), (OWN, 1, 0, 1), (PASS_Z, 1, 0), (PASS_Z, 3, 0),)),
        (5, ((OWN, 0, 2, 0),)),
        (6, ((OWN, 0, 2, 1), (FWD_Y, 0, 0), (FWD_Y, 0, 1),)),
        (7, ((OWN, 1, 1, 0),)),
        (8, ((OWN, 1, 3, 0), (PASS_Z, 1, 1), (PASS_Z, 3, 1),)),
        (9, ((OWN, 1, 1, 1), (PAR, 0, 0, 0), (PAR, 1, 0, 0),)),
        (10, ((OWN, 1, 3, 1), (FWD_Y, 1, 0), (FWD_Y, 3, 0), (PAR, 1, 0, 1), (PAR, 0, 0, 1),)),
        (11, ((OWN, 1, 2, 0), (OWN, 1, 2, 1), (PASS_Z, 2, 0), (PASS_Z, 2, 1), (PAR, 0, 1, 0),)),
        (12, ((FWD_Y, 1, 1), (FWD_Y, 3, 1), (PAR, 1, 1, 0),)),
        (13, ((PAR, 0, 3, 0),)),
        (14, ((FWD_Y, 2, 0), (FWD_Y, 2, 1), (PAR, 1, 3, 0),)),
        (15, ((PAR, 0, 1, 1), (PAR, 1, 1, 1),)),
        (17, ((PAR, 0, 3, 1), (PAR, 1, 3, 1),)),
        (18, ((PAR, 0, 2, 0), (PAR, 1, 2, 0),)),
        (19, ((PAR, 0, 2, 1),)),
        (20, ((PAR, 1, 2, 1),)),
    ),
    (
        (2, ((CROSSF, 0), (CROSSF, 1), (OWN, 0, 1, 0), (OWN, 0, 3, 0), (PASS_Z, 0, 0), (PASS_Z, 0, 1),)),
        (3, ((OWN, 0, 1, 1), (OWN, 0, 3, 1),)),
        (4, ((OWN, 1, 0, 0), (PASS_Z, 1, 0), (PASS_Z, 3, 0),)),
        (5, ((OWN, 0, 2, 0),)),
        (6, ((OWN, 0, 2, 1), (OWN, 1, 0, 1), (FWD_Y, 0, 0), (FWD_Y, 0, 1),)),
        (7, ((OWN, 1, 1, 0),)),
        (8, ((OWN, 1, 3, 0), (PASS_Z, 1, 1), (PASS_Z, 3, 1),)),
        (9, ((OWN, 1, 1, 1), (PAR, 0, 0, 0), (PAR, 1, 0, 0),)),
        (10, ((OWN, 1, 3, 1), (FWD_Y, 1, 0), (FWD_Y, 3, 0), (PAR, 1, 0, 1), (PAR, 0, 0, 1),)),
        (11, ((OWN, 1, 2, 0), (OWN, 1, 2, 1), (PASS_Z, 2, 0), (PASS_Z, 2, 1), (PAR, 0, 1, 0),)),
        (12, ((FWD_Y, 1, 1), (FWD_Y, 3, 1), (PAR, 1, 1, 0),)),
        (13, ((PAR, 0, 3, 0),)),
        (14, ((FWD_Y, 2, 0), (FWD_Y, 2, 1), (PAR, 1, 3, 0),)),
        (15, ((PAR, 0, 1, 1), (PAR, 1, 1, 1),)),
        (17, ((PAR, 0, 3, 1), (PAR, 1, 3, 1),)),
        (18, ((PAR, 0, 2, 0), (PAR, 1, 2, 0),)),
        (19, ((PAR, 0, 2, 1),)),
        (20, ((PAR, 1, 2, 1),)),
    ),
    (
        (2, ((CROSSF, 0), (CROSSF, 1), (OWN, 0, 1, 0), (OWN, 0, 3, 0), (FWD_Y, 0, 0), (PAR, 0, 0, 0),)),
        (3, ((OWN, 0, 1, 1), (OWN, 0, 3, 1), (FWD_Y, 0, 1), (PAR, 0, 0, 1),)),
        (4, ((OWN, 1, 0, 0), (OWN, 1, 0, 1),)),
        (5, ((OWN, 0, 2, 0), (FWD_Y, 1, 0), (PAR, 0, 1, 0),)),
        (6, ((OWN, 0, 2, 1), (PASS_Y, 0, 0), (PASS_Y, 0, 1),)),
        (7, ((FWD_Y, 3, 0), (PAR, 0, 3, 0),)),
        (8, ((OWN, 1, 3, 0), (PASS_Y, 1, 0),)),
        (9, ((FWD_Y, 1, 1), (PAR, 0, 1, 1), (PAR, 1, 0, 0),)),
        (10, ((OWN, 1, 3, 1), (PAR, 1, 0, 1),)),
        (11, ((OWN, 1, 1, 0), (FWD_Y, 3, 1), (PASS_Y, 3, 0), (PAR, 0, 3, 1),)),
        (12, ((OWN, 1, 2, 0), (OWN, 1, 2, 1), (PAR, 1, 1, 0),)),
        (13, ((FWD_Y, 2, 0), (PASS_Y, 1, 1), (PAR, 0, 2, 0),)),
        (14, ((OWN, 1, 1, 1), (FWD_Y, 2, 1), (PASS_Y, 3, 1), (PAR, 0, 2, 1), (PAR, 1, 3, 0),)),
        (15, ((PASS_Y, 2, 0),)),
        (16, ((PAR, 1, 1, 1),)),
        (17, ((PASS_Y, 2, 1), (PAR, 1, 3, 1),)),
        (18, ((PAR, 1, 2, 0),)),
        (20, ((PAR, 1, 2, 1),)),
    ),
    (
        (2, ((CROSSF, 0), (CROSSF, 1), (OWN, 0, 1, 0), (OWN, 0, 3, 0), (FWD_Y, 0, 0), (PAR, 0, 0, 0),)),
        (3, ((OWN, 0, 1, 1), (OWN, 0, 3, 1), (FWD_Y, 0, 1), (PAR, 0, 0, 1),)),
        (4, ((OWN, 1, 0, 0), (OWN, 1, 0, 1),)),
        (5, ((OWN, 0, 2, 0), (FWD_Y, 1, 0), (PAR, 0, 1, 0),)),
        (6, ((OWN, 0, 2, 1), (PASS_Y, 0, 0), (PASS_Y, 0, 1),)),
        (7, ((FWD_Y, 3, 0), (PAR, 0, 3, 0),)),
        (8, ((OWN, 1, 3, 0), (PASS_Y, 1, 0),)),
        (9, ((FWD_Y, 1, 1), (PAR, 0, 1, 1), (PAR, 1, 0, 0),)),
        (10, ((OWN, 1, 3, 1), (PAR, 1, 0, 1),)),
        (11, ((OWN, 1, 1, 0), (FWD_Y, 3, 1), (PASS_Y, 3, 0), (PAR, 0, 3, 1),)),
        (12, ((OWN, 1, 1, 1), (OWN, 1, 2, 0), (PAR, 1, 1, 0),)),
        (13, ((FWD_Y, 2, 0), (PASS_Y, 1, 1), (PAR, 0, 2, 0),)),
        (14, ((OWN, 1, 2, 1), (FWD_Y, 2, 1), (PASS_Y, 3, 1), (PAR, 0, 2, 1), (PAR, 1, 3, 0),)),
        (16, ((PASS_Y, 2, 0), (PAR, 1, 1, 1),)),
        (17, ((PAR, 1, 3, 1),)),
        (18, ((PASS_Y, 2, 1),)),
        (19, ((PAR, 1, 2, 0),)),
        (20, ((PAR, 1, 2, 1),)),
    ),
    (
        (2, ((CROSSF, 0), (CROSSF, 1), (OWN, 0, 1, 0), (OWN, 0, 3, 0), (FWD_Y, 0, 0), (PAR, 0, 0, 0),)),
        (3, ((OWN, 0, 1, 1), (OWN, 0, 3, 1), (FWD_Y, 0, 1), (PAR, 0, 0, 1),)),
        (4, ((OWN, 1, 0, 0), (OWN, 1, 0, 1),)),
        (5, ((OWN, 0, 2, 0), (FWD_Y, 1, 0), (PAR, 0, 1, 0),)),
        (6, ((OWN, 0, 2, 1), (PASS_Y, 0, 0), (PASS_Y, 0, 1),)),
        (7, ((OWN, 1, 1, 0), (FWD_Y, 3, 0), (PAR, 0, 3, 0),)),
        (8, ((OWN, 1, 3, 0), (PASS_Y, 1, 0),)),
        (9, ((OWN, 1, 1, 1), (FWD_Y, 1, 1), (PAR, 0, 1, 1), (PAR, 1, 0, 0),)),
        (10, ((OWN, 1, 3, 1), (PAR, 1, 0, 1),)),
        (11, ((OWN, 1, 2, 1), (FWD_Y, 3, 1), (PASS_Y, 3, 0), (PAR, 0, 3, 1),)),
        (12, ((OWN, 1, 2, 0), (PAR, 1, 1, 0),)),
        (13, ((FWD_Y, 2, 0), (PASS_Y, 1, 1), (PAR, 0, 2, 0),)),
        (14, ((FWD_Y, 2, 1), (PASS_Y, 3, 1), (PAR, 0, 2, 1), (PAR, 1, 3, 0),)),
        (16, ((PASS_Y, 2, 0), (PAR, 1, 1, 1),)),
        (17, ((PAR, 1, 3, 1),)),
        (18, ((PASS_Y, 2, 1),)),
        (19, ((PAR, 1, 2, 0),)),
        (20, ((PAR, 1, 2, 1),)),
    ),
    (
        (2, ((CROSSF, 0), (CROSSF, 1), (OWN, 0, 1, 0), (OWN, 0, 3, 0), (FWD_Y, 0, 0), (PAR, 0, 0, 0),)),
        (3, ((OWN, 0, 1, 1), (OWN, 0, 3, 1), (FWD_Y, 0, 1), (PAR, 0, 0, 1),)),
        (4, ((OWN, 1, 0, 0), (OWN, 1, 0, 1),)),
        (5, ((OWN, 0, 2, 0), (FWD_Y, 1, 0), (PAR, 0, 1, 0),)),
        (6, ((OWN, 0, 2, 1), (PASS_Y, 0, 0), (PASS_Y, 0, 1),)),
        (7, ((OWN, 1, 1, 0), (FWD_Y, 3, 0), (PAR, 0, 3, 0),)),
        (8, ((OWN, 1, 3, 0), (PASS_Y, 1, 0),)),
        (9, ((OWN, 1, 1, 1), (FWD_Y, 1, 1), (PAR, 0, 1, 1), (PAR, 1, 0, 0),)),
        (10, ((OWN, 1, 3, 1), (PAR, 1, 0, 1),)),
        (11, ((OWN, 1, 2, 1), (FWD_Y, 3, 1), (PASS_Y, 3, 0), (PAR, 0, 3, 1),)),
        (12, ((OWN, 1, 2, 0), (PAR, 1, 1, 0),)),
        (13, ((FWD_Y, 2, 0), (PASS_Y, 1, 1), (PAR, 0, 2, 0),)),
        (14, ((FWD_Y, 2, 1), (PASS_Y, 3, 1), (PAR, 0, 2, 1), (PAR, 1, 3, 0),)),
        (16, ((PASS_Y, 2, 0), (PAR, 1, 1, 1),)),
        (17, ((PAR, 1, 3, 1),)),
        (18, ((PASS_Y, 2, 1),)),
        (19, ((PAR, 1, 2, 0),)),
        (20, ((PAR, 1, 2, 1),)),
    ),
    (
        (2, ((CROSSF, 0), (CROSSF, 1), (OWN, 0, 1, 0), (OWN, 0, 3, 0), (FWD_Y, 0, 0),)),
        (3, ((OWN, 0, 1, 1), (OWN, 0, 3, 1), (FWD_Y, 0, 1),)),
        (4, ((OWN, 1, 0, 0), (OWN, 1, 0, 1),)),
        (5, ((OWN, 0, 2, 0), (FWD_Y, 1, 0),)),
        (6, ((OWN, 0, 2, 1), (PAR, 0, 0, 0), (PAR, 1, 0, 0),)),
        (7, ((OWN, 1, 1, 0), (FWD_Y, 3, 0),)),
        (8, ((OWN, 1, 3, 0), (PAR, 0, 0, 1), (PAR, 1, 0, 1),)),
        (9, ((OWN, 1, 1, 1), (FWD_Y, 1, 1),)),
        (10, ((OWN, 1, 3, 1), (PAR, 0, 1, 0), (PAR, 1, 1, 0),)),
        (11, ((FWD_Y, 3, 1),)),
        (12, ((PAR, 0, 3, 0), (PAR, 1, 3, 0),)),
        (13, ((FWD_Y, 2, 0),)),
        (14, ((OWN, 1, 2, 0), (FWD_Y, 2, 1), (PAR, 0, 1, 1), (PAR, 1, 1, 1),)),
        (15, ((PAR, 0, 3, 1), (PAR, 1, 3, 1),)),
        (17, ((OWN, 1, 2, 1), (PAR, 0, 2, 0), (PAR, 1, 2, 0),)),
        (18, ((PAR, 0, 2, 1), (PAR, 1, 2, 1),)),
    ),
    (
        (2, ((CROSSF, 0), (CROSSF, 1), (OWN, 0, 1, 0), (OWN, 0, 3, 0), (FWD_Y, 0, 0),)),
        (3, ((OWN, 0, 1, 1), (OWN, 0, 3, 1), (FWD_Y, 0, 1),)),
        (4, ((OWN, 1, 0, 0), (OWN, 1, 0, 1),)),
        (5, ((OWN, 0, 2, 0), (FWD_Y, 1, 0),)),
        (6, ((OWN, 0, 2, 1), (PAR, 0, 0, 0), (PAR, 1, 0, 0),)),
        (7, ((OWN, 1, 1, 0), (FWD_Y, 3, 0),)),
        (8, ((OWN, 1, 3, 0), (PAR, 0, 0, 1), (PAR, 1, 0, 1),)),
        (9, ((OWN, 1, 1, 1), (FWD_Y, 1, 1),)),
        (10, ((OWN, 1, 3, 1), (PAR, 0, 1, 0), (PAR, 1, 1, 0),)),
        (11, ((FWD_Y, 3, 1),)),
        (12, ((PAR, 0, 3, 0), (PAR, 1, 3, 0),)),
        (13, ((FWD_Y, 2, 0),)),
        (14, ((OWN, 1, 2, 0), (FWD_Y, 2, 1), (PAR, 0, 1, 1), (PAR, 1, 1, 1),)),
        (15, ((OWN, 1, 2, 1), (PAR, 0, 3, 1), (PAR, 1, 3, 1),)),
        (17, ((PAR, 0, 2, 0), (PAR, 1, 2, 0),)),
        (18, ((PAR, 0, 2, 1), (PAR, 1, 2, 1),)),
    ),
    (
        (2, ((CROSSF, 0), (CROSSF, 1), (OWN, 0, 1, 0), (OWN, 0, 3, 0), (FWD_Y, 0, 0),)),
        (3, ((OWN, 0, 1, 1), (OWN, 0, 3, 1), (FWD_Y, 0, 1),)),
        (4, ((OWN, 1, 0, 0), (OWN, 1, 0, 1),)),
        (5, ((OWN, 0, 2, 0), (FWD_Y, 1, 0),)),
        (6, ((OWN, 0, 2, 1), (PAR, 0, 0, 0), (PAR, 1, 0, 0),)),
        (7, ((OWN, 1, 1, 0), (FWD_Y, 3, 0),)),
        (8, ((OWN, 1, 3, 0), (PAR, 0, 0, 1), (PAR, 1, 0, 1),)),
        (9, ((OWN, 1, 1, 1), (FWD_Y, 1, 1),)),
        (10, ((OWN, 1, 3, 1), (PAR, 0, 1, 0), (PAR, 1, 1, 0),)),
        (11, ((OWN, 1, 2, 1), (FWD_Y, 3, 1),)),
        (12, ((OWN, 1, 2, 0), (PAR, 0, 3, 0), (PAR, 1, 3, 0),)),
        (13, ((FWD_Y, 2, 0),)),
        (14, ((FWD_Y, 2, 1), (PAR, 0, 1, 1), (PAR, 1, 1, 1),)),
        (15, ((PAR, 0, 3, 1), (PAR, 1, 3, 1),)),
        (17, ((PAR, 0, 2, 0), (PAR, 1, 2, 0),)),
        (18, ((PAR, 0, 2, 1), (PAR, 1, 2, 1),)),
    ),
    (
        (2, ((CROSSF, 0), (CROSSF, 1), (OWN, 0, 1, 0), (OWN, 0, 3, 0), (FWD_Y, 0, 0),)),
        (3, ((OWN, 0, 1, 1), (OWN, 0, 3, 1), (FWD_Y, 0, 1),)),
        (4, ((OWN, 1, 0, 0), (OWN, 1, 0, 1),)),
        (5, ((OWN, 0, 2, 0), (FWD_Y, 1, 0),)),
        (6, ((OWN, 0, 2, 1), (PAR, 0, 0, 0), (PAR, 1, 0, 0),)),
        (7, ((OWN, 1, 1, 0), (FWD_Y, 3, 0),)),
        (8, ((OWN, 1, 3, 0), (PAR, 0, 0, 1), (PAR, 1, 0, 1),)),
        (9, ((OWN, 1, 1, 1), (FWD_Y, 1, 1),)),
        (10, ((OWN, 1, 3, 1), (PAR, 0, 1, 0), (PAR, 1, 1, 0),)),
        (11, ((OWN, 1, 2, 1), (FWD_Y, 3, 1),)),
        (12, ((OWN, 1, 2, 0), (PAR, 0, 3, 0), (PAR, 1, 3, 0),)),
        (13, ((FWD_Y, 2, 0),)),
        (14, ((FWD_Y, 2, 1), (PAR, 0, 1, 1), (PAR, 1, 1, 1),)),
        (15, ((PAR, 0, 3, 1), (PAR, 1, 3, 1),)),
        (17, ((PAR, 0, 2, 0), (PAR, 1, 2, 0),)),
        (18, ((PAR, 0, 2, 1), (PAR, 1, 2, 1),)),
    ),
)

STAGES = len(SEQUENCE)
BASES = [sum(PARTS[stage] for stage in SEQUENCE[:n]) for n in range(STAGES + 1)]
POINTS = BASES[-1] + 1
PAR_AT, T1_AT, T2_AT, T3_AT, TC_AT, SLOTS = 32, 64, 72, 80, 88, 90
WAYS = ("x+", "x-", "y+", "y-", "z+", "z-", "core", "ya", "yb", "za", "zb")
WAIT = 15
CLASSES = [(x, y) for x in range(4) for y in range(4)]


def sign_of(j, k):
    return "+" if (k + (0, 1, 1, 0)[j]) % 2 == 0 else "-"


def name_of(x, y, row, j):
    return (y // 2 + row) % 2 * 4 + (x + 4 - j) % 4


def row_behind(y, sign):
    return (y + 3) % 4 // 2 if sign == "+" else (y + 1) % 4 // 2


def feed(x, y, j, k, src):
    up = y // 2 == 1
    final, via1, via2 = ("par", name_of(x, y, 0, j), k), ("t1", j, k), ("t2", j, k)
    sends = []
    if x in (0, 1):
        sends.append((src, via1, "z" + sign_of(j, k)))
    if x == 1:
        sends.append((src, final, "ya"))
    if x in (2, 3):
        sends.append((src, final if x == 2 and not up else via1, "za"))
        sends.append((src, final if x == 2 and up else via2, "zb"))
    return sends


def expand(x, y, event):
    kind, args = event[0], event[1:]
    up = y // 2 == 1
    ops = []
    if kind == CROSSF:
        (k,) = args
        sign = "+-"[k]
        ops = [("tc", k), (("tc", k), ("own", row_behind(y, sign) * 4 + x, k), "y" + sign)]
    if kind == OWN:
        row, j, k = args
        here = ("own", name_of(x, y, row, j), k)
        ops = [here]
        if (row, j) == (1, 0) or (j == 1 and (k + row) % 2 == 0):
            ops.append((here, here, "x+"))
        if (row, j) == (1, 0) or (j == 3 and (k + row) % 2 == 1):
            ops.append((here, here, "x-"))
        if row == 0:
            ops += feed(x, y, j, k, here)
        ops.append((here, here, "core"))
    if kind == PASS_Z:
        j, k = args
        here = ("t1", j, k)
        there = ("par", name_of(x, y, 0, j), k) if x == 0 and up else ("t2", j, k)
        ops = [here, (here, there, "z" + sign_of(j, k))]
    if kind == FWD_Y:
        j, k = args
        final, there, way = ("par", name_of(x, y, 0, j), k), ("t3", j, k), "y" + sign_of(j, k)
        if x == 3 or (x == 2 and up):
            ops += [("t1", j, k), (("t1", j, k), final, "ya") if x == 3 else (("t1", j, k), there, way)]
        if x in (1, 3) or not up:
            ops += [("t2", j, k), (("t2", j, k), final, "yb") if x in (1, 3) else (("t2", j, k), there, way)]
    if kind == PASS_Y:
        j, k = args
        sign = sign_of(j, k)
        row = row_behind(y, sign)
        if x == 2 or row == 0:
            ops = [("t3", j, k), (("t3", j, k), ("par", row * 4 + (x + 4 - j) % 4, k), "y" + sign)]
    if kind == PAR:
        row, j, k = args
        here = ("par", name_of(x, y, row, j), k)
        ops = [here, (here, here, "core")]
    return ops


def slot(place, c):
    kind, rest = place[0], place[1:]
    if kind in ("own", "par"):
        q, k = rest
        return (PAR_AT if kind == "par" else 0) + q * 4 + c * 2 + k
    if kind == "tc":
        return TC_AT + rest[0]
    return {"t1": T1_AT, "t2": T2_AT, "t3": T3_AT}[kind] + rest[0] * 2 + rest[1]


def tables(x, y):
    per_core = []
    for c in range(2):
        ops, begins, sends, at = [], [], 0, dict(EVENTS[CLASSES.index((x, y))])
        for point in range(POINTS):
            begins.append(len(ops))
            for event in at.get(point, ()):
                for op in expand(x, y, event):
                    if isinstance(op[0], str):
                        ops.append(slot(op, c) + 2097152 * WAIT)
                    else:
                        src, dst, way = op
                        ops.append(slot(src, c) + 128 * slot(dst, c) + 16384 * sends + 2097152 * WAYS.index(way))
                        sends += 1
        per_core.append((ops, begins + [len(ops), sends], sends))
    return per_core


TABLES = {cls: tables(*cls) for cls in CLASSES}
MOST_OPS = max(len(ops) for cores in TABLES.values() for ops, _, _ in cores)
MOST_SENDS = max(sends for cores in TABLES.values() for _, _, sends in cores)
FIRST_SENDS = 12


def columns(t):
    first, last = t * 256, (t + 1) * 256
    cuts = [first] + [cut for cut in range(0, NI * V, V) if first < cut < last] + [last]
    return [(u - first, w - first, u // V, u % V) for u, w in zip(cuts, cuts[1:])]


def kernel(dims, mine, amps, out, out_own, out_par, buf, rc, half, acc, ops, begins, devs,
           ssem, first_sem, rsem, local_sem):
    sym, tile, c = lax.axis_index("sym"), lax.axis_index("tile"), lax.axis_index("occ")
    x, yhi = sym % 4, sym // 4
    x0, x1 = x % 2, x // 2
    z, ylo = tile // 2, tile % 2
    z0, z1 = z % 2, z // 2
    y = 2 * yhi + ylo
    none = sym == 0

    def dev(dx=0, dy=0, dz=0, dc=0):
        xx, yy, zz = (x + 4 + dx) % 4, (y + 4 + dy) % 4, (z + 4 + dz) % 4
        return ((yy // 2) * 4 + xx) * 16 + (zz * 2 + yy % 2) * 2 + (c + dc) % 2

    step_a = 1 - 2 * (yhi + ylo - 2 * yhi * ylo)
    step_z = 1 - 2 * z0
    to = {
        "x+": dev(dx=1), "x-": dev(dx=-1), "y+": dev(dy=1), "y-": dev(dy=-1), "z+": dev(dz=1), "z-": dev(dz=-1),
        "core": dev(dc=1), "ya": dev(dy=step_a), "yb": dev(dy=-step_a), "za": dev(dz=step_z), "zb": dev(dz=-step_z),
    }
    barrier = pltpu.get_barrier_semaphore()
    for way in WAYS[:7]:
        pl.semaphore_signal(barrier, inc=1, device_id=to[way], device_id_type=pl.DeviceIdType.LOGICAL)

    def own_slot(q, core, k):
        return q * 4 + core * 2 + k

    keep = []
    for k in range(PIECES):
        keep.append(pltpu.make_async_copy(mine.at[pl.ds(k * PV, PV)], buf.at[own_slot(sym, c, k)], local_sem.at[8 + k]))
        keep[-1].start()
    loads = [pltpu.make_async_copy(amps.at[i], rc.at[:, pl.ds(i * V, V)], local_sem.at[i]) for i in range(NI)]
    for load in loads:
        load.start()

    pl.semaphore_wait(barrier, 7)

    def remote(src, dst_slot, sem, where):
        return pltpu.make_async_remote_copy(
            src, buf.at[dst_slot], sem, rsem.at[dst_slot], device_id=where, device_id_type=pl.DeviceIdType.LOGICAL
        )

    def arrived(at):
        remote(buf.at[at], at, first_sem.at[0], to["core"]).wait_recv()

    firsts = []

    def first(src, place, where, cond=None):
        index = len(firsts)
        if cond is None:
            remote(src, place, first_sem.at[index], where).start()
        else:
            pl.when(cond)(lambda: remote(src, place, first_sem.at[index], where).start())
        firsts.append((src, place, cond, index))

    step_2 = {k: {"+": to["z+"], "-": to["z-"]}[sign_of(0, k)] for k in range(PIECES)}
    for k in range(PIECES):
        src = mine.at[pl.ds(k * PV, PV)]
        home = own_slot(sym, c, k)
        final, via1, via2 = PAR_AT + home, T1_AT + k, T2_AT + k
        first(src, home, to["core"])
        first(src, home, to["x+"])
        first(src, home, to["x-"])
        first(src, TC_AT + k, to["y" + "+-"[k]])
        direct_b, direct_a = x0 + 2 * (1 - x1) + (1 - yhi) == 0, x0 + 2 * (1 - x1) + yhi == 0
        where_b = x1 * to["zb"] + (1 - x1) * step_2[k]
        place_b = jnp.where(direct_b, final, x1 * via2 + (1 - x1) * via1)
        first(src, place_b, where_b)
        where_a = x1 * to["za"] + (1 - x1) * to["ya"]
        place_a = jnp.where(direct_a | (x1 == 0), final, via1)
        first(src, place_a, where_a, x > 0)

    for (at_x, at_y), cores in TABLES.items():
        @pl.when((x == at_x) & (y == at_y))
        def _():
            (ops0, begins0, _), (ops1, _, _) = cores
            for n, (op0, op1) in enumerate(zip(ops0, ops1)):
                ops[n] = op0 + (op1 - op0) * c if op0 != op1 else op0
            for n, begin in enumerate(begins0):
                begins[n] = begin
    for n, way in enumerate(WAYS):
        devs[n] = to[way]

    n_row = dims[tile]
    n_col = dims[(z1 + yhi - 2 * z1 * yhi) * 4 + (z0 + x1 - 2 * z0 * x1) * 2 + (ylo + x0 - 2 * ylo * x0)]
    live_r = jnp.where(lax.broadcasted_iota(jnp.int32, (V, V), 0) < n_row, 1.0, 0.0)
    live = jnp.where(lax.broadcasted_iota(jnp.int32, (V, V), 1) < n_col, live_r, 0.0).astype(jnp.bfloat16)
    acc[...] = jnp.zeros_like(acc)
    for load in loads:
        load.wait()
    for i in range(NI):
        rc[:, i * V:(i + 1) * V] = rc[:, i * V:(i + 1) * V] * live
    for copy in keep:
        copy.wait()

    def decoded(n):
        op = ops[n]
        src, rest = lax.rem(op, 128), lax.div(op, 128)
        dst, rest = lax.rem(rest, 128), lax.div(rest, 128)
        return src, dst, lax.rem(rest, 128), lax.div(rest, 128)

    def events(point):
        @pl.loop(begins[point], begins[point + 1])
        def _(n):
            src, dst, index, way = decoded(n)

            @pl.when(way == WAIT)
            def _():
                arrived(src)

            @pl.when(way != WAIT)
            def _():
                remote(buf.at[src], dst, ssem.at[index], devs[way]).start()

    digit = (1 + 15 * x0) * (1 + 255 * x1)

    def chosen(groups, n):
        code = 0
        for number, names in enumerate(groups):
            of_y = [0] * 4
            for (at_x, at_y), (row, j, k) in zip(CLASSES, names):
                of_y[at_y] += (row * 8 + j * 2 + k) * 16 ** at_x
            value = of_y[0]
            if len(set(of_y)) > 1:
                value = value + (of_y[1] - of_y[0]) * ylo + (of_y[2] - of_y[0]) * yhi
                value = value + (of_y[3] - of_y[2] - of_y[1] + of_y[0]) * (yhi * ylo)
            code = code + (n == number) * 1 * value
        code = lax.rem(lax.div(code, digit), 16)
        return (yhi + code // 8) % 2 * 4 + (x + 4 - code // 2 % 4) % 4, code % 2

    def base_of(n):
        return sum((n == number) * base for number, base in enumerate(BASES[:-1]) if base)

    par_base = PAR_AT * (1 - (sym == 0) * 1)

    def unit(base, q, core):
        at = base + q * 4 + core * 2
        return buf[pl.ds(at, 2)].reshape(V, V)

    def first_stage(base, halves):
        for q, k in halves:
            arrived(own_slot(q, 1 - c, k))
        for h in range(PARTS[1]):
            if h:
                events(base + h)
            for t in range(h * 12 // PARTS[1], (h + 1) * 12 // PARTS[1]):
                left = jnp.concatenate([buf[q * 4 + 2 * p + k] for q, k in halves for p in range(2)], axis=0)
                r = jnp.dot(left, rc[:, t * 256:(t + 1) * 256], preferred_element_type=jnp.float32).astype(jnp.bfloat16)
                for lo_col, hi_col, pair, at in columns(t):
                    for number, (q, k) in enumerate(halves):
                        rows = pl.ds(pl.multiple_of(pair * V + k * PV, PV), PV)
                        for p in range(2):
                            lanes = pl.ds(p * V + at, hi_col - lo_col)
                            first = (2 * number + p) * PV
                            half[q, rows, lanes] = r[first:first + PV, lo_col:hi_col]

    def second_stage(base, q, last=False):
        @pl.when(jnp.logical_not(none))
        def _():
            for k in range(PIECES):
                arrived(PAR_AT + own_slot(q, 1 - c, k))

        for h in range(2):
            if h and PARTS[2] > 1:
                events(base + h)
            rows = pl.ds(h * HALF, HALF)
            for b0, b1 in ((0, 256), (256, 384)):
                right = jnp.concatenate([unit(par_base, q, p)[b0:b1] for p in range(2)], axis=1)
                acc[rows, b0:b1] += lax.dot_general(
                    half[q, rows, :], right, (((1,), (1,)), ((), ())), preferred_element_type=jnp.float32
                )
            if last:
                pltpu.make_async_copy(acc.at[rows], out.at[rows], local_sem.at[h]).start()

    @pl.loop(0, STAGES - 1)
    def _(n):
        second = sum((n == k) * 1 for k, stage in enumerate(SEQUENCE) if stage == 2)
        halves = [chosen(group, n) for group in UNITS]
        base = base_of(n)
        events(base)
        pl.when(second == 0)(lambda: first_stage(base, halves))
        pl.when(second == 1)(lambda: second_stage(base, halves[0][0]))

    events(BASES[-2])
    second_stage(BASES[-2], chosen(UNITS[0], jnp.int32(STAGES - 1))[0], last=True)
    events(POINTS - 1)

    leaving = []
    for r in range(len(REST)):
        q, _ = chosen(REST, jnp.int32(r))
        for k in range(PIECES):
            arrived(own_slot(q, 1 - c, k))

        @pl.when(jnp.logical_not(none))
        def _():
            for k in range(PIECES):
                arrived(PAR_AT + own_slot(q, 1 - c, k))

        par_at = par_base + q * 4
        for source, target, sem in ((q * 4, out_own.at[r], 18 + 2 * r), (par_at, out_par.at[r], 19 + 2 * r)):
            leaving.append(pltpu.make_async_copy(buf.at[pl.ds(source, 4)], target, local_sem.at[sem - 8]))
            leaving[-1].start()

    for src, place, cond, index in firsts:
        def sent(src=src, place=place, index=index):
            remote(src, place, first_sem.at[index], to["core"]).wait_send()

        if cond is None:
            sent()
        else:
            pl.when(cond)(sent)

    @pl.loop(0, begins[POINTS + 1])
    def _(n):
        remote(buf.at[0], 0, ssem.at[n], to["core"]).wait_send()

    for h in range(2):
        rows = pl.ds(h * HALF, HALF)
        pltpu.make_async_copy(acc.at[rows], out.at[rows], local_sem.at[h]).wait()
    for copy in leaving:
        copy.wait()


ALL = [(row, j) for j in (0, 1, 3, 2) for row in range(2)]


def left_over():
    by_class = []
    for at in range(len(CLASSES)):
        done = [names[at][:2] for group in UNITS for stage, names in zip(SEQUENCE, group) if stage == 1]
        by_class.append([name + (0,) for name in ALL if name not in done])
    return tuple(zip(*by_class))


REST = left_over()


def rest_kernel(dims, own_hbm, par_hbm, amps, raw, out, own, par, rc, half, acc, sems):
    sym, tile = lax.axis_index("sym"), lax.axis_index("tile")
    n, hi = len(REST), NI // 2
    get_own = pltpu.make_async_copy(own_hbm, own, sems.at[0])
    get_par = pltpu.make_async_copy(par_hbm, par, sems.at[1])
    get_amps = [pltpu.make_async_copy(amps.at[i], rc.at[:, pl.ds(i * V, V)], sems.at[2 + i]) for i in range(NI)]
    get_raw = [
        pltpu.make_async_copy(raw.at[pl.ds(h * HALF, HALF)], acc.at[pl.ds(h * HALF, HALF)], sems.at[2 + NI + h])
        for h in range(2)
    ]
    for copy in get_amps[:hi] + [get_own, get_par, get_raw[0]] + get_amps[hi:] + [get_raw[1]]:
        copy.start()
    n_row, n_col = dims[tile], dims[jnp.bitwise_xor(tile, sym)]
    live = (lax.broadcasted_iota(jnp.int32, (V, V), 0) < n_row) & (lax.broadcasted_iota(jnp.int32, (V, V), 1) < n_col)
    live_b = jnp.where(live, 1.0, 0.0).astype(jnp.bfloat16)
    puts = []
    for h in range(2):
        for i in range(h * hi, (h + 1) * hi):
            get_amps[i].wait()
            rc[:, i * V:(i + 1) * V] = rc[:, i * V:(i + 1) * V] * live_b
        if h == 0:
            get_own.wait()
        for t in range(6 * h, 6 * (h + 1)):
            left = own[...].reshape(n * 2 * V, V)
            r = jnp.dot(left, rc[:, t * 256:(t + 1) * 256], preferred_element_type=jnp.float32).astype(jnp.bfloat16)
            for lo_col, hi_col, pair, at in columns(t):
                for p in range(2 * n):
                    lanes = pl.ds(p * V + at, hi_col - lo_col)
                    half[(pair - h * hi) * V:(pair - h * hi + 1) * V, lanes] = r[p * V:(p + 1) * V, lo_col:hi_col]
        if h == 0:
            get_par.wait()
        get_raw[h].wait()
        rows = pl.ds(h * HALF, HALF)
        for b0, b1 in ((0, 256), (256, 384)):
            right = [par[r, pl.ds(2 * p, 2)].reshape(V, V)[b0:b1] for r in range(n) for p in range(2)]
            right = jnp.concatenate(right, axis=1)
            r = lax.dot_general(half[...], right, (((1,), (1,)), ((), ())), preferred_element_type=jnp.float32)
            r = r + acc[rows, b0:b1]
            for i in range(hi):
                at = pl.ds((h * hi + i) * V, V)
                acc[at, b0:b1] = jnp.where(live[:, b0:b1], r[i * V:(i + 1) * V], 0.0)
            lanes = pl.ds(b0, b1 - b0)
            puts.append(pltpu.make_async_copy(acc.at[rows, lanes], out.at[rows, lanes], sems.at[4 + NI + len(puts)]))
            puts[-1].start()
    for copy in puts:
        copy.wait()


def shards(irrep_dims, chol_vectors, amplitudes):
    bf, sem = jnp.bfloat16, pltpu.SemaphoreType.DMA
    n = len(REST)
    own, chol, amps = (n, 4, PV, V), chol_vectors.reshape(V, V), amplitudes.reshape(NI, V, V)
    anywhere = pl.BlockSpec(memory_space=pl.ANY)
    raw, rest_own, rest_par = pl.pallas_call(
        kernel,
        out_shape=[
            jax.ShapeDtypeStruct((NI * V, V), jnp.float32),
            jax.ShapeDtypeStruct(own, bf),
            jax.ShapeDtypeStruct(own, bf),
        ],
        in_specs=[pl.BlockSpec(memory_space=pltpu.SMEM), anywhere, anywhere],
        out_specs=[anywhere] * 3,
        scratch_shapes=[
            pltpu.VMEM((SLOTS, PV, V), bf),
            pltpu.VMEM((V, NI * V), bf),
            pltpu.VMEM((8, NI * V, 2 * V), bf),
            pltpu.VMEM((NI * V, V), jnp.float32),
            pltpu.SMEM((MOST_OPS,), jnp.int32),
            pltpu.SMEM((POINTS + 2,), jnp.int32),
            pltpu.SMEM((len(WAYS),), jnp.int32),
            sem((MOST_SENDS,)), sem((FIRST_SENDS,)), sem((SLOTS,)), sem((10 + 2 * n,)),
        ],
        compiler_params=pltpu.CompilerParams(
            collective_id=0, has_side_effects=True, vmem_limit_bytes=63 * 1024 * 1024
        ),
        cost_estimate=pl.CostEstimate(flops=(8 - n) * 3_600_000_000, bytes_accessed=12_000_000, transcendentals=0),
        name="ladder",
    )(irrep_dims, chol, amps)
    total = pl.pallas_call(
        rest_kernel,
        out_shape=jax.ShapeDtypeStruct((NI * V, V), jnp.float32),
        in_specs=[pl.BlockSpec(memory_space=pltpu.SMEM)] + [anywhere] * 4,
        out_specs=anywhere,
        scratch_shapes=[
            pltpu.VMEM(own, bf),
            pltpu.VMEM(own, bf),
            pltpu.VMEM((V, NI * V), bf),
            pltpu.VMEM((HALF, n * 2 * V), bf),
            pltpu.VMEM((NI * V, V), jnp.float32),
            sem((8 + NI,)),
        ],
        compiler_params=pltpu.CompilerParams(vmem_limit_bytes=60 * 1024 * 1024),
        cost_estimate=pl.CostEstimate(flops=n * 3_600_000_000, bytes_accessed=16_000_000, transcendentals=0),
        name="rest",
    )(irrep_dims, rest_own, rest_par, amps, raw)
    return total.reshape(1, NI, V, V)


def solution(mesh):
    return jax.shard_map(
        shards,
        mesh=mesh,
        in_specs=(P(), P(("sym", "occ"), "tile", None), P("sym", "occ", "tile", None)),
        out_specs=P("sym", "occ", "tile", None),
        check_vma=False,
    )
```

```python
import jax
import jax.numpy as jnp
from jax import lax
from jax.experimental import pallas as pl
from jax.experimental.pallas import tpu as pltpu
from jax.sharding import PartitionSpec as P

V = 384
NI = 8
PIECES = 2
PV = V // PIECES
HALF = NI * V // 2
CROSSF, OWN, PASS_Z, FWD_Y, PASS_Y, PAR = range(6)
PARTS = {1: 2, 2: 1}
SEQUENCE = (1, 1, 1, 1, 1, 2, 1, 2, 1, 2, 2, 2, 2, 2)
UNITS = (
    (
        ((0, 0, 0), (0, 0, 0), (0, 0, 0), (0, 0, 0), (0, 0, 0), (0, 0, 0), (0, 0, 0), (0, 0, 0), (0, 0, 0), (0, 0, 0), (0, 0, 0), (0, 0, 0), (0, 0, 0), (0, 0, 0), (0, 0, 0), (0, 0, 0)),
        ((0, 1, 0), (0, 1, 0), (0, 1, 0), (0, 1, 0), (0, 1, 0), (0, 1, 0), (0, 1, 0), (0, 1, 0), (0, 1, 0), (0, 1, 0), (0, 1, 0), (0, 1, 0), (0, 1, 0), (0, 1, 0), (0, 1, 0), (0, 1, 0)),
        ((0, 1, 1), (0, 1, 1), (0, 1, 1), (0, 1, 1), (0, 1, 1), (0, 1, 1), (0, 1, 1), (0, 1, 1), (0, 1, 1), (0, 1, 1), (0, 1, 1), (0, 1, 1), (0, 1, 1), (0, 1, 1), (0, 1, 1), (0, 1, 1)),
        ((1, 0, 0), (1, 0, 0), (1, 0, 0), (1, 0, 0), (0, 2, 0), (0, 2, 0), (1, 0, 0), (1, 0, 0), (1, 0, 0), (1, 0, 0), (1, 0, 0), (1, 0, 0), (1, 0, 0), (1, 0, 0), (1, 0, 0), (1, 0, 0)),
        ((0, 2, 0), (0, 2, 0), (0, 2, 0), (0, 2, 0), (1, 0, 0), (1, 0, 0), (0, 2, 0), (1, 0, 1), (0, 2, 0), (0, 2, 0), (0, 2, 0), (0, 2, 0), (0, 2, 0), (0, 2, 0), (0, 2, 0), (0, 2, 0)),
        ((0, 0, 0), (0, 0, 0), (0, 0, 0), (0, 0, 0), (0, 0, 0), (0, 0, 0), (1, 0, 0), (1, 0, 0), (0, 0, 0), (0, 0, 0), (0, 0, 0), (0, 0, 0), (0, 0, 0), (0, 0, 0), (0, 0, 0), (0, 0, 0)),
        ((1, 1, 0), (1, 1, 0), (1, 1, 0), (1, 1, 0), (1, 3, 0), (1, 1, 0), (1, 1, 0), (1, 1, 0), (1, 3, 0), (1, 3, 0), (1, 1, 0), (1, 1, 0), (1, 1, 0), (1, 1, 0), (1, 1, 0), (1, 1, 0)),
        ((1, 0, 0), (1, 0, 0), (1, 0, 0), (1, 0, 0), (0, 1, 0), (1, 0, 0), (0, 0, 0), (0, 0, 0), (1, 0, 0), (1, 0, 0), (1, 0, 0), (1, 0, 0), (1, 0, 0), (1, 0, 0), (1, 0, 0), (1, 0, 0)),
        ((1, 3, 0), (1, 3, 0), (1, 1, 1), (1, 1, 1), (1, 0, 1), (1, 1, 1), (1, 1, 1), (1, 1, 1), (1, 1, 0), (1, 1, 0), (1, 1, 1), (1, 1, 1), (1, 1, 1), (1, 1, 1), (1, 1, 1), (1, 1, 1)),
        ((0, 1, 0), (0, 1, 0), (0, 1, 0), (0, 1, 0), (1, 0, 0), (0, 1, 0), (0, 1, 0), (0, 1, 0), (0, 1, 0), (0, 1, 0), (0, 1, 0), (0, 1, 0), (0, 1, 0), (0, 1, 0), (0, 1, 0), (0, 1, 0)),
        ((1, 1, 0), (1, 1, 0), (0, 3, 0), (0, 3, 0), (1, 1, 0), (1, 1, 0), (1, 1, 0), (1, 1, 0), (1, 1, 0), (1, 1, 0), (1, 1, 0), (1, 1, 0), (1, 1, 0), (1, 1, 0), (1, 1, 0), (1, 1, 0)),
        ((0, 3, 0), (0, 3, 0), (0, 2, 0), (0, 2, 0), (0, 3, 0), (0, 3, 0), (0, 3, 0), (0, 3, 0), (0, 3, 0), (0, 3, 0), (0, 3, 0), (0, 3, 0), (0, 3, 0), (0, 3, 0), (0, 3, 0), (0, 3, 0)),
        ((1, 3, 0), (1, 3, 0), (1, 3, 0), (1, 1, 0), (1, 3, 0), (1, 3, 0), (1, 3, 0), (1, 3, 0), (1, 3, 0), (1, 3, 0), (1, 3, 0), (1, 3, 0), (1, 3, 0), (1, 3, 0), (1, 3, 0), (1, 3, 0)),
        ((0, 2, 0), (0, 2, 0), (1, 1, 0), (1, 3, 0), (0, 2, 0), (0, 2, 0), (0, 2, 0), (0, 2, 0), (0, 2, 0), (0, 2, 0), (0, 2, 0), (0, 2, 0), (0, 2, 0), (0, 2, 0), (0, 2, 0), (0, 2, 0)),
    ),
    (
        ((0, 0, 1), (0, 0, 1), (0, 0, 1), (0, 0, 1), (0, 0, 1), (0, 0, 1), (0, 0, 1), (0, 0, 1), (0, 0, 1), (0, 0, 1), (0, 0, 1), (0, 0, 1), (0, 0, 1), (0, 0, 1), (0, 0, 1), (0, 0, 1)),
        ((0, 3, 0), (0, 3, 0), (0, 3, 0), (0, 3, 0), (0, 3, 0), (0, 3, 0), (0, 3, 0), (0, 3, 0), (0, 3, 0), (0, 3, 0), (0, 3, 0), (0, 3, 0), (0, 3, 0), (0, 3, 0), (0, 3, 0), (0, 3, 0)),
        ((0, 3, 1), (0, 3, 1), (0, 3, 1), (0, 3, 1), (0, 3, 1), (0, 3, 1), (0, 3, 1), (0, 3, 1), (0, 3, 1), (0, 3, 1), (0, 3, 1), (0, 3, 1), (0, 3, 1), (0, 3, 1), (0, 3, 1), (0, 3, 1)),
        ((1, 0, 1), (1, 0, 1), (1, 0, 1), (1, 0, 1), (0, 2, 1), (0, 2, 1), (1, 0, 1), (0, 2, 0), (1, 0, 1), (1, 0, 1), (1, 0, 1), (1, 0, 1), (1, 0, 1), (1, 0, 1), (1, 0, 1), (1, 0, 1)),
        ((0, 2, 1), (0, 2, 1), (0, 2, 1), (0, 2, 1), (1, 1, 0), (1, 0, 1), (0, 2, 1), (0, 2, 1), (0, 2, 1), (0, 2, 1), (0, 2, 1), (0, 2, 1), (0, 2, 1), (0, 2, 1), (0, 2, 1), (0, 2, 1)),
        ((0, 0, 0), (0, 0, 0), (0, 0, 0), (0, 0, 0), (0, 0, 0), (0, 0, 0), (1, 0, 0), (1, 0, 0), (0, 0, 0), (0, 0, 0), (0, 0, 0), (0, 0, 0), (0, 0, 0), (0, 0, 0), (0, 0, 0), (0, 0, 0)),
        ((1, 1, 1), (1, 1, 1), (1, 3, 0), (1, 3, 0), (1, 1, 1), (1, 3, 0), (1, 3, 0), (1, 3, 0), (1, 3, 1), (1, 3, 1), (1, 3, 0), (1, 3, 0), (1, 3, 0), (1, 3, 0), (1, 3, 0), (1, 3, 0)),
        ((1, 0, 0), (1, 0, 0), (1, 0, 0), (1, 0, 0), (0, 1, 0), (1, 0, 0), (0, 0, 0), (0, 0, 0), (1, 0, 0), (1, 0, 0), (1, 0, 0), (1, 0, 0), (1, 0, 0), (1, 0, 0), (1, 0, 0), (1, 0, 0)),
        ((1, 3, 1), (1, 3, 1), (1, 3, 1), (1, 3, 1), (1, 3, 1), (1, 3, 1), (1, 3, 1), (1, 3, 1), (1, 1, 1), (1, 1, 1), (1, 3, 1), (1, 3, 1), (1, 3, 1), (1, 3, 1), (1, 3, 1), (1, 3, 1)),
        ((0, 1, 0), (0, 1, 0), (0, 1, 0), (0, 1, 0), (1, 0, 0), (0, 1, 0), (0, 1, 0), (0, 1, 0), (0, 1, 0), (0, 1, 0), (0, 1, 0), (0, 1, 0), (0, 1, 0), (0, 1, 0), (0, 1, 0), (0, 1, 0)),
        ((1, 1, 0), (1, 1, 0), (0, 3, 0), (0, 3, 0), (1, 1, 0), (1, 1, 0), (1, 1, 0), (1, 1, 0), (1, 1, 0), (1, 1, 0), (1, 1, 0), (1, 1, 0), (1, 1, 0), (1, 1, 0), (1, 1, 0), (1, 1, 0)),
        ((0, 3, 0), (0, 3, 0), (0, 2, 0), (0, 2, 0), (0, 3, 0), (0, 3, 0), (0, 3, 0), (0, 3, 0), (0, 3, 0), (0, 3, 0), (0, 3, 0), (0, 3, 0), (0, 3, 0), (0, 3, 0), (0, 3, 0), (0, 3, 0)),
        ((1, 3, 0), (1, 3, 0), (1, 3, 0), (1, 1, 0), (1, 3, 0), (1, 3, 0), (1, 3, 0), (1, 3, 0), (1, 3, 0), (1, 3, 0), (1, 3, 0), (1, 3, 0), (1, 3, 0), (1, 3, 0), (1, 3, 0), (1, 3, 0)),
        ((0, 2, 0), (0, 2, 0), (1, 1, 0), (1, 3, 0), (0, 2, 0), (0, 2, 0), (0, 2, 0), (0, 2, 0), (0, 2, 0), (0, 2, 0), (0, 2, 0), (0, 2, 0), (0, 2, 0), (0, 2, 0), (0, 2, 0), (0, 2, 0)),
    ),
)
EVENTS = (
    (
        (2, ((CROSSF, 0), (CROSSF, 1), (OWN, 0, 1, 0), (OWN, 0, 3, 0), (PASS_Z, 0, 0), (PASS_Z, 0, 1),)),
        (3, ((OWN, 0, 1, 1), (OWN, 0, 3, 1),)),
        (4, ((OWN, 1, 0, 0), (OWN, 1, 0, 1), (PASS_Z, 1, 0), (PASS_Z, 3, 0),)),
        (5, ((OWN, 0, 2, 0),)),
        (6, ((OWN, 0, 2, 1), (FWD_Y, 0, 0), (FWD_Y, 0, 1),)),
        (8, ((OWN, 1, 1, 0), (PASS_Z, 1, 1), (PASS_Z, 3, 1),)),
        (9, ((PASS_Y, 0, 1),)),
        (10, ((OWN, 1, 1, 1),)),
        (11, ((OWN, 1, 3, 0), (FWD_Y, 1, 0), (FWD_Y, 3, 0),)),
        (12, ((OWN, 1, 2, 1), (PASS_Z, 2, 0), (PASS_Z, 2, 1),)),
        (13, ((OWN, 1, 2, 0),)),
        (14, ((FWD_Y, 1, 1), (FWD_Y, 3, 1), (PASS_Y, 1, 0), (OWN, 1, 3, 1),)),
        (15, ((FWD_Y, 2, 0), (FWD_Y, 2, 1),)),
        (17, ((PASS_Y, 3, 1),)),
        (18, ((PASS_Y, 2, 0),)),
    ),
    (
        (2, ((CROSSF, 0), (CROSSF, 1), (OWN, 0, 1, 0), (OWN, 0, 3, 0), (PASS_Z, 0, 0), (PASS_Z, 0, 1),)),
        (3, ((OWN, 0, 1, 1), (OWN, 0, 3, 1),)),
        (4, ((OWN, 1, 0, 0), (OWN, 1, 0, 1), (PASS_Z, 1, 0), (PASS_Z, 3, 0),)),
        (5, ((OWN, 0, 2, 0),)),
        (6, ((OWN, 0, 2, 1), (FWD_Y, 0, 0), (FWD_Y, 0, 1),)),
        (8, ((OWN, 1, 1, 0), (PASS_Z, 1, 1), (PASS_Z, 3, 1),)),
        (9, ((PASS_Y, 0, 0),)),
        (10, ((OWN, 1, 1, 1),)),
        (11, ((OWN, 1, 3, 0), (FWD_Y, 1, 0), (FWD_Y, 3, 0),)),
        (12, ((OWN, 1, 2, 1), (PASS_Z, 2, 0), (PASS_Z, 2, 1),)),
        (13, ((OWN, 1, 3, 1),)),
        (14, ((OWN, 1, 2, 0), (FWD_Y, 1, 1), (FWD_Y, 3, 1), (PASS_Y, 3, 0),)),
        (16, ((FWD_Y, 2, 0), (FWD_Y, 2, 1),)),
        (17, ((PASS_Y, 1, 1),)),
        (18, ((PASS_Y, 2, 1),)),
    ),
    (
        (2, ((CROSSF, 0), (CROSSF, 1), (OWN, 0, 1, 0), (OWN, 0, 3, 0), (PASS_Z, 0, 0), (PASS_Z, 0, 1),)),
        (3, ((OWN, 0, 1, 1), (OWN, 0, 3, 1),)),
        (4, ((OWN, 1, 0, 0), (OWN, 1, 0, 1), (PASS_Z, 1, 0), (PASS_Z, 3, 0),)),
        (5, ((OWN, 0, 2, 0),)),
        (6, ((OWN, 0, 2, 1), (PAR, 0, 0, 0), (PAR, 0, 0, 1),)),
        (8, ((OWN, 1, 1, 0), (OWN, 1, 3, 0), (PASS_Z, 1, 1), (PASS_Z, 3, 1),)),
        (9, ((PASS_Y, 0, 0),)),
        (10, ((OWN, 1, 1, 1),)),
        (11, ((OWN, 1, 3, 1), (PAR, 0, 1, 0), (PAR, 0, 3, 0),)),
        (12, ((OWN, 1, 2, 0), (OWN, 1, 2, 1), (PASS_Z, 2, 0), (PASS_Z, 2, 1), (PAR, 1, 0, 0), (PAR, 1, 0, 1),)),
        (13, ((PAR, 0, 3, 1), (PAR, 0, 1, 1),)),
        (14, ((PASS_Y, 3, 0),)),
        (15, ((PAR, 0, 2, 0), (PAR, 0, 2, 1),)),
        (17, ((PASS_Y, 1, 1), (PAR, 1, 1, 0),)),
        (18, ((PAR, 1, 3, 0),)),
        (19, ((PASS_Y, 2, 1), (PAR, 1, 3, 1),)),
        (20, ((PAR, 1, 1, 1), (PAR, 1, 2, 0),)),
        (21, ((PAR, 1, 2, 1),)),
    ),
    (
        (2, ((CROSSF, 0), (CROSSF, 1), (OWN, 0, 1, 0), (OWN, 0, 3, 0), (PASS_Z, 0, 0), (PASS_Z, 0, 1),)),
        (3, ((OWN, 0, 1, 1), (OWN, 0, 3, 1),)),
        (4, ((OWN, 1, 0, 0), (OWN, 1, 0, 1), (PASS_Z, 1, 0), (PASS_Z, 3, 0),)),
        (5, ((OWN, 0, 2, 0),)),
        (6, ((OWN, 0, 2, 1), (PAR, 0, 0, 0), (PAR, 0, 0, 1),)),
        (8, ((OWN, 1, 1, 0), (OWN, 1, 3, 0), (PASS_Z, 1, 1), (PASS_Z, 3, 1),)),
        (9, ((PASS_Y, 0, 1),)),
        (10, ((OWN, 1, 1, 1),)),
        (11, ((OWN, 1, 3, 1), (PAR, 0, 1, 0), (PAR, 0, 3, 0),)),
        (12, ((OWN, 1, 2, 0), (OWN, 1, 2, 1), (PASS_Z, 2, 0), (PASS_Z, 2, 1), (PAR, 1, 0, 0), (PAR, 1, 0, 1),)),
        (13, ((PAR, 0, 3, 1), (PAR, 0, 1, 1),)),
        (14, ((PASS_Y, 1, 0),)),
        (15, ((PAR, 0, 2, 0), (PAR, 0, 2, 1),)),
        (17, ((PASS_Y, 3, 1), (PAR, 1, 3, 0),)),
        (18, ((PAR, 1, 1, 0),)),
        (19, ((PASS_Y, 2, 0), (PAR, 1, 1, 1),)),
        (20, ((PAR, 1, 3, 1), (PAR, 1, 2, 1),)),
        (21, ((PAR, 1, 2, 0),)),
    ),
    (
        (2, ((CROSSF, 0), (OWN, 0, 1, 0), (OWN, 0, 3, 0), (PASS_Z, 0, 0), (PASS_Z, 0, 1), (PAR, 0, 0, 0),)),
        (3, ((CROSSF, 1), (OWN, 0, 1, 1), (OWN, 0, 3, 1), (PAR, 1, 0, 0),)),
        (4, ((PASS_Z, 1, 0), (PASS_Z, 3, 0),)),
        (5, ((OWN, 0, 2, 0), (PAR, 0, 0, 1), (PAR, 1, 0, 1),)),
        (6, ((OWN, 0, 2, 1), (FWD_Y, 0, 0), (FWD_Y, 0, 1),)),
        (7, ((OWN, 1, 0, 0), (OWN, 1, 1, 0), (PAR, 0, 1, 0),)),
        (8, ((OWN, 1, 3, 0), (PASS_Z, 1, 1), (PASS_Z, 3, 1),)),
        (9, ((OWN, 1, 1, 1), (PAR, 0, 3, 0), (PAR, 1, 1, 0),)),
        (10, ((OWN, 1, 3, 1), (FWD_Y, 1, 0), (FWD_Y, 3, 0),)),
        (11, ((OWN, 1, 0, 1), (OWN, 1, 2, 0), (PASS_Z, 2, 0), (PASS_Z, 2, 1), (PAR, 1, 3, 0),)),
        (12, ((OWN, 1, 2, 1), (PAR, 0, 1, 1), (PAR, 1, 1, 1),)),
        (13, ((FWD_Y, 1, 1), (FWD_Y, 3, 1),)),
        (14, ((FWD_Y, 2, 0), (PAR, 0, 3, 1), (PAR, 1, 3, 1),)),
        (15, ((FWD_Y, 2, 1),)),
        (16, ((PAR, 0, 2, 0), (PAR, 1, 2, 0),)),
        (17, ((PAR, 0, 2, 1), (PAR, 1, 2, 1),)),
    ),
    (
        (2, ((CROSSF, 0), (OWN, 0, 1, 0), (OWN, 0, 3, 0), (PASS_Z, 0, 0), (PASS_Z, 0, 1), (PAR, 1, 0, 0),)),
        (3, ((CROSSF, 1), (OWN, 0, 1, 1), (OWN, 0, 3, 1), (PAR, 0, 0, 0),)),
        (4, ((PASS_Z, 1, 0), (PASS_Z, 3, 0),)),
        (5, ((OWN, 0, 2, 0), (PAR, 0, 0, 1), (PAR, 1, 0, 1),)),
        (6, ((OWN, 0, 2, 1), (FWD_Y, 0, 0), (FWD_Y, 0, 1),)),
        (7, ((OWN, 1, 0, 0), (OWN, 1, 0, 1), (OWN, 1, 1, 0),)),
        (8, ((OWN, 1, 3, 0), (PASS_Z, 1, 1), (PASS_Z, 3, 1),)),
        (9, ((OWN, 1, 1, 1), (PAR, 0, 1, 0), (PAR, 1, 1, 0),)),
        (10, ((OWN, 1, 3, 1), (FWD_Y, 1, 0), (FWD_Y, 3, 0),)),
        (11, ((OWN, 1, 2, 0), (OWN, 1, 2, 1), (PASS_Z, 2, 0), (PASS_Z, 2, 1), (PAR, 0, 3, 0), (PAR, 1, 3, 0),)),
        (12, ((PAR, 0, 1, 1), (PAR, 1, 1, 1),)),
        (13, ((FWD_Y, 1, 1), (FWD_Y, 3, 1),)),
        (14, ((FWD_Y, 2, 0), (FWD_Y, 2, 1), (PAR, 0, 3, 1), (PAR, 1, 3, 1),)),
        (16, ((PAR, 0, 2, 0), (PAR, 1, 2, 0),)),
        (17, ((PAR, 0, 2, 1), (PAR, 1, 2, 1),)),
    ),
    (
        (2, ((CROSSF, 0), (CROSSF, 1), (OWN, 0, 1, 0), (OWN, 0, 3, 0), (PASS_Z, 0, 0), (PASS_Z, 0, 1),)),
        (3, ((OWN, 0, 1, 1), (OWN, 0, 3, 1),)),
        (4, ((OWN, 1, 0, 0), (OWN, 1, 0, 1), (PASS_Z, 1, 0), (PASS_Z, 3, 0),)),
        (5, ((OWN, 0, 2, 0),)),
        (6, ((OWN, 0, 2, 1), (FWD_Y, 0, 0), (FWD_Y, 0, 1),)),
        (7, ((OWN, 1, 1, 0),)),
        (8, ((OWN, 1, 3, 0), (PASS_Z, 1, 1), (PASS_Z, 3, 1),)),
        (9, ((OWN, 1, 1, 1), (PAR, 0, 0, 0), (PAR, 1, 0, 0),)),
        (10, ((OWN, 1, 3, 1), (FWD_Y, 1, 0), (FWD_Y, 3, 0), (PAR, 1, 0, 1), (PAR, 0, 0, 1),)),
        (11, ((OWN, 1, 2, 0), (OWN, 1, 2, 1), (PASS_Z, 2, 0), (PASS_Z, 2, 1), (PAR, 0, 1, 0),)),
        (12, ((FWD_Y, 1, 1), (FWD_Y, 3, 1), (PAR, 1, 1, 0),)),
        (13, ((PAR, 0, 3, 0),)),
        (14, ((FWD_Y, 2, 0), (FWD_Y, 2, 1), (PAR, 1, 3, 0),)),
        (15, ((PAR, 0, 1, 1), (PAR, 1, 1, 1),)),
        (17, ((PAR, 0, 3, 1), (PAR, 1, 3, 1),)),
        (18, ((PAR, 0, 2, 0), (PAR, 1, 2, 0),)),
        (19, ((PAR, 0, 2, 1),)),
        (20, ((PAR, 1, 2, 1),)),
    ),
    (
        (2, ((CROSSF, 0), (CROSSF, 1), (OWN, 0, 1, 0), (OWN, 0, 3, 0), (PASS_Z, 0, 0), (PASS_Z, 0, 1),)),
        (3, ((OWN, 0, 1, 1), (OWN, 0, 3, 1),)),
        (4, ((OWN, 1, 0, 0), (PASS_Z, 1, 0), (PASS_Z, 3, 0),)),
        (5, ((OWN, 0, 2, 0),)),
        (6, ((OWN, 0, 2, 1), (OWN, 1, 0, 1), (FWD_Y, 0, 0), (FWD_Y, 0, 1),)),
        (7, ((OWN, 1, 1, 0),)),
        (8, ((OWN, 1, 3, 0), (PASS_Z, 1, 1), (PASS_Z, 3, 1),)),
        (9, ((OWN, 1, 1, 1), (PAR, 0, 0, 0), (PAR, 1, 0, 0),)),
        (10, ((OWN, 1, 3, 1), (FWD_Y, 1, 0), (FWD_Y, 3, 0), (PAR, 1, 0, 1), (PAR, 0, 0, 1),)),
        (11, ((OWN, 1, 2, 0), (OWN, 1, 2, 1), (PASS_Z, 2, 0), (PASS_Z, 2, 1), (PAR, 0, 1, 0),)),
        (12, ((FWD_Y, 1, 1), (FWD_Y, 3, 1), (PAR, 1, 1, 0),)),
        (13, ((PAR, 0, 3, 0),)),
        (14, ((FWD_Y, 2, 0), (FWD_Y, 2, 1), (PAR, 1, 3, 0),)),
        (15, ((PAR, 0, 1, 1), (PAR, 1, 1, 1),)),
        (17, ((PAR, 0, 3, 1), (PAR, 1, 3, 1),)),
        (18, ((PAR, 0, 2, 0), (PAR, 1, 2, 0),)),
        (19, ((PAR, 0, 2, 1),)),
        (20, ((PAR, 1, 2, 1),)),
    ),
    (
        (2, ((CROSSF, 0), (CROSSF, 1), (OWN, 0, 1, 0), (OWN, 0, 3, 0), (FWD_Y, 0, 0), (PAR, 0, 0, 0),)),
        (3, ((OWN, 0, 1, 1), (OWN, 0, 3, 1), (FWD_Y, 0, 1), (PAR, 0, 0, 1),)),
        (4, ((OWN, 1, 0, 0), (OWN, 1, 0, 1),)),
        (5, ((OWN, 0, 2, 0), (FWD_Y, 1, 0), (PAR, 0, 1, 0),)),
        (6, ((OWN, 0, 2, 1), (PASS_Y, 0, 0), (PASS_Y, 0, 1),)),
        (7, ((FWD_Y, 3, 0), (PAR, 0, 3, 0),)),
        (8, ((OWN, 1, 3, 0), (PASS_Y, 1, 0),)),
        (9, ((FWD_Y, 1, 1), (PAR, 0, 1, 1), (PAR, 1, 0, 0),)),
        (10, ((OWN, 1, 3, 1), (PAR, 1, 0, 1),)),
        (11, ((OWN, 1, 1, 0), (FWD_Y, 3, 1), (PASS_Y, 3, 0), (PAR, 0, 3, 1),)),
        (12, ((OWN, 1, 2, 0), (OWN, 1, 2, 1), (PAR, 1, 1, 0),)),
        (13, ((FWD_Y, 2, 0), (PASS_Y, 1, 1), (PAR, 0, 2, 0),)),
        (14, ((OWN, 1, 1, 1), (FWD_Y, 2, 1), (PASS_Y, 3, 1), (PAR, 0, 2, 1), (PAR, 1, 3, 0),)),
        (15, ((PASS_Y, 2, 0),)),
        (16, ((PAR, 1, 1, 1),)),
        (17, ((PASS_Y, 2, 1), (PAR, 1, 3, 1),)),
        (18, ((PAR, 1, 2, 0),)),
        (20, ((PAR, 1, 2, 1),)),
    ),
    (
        (2, ((CROSSF, 0), (CROSSF, 1), (OWN, 0, 1, 0), (OWN, 0, 3, 0), (FWD_Y, 0, 0), (PAR, 0, 0, 0),)),
        (3, ((OWN, 0, 1, 1), (OWN, 0, 3, 1), (FWD_Y, 0, 1), (PAR, 0, 0, 1),)),
        (4, ((OWN, 1, 0, 0), (OWN, 1, 0, 1),)),
        (5, ((OWN, 0, 2, 0), (FWD_Y, 1, 0), (PAR, 0, 1, 0),)),
        (6, ((OWN, 0, 2, 1), (PASS_Y, 0, 0), (PASS_Y, 0, 1),)),
        (7, ((FWD_Y, 3, 0), (PAR, 0, 3, 0),)),
        (8, ((OWN, 1, 3, 0), (PASS_Y, 1, 0),)),
        (9, ((FWD_Y, 1, 1), (PAR, 0, 1, 1), (PAR, 1, 0, 0),)),
        (10, ((OWN, 1, 3, 1), (PAR, 1, 0, 1),)),
        (11, ((OWN, 1, 1, 0), (FWD_Y, 3, 1), (PASS_Y, 3, 0), (PAR, 0, 3, 1),)),
        (12, ((OWN, 1, 1, 1), (OWN, 1, 2, 0), (PAR, 1, 1, 0),)),
        (13, ((FWD_Y, 2, 0), (PASS_Y, 1, 1), (PAR, 0, 2, 0),)),
        (14, ((OWN, 1, 2, 1), (FWD_Y, 2, 1), (PASS_Y, 3, 1), (PAR, 0, 2, 1), (PAR, 1, 3, 0),)),
        (16, ((PASS_Y, 2, 0), (PAR, 1, 1, 1),)),
        (17, ((PAR, 1, 3, 1),)),
        (18, ((PASS_Y, 2, 1),)),
        (19, ((PAR, 1, 2, 0),)),
        (20, ((PAR, 1, 2, 1),)),
    ),
    (
        (2, ((CROSSF, 0), (CROSSF, 1), (OWN, 0, 1, 0), (OWN, 0, 3, 0), (FWD_Y, 0, 0), (PAR, 0, 0, 0),)),
        (3, ((OWN, 0, 1, 1), (OWN, 0, 3, 1), (FWD_Y, 0, 1), (PAR, 0, 0, 1),)),
        (4, ((OWN, 1, 0, 0), (OWN, 1, 0, 1),)),
        (5, ((OWN, 0, 2, 0), (FWD_Y, 1, 0), (PAR, 0, 1, 0),)),
        (6, ((OWN, 0, 2, 1), (PASS_Y, 0, 0), (PASS_Y, 0, 1),)),
        (7, ((OWN, 1, 1, 0), (FWD_Y, 3, 0), (PAR, 0, 3, 0),)),
        (8, ((OWN, 1, 3, 0), (PASS_Y, 1, 0),)),
        (9, ((OWN, 1, 1, 1), (FWD_Y, 1, 1), (PAR, 0, 1, 1), (PAR, 1, 0, 0),)),
        (10, ((OWN, 1, 3, 1), (PAR, 1, 0, 1),)),
        (11, ((OWN, 1, 2, 1), (FWD_Y, 3, 1), (PASS_Y, 3, 0), (PAR, 0, 3, 1),)),
        (12, ((OWN, 1, 2, 0), (PAR, 1, 1, 0),)),
        (13, ((FWD_Y, 2, 0), (PASS_Y, 1, 1), (PAR, 0, 2, 0),)),
        (14, ((FWD_Y, 2, 1), (PASS_Y, 3, 1), (PAR, 0, 2, 1), (PAR, 1, 3, 0),)),
        (16, ((PASS_Y, 2, 0), (PAR, 1, 1, 1),)),
        (17, ((PAR, 1, 3, 1),)),
        (18, ((PASS_Y, 2, 1),)),
        (19, ((PAR, 1, 2, 0),)),
        (20, ((PAR, 1, 2, 1),)),
    ),
    (
        (2, ((CROSSF, 0), (CROSSF, 1), (OWN, 0, 1, 0), (OWN, 0, 3, 0), (FWD_Y, 0, 0), (PAR, 0, 0, 0),)),
        (3, ((OWN, 0, 1, 1), (OWN, 0, 3, 1), (FWD_Y, 0, 1), (PAR, 0, 0, 1),)),
        (4, ((OWN, 1, 0, 0), (OWN, 1, 0, 1),)),
        (5, ((OWN, 0, 2, 0), (FWD_Y, 1, 0), (PAR, 0, 1, 0),)),
        (6, ((OWN, 0, 2, 1), (PASS_Y, 0, 0), (PASS_Y, 0, 1),)),
        (7, ((OWN, 1, 1, 0), (FWD_Y, 3, 0), (PAR, 0, 3, 0),)),
        (8, ((OWN, 1, 3, 0), (PASS_Y, 1, 0),)),
        (9, ((OWN, 1, 1, 1), (FWD_Y, 1, 1), (PAR, 0, 1, 1), (PAR, 1, 0, 0),)),
        (10, ((OWN, 1, 3, 1), (PAR, 1, 0, 1),)),
        (11, ((OWN, 1, 2, 1), (FWD_Y, 3, 1), (PASS_Y, 3, 0), (PAR, 0, 3, 1),)),
        (12, ((OWN, 1, 2, 0), (PAR, 1, 1, 0),)),
        (13, ((FWD_Y, 2, 0), (PASS_Y, 1, 1), (PAR, 0, 2, 0),)),
        (14, ((FWD_Y, 2, 1), (PASS_Y, 3, 1), (PAR, 0, 2, 1), (PAR, 1, 3, 0),)),
        (16, ((PASS_Y, 2, 0), (PAR, 1, 1, 1),)),
        (17, ((PAR, 1, 3, 1),)),
        (18, ((PASS_Y, 2, 1),)),
        (19, ((PAR, 1, 2, 0),)),
        (20, ((PAR, 1, 2, 1),)),
    ),
    (
        (2, ((CROSSF, 0), (CROSSF, 1), (OWN, 0, 1, 0), (OWN, 0, 3, 0), (FWD_Y, 0, 0),)),
        (3, ((OWN, 0, 1, 1), (OWN, 0, 3, 1), (FWD_Y, 0, 1),)),
        (4, ((OWN, 1, 0, 0), (OWN, 1, 0, 1),)),
        (5, ((OWN, 0, 2, 0), (FWD_Y, 1, 0),)),
        (6, ((OWN, 0, 2, 1), (PAR, 0, 0, 0), (PAR, 1, 0, 0),)),
        (7, ((OWN, 1, 1, 0), (FWD_Y, 3, 0),)),
        (8, ((OWN, 1, 3, 0), (PAR, 0, 0, 1), (PAR, 1, 0, 1),)),
        (9, ((OWN, 1, 1, 1), (FWD_Y, 1, 1),)),
        (10, ((OWN, 1, 3, 1), (PAR, 0, 1, 0), (PAR, 1, 1, 0),)),
        (11, ((FWD_Y, 3, 1),)),
        (12, ((PAR, 0, 3, 0), (PAR, 1, 3, 0),)),
        (13, ((FWD_Y, 2, 0),)),
        (14, ((OWN, 1, 2, 0), (FWD_Y, 2, 1), (PAR, 0, 1, 1), (PAR, 1, 1, 1),)),
        (15, ((PAR, 0, 3, 1), (PAR, 1, 3, 1),)),
        (17, ((OWN, 1, 2, 1), (PAR, 0, 2, 0), (PAR, 1, 2, 0),)),
        (18, ((PAR, 0, 2, 1), (PAR, 1, 2, 1),)),
    ),
    (
        (2, ((CROSSF, 0), (CROSSF, 1), (OWN, 0, 1, 0), (OWN, 0, 3, 0), (FWD_Y, 0, 0),)),
        (3, ((OWN, 0, 1, 1), (OWN, 0, 3, 1), (FWD_Y, 0, 1),)),
        (4, ((OWN, 1, 0, 0), (OWN, 1, 0, 1),)),
        (5, ((OWN, 0, 2, 0), (FWD_Y, 1, 0),)),
        (6, ((OWN, 0, 2, 1), (PAR, 0, 0, 0), (PAR, 1, 0, 0),)),
        (7, ((OWN, 1, 1, 0), (FWD_Y, 3, 0),)),
        (8, ((OWN, 1, 3, 0), (PAR, 0, 0, 1), (PAR, 1, 0, 1),)),
        (9, ((OWN, 1, 1, 1), (FWD_Y, 1, 1),)),
        (10, ((OWN, 1, 3, 1), (PAR, 0, 1, 0), (PAR, 1, 1, 0),)),
        (11, ((FWD_Y, 3, 1),)),
        (12, ((PAR, 0, 3, 0), (PAR, 1, 3, 0),)),
        (13, ((FWD_Y, 2, 0),)),
        (14, ((OWN, 1, 2, 0), (FWD_Y, 2, 1), (PAR, 0, 1, 1), (PAR, 1, 1, 1),)),
        (15, ((OWN, 1, 2, 1), (PAR, 0, 3, 1), (PAR, 1, 3, 1),)),
        (17, ((PAR, 0, 2, 0), (PAR, 1, 2, 0),)),
        (18, ((PAR, 0, 2, 1), (PAR, 1, 2, 1),)),
    ),
    (
        (2, ((CROSSF, 0), (CROSSF, 1), (OWN, 0, 1, 0), (OWN, 0, 3, 0), (FWD_Y, 0, 0),)),
        (3, ((OWN, 0, 1, 1), (OWN, 0, 3, 1), (FWD_Y, 0, 1),)),
        (4, ((OWN, 1, 0, 0), (OWN, 1, 0, 1),)),
        (5, ((OWN, 0, 2, 0), (FWD_Y, 1, 0),)),
        (6, ((OWN, 0, 2, 1), (PAR, 0, 0, 0), (PAR, 1, 0, 0),)),
        (7, ((OWN, 1, 1, 0), (FWD_Y, 3, 0),)),
        (8, ((OWN, 1, 3, 0), (PAR, 0, 0, 1), (PAR, 1, 0, 1),)),
        (9, ((OWN, 1, 1, 1), (FWD_Y, 1, 1),)),
        (10, ((OWN, 1, 3, 1), (PAR, 0, 1, 0), (PAR, 1, 1, 0),)),
        (11, ((OWN, 1, 2, 1), (FWD_Y, 3, 1),)),
        (12, ((OWN, 1, 2, 0), (PAR, 0, 3, 0), (PAR, 1, 3, 0),)),
        (13, ((FWD_Y, 2, 0),)),
        (14, ((FWD_Y, 2, 1), (PAR, 0, 1, 1), (PAR, 1, 1, 1),)),
        (15, ((PAR, 0, 3, 1), (PAR, 1, 3, 1),)),
        (17, ((PAR, 0, 2, 0), (PAR, 1, 2, 0),)),
        (18, ((PAR, 0, 2, 1), (PAR, 1, 2, 1),)),
    ),
    (
        (2, ((CROSSF, 0), (CROSSF, 1), (OWN, 0, 1, 0), (OWN, 0, 3, 0), (FWD_Y, 0, 0),)),
        (3, ((OWN, 0, 1, 1), (OWN, 0, 3, 1), (FWD_Y, 0, 1),)),
        (4, ((OWN, 1, 0, 0), (OWN, 1, 0, 1),)),
        (5, ((OWN, 0, 2, 0), (FWD_Y, 1, 0),)),
        (6, ((OWN, 0, 2, 1), (PAR, 0, 0, 0), (PAR, 1, 0, 0),)),
        (7, ((OWN, 1, 1, 0), (FWD_Y, 3, 0),)),
        (8, ((OWN, 1, 3, 0), (PAR, 0, 0, 1), (PAR, 1, 0, 1),)),
        (9, ((OWN, 1, 1, 1), (FWD_Y, 1, 1),)),
        (10, ((OWN, 1, 3, 1), (PAR, 0, 1, 0), (PAR, 1, 1, 0),)),
        (11, ((OWN, 1, 2, 1), (FWD_Y, 3, 1),)),
        (12, ((OWN, 1, 2, 0), (PAR, 0, 3, 0), (PAR, 1, 3, 0),)),
        (13, ((FWD_Y, 2, 0),)),
        (14, ((FWD_Y, 2, 1), (PAR, 0, 1, 1), (PAR, 1, 1, 1),)),
        (15, ((PAR, 0, 3, 1), (PAR, 1, 3, 1),)),
        (17, ((PAR, 0, 2, 0), (PAR, 1, 2, 0),)),
        (18, ((PAR, 0, 2, 1), (PAR, 1, 2, 1),)),
    ),
)

STAGES = len(SEQUENCE)
BASES = [sum(PARTS[stage] for stage in SEQUENCE[:n]) for n in range(STAGES + 1)]
POINTS = BASES[-1] + 1
PAR_AT, T1_AT, T2_AT, T3_AT, TC_AT, SLOTS = 32, 64, 72, 80, 88, 90
WAYS = ("x+", "x-", "y+", "y-", "z+", "z-", "core", "ya", "yb", "za", "zb")
WAIT = 15
CLASSES = [(x, y) for x in range(4) for y in range(4)]


def sign_of(j, k):
    return "+" if (k + (0, 1, 1, 0)[j]) % 2 == 0 else "-"


def name_of(x, y, row, j):
    return (y // 2 + row) % 2 * 4 + (x + 4 - j) % 4


def row_behind(y, sign):
    return (y + 3) % 4 // 2 if sign == "+" else (y + 1) % 4 // 2


def feed(x, y, j, k, src):
    up = y // 2 == 1
    final, via1, via2 = ("par", name_of(x, y, 0, j), k), ("t1", j, k), ("t2", j, k)
    sends = []
    if x in (0, 1):
        sends.append((src, via1, "z" + sign_of(j, k)))
    if x == 1:
        sends.append((src, final, "ya"))
    if x in (2, 3):
        sends.append((src, final if x == 2 and not up else via1, "za"))
        sends.append((src, final if x == 2 and up else via2, "zb"))
    return sends


def expand(x, y, event):
    kind, args = event[0], event[1:]
    up = y // 2 == 1
    ops = []
    if kind == CROSSF:
        (k,) = args
        sign = "+-"[k]
        ops = [("tc", k), (("tc", k), ("own", row_behind(y, sign) * 4 + x, k), "y" + sign)]
    if kind == OWN:
        row, j, k = args
        here = ("own", name_of(x, y, row, j), k)
        ops = [here]
        if (row, j) == (1, 0) or (j == 1 and (k + row) % 2 == 0):
            ops.append((here, here, "x+"))
        if (row, j) == (1, 0) or (j == 3 and (k + row) % 2 == 1):
            ops.append((here, here, "x-"))
        if row == 0:
            ops += feed(x, y, j, k, here)
        ops.append((here, here, "core"))
    if kind == PASS_Z:
        j, k = args
        here = ("t1", j, k)
        there = ("par", name_of(x, y, 0, j), k) if x == 0 and up else ("t2", j, k)
        ops = [here, (here, there, "z" + sign_of(j, k))]
    if kind == FWD_Y:
        j, k = args
        final, there, way = ("par", name_of(x, y, 0, j), k), ("t3", j, k), "y" + sign_of(j, k)
        if x == 3 or (x == 2 and up):
            ops += [("t1", j, k), (("t1", j, k), final, "ya") if x == 3 else (("t1", j, k), there, way)]
        if x in (1, 3) or not up:
            ops += [("t2", j, k), (("t2", j, k), final, "yb") if x in (1, 3) else (("t2", j, k), there, way)]
    if kind == PASS_Y:
        j, k = args
        sign = sign_of(j, k)
        row = row_behind(y, sign)
        if x == 2 or row == 0:
            ops = [("t3", j, k), (("t3", j, k), ("par", row * 4 + (x + 4 - j) % 4, k), "y" + sign)]
    if kind == PAR:
        row, j, k = args
        here = ("par", name_of(x, y, row, j), k)
        ops = [here, (here, here, "core")]
    return ops


def slot(place, c):
    kind, rest = place[0], place[1:]
    if kind in ("own", "par"):
        q, k = rest
        return (PAR_AT if kind == "par" else 0) + q * 4 + c * 2 + k
    if kind == "tc":
        return TC_AT + rest[0]
    return {"t1": T1_AT, "t2": T2_AT, "t3": T3_AT}[kind] + rest[0] * 2 + rest[1]


def tables(x, y):
    per_core = []
    for c in range(2):
        ops, begins, sends, at = [], [], 0, dict(EVENTS[CLASSES.index((x, y))])
        for point in range(POINTS):
            begins.append(len(ops))
            for event in at.get(point, ()):
                for op in expand(x, y, event):
                    if isinstance(op[0], str):
                        ops.append(slot(op, c) + 2097152 * WAIT)
                    else:
                        src, dst, way = op
                        ops.append(slot(src, c) + 128 * slot(dst, c) + 16384 * sends + 2097152 * WAYS.index(way))
                        sends += 1
        per_core.append((ops, begins + [len(ops), sends], sends))
    return per_core


TABLES = {cls: tables(*cls) for cls in CLASSES}
MOST_OPS = max(len(ops) for cores in TABLES.values() for ops, _, _ in cores)
MOST_SENDS = max(sends for cores in TABLES.values() for _, _, sends in cores)
FIRST_SENDS = 12


def columns(t):
    first, last = t * 256, (t + 1) * 256
    cuts = [first] + [cut for cut in range(0, NI * V, V) if first < cut < last] + [last]
    return [(u - first, w - first, u // V, u % V) for u, w in zip(cuts, cuts[1:])]


def kernel(dims, mine, amps, out, out_own, out_par, buf, rc, half, acc, ops, begins, devs,
           ssem, first_sem, rsem, local_sem):
    sym, tile, c = lax.axis_index("sym"), lax.axis_index("tile"), lax.axis_index("occ")
    x, yhi = sym % 4, sym // 4
    x0, x1 = x % 2, x // 2
    z, ylo = tile // 2, tile % 2
    z0, z1 = z % 2, z // 2
    y = 2 * yhi + ylo
    none = sym == 0

    def dev(dx=0, dy=0, dz=0, dc=0):
        xx, yy, zz = (x + 4 + dx) % 4, (y + 4 + dy) % 4, (z + 4 + dz) % 4
        return ((yy // 2) * 4 + xx) * 16 + (zz * 2 + yy % 2) * 2 + (c + dc) % 2

    step_a = 1 - 2 * (yhi + ylo - 2 * yhi * ylo)
    step_z = 1 - 2 * z0
    to = {
        "x+": dev(dx=1), "x-": dev(dx=-1), "y+": dev(dy=1), "y-": dev(dy=-1), "z+": dev(dz=1), "z-": dev(dz=-1),
        "core": dev(dc=1), "ya": dev(dy=step_a), "yb": dev(dy=-step_a), "za": dev(dz=step_z), "zb": dev(dz=-step_z),
    }
    barrier = pltpu.get_barrier_semaphore()
    for way in WAYS[:7]:
        pl.semaphore_signal(barrier, inc=1, device_id=to[way], device_id_type=pl.DeviceIdType.LOGICAL)

    def own_slot(q, core, k):
        return q * 4 + core * 2 + k

    keep = []
    for k in range(PIECES):
        keep.append(pltpu.make_async_copy(mine.at[pl.ds(k * PV, PV)], buf.at[own_slot(sym, c, k)], local_sem.at[8 + k]))
        keep[-1].start()
    loads = [pltpu.make_async_copy(amps.at[i], rc.at[:, pl.ds(i * V, V)], local_sem.at[i]) for i in range(NI)]
    for load in loads:
        load.start()

    pl.semaphore_wait(barrier, 7)

    def remote(src, dst_slot, sem, where):
        return pltpu.make_async_remote_copy(
            src, buf.at[dst_slot], sem, rsem.at[dst_slot], device_id=where, device_id_type=pl.DeviceIdType.LOGICAL
        )

    def arrived(at):
        remote(buf.at[at], at, first_sem.at[0], to["core"]).wait_recv()

    firsts = []

    def first(src, place, where, cond=None):
        index = len(firsts)
        if cond is None:
            remote(src, place, first_sem.at[index], where).start()
        else:
            pl.when(cond)(lambda: remote(src, place, first_sem.at[index], where).start())
        firsts.append((src, place, cond, index))

    step_2 = {k: {"+": to["z+"], "-": to["z-"]}[sign_of(0, k)] for k in range(PIECES)}
    for k in range(PIECES):
        src = mine.at[pl.ds(k * PV, PV)]
        home = own_slot(sym, c, k)
        final, via1, via2 = PAR_AT + home, T1_AT + k, T2_AT + k
        first(src, home, to["core"])
        first(src, home, to["x+"])
        first(src, home, to["x-"])
        first(src, TC_AT + k, to["y" + "+-"[k]])
        direct_b, direct_a = x0 + 2 * (1 - x1) + (1 - yhi) == 0, x0 + 2 * (1 - x1) + yhi == 0
        where_b = x1 * to["zb"] + (1 - x1) * step_2[k]
        place_b = jnp.where(direct_b, final, x1 * via2 + (1 - x1) * via1)
        first(src, place_b, where_b)
        where_a = x1 * to["za"] + (1 - x1) * to["ya"]
        place_a = jnp.where(direct_a | (x1 == 0), final, via1)
        first(src, place_a, where_a, x > 0)

    for (at_x, at_y), cores in TABLES.items():
        @pl.when((x == at_x) & (y == at_y))
        def _():
            (ops0, begins0, _), (ops1, _, _) = cores
            for n, (op0, op1) in enumerate(zip(ops0, ops1)):
                ops[n] = op0 + (op1 - op0) * c if op0 != op1 else op0
            for n, begin in enumerate(begins0):
                begins[n] = begin
    for n, way in enumerate(WAYS):
        devs[n] = to[way]

    n_row = dims[tile]
    n_col = dims[(z1 + yhi - 2 * z1 * yhi) * 4 + (z0 + x1 - 2 * z0 * x1) * 2 + (ylo + x0 - 2 * ylo * x0)]
    live_r = jnp.where(lax.broadcasted_iota(jnp.int32, (V, V), 0) < n_row, 1.0, 0.0)
    live = jnp.where(lax.broadcasted_iota(jnp.int32, (V, V), 1) < n_col, live_r, 0.0).astype(jnp.bfloat16)
    acc[...] = jnp.zeros_like(acc)
    for load in loads:
        load.wait()
    for i in range(NI):
        rc[:, i * V:(i + 1) * V] = rc[:, i * V:(i + 1) * V] * live
    for copy in keep:
        copy.wait()

    def decoded(n):
        op = ops[n]
        src, rest = lax.rem(op, 128), lax.div(op, 128)
        dst, rest = lax.rem(rest, 128), lax.div(rest, 128)
        return src, dst, lax.rem(rest, 128), lax.div(rest, 128)

    def events(point):
        @pl.loop(begins[point], begins[point + 1])
        def _(n):
            src, dst, index, way = decoded(n)

            @pl.when(way == WAIT)
            def _():
                arrived(src)

            @pl.when(way != WAIT)
            def _():
                remote(buf.at[src], dst, ssem.at[index], devs[way]).start()

    digit = (1 + 15 * x0) * (1 + 255 * x1)

    def chosen(groups, n):
        code = 0
        for number, names in enumerate(groups):
            of_y = [0] * 4
            for (at_x, at_y), (row, j, k) in zip(CLASSES, names):
                of_y[at_y] += (row * 8 + j * 2 + k) * 16 ** at_x
            value = of_y[0]
            if len(set(of_y)) > 1:
                value = value + (of_y[1] - of_y[0]) * ylo + (of_y[2] - of_y[0]) * yhi
                value = value + (of_y[3] - of_y[2] - of_y[1] + of_y[0]) * (yhi * ylo)
            code = code + (n == number) * 1 * value
        code = lax.rem(lax.div(code, digit), 16)
        return (yhi + code // 8) % 2 * 4 + (x + 4 - code // 2 % 4) % 4, code % 2

    def base_of(n):
        return sum((n == number) * base for number, base in enumerate(BASES[:-1]) if base)

    par_base = PAR_AT * (1 - (sym == 0) * 1)

    def unit(base, q, core):
        at = base + q * 4 + core * 2
        return buf[pl.ds(at, 2)].reshape(V, V)

    def first_stage(base, halves):
        for q, k in halves:
            arrived(own_slot(q, 1 - c, k))
        for h in range(PARTS[1]):
            if h:
                events(base + h)
            for t in range(h * 12 // PARTS[1], (h + 1) * 12 // PARTS[1]):
                left = jnp.concatenate([buf[q * 4 + 2 * p + k] for q, k in halves for p in range(2)], axis=0)
                r = jnp.dot(left, rc[:, t * 256:(t + 1) * 256], preferred_element_type=jnp.float32).astype(jnp.bfloat16)
                for lo_col, hi_col, pair, at in columns(t):
                    for number, (q, k) in enumerate(halves):
                        rows = pl.ds(pl.multiple_of(pair * V + k * PV, PV), PV)
                        for p in range(2):
                            lanes = pl.ds(p * V + at, hi_col - lo_col)
                            first = (2 * number + p) * PV
                            half[q, rows, lanes] = r[first:first + PV, lo_col:hi_col]

    def second_stage(base, q, last=False):
        @pl.when(jnp.logical_not(none))
        def _():
            for k in range(PIECES):
                arrived(PAR_AT + own_slot(q, 1 - c, k))

        for h in range(2):
            if h and PARTS[2] > 1:
                events(base + h)
            rows = pl.ds(h * HALF, HALF)
            right = jnp.concatenate([unit(par_base, q, p) for p in range(2)], axis=1)
            for m in range(2 * h, 2 * h + 2):
                pairs = pl.ds(m * 2 * V, 2 * V)
                acc[pairs, :] += lax.dot_general(
                    half[q, pairs, :], right, (((1,), (1,)), ((), ())), preferred_element_type=jnp.float32
                )
            if last:
                pltpu.make_async_copy(acc.at[rows], out.at[rows], local_sem.at[h]).start()

    @pl.loop(0, STAGES - 1)
    def _(n):
        second = sum((n == k) * 1 for k, stage in enumerate(SEQUENCE) if stage == 2)
        halves = [chosen(group, n) for group in UNITS]
        base = base_of(n)
        events(base)
        pl.when(second == 0)(lambda: first_stage(base, halves))
        pl.when(second == 1)(lambda: second_stage(base, halves[0][0]))

    events(BASES[-2])
    second_stage(BASES[-2], chosen(UNITS[0], jnp.int32(STAGES - 1))[0], last=True)
    events(POINTS - 1)

    leaving = []
    for r in range(len(REST)):
        q, _ = chosen(REST, jnp.int32(r))
        for k in range(PIECES):
            arrived(own_slot(q, 1 - c, k))

        @pl.when(jnp.logical_not(none))
        def _():
            for k in range(PIECES):
                arrived(PAR_AT + own_slot(q, 1 - c, k))

        par_at = par_base + q * 4
        for source, target, sem in ((q * 4, out_own.at[r], 18 + 2 * r), (par_at, out_par.at[r], 19 + 2 * r)):
            leaving.append(pltpu.make_async_copy(buf.at[pl.ds(source, 4)], target, local_sem.at[sem - 8]))
            leaving[-1].start()

    for src, place, cond, index in firsts:
        def sent(src=src, place=place, index=index):
            remote(src, place, first_sem.at[index], to["core"]).wait_send()

        if cond is None:
            sent()
        else:
            pl.when(cond)(sent)

    @pl.loop(0, begins[POINTS + 1])
    def _(n):
        remote(buf.at[0], 0, ssem.at[n], to["core"]).wait_send()

    for h in range(2):
        rows = pl.ds(h * HALF, HALF)
        pltpu.make_async_copy(acc.at[rows], out.at[rows], local_sem.at[h]).wait()
    for copy in leaving:
        copy.wait()


ALL = [(row, j) for j in (0, 1, 3, 2) for row in range(2)]


def left_over():
    by_class = []
    for at in range(len(CLASSES)):
        done = [names[at][:2] for group in UNITS for stage, names in zip(SEQUENCE, group) if stage == 1]
        by_class.append([name + (0,) for name in ALL if name not in done])
    return tuple(zip(*by_class))


REST = left_over()


def rest_kernel(dims, own_hbm, par_hbm, amps, raw, out, own, par, rc, half, acc, sems):
    sym, tile = lax.axis_index("sym"), lax.axis_index("tile")
    n, hi = len(REST), NI // 2
    get_own = pltpu.make_async_copy(own_hbm, own, sems.at[0])
    get_par = pltpu.make_async_copy(par_hbm, par, sems.at[1])
    get_amps = [pltpu.make_async_copy(amps.at[i], rc.at[:, pl.ds(i * V, V)], sems.at[2 + i]) for i in range(NI)]
    get_raw = [
        pltpu.make_async_copy(raw.at[pl.ds(h * HALF, HALF)], acc.at[pl.ds(h * HALF, HALF)], sems.at[2 + NI + h])
        for h in range(2)
    ]
    for copy in get_amps[:hi] + [get_own, get_par, get_raw[0]] + get_amps[hi:] + [get_raw[1]]:
        copy.start()
    n_row, n_col = dims[tile], dims[jnp.bitwise_xor(tile, sym)]
    live = (lax.broadcasted_iota(jnp.int32, (V, V), 0) < n_row) & (lax.broadcasted_iota(jnp.int32, (V, V), 1) < n_col)
    live_b = jnp.where(live, 1.0, 0.0).astype(jnp.bfloat16)
    puts = []
    for h in range(2):
        for i in range(h * hi, (h + 1) * hi):
            get_amps[i].wait()
            rc[:, i * V:(i + 1) * V] = rc[:, i * V:(i + 1) * V] * live_b
        if h == 0:
            get_own.wait()
        for t in range(6 * h, 6 * (h + 1)):
            left = own[...].reshape(n * 2 * V, V)
            r = jnp.dot(left, rc[:, t * 256:(t + 1) * 256], preferred_element_type=jnp.float32).astype(jnp.bfloat16)
            for lo_col, hi_col, pair, at in columns(t):
                for p in range(2 * n):
                    lanes = pl.ds(p * V + at, hi_col - lo_col)
                    half[(pair - h * hi) * V:(pair - h * hi + 1) * V, lanes] = r[p * V:(p + 1) * V, lo_col:hi_col]
        if h == 0:
            get_par.wait()
        get_raw[h].wait()
        rows = pl.ds(h * HALF, HALF)
        for b0, b1 in ((0, 256), (256, 384)):
            right = [par[r, pl.ds(2 * p, 2)].reshape(V, V)[b0:b1] for r in range(n) for p in range(2)]
            right = jnp.concatenate(right, axis=1)
            r = lax.dot_general(half[...], right, (((1,), (1,)), ((), ())), preferred_element_type=jnp.float32)
            r = r + acc[rows, b0:b1]
            for i in range(hi):
                at = pl.ds((h * hi + i) * V, V)
                acc[at, b0:b1] = jnp.where(live[:, b0:b1], r[i * V:(i + 1) * V], 0.0)
            lanes = pl.ds(b0, b1 - b0)
            puts.append(pltpu.make_async_copy(acc.at[rows, lanes], out.at[rows, lanes], sems.at[4 + NI + len(puts)]))
            puts[-1].start()
    for copy in puts:
        copy.wait()


def shards(irrep_dims, chol_vectors, amplitudes):
    bf, sem = jnp.bfloat16, pltpu.SemaphoreType.DMA
    n = len(REST)
    own, chol, amps = (n, 4, PV, V), chol_vectors.reshape(V, V), amplitudes.reshape(NI, V, V)
    anywhere = pl.BlockSpec(memory_space=pl.ANY)
    raw, rest_own, rest_par = pl.pallas_call(
        kernel,
        out_shape=[
            jax.ShapeDtypeStruct((NI * V, V), jnp.float32),
            jax.ShapeDtypeStruct(own, bf),
            jax.ShapeDtypeStruct(own, bf),
        ],
        in_specs=[pl.BlockSpec(memory_space=pltpu.SMEM), anywhere, anywhere],
        out_specs=[anywhere] * 3,
        scratch_shapes=[
            pltpu.VMEM((SLOTS, PV, V), bf),
            pltpu.VMEM((V, NI * V), bf),
            pltpu.VMEM((8, NI * V, 2 * V), bf),
            pltpu.VMEM((NI * V, V), jnp.float32),
            pltpu.SMEM((MOST_OPS,), jnp.int32),
            pltpu.SMEM((POINTS + 2,), jnp.int32),
            pltpu.SMEM((len(WAYS),), jnp.int32),
            sem((MOST_SENDS,)), sem((FIRST_SENDS,)), sem((SLOTS,)), sem((10 + 2 * n,)),
        ],
        compiler_params=pltpu.CompilerParams(
            collective_id=0, has_side_effects=True, vmem_limit_bytes=63 * 1024 * 1024
        ),
        cost_estimate=pl.CostEstimate(flops=(8 - n) * 3_600_000_000, bytes_accessed=12_000_000, transcendentals=0),
        name="ladder",
    )(irrep_dims, chol, amps)
    total = pl.pallas_call(
        rest_kernel,
        out_shape=jax.ShapeDtypeStruct((NI * V, V), jnp.float32),
        in_specs=[pl.BlockSpec(memory_space=pltpu.SMEM)] + [anywhere] * 4,
        out_specs=anywhere,
        scratch_shapes=[
            pltpu.VMEM(own, bf),
            pltpu.VMEM(own, bf),
            pltpu.VMEM((V, NI * V), bf),
            pltpu.VMEM((HALF, n * 2 * V), bf),
            pltpu.VMEM((NI * V, V), jnp.float32),
            sem((8 + NI,)),
        ],
        compiler_params=pltpu.CompilerParams(vmem_limit_bytes=60 * 1024 * 1024),
        cost_estimate=pl.CostEstimate(flops=n * 3_600_000_000, bytes_accessed=16_000_000, transcendentals=0),
        name="rest",
    )(irrep_dims, rest_own, rest_par, amps, raw)
    return total.reshape(1, NI, V, V)


def solution(mesh):
    return jax.shard_map(
        shards,
        mesh=mesh,
        in_specs=(P(), P(("sym", "occ"), "tile", None), P("sym", "occ", "tile", None)),
        out_specs=P("sym", "occ", "tile", None),
        check_vma=False,
    )
```

```python
import jax
import jax.numpy as jnp
from jax import lax
from jax.experimental import pallas as pl
from jax.experimental.pallas import tpu as pltpu
from jax.sharding import PartitionSpec as P

V = 384
NI = 8
PIECES = 2
PV = V // PIECES
HALF = NI * V // 2
CROSSF, OWN, PASS_Z, FWD_Y, PASS_Y, PAR = range(6)
PARTS = {1: 2, 2: 2}
SEQUENCE = (1, 1, 1, 1, 1, 1, 2, 2, 1, 2, 2, 2, 2, 2)
UNITS = (
    (
        ((0, 0, 0), (0, 0, 0), (0, 0, 0), (0, 0, 0), (0, 0, 0), (0, 0, 0), (0, 0, 0), (0, 0, 0), (0, 0, 0), (0, 0, 0), (0, 0, 0), (0, 0, 0), (0, 0, 0), (0, 0, 0), (0, 0, 0), (0, 0, 0)),
        ((0, 1, 0), (0, 1, 0), (0, 1, 0), (0, 1, 0), (0, 1, 0), (0, 1, 0), (0, 1, 0), (0, 1, 0), (0, 1, 0), (0, 1, 0), (0, 1, 0), (0, 1, 0), (0, 1, 0), (0, 1, 0), (0, 1, 0), (0, 1, 0)),
        ((0, 1, 1), (0, 1, 1), (0, 1, 1), (0, 1, 1), (0, 1, 1), (0, 1, 1), (0, 1, 1), (0, 1, 1), (0, 1, 1), (0, 1, 1), (0, 1, 1), (0, 1, 1), (0, 1, 1), (0, 1, 1), (0, 1, 1), (0, 1, 1)),
        ((1, 0, 0), (1, 0, 0), (1, 0, 0), (1, 0, 0), (0, 2, 0), (0, 2, 0), (1, 0, 0), (1, 0, 0), (1, 0, 0), (1, 0, 0), (1, 0, 0), (1, 0, 0), (1, 0, 0), (1, 0, 0), (1, 0, 0), (1, 0, 0)),
        ((0, 2, 0), (0, 2, 0), (0, 2, 0), (0, 2, 0), (1, 0, 0), (1, 0, 0), (0, 2, 0), (1, 0, 1), (0, 2, 0), (0, 2, 0), (0, 2, 0), (0, 2, 0), (0, 2, 0), (0, 2, 0), (0, 2, 0), (0, 2, 0)),
        ((1, 1, 0), (1, 1, 0), (1, 1, 0), (1, 1, 0), (1, 3, 0), (1, 1, 0), (1, 1, 0), (1, 1, 0), (1, 3, 0), (1, 3, 0), (1, 1, 0), (1, 1, 0), (1, 1, 0), (1, 1, 0), (1, 1, 0), (1, 1, 0)),
        ((0, 0, 0), (0, 0, 0), (0, 0, 0), (0, 0, 0), (0, 0, 0), (0, 0, 0), (0, 0, 0), (0, 0, 0), (0, 0, 0), (0, 0, 0), (0, 0, 0), (0, 0, 0), (0, 0, 0), (0, 0, 0), (0, 0, 0), (0, 0, 0)),
        ((1, 0, 0), (1, 0, 0), (1, 0, 0), (1, 0, 0), (0, 1, 0), (1, 0, 0), (1, 0, 0), (1, 0, 0), (1, 0, 0), (1, 0, 0), (1, 0, 0), (1, 0, 0), (1, 0, 0), (1, 0, 0), (1, 0, 0), (1, 0, 0)),
        ((1, 3, 0), (1, 3, 0), (1, 1, 1), (1, 1, 1), (1, 0, 1), (1, 1, 1), (1, 1, 1), (1, 1, 1), (1, 1, 0), (1, 1, 0), (1, 1, 1), (1, 1, 1), (1, 1, 1), (1, 1, 1), (1, 1, 1), (1, 1, 1)),
        ((0, 1, 0), (0, 1, 0), (0, 1, 0), (0, 1, 0), (1, 0, 0), (0, 1, 0), (0, 3, 0), (0, 3, 0), (0, 1, 0), (0, 1, 0), (0, 1, 0), (0, 1, 0), (0, 1, 0), (0, 1, 0), (0, 1, 0), (0, 1, 0)),
        ((1, 1, 0), (1, 1, 0), (0, 3, 0), (0, 3, 0), (1, 1, 0), (1, 1, 0), (0, 1, 0), (0, 1, 0), (1, 1, 0), (1, 1, 0), (1, 1, 0), (1, 1, 0), (1, 1, 0), (1, 1, 0), (1, 1, 0), (1, 1, 0)),
        ((0, 3, 0), (0, 3, 0), (0, 2, 0), (0, 2, 0), (0, 3, 0), (0, 3, 0), (1, 1, 0), (1, 1, 0), (0, 3, 0), (0, 3, 0), (0, 3, 0), (0, 3, 0), (0, 3, 0), (0, 3, 0), (0, 3, 0), (0, 3, 0)),
        ((1, 3, 0), (1, 3, 0), (1, 1, 0), (1, 1, 0), (1, 3, 0), (1, 3, 0), (1, 3, 0), (1, 3, 0), (1, 3, 0), (1, 3, 0), (1, 3, 0), (1, 3, 0), (1, 3, 0), (1, 3, 0), (1, 3, 0), (1, 3, 0)),
        ((0, 2, 0), (0, 2, 0), (1, 3, 0), (1, 3, 0), (0, 2, 0), (0, 2, 0), (0, 2, 0), (0, 2, 0), (0, 2, 0), (0, 2, 0), (0, 2, 0), (0, 2, 0), (0, 2, 0), (0, 2, 0), (0, 2, 0), (0, 2, 0)),
    ),
    (
        ((0, 0, 1), (0, 0, 1), (0, 0, 1), (0, 0, 1), (0, 0, 1), (0, 0, 1), (0, 0, 1), (0, 0, 1), (0, 0, 1), (0, 0, 1), (0, 0, 1), (0, 0, 1), (0, 0, 1), (0, 0, 1), (0, 0, 1), (0, 0, 1)),
        ((0, 3, 0), (0, 3, 0), (0, 3, 0), (0, 3, 0), (0, 3, 0), (0, 3, 0), (0, 3, 0), (0, 3, 0), (0, 3, 0), (0, 3, 0), (0, 3, 0), (0, 3, 0), (0, 3, 0), (0, 3, 0), (0, 3, 0), (0, 3, 0)),
        ((0, 3, 1), (0, 3, 1), (0, 3, 1), (0, 3, 1), (0, 3, 1), (0, 3, 1), (0, 3, 1), (0, 3, 1), (0, 3, 1), (0, 3, 1), (0, 3, 1), (0, 3, 1), (0, 3, 1), (0, 3, 1), (0, 3, 1), (0, 3, 1)),
        ((1, 0, 1), (1, 0, 1), (1, 0, 1), (1, 0, 1), (0, 2, 1), (0, 2, 1), (1, 0, 1), (0, 2, 0), (1, 0, 1), (1, 0, 1), (1, 0, 1), (1, 0, 1), (1, 0, 1), (1, 0, 1), (1, 0, 1), (1, 0, 1)),
        ((0, 2, 1), (0, 2, 1), (0, 2, 1), (0, 2, 1), (1, 1, 0), (1, 0, 1), (0, 2, 1), (0, 2, 1), (0, 2, 1), (0, 2, 1), (0, 2, 1), (0, 2, 1), (0, 2, 1), (0, 2, 1), (0, 2, 1), (0, 2, 1)),
        ((1, 1, 1), (1, 1, 1), (1, 3, 0), (1, 3, 0), (1, 1, 1), (1, 3, 0), (1, 3, 0), (1, 3, 0), (1, 3, 1), (1, 3, 1), (1, 3, 0), (1, 3, 0), (1, 3, 0), (1, 3, 0), (1, 3, 0), (1, 3, 0)),
        ((0, 0, 0), (0, 0, 0), (0, 0, 0), (0, 0, 0), (0, 0, 0), (0, 0, 0), (0, 0, 0), (0, 0, 0), (0, 0, 0), (0, 0, 0), (0, 0, 0), (0, 0, 0), (0, 0, 0), (0, 0, 0), (0, 0, 0), (0, 0, 0)),
        ((1, 0, 0), (1, 0, 0), (1, 0, 0), (1, 0, 0), (0, 1, 0), (1, 0, 0), (1, 0, 0), (1, 0, 0), (1, 0, 0), (1, 0, 0), (1, 0, 0), (1, 0, 0), (1, 0, 0), (1, 0, 0), (1, 0, 0), (1, 0, 0)),
        ((1, 3, 1), (1, 3, 1), (1, 3, 1), (1, 3, 1), (1, 3, 1), (1, 3, 1), (1, 3, 1), (1, 3, 1), (1, 1, 1), (1, 1, 1), (1, 3, 1), (1, 3, 1), (1, 3, 1), (1, 3, 1), (1, 3, 1), (1, 3, 1)),
        ((0, 1, 0), (0, 1, 0), (0, 1, 0), (0, 1, 0), (1, 0, 0), (0, 1, 0), (0, 3, 0), (0, 3, 0), (0, 1, 0), (0, 1, 0), (0, 1, 0), (0, 1, 0), (0, 1, 0), (0, 1, 0), (0, 1, 0), (0, 1, 0)),
        ((1, 1, 0), (1, 1, 0), (0, 3, 0), (0, 3, 0), (1, 1, 0), (1, 1, 0), (0, 1, 0), (0, 1, 0), (1, 1, 0), (1, 1, 0), (1, 1, 0), (1, 1, 0), (1, 1, 0), (1, 1, 0), (1, 1, 0), (1, 1, 0)),
        ((0, 3, 0), (0, 3, 0), (0, 2, 0), (0, 2, 0), (0, 3, 0), (0, 3, 0), (1, 1, 0), (1, 1, 0), (0, 3, 0), (0, 3, 0), (0, 3, 0), (0, 3, 0), (0, 3, 0), (0, 3, 0), (0, 3, 0), (0, 3, 0)),
        ((1, 3, 0), (1, 3, 0), (1, 1, 0), (1, 1, 0), (1, 3, 0), (1, 3, 0), (1, 3, 0), (1, 3, 0), (1, 3, 0), (1, 3, 0), (1, 3, 0), (1, 3, 0), (1, 3, 0), (1, 3, 0), (1, 3, 0), (1, 3, 0)),
        ((0, 2, 0), (0, 2, 0), (1, 3, 0), (1, 3, 0), (0, 2, 0), (0, 2, 0), (0, 2, 0), (0, 2, 0), (0, 2, 0), (0, 2, 0), (0, 2, 0), (0, 2, 0), (0, 2, 0), (0, 2, 0), (0, 2, 0), (0, 2, 0)),
    ),
)
EVENTS = (
    (
        (2, ((CROSSF, 0), (CROSSF, 1), (OWN, 0, 1, 0), (OWN, 0, 3, 0), (PASS_Z, 0, 0), (PASS_Z, 0, 1),)),
        (3, ((OWN, 0, 1, 1), (OWN, 0, 3, 1),)),
        (4, ((OWN, 1, 0, 0), (OWN, 1, 0, 1), (PASS_Z, 1, 0), (PASS_Z, 3, 0),)),
        (5, ((OWN, 0, 2, 0),)),
        (6, ((OWN, 0, 2, 1), (FWD_Y, 0, 0), (FWD_Y, 0, 1),)),
        (8, ((OWN, 1, 1, 0), (PASS_Z, 1, 1), (PASS_Z, 3, 1),)),
        (9, ((PASS_Y, 0, 1),)),
        (10, ((OWN, 1, 1, 1), (FWD_Y, 1, 0), (FWD_Y, 3, 0), (OWN, 1, 3, 0),)),
        (12, ((OWN, 1, 2, 1), (PASS_Z, 2, 0), (PASS_Z, 2, 1),)),
        (13, ((OWN, 1, 2, 0), (PASS_Y, 1, 0),)),
        (14, ((FWD_Y, 1, 1), (FWD_Y, 3, 1),)),
        (15, ((OWN, 1, 3, 1),)),
        (16, ((FWD_Y, 2, 0), (FWD_Y, 2, 1),)),
        (17, ((PASS_Y, 3, 1),)),
        (19, ((PASS_Y, 2, 0),)),
    ),
    (
        (2, ((CROSSF, 0), (CROSSF, 1), (OWN, 0, 1, 0), (OWN, 0, 3, 0), (PASS_Z, 0, 0), (PASS_Z, 0, 1),)),
        (3, ((OWN, 0, 1, 1), (OWN, 0, 3, 1),)),
        (4, ((OWN, 1, 0, 0), (OWN, 1, 0, 1), (PASS_Z, 1, 0), (PASS_Z, 3, 0),)),
        (5, ((OWN, 0, 2, 0),)),
        (6, ((OWN, 0, 2, 1), (FWD_Y, 0, 0), (FWD_Y, 0, 1),)),
        (8, ((OWN, 1, 1, 0), (PASS_Z, 1, 1), (PASS_Z, 3, 1),)),
        (9, ((PASS_Y, 0, 0),)),
        (10, ((OWN, 1, 1, 1), (FWD_Y, 1, 0), (FWD_Y, 3, 0), (OWN, 1, 3, 0),)),
        (12, ((OWN, 1, 2, 1), (PASS_Z, 2, 0), (PASS_Z, 2, 1),)),
        (13, ((OWN, 1, 3, 1), (PASS_Y, 3, 0),)),
        (14, ((FWD_Y, 1, 1), (FWD_Y, 3, 1),)),
        (15, ((OWN, 1, 2, 0),)),
        (16, ((FWD_Y, 2, 0), (FWD_Y, 2, 1),)),
        (17, ((PASS_Y, 1, 1),)),
        (19, ((PASS_Y, 2, 1),)),
    ),
    (
        (2, ((CROSSF, 0), (CROSSF, 1), (OWN, 0, 1, 0), (OWN, 0, 3, 0), (PASS_Z, 0, 0), (PASS_Z, 0, 1),)),
        (3, ((OWN, 0, 1, 1), (OWN, 0, 3, 1),)),
        (4, ((OWN, 1, 0, 0), (OWN, 1, 0, 1), (PASS_Z, 1, 0), (PASS_Z, 3, 0),)),
        (5, ((OWN, 0, 2, 0),)),
        (6, ((OWN, 0, 2, 1), (PAR, 0, 0, 0), (PAR, 0, 0, 1),)),
        (8, ((OWN, 1, 1, 0), (OWN, 1, 3, 0), (PASS_Z, 1, 1), (PASS_Z, 3, 1),)),
        (9, ((PASS_Y, 0, 0),)),
        (10, ((OWN, 1, 1, 1),)),
        (11, ((OWN, 1, 3, 1), (PAR, 0, 1, 0), (PAR, 0, 3, 0),)),
        (12, ((PAR, 1, 0, 0), (PAR, 1, 0, 1),)),
        (13, ((OWN, 1, 2, 0), (OWN, 1, 2, 1), (PASS_Z, 2, 0), (PASS_Z, 2, 1),)),
        (14, ((PASS_Y, 3, 0),)),
        (15, ((PAR, 0, 1, 1), (PAR, 0, 3, 1),)),
        (17, ((PAR, 0, 2, 0), (PAR, 0, 2, 1), (PAR, 1, 1, 0), (PAR, 1, 3, 0),)),
        (19, ((PASS_Y, 1, 1),)),
        (21, ((PASS_Y, 2, 1),)),
        (22, ((PAR, 1, 3, 1),)),
        (23, ((PAR, 1, 1, 1),)),
        (24, ((PAR, 1, 2, 0),)),
        (26, ((PAR, 1, 2, 1),)),
    ),
    (
        (2, ((CROSSF, 0), (CROSSF, 1), (OWN, 0, 1, 0), (OWN, 0, 3, 0), (PASS_Z, 0, 0), (PASS_Z, 0, 1),)),
        (3, ((OWN, 0, 1, 1), (OWN, 0, 3, 1),)),
        (4, ((OWN, 1, 0, 0), (OWN, 1, 0, 1), (PASS_Z, 1, 0), (PASS_Z, 3, 0),)),
        (5, ((OWN, 0, 2, 0),)),
        (6, ((OWN, 0, 2, 1), (PAR, 0, 0, 0), (PAR, 0, 0, 1),)),
        (8, ((OWN, 1, 1, 0), (OWN, 1, 3, 0), (PASS_Z, 1, 1), (PASS_Z, 3, 1),)),
        (9, ((PASS_Y, 0, 1),)),
        (10, ((OWN, 1, 1, 1),)),
        (11, ((OWN, 1, 3, 1), (PAR, 0, 1, 0), (PAR, 0, 3, 0),)),
        (12, ((PAR, 1, 0, 0), (PAR, 1, 0, 1),)),
        (13, ((OWN, 1, 2, 0), (OWN, 1, 2, 1), (PASS_Z, 2, 0), (PASS_Z, 2, 1),)),
        (14, ((PASS_Y, 1, 0),)),
        (15, ((PAR, 0, 1, 1), (PAR, 0, 3, 1),)),
        (17, ((PAR, 0, 2, 0), (PAR, 0, 2, 1), (PAR, 1, 1, 0), (PAR, 1, 3, 0),)),
        (19, ((PASS_Y, 3, 1),)),
        (21, ((PASS_Y, 2, 0),)),
        (22, ((PAR, 1, 1, 1),)),
        (23, ((PAR, 1, 3, 1),)),
        (24, ((PAR, 1, 2, 1),)),
        (26, ((PAR, 1, 2, 0),)),
    ),
    (
        (2, ((CROSSF, 0), (OWN, 0, 1, 0), (OWN, 0, 3, 0), (PASS_Z, 0, 0), (PASS_Z, 0, 1), (PAR, 0, 0, 0),)),
        (3, ((CROSSF, 1), (OWN, 0, 1, 1), (OWN, 0, 3, 1), (PAR, 1, 0, 0),)),
        (4, ((PASS_Z, 1, 0), (PASS_Z, 3, 0),)),
        (5, ((OWN, 0, 2, 0), (PAR, 0, 0, 1), (PAR, 1, 0, 1),)),
        (6, ((OWN, 0, 2, 1), (FWD_Y, 0, 0), (FWD_Y, 0, 1),)),
        (7, ((OWN, 1, 0, 0), (OWN, 1, 1, 0), (PAR, 0, 1, 0),)),
        (8, ((OWN, 1, 3, 0), (PASS_Z, 1, 1), (PASS_Z, 3, 1),)),
        (9, ((OWN, 1, 1, 1), (PAR, 0, 3, 0), (PAR, 1, 1, 0),)),
        (10, ((OWN, 1, 3, 1), (FWD_Y, 1, 0), (FWD_Y, 3, 0),)),
        (11, ((OWN, 1, 0, 1), (PAR, 1, 3, 0),)),
        (12, ((OWN, 1, 2, 0), (OWN, 1, 2, 1), (PASS_Z, 2, 0), (PASS_Z, 2, 1),)),
        (13, ((PAR, 0, 1, 1), (PAR, 1, 1, 1),)),
        (14, ((FWD_Y, 1, 1), (FWD_Y, 3, 1),)),
        (15, ((PAR, 0, 3, 1), (PAR, 1, 3, 1),)),
        (16, ((FWD_Y, 2, 0), (FWD_Y, 2, 1),)),
        (17, ((PAR, 0, 2, 0), (PAR, 1, 2, 0),)),
        (19, ((PAR, 0, 2, 1), (PAR, 1, 2, 1),)),
    ),
    (
        (2, ((CROSSF, 0), (OWN, 0, 1, 0), (OWN, 0, 3, 0), (PASS_Z, 0, 0), (PASS_Z, 0, 1), (PAR, 1, 0, 0),)),
        (3, ((CROSSF, 1), (OWN, 0, 1, 1), (OWN, 0, 3, 1), (PAR, 0, 0, 0),)),
        (4, ((PASS_Z, 1, 0), (PASS_Z, 3, 0),)),
        (5, ((OWN, 0, 2, 0), (PAR, 0, 0, 1), (PAR, 1, 0, 1),)),
        (6, ((OWN, 0, 2, 1), (FWD_Y, 0, 0), (FWD_Y, 0, 1),)),
        (7, ((OWN, 1, 0, 0), (OWN, 1, 0, 1), (OWN, 1, 1, 0),)),
        (8, ((OWN, 1, 3, 0), (PASS_Z, 1, 1), (PASS_Z, 3, 1),)),
        (9, ((OWN, 1, 1, 1), (PAR, 0, 1, 0), (PAR, 1, 1, 0),)),
        (10, ((OWN, 1, 3, 1), (FWD_Y, 1, 0), (FWD_Y, 3, 0),)),
        (11, ((PAR, 0, 3, 0), (PAR, 1, 3, 0),)),
        (12, ((OWN, 1, 2, 0), (OWN, 1, 2, 1), (PASS_Z, 2, 0), (PASS_Z, 2, 1),)),
        (13, ((PAR, 0, 1, 1), (PAR, 1, 1, 1),)),
        (14, ((FWD_Y, 1, 1), (FWD_Y, 3, 1),)),
        (15, ((PAR, 0, 3, 1), (PAR, 1, 3, 1),)),
        (16, ((FWD_Y, 2, 0), (FWD_Y, 2, 1),)),
        (17, ((PAR, 0, 2, 0), (PAR, 1, 2, 0),)),
        (19, ((PAR, 0, 2, 1), (PAR, 1, 2, 1),)),
    ),
    (
        (2, ((CROSSF, 0), (CROSSF, 1), (OWN, 0, 1, 0), (OWN, 0, 3, 0), (PASS_Z, 0, 0), (PASS_Z, 0, 1),)),
        (3, ((OWN, 0, 1, 1), (OWN, 0, 3, 1),)),
        (4, ((OWN, 1, 0, 0), (OWN, 1, 0, 1), (PASS_Z, 1, 0), (PASS_Z, 3, 0),)),
        (5, ((OWN, 0, 2, 0),)),
        (6, ((OWN, 0, 2, 1), (FWD_Y, 0, 0), (FWD_Y, 0, 1),)),
        (7, ((OWN, 1, 1, 0),)),
        (8, ((OWN, 1, 3, 0), (PASS_Z, 1, 1), (PASS_Z, 3, 1),)),
        (9, ((OWN, 1, 1, 1), (PAR, 0, 0, 0), (PAR, 1, 0, 0),)),
        (10, ((OWN, 1, 3, 1), (FWD_Y, 1, 0), (FWD_Y, 3, 0),)),
        (11, ((PAR, 0, 0, 1), (PAR, 1, 0, 1),)),
        (12, ((OWN, 1, 2, 0), (PASS_Z, 2, 0), (PASS_Z, 2, 1),)),
        (13, ((OWN, 1, 2, 1), (PAR, 0, 1, 0),)),
        (14, ((FWD_Y, 3, 1), (PAR, 1, 1, 0),)),
        (15, ((FWD_Y, 1, 1),)),
        (16, ((PAR, 0, 3, 0), (PAR, 1, 3, 0),)),
        (17, ((FWD_Y, 2, 0), (FWD_Y, 2, 1),)),
        (18, ((PAR, 0, 3, 1), (PAR, 1, 1, 1),)),
        (19, ((PAR, 0, 1, 1),)),
        (20, ((PAR, 1, 3, 1),)),
        (21, ((PAR, 0, 2, 0),)),
        (22, ((PAR, 1, 2, 0),)),
        (23, ((PAR, 0, 2, 1),)),
        (24, ((PAR, 1, 2, 1),)),
    ),
    (
        (2, ((CROSSF, 0), (CROSSF, 1), (OWN, 0, 1, 0), (OWN, 0, 3, 0), (PASS_Z, 0, 0), (PASS_Z, 0, 1),)),
        (3, ((OWN, 0, 1, 1), (OWN, 0, 3, 1),)),
        (4, ((OWN, 1, 0, 0), (PASS_Z, 1, 0), (PASS_Z, 3, 0),)),
        (5, ((OWN, 0, 2, 0),)),
        (6, ((OWN, 0, 2, 1), (OWN, 1, 0, 1), (FWD_Y, 0, 0), (FWD_Y, 0, 1),)),
        (7, ((OWN, 1, 1, 0),)),
        (8, ((OWN, 1, 3, 0), (PASS_Z, 1, 1), (PASS_Z, 3, 1),)),
        (9, ((OWN, 1, 1, 1), (PAR, 0, 0, 0), (PAR, 1, 0, 0),)),
        (10, ((OWN, 1, 3, 1), (FWD_Y, 1, 0), (FWD_Y, 3, 0),)),
        (11, ((PAR, 0, 0, 1), (PAR, 1, 0, 1),)),
        (12, ((OWN, 1, 2, 0), (PASS_Z, 2, 0), (PASS_Z, 2, 1),)),
        (13, ((OWN, 1, 2, 1), (PAR, 0, 1, 0),)),
        (14, ((FWD_Y, 3, 1), (PAR, 1, 1, 0),)),
        (15, ((FWD_Y, 1, 1),)),
        (16, ((PAR, 0, 3, 0), (PAR, 1, 3, 0),)),
        (17, ((FWD_Y, 2, 0), (FWD_Y, 2, 1),)),
        (18, ((PAR, 0, 3, 1), (PAR, 1, 1, 1),)),
        (19, ((PAR, 0, 1, 1),)),
        (20, ((PAR, 1, 3, 1),)),
        (21, ((PAR, 0, 2, 0),)),
        (22, ((PAR, 1, 2, 0),)),
        (23, ((PAR, 0, 2, 1),)),
        (24, ((PAR, 1, 2, 1),)),
    ),
    (
        (2, ((CROSSF, 0), (CROSSF, 1), (OWN, 0, 1, 0), (OWN, 0, 3, 0), (FWD_Y, 0, 0), (PAR, 0, 0, 0),)),
        (3, ((OWN, 0, 1, 1), (OWN, 0, 3, 1), (FWD_Y, 0, 1), (PAR, 0, 0, 1),)),
        (4, ((OWN, 1, 0, 0), (OWN, 1, 0, 1),)),
        (5, ((OWN, 0, 2, 0), (FWD_Y, 1, 0), (PAR, 0, 1, 0),)),
        (6, ((OWN, 0, 2, 1), (PASS_Y, 0, 0), (PASS_Y, 0, 1),)),
        (7, ((FWD_Y, 3, 0), (PAR, 0, 3, 0),)),
        (8, ((OWN, 1, 3, 0), (PASS_Y, 1, 0),)),
        (9, ((FWD_Y, 1, 1), (PAR, 0, 1, 1), (PAR, 1, 0, 0),)),
        (10, ((OWN, 1, 3, 1), (PAR, 1, 0, 1), (OWN, 1, 1, 0),)),
        (11, ((FWD_Y, 3, 1), (PASS_Y, 3, 0), (PAR, 0, 3, 1),)),
        (12, ((OWN, 1, 2, 0), (OWN, 1, 2, 1), (PAR, 1, 1, 0),)),
        (13, ((FWD_Y, 2, 0), (PASS_Y, 1, 1), (PAR, 0, 2, 0),)),
        (14, ((OWN, 1, 1, 1), (PASS_Y, 3, 1),)),
        (15, ((FWD_Y, 2, 1), (PAR, 0, 2, 1), (PAR, 1, 3, 0),)),
        (16, ((PASS_Y, 2, 0),)),
        (17, ((PAR, 1, 1, 1),)),
        (18, ((PAR, 1, 3, 1),)),
        (19, ((PASS_Y, 2, 1),)),
        (21, ((PAR, 1, 2, 0),)),
        (23, ((PAR, 1, 2, 1),)),
    ),
    (
        (2, ((CROSSF, 0), (CROSSF, 1), (OWN, 0, 1, 0), (OWN, 0, 3, 0), (FWD_Y, 0, 0), (PAR, 0, 0, 0),)),
        (3, ((OWN, 0, 1, 1), (OWN, 0, 3, 1), (FWD_Y, 0, 1), (PAR, 0, 0, 1),)),
        (4, ((OWN, 1, 0, 0), (OWN, 1, 0, 1),)),
        (5, ((OWN, 0, 2, 0), (FWD_Y, 1, 0), (PAR, 0, 1, 0),)),
        (6, ((OWN, 0, 2, 1), (PASS_Y, 0, 0), (PASS_Y, 0, 1),)),
        (7, ((FWD_Y, 3, 0), (PAR, 0, 3, 0),)),
        (8, ((OWN, 1, 3, 0), (PASS_Y, 1, 0),)),
        (9, ((FWD_Y, 1, 1), (PAR, 0, 1, 1), (PAR, 1, 0, 0),)),
        (10, ((OWN, 1, 3, 1), (PAR, 1, 0, 1), (OWN, 1, 1, 0),)),
        (11, ((FWD_Y, 3, 1), (PASS_Y, 3, 0), (PAR, 0, 3, 1),)),
        (12, ((OWN, 1, 1, 1), (OWN, 1, 2, 0), (PAR, 1, 1, 0),)),
        (13, ((FWD_Y, 2, 0), (PASS_Y, 1, 1), (PAR, 0, 2, 0),)),
        (14, ((OWN, 1, 2, 1), (PASS_Y, 3, 1),)),
        (15, ((FWD_Y, 2, 1), (PAR, 0, 2, 1), (PAR, 1, 3, 0),)),
        (17, ((PASS_Y, 2, 0), (PAR, 1, 1, 1),)),
        (19, ((PASS_Y, 2, 1), (PAR, 1, 3, 1),)),
        (21, ((PAR, 1, 2, 0),)),
        (22, ((PAR, 1, 2, 1),)),
    ),
    (
        (2, ((CROSSF, 0), (CROSSF, 1), (OWN, 0, 1, 0), (OWN, 0, 3, 0), (FWD_Y, 0, 0), (PAR, 0, 0, 0),)),
        (3, ((OWN, 0, 1, 1), (OWN, 0, 3, 1), (FWD_Y, 0, 1), (PAR, 0, 0, 1),)),
        (4, ((OWN, 1, 0, 0), (OWN, 1, 0, 1),)),
        (5, ((OWN, 0, 2, 0), (FWD_Y, 1, 0), (PAR, 0, 1, 0),)),
        (6, ((OWN, 0, 2, 1), (PASS_Y, 0, 0), (PASS_Y, 0, 1),)),
        (7, ((OWN, 1, 1, 0), (FWD_Y, 3, 0), (PAR, 0, 3, 0),)),
        (8, ((OWN, 1, 3, 0), (PASS_Y, 1, 0),)),
        (9, ((OWN, 1, 1, 1), (FWD_Y, 1, 1), (PAR, 0, 1, 1), (PAR, 1, 0, 0),)),
        (10, ((OWN, 1, 3, 1), (PAR, 1, 0, 1),)),
        (11, ((FWD_Y, 3, 1), (PASS_Y, 3, 0),)),
        (12, ((OWN, 1, 2, 0), (OWN, 1, 2, 1), (PAR, 0, 3, 1), (PAR, 1, 1, 0),)),
        (13, ((PASS_Y, 1, 1),)),
        (14, ((FWD_Y, 2, 0), (PASS_Y, 3, 1), (PAR, 0, 2, 0),)),
        (16, ((FWD_Y, 2, 1), (PAR, 0, 2, 1), (PAR, 1, 3, 0),)),
        (17, ((PASS_Y, 2, 0),)),
        (18, ((PAR, 1, 1, 1),)),
        (19, ((PAR, 1, 3, 1),)),
        (20, ((PASS_Y, 2, 1),)),
        (22, ((PAR, 1, 2, 0),)),
        (23, ((PAR, 1, 2, 1),)),
    ),
    (
        (2, ((CROSSF, 0), (CROSSF, 1), (OWN, 0, 1, 0), (OWN, 0, 3, 0), (FWD_Y, 0, 0), (PAR, 0, 0, 0),)),
        (3, ((OWN, 0, 1, 1), (OWN, 0, 3, 1), (FWD_Y, 0, 1), (PAR, 0, 0, 1),)),
        (4, ((OWN, 1, 0, 0), (OWN, 1, 0, 1),)),
        (5, ((OWN, 0, 2, 0), (FWD_Y, 1, 0), (PAR, 0, 1, 0),)),
        (6, ((OWN, 0, 2, 1), (PASS_Y, 0, 0), (PASS_Y, 0, 1),)),
        (7, ((OWN, 1, 1, 0), (FWD_Y, 3, 0), (PAR, 0, 3, 0),)),
        (8, ((OWN, 1, 3, 0), (PASS_Y, 1, 0),)),
        (9, ((OWN, 1, 1, 1), (FWD_Y, 1, 1), (PAR, 0, 1, 1), (PAR, 1, 0, 0),)),
        (10, ((OWN, 1, 3, 1), (PAR, 1, 0, 1),)),
        (11, ((FWD_Y, 3, 1), (PASS_Y, 3, 0),)),
        (12, ((OWN, 1, 2, 0), (OWN, 1, 2, 1), (PAR, 0, 3, 1), (PAR, 1, 1, 0),)),
        (13, ((PASS_Y, 1, 1),)),
        (14, ((FWD_Y, 2, 0), (PAR, 0, 2, 0),)),
        (15, ((PASS_Y, 3, 1),)),
        (16, ((FWD_Y, 2, 1), (PAR, 0, 2, 1), (PAR, 1, 3, 0),)),
        (17, ((PASS_Y, 2, 0),)),
        (18, ((PAR, 1, 1, 1),)),
        (19, ((PAR, 1, 3, 1),)),
        (20, ((PASS_Y, 2, 1),)),
        (21, ((PAR, 1, 2, 0),)),
        (23, ((PAR, 1, 2, 1),)),
    ),
    (
        (2, ((CROSSF, 0), (CROSSF, 1), (OWN, 0, 1, 0), (OWN, 0, 3, 0), (FWD_Y, 0, 0),)),
        (3, ((OWN, 0, 1, 1), (OWN, 0, 3, 1), (FWD_Y, 0, 1),)),
        (4, ((OWN, 1, 0, 0), (OWN, 1, 0, 1),)),
        (5, ((OWN, 0, 2, 0), (FWD_Y, 1, 0),)),
        (6, ((OWN, 0, 2, 1), (PAR, 0, 0, 0), (PAR, 1, 0, 0),)),
        (7, ((OWN, 1, 1, 0), (FWD_Y, 3, 0),)),
        (8, ((OWN, 1, 3, 0), (PAR, 0, 0, 1), (PAR, 1, 0, 1),)),
        (9, ((OWN, 1, 1, 1), (FWD_Y, 1, 1),)),
        (10, ((OWN, 1, 3, 1), (PAR, 0, 1, 0), (PAR, 1, 1, 0),)),
        (11, ((FWD_Y, 3, 1),)),
        (12, ((PAR, 0, 3, 0), (PAR, 1, 3, 0),)),
        (14, ((OWN, 1, 2, 0), (FWD_Y, 2, 0), (PAR, 0, 1, 1), (PAR, 1, 1, 1),)),
        (16, ((FWD_Y, 2, 1),)),
        (17, ((PAR, 0, 3, 1), (PAR, 1, 3, 1),)),
        (18, ((OWN, 1, 2, 1),)),
        (19, ((PAR, 0, 2, 0), (PAR, 1, 2, 0),)),
        (21, ((PAR, 0, 2, 1), (PAR, 1, 2, 1),)),
    ),
    (
        (2, ((CROSSF, 0), (CROSSF, 1), (OWN, 0, 1, 0), (OWN, 0, 3, 0), (FWD_Y, 0, 0),)),
        (3, ((OWN, 0, 1, 1), (OWN, 0, 3, 1), (FWD_Y, 0, 1),)),
        (4, ((OWN, 1, 0, 0), (OWN, 1, 0, 1),)),
        (5, ((OWN, 0, 2, 0), (FWD_Y, 1, 0),)),
        (6, ((OWN, 0, 2, 1), (PAR, 0, 0, 0), (PAR, 1, 0, 0),)),
        (7, ((OWN, 1, 1, 0), (FWD_Y, 3, 0),)),
        (8, ((OWN, 1, 3, 0), (PAR, 0, 0, 1), (PAR, 1, 0, 1),)),
        (9, ((OWN, 1, 1, 1), (FWD_Y, 1, 1),)),
        (10, ((OWN, 1, 3, 1), (PAR, 0, 1, 0), (PAR, 1, 1, 0),)),
        (11, ((FWD_Y, 3, 1),)),
        (12, ((PAR, 0, 3, 0), (PAR, 1, 3, 0),)),
        (14, ((OWN, 1, 2, 0), (FWD_Y, 2, 0), (PAR, 0, 1, 1), (PAR, 1, 1, 1),)),
        (16, ((OWN, 1, 2, 1), (FWD_Y, 2, 1),)),
        (17, ((PAR, 0, 3, 1), (PAR, 1, 3, 1),)),
        (19, ((PAR, 0, 2, 0), (PAR, 1, 2, 0),)),
        (21, ((PAR, 0, 2, 1), (PAR, 1, 2, 1),)),
    ),
    (
        (2, ((CROSSF, 0), (CROSSF, 1), (OWN, 0, 1, 0), (OWN, 0, 3, 0), (FWD_Y, 0, 0),)),
        (3, ((OWN, 0, 1, 1), (OWN, 0, 3, 1), (FWD_Y, 0, 1),)),
        (4, ((OWN, 1, 0, 0), (OWN, 1, 0, 1),)),
        (5, ((OWN, 0, 2, 0), (FWD_Y, 1, 0),)),
        (6, ((OWN, 0, 2, 1), (PAR, 0, 0, 0), (PAR, 1, 0, 0),)),
        (7, ((OWN, 1, 1, 0), (FWD_Y, 3, 0),)),
        (8, ((OWN, 1, 3, 0), (PAR, 0, 0, 1), (PAR, 1, 0, 1),)),
        (9, ((OWN, 1, 1, 1), (FWD_Y, 1, 1),)),
        (10, ((OWN, 1, 3, 1), (PAR, 0, 1, 0), (PAR, 1, 1, 0),)),
        (11, ((FWD_Y, 3, 1),)),
        (12, ((OWN, 1, 2, 0), (OWN, 1, 2, 1), (PAR, 0, 3, 0), (PAR, 1, 3, 0),)),
        (14, ((FWD_Y, 2, 0), (PAR, 0, 1, 1), (PAR, 1, 1, 1),)),
        (16, ((FWD_Y, 2, 1),)),
        (17, ((PAR, 0, 3, 1), (PAR, 1, 3, 1),)),
        (19, ((PAR, 0, 2, 0), (PAR, 1, 2, 0),)),
        (21, ((PAR, 0, 2, 1), (PAR, 1, 2, 1),)),
    ),
    (
        (2, ((CROSSF, 0), (CROSSF, 1), (OWN, 0, 1, 0), (OWN, 0, 3, 0), (FWD_Y, 0, 0),)),
        (3, ((OWN, 0, 1, 1), (OWN, 0, 3, 1), (FWD_Y, 0, 1),)),
        (4, ((OWN, 1, 0, 0), (OWN, 1, 0, 1),)),
        (5, ((OWN, 0, 2, 0), (FWD_Y, 1, 0),)),
        (6, ((OWN, 0, 2, 1), (PAR, 0, 0, 0), (PAR, 1, 0, 0),)),
        (7, ((OWN, 1, 1, 0), (FWD_Y, 3, 0),)),
        (8, ((OWN, 1, 3, 0), (PAR, 0, 0, 1), (PAR, 1, 0, 1),)),
        (9, ((OWN, 1, 1, 1), (FWD_Y, 1, 1),)),
        (10, ((OWN, 1, 3, 1), (PAR, 0, 1, 0), (PAR, 1, 1, 0),)),
        (11, ((FWD_Y, 3, 1),)),
        (12, ((OWN, 1, 2, 0), (OWN, 1, 2, 1), (PAR, 0, 3, 0), (PAR, 1, 3, 0),)),
        (14, ((FWD_Y, 2, 0), (PAR, 0, 1, 1), (PAR, 1, 1, 1),)),
        (16, ((FWD_Y, 2, 1),)),
        (17, ((PAR, 0, 3, 1), (PAR, 1, 3, 1),)),
        (19, ((PAR, 0, 2, 0), (PAR, 1, 2, 0),)),
        (21, ((PAR, 0, 2, 1), (PAR, 1, 2, 1),)),
    ),
)

STAGES = len(SEQUENCE)
BASES = [sum(PARTS[stage] for stage in SEQUENCE[:n]) for n in range(STAGES + 1)]
POINTS = BASES[-1] + 1
PAR_AT, T1_AT, T2_AT, T3_AT, TC_AT, SLOTS = 32, 64, 72, 80, 88, 90
WAYS = ("x+", "x-", "y+", "y-", "z+", "z-", "core", "ya", "yb", "za", "zb")
WAIT = 15
CLASSES = [(x, y) for x in range(4) for y in range(4)]


def sign_of(j, k):
    return "+" if (k + (0, 1, 1, 0)[j]) % 2 == 0 else "-"


def name_of(x, y, row, j):
    return (y // 2 + row) % 2 * 4 + (x + 4 - j) % 4


def row_behind(y, sign):
    return (y + 3) % 4 // 2 if sign == "+" else (y + 1) % 4 // 2


def feed(x, y, j, k, src):
    up = y // 2 == 1
    final, via1, via2 = ("par", name_of(x, y, 0, j), k), ("t1", j, k), ("t2", j, k)
    sends = []
    if x in (0, 1):
        sends.append((src, via1, "z" + sign_of(j, k)))
    if x == 1:
        sends.append((src, final, "ya"))
    if x in (2, 3):
        sends.append((src, final if x == 2 and not up else via1, "za"))
        sends.append((src, final if x == 2 and up else via2, "zb"))
    return sends


def expand(x, y, event):
    kind, args = event[0], event[1:]
    up = y // 2 == 1
    ops = []
    if kind == CROSSF:
        (k,) = args
        sign = "+-"[k]
        ops = [("tc", k), (("tc", k), ("own", row_behind(y, sign) * 4 + x, k), "y" + sign)]
    if kind == OWN:
        row, j, k = args
        here = ("own", name_of(x, y, row, j), k)
        ops = [here]
        if (row, j) == (1, 0) or (j == 1 and (k + row) % 2 == 0):
            ops.append((here, here, "x+"))
        if (row, j) == (1, 0) or (j == 3 and (k + row) % 2 == 1):
            ops.append((here, here, "x-"))
        if row == 0:
            ops += feed(x, y, j, k, here)
        ops.append((here, here, "core"))
    if kind == PASS_Z:
        j, k = args
        here = ("t1", j, k)
        there = ("par", name_of(x, y, 0, j), k) if x == 0 and up else ("t2", j, k)
        ops = [here, (here, there, "z" + sign_of(j, k))]
    if kind == FWD_Y:
        j, k = args
        final, there, way = ("par", name_of(x, y, 0, j), k), ("t3", j, k), "y" + sign_of(j, k)
        if x == 3 or (x == 2 and up):
            ops += [("t1", j, k), (("t1", j, k), final, "ya") if x == 3 else (("t1", j, k), there, way)]
        if x in (1, 3) or not up:
            ops += [("t2", j, k), (("t2", j, k), final, "yb") if x in (1, 3) else (("t2", j, k), there, way)]
    if kind == PASS_Y:
        j, k = args
        sign = sign_of(j, k)
        row = row_behind(y, sign)
        if x == 2 or row == 0:
            ops = [("t3", j, k), (("t3", j, k), ("par", row * 4 + (x + 4 - j) % 4, k), "y" + sign)]
    if kind == PAR:
        row, j, k = args
        here = ("par", name_of(x, y, row, j), k)
        ops = [here, (here, here, "core")]
    return ops


def slot(place, c):
    kind, rest = place[0], place[1:]
    if kind in ("own", "par"):
        q, k = rest
        return (PAR_AT if kind == "par" else 0) + q * 4 + c * 2 + k
    if kind == "tc":
        return TC_AT + rest[0]
    return {"t1": T1_AT, "t2": T2_AT, "t3": T3_AT}[kind] + rest[0] * 2 + rest[1]


def tables(x, y):
    per_core = []
    for c in range(2):
        ops, begins, sends, at = [], [], 0, dict(EVENTS[CLASSES.index((x, y))])
        for point in range(POINTS):
            begins.append(len(ops))
            for event in at.get(point, ()):
                for op in expand(x, y, event):
                    if isinstance(op[0], str):
                        ops.append(slot(op, c) + 2097152 * WAIT)
                    else:
                        src, dst, way = op
                        ops.append(slot(src, c) + 128 * slot(dst, c) + 16384 * sends + 2097152 * WAYS.index(way))
                        sends += 1
        per_core.append((ops, begins + [len(ops), sends], sends))
    return per_core


TABLES = {cls: tables(*cls) for cls in CLASSES}
MOST_OPS = max(len(ops) for cores in TABLES.values() for ops, _, _ in cores)
MOST_SENDS = max(sends for cores in TABLES.values() for _, _, sends in cores)
FIRST_SENDS = 12


def columns(t):
    first, last = t * 256, (t + 1) * 256
    cuts = [first] + [cut for cut in range(0, NI * V, V) if first < cut < last] + [last]
    return [(u - first, w - first, u // V, u % V) for u, w in zip(cuts, cuts[1:])]


def kernel(dims, mine, amps, out, out_own, out_par, buf, rc, half, acc, ops, begins, devs,
           ssem, first_sem, rsem, local_sem):
    sym, tile, c = lax.axis_index("sym"), lax.axis_index("tile"), lax.axis_index("occ")
    x, yhi = sym % 4, sym // 4
    x0, x1 = x % 2, x // 2
    z, ylo = tile // 2, tile % 2
    z0, z1 = z % 2, z // 2
    y = 2 * yhi + ylo
    none = sym == 0

    def dev(dx=0, dy=0, dz=0, dc=0):
        xx, yy, zz = (x + 4 + dx) % 4, (y + 4 + dy) % 4, (z + 4 + dz) % 4
        return ((yy // 2) * 4 + xx) * 16 + (zz * 2 + yy % 2) * 2 + (c + dc) % 2

    step_a = 1 - 2 * (yhi + ylo - 2 * yhi * ylo)
    step_z = 1 - 2 * z0
    to = {
        "x+": dev(dx=1), "x-": dev(dx=-1), "y+": dev(dy=1), "y-": dev(dy=-1), "z+": dev(dz=1), "z-": dev(dz=-1),
        "core": dev(dc=1), "ya": dev(dy=step_a), "yb": dev(dy=-step_a), "za": dev(dz=step_z), "zb": dev(dz=-step_z),
    }
    barrier = pltpu.get_barrier_semaphore()
    for way in WAYS[:7]:
        pl.semaphore_signal(barrier, inc=1, device_id=to[way], device_id_type=pl.DeviceIdType.LOGICAL)

    def own_slot(q, core, k):
        return q * 4 + core * 2 + k

    keep = []
    for k in range(PIECES):
        keep.append(pltpu.make_async_copy(mine.at[pl.ds(k * PV, PV)], buf.at[own_slot(sym, c, k)], local_sem.at[8 + k]))
        keep[-1].start()
    loads = [pltpu.make_async_copy(amps.at[i], rc.at[:, pl.ds(i * V, V)], local_sem.at[i]) for i in range(NI)]
    for load in loads:
        load.start()

    pl.semaphore_wait(barrier, 7)

    def remote(src, dst_slot, sem, where):
        return pltpu.make_async_remote_copy(
            src, buf.at[dst_slot], sem, rsem.at[dst_slot], device_id=where, device_id_type=pl.DeviceIdType.LOGICAL
        )

    def arrived(at):
        remote(buf.at[at], at, first_sem.at[0], to["core"]).wait_recv()

    firsts = []

    def first(src, place, where, cond=None):
        index = len(firsts)
        if cond is None:
            remote(src, place, first_sem.at[index], where).start()
        else:
            pl.when(cond)(lambda: remote(src, place, first_sem.at[index], where).start())
        firsts.append((src, place, cond, index))

    step_2 = {k: {"+": to["z+"], "-": to["z-"]}[sign_of(0, k)] for k in range(PIECES)}
    for k in range(PIECES):
        src = mine.at[pl.ds(k * PV, PV)]
        home = own_slot(sym, c, k)
        final, via1, via2 = PAR_AT + home, T1_AT + k, T2_AT + k
        first(src, home, to["core"])
        first(src, home, to["x+"])
        first(src, home, to["x-"])
        first(src, TC_AT + k, to["y" + "+-"[k]])
        direct_b, direct_a = x0 + 2 * (1 - x1) + (1 - yhi) == 0, x0 + 2 * (1 - x1) + yhi == 0
        where_b = x1 * to["zb"] + (1 - x1) * step_2[k]
        place_b = jnp.where(direct_b, final, x1 * via2 + (1 - x1) * via1)
        first(src, place_b, where_b)
        where_a = x1 * to["za"] + (1 - x1) * to["ya"]
        place_a = jnp.where(direct_a | (x1 == 0), final, via1)
        first(src, place_a, where_a, x > 0)

    for (at_x, at_y), cores in TABLES.items():
        @pl.when((x == at_x) & (y == at_y))
        def _():
            (ops0, begins0, _), (ops1, _, _) = cores
            for n, (op0, op1) in enumerate(zip(ops0, ops1)):
                ops[n] = op0 + (op1 - op0) * c if op0 != op1 else op0
            for n, begin in enumerate(begins0):
                begins[n] = begin
    for n, way in enumerate(WAYS):
        devs[n] = to[way]

    n_row = dims[tile]
    n_col = dims[(z1 + yhi - 2 * z1 * yhi) * 4 + (z0 + x1 - 2 * z0 * x1) * 2 + (ylo + x0 - 2 * ylo * x0)]
    live_r = jnp.where(lax.broadcasted_iota(jnp.int32, (V, V), 0) < n_row, 1.0, 0.0)
    live = jnp.where(lax.broadcasted_iota(jnp.int32, (V, V), 1) < n_col, live_r, 0.0).astype(jnp.bfloat16)
    acc[...] = jnp.zeros_like(acc)
    for load in loads:
        load.wait()
    for i in range(NI):
        rc[:, i * V:(i + 1) * V] = rc[:, i * V:(i + 1) * V] * live
    for copy in keep:
        copy.wait()

    def decoded(n):
        op = ops[n]
        src, rest = lax.rem(op, 128), lax.div(op, 128)
        dst, rest = lax.rem(rest, 128), lax.div(rest, 128)
        return src, dst, lax.rem(rest, 128), lax.div(rest, 128)

    def events(point):
        @pl.loop(begins[point], begins[point + 1])
        def _(n):
            src, dst, index, way = decoded(n)

            @pl.when(way == WAIT)
            def _():
                arrived(src)

            @pl.when(way != WAIT)
            def _():
                remote(buf.at[src], dst, ssem.at[index], devs[way]).start()

    digit = (1 + 15 * x0) * (1 + 255 * x1)

    def chosen(groups, n):
        code = 0
        for number, names in enumerate(groups):
            of_y = [0] * 4
            for (at_x, at_y), (row, j, k) in zip(CLASSES, names):
                of_y[at_y] += (row * 8 + j * 2 + k) * 16 ** at_x
            value = of_y[0]
            if len(set(of_y)) > 1:
                value = value + (of_y[1] - of_y[0]) * ylo + (of_y[2] - of_y[0]) * yhi
                value = value + (of_y[3] - of_y[2] - of_y[1] + of_y[0]) * (yhi * ylo)
            code = code + (n == number) * 1 * value
        code = lax.rem(lax.div(code, digit), 16)
        return (yhi + code // 8) % 2 * 4 + (x + 4 - code // 2 % 4) % 4, code % 2

    def base_of(n):
        return sum((n == number) * base for number, base in enumerate(BASES[:-1]) if base)

    par_base = PAR_AT * (1 - (sym == 0) * 1)

    def unit(base, q, core):
        at = base + q * 4 + core * 2
        return buf[pl.ds(at, 2)].reshape(V, V)

    def first_stage(base, halves):
        for q, k in halves:
            arrived(own_slot(q, 1 - c, k))
        for h in range(PARTS[1]):
            if h:
                events(base + h)
            for t in range(h * 12 // PARTS[1], (h + 1) * 12 // PARTS[1]):
                left = jnp.concatenate([buf[q * 4 + 2 * p + k] for q, k in halves for p in range(2)], axis=0)
                r = jnp.dot(left, rc[:, t * 256:(t + 1) * 256], preferred_element_type=jnp.float32).astype(jnp.bfloat16)
                for lo_col, hi_col, pair, at in columns(t):
                    for number, (q, k) in enumerate(halves):
                        rows = pl.ds(pl.multiple_of(pair * V + k * PV, PV), PV)
                        for p in range(2):
                            lanes = pl.ds(p * V + at, hi_col - lo_col)
                            first = (2 * number + p) * PV
                            half[q, rows, lanes] = r[first:first + PV, lo_col:hi_col]

    def second_stage(base, q, last=False):
        @pl.when(jnp.logical_not(none))
        def _():
            for k in range(PIECES):
                arrived(PAR_AT + own_slot(q, 1 - c, k))

        for h in range(2):
            if h and PARTS[2] > 1:
                events(base + h)
            rows = pl.ds(h * HALF, HALF)
            for b0, b1 in ((0, 256), (256, 384)):
                right = jnp.concatenate([unit(par_base, q, p)[b0:b1] for p in range(2)], axis=1)
                acc[rows, b0:b1] += lax.dot_general(
                    half[q, rows, :], right, (((1,), (1,)), ((), ())), preferred_element_type=jnp.float32
                )
            if last:
                pltpu.make_async_copy(acc.at[rows], out.at[rows], local_sem.at[h]).start()

    @pl.loop(0, STAGES - 1)
    def _(n):
        second = sum((n == k) * 1 for k, stage in enumerate(SEQUENCE) if stage == 2)
        halves = [chosen(group, n) for group in UNITS]
        base = base_of(n)
        events(base)
        pl.when(second == 0)(lambda: first_stage(base, halves))
        pl.when(second == 1)(lambda: second_stage(base, halves[0][0]))

    events(BASES[-2])
    second_stage(BASES[-2], chosen(UNITS[0], jnp.int32(STAGES - 1))[0], last=True)
    events(POINTS - 1)

    leaving = []
    for r in range(len(REST)):
        q, _ = chosen(REST, jnp.int32(r))
        for k in range(PIECES):
            arrived(own_slot(q, 1 - c, k))

        @pl.when(jnp.logical_not(none))
        def _():
            for k in range(PIECES):
                arrived(PAR_AT + own_slot(q, 1 - c, k))

        par_at = par_base + q * 4
        for source, target, sem in ((q * 4, out_own.at[r], 18 + 2 * r), (par_at, out_par.at[r], 19 + 2 * r)):
            leaving.append(pltpu.make_async_copy(buf.at[pl.ds(source, 4)], target, local_sem.at[sem - 8]))
            leaving[-1].start()

    for src, place, cond, index in firsts:
        def sent(src=src, place=place, index=index):
            remote(src, place, first_sem.at[index], to["core"]).wait_send()

        if cond is None:
            sent()
        else:
            pl.when(cond)(sent)

    @pl.loop(0, begins[POINTS + 1])
    def _(n):
        remote(buf.at[0], 0, ssem.at[n], to["core"]).wait_send()

    for h in range(2):
        rows = pl.ds(h * HALF, HALF)
        pltpu.make_async_copy(acc.at[rows], out.at[rows], local_sem.at[h]).wait()
    for copy in leaving:
        copy.wait()


ALL = [(row, j) for j in (0, 1, 3, 2) for row in range(2)]


def left_over():
    by_class = []
    for at in range(len(CLASSES)):
        done = [names[at][:2] for group in UNITS for stage, names in zip(SEQUENCE, group) if stage == 1]
        by_class.append([name + (0,) for name in ALL if name not in done])
    return tuple(zip(*by_class))


REST = left_over()


def rest_kernel(dims, own_hbm, par_hbm, amps, raw, out, own, par, rc, half, acc, sems):
    sym, tile = lax.axis_index("sym"), lax.axis_index("tile")
    n, hi = len(REST), NI // 2
    get_own = pltpu.make_async_copy(own_hbm, own, sems.at[0])
    get_par = pltpu.make_async_copy(par_hbm, par, sems.at[1])
    get_amps = [pltpu.make_async_copy(amps.at[i], rc.at[:, pl.ds(i * V, V)], sems.at[2 + i]) for i in range(NI)]
    get_raw = [
        pltpu.make_async_copy(raw.at[pl.ds(h * HALF, HALF)], acc.at[pl.ds(h * HALF, HALF)], sems.at[2 + NI + h])
        for h in range(2)
    ]
    for copy in [get_own] + get_amps[:hi] + [get_par, get_raw[0]] + get_amps[hi:] + [get_raw[1]]:
        copy.start()
    n_row, n_col = dims[tile], dims[jnp.bitwise_xor(tile, sym)]
    live = (lax.broadcasted_iota(jnp.int32, (V, V), 0) < n_row) & (lax.broadcasted_iota(jnp.int32, (V, V), 1) < n_col)
    live_b = jnp.where(live, 1.0, 0.0).astype(jnp.bfloat16)
    puts, masked = [], 0
    for h in range(2):
        if h == 0:
            get_own.wait()
        for t in range(6 * h, 6 * (h + 1)):
            while masked <= columns(t)[-1][2]:
                get_amps[masked].wait()
                rc[:, masked * V:(masked + 1) * V] = rc[:, masked * V:(masked + 1) * V] * live_b
                masked += 1
            left = own[...].reshape(n * 2 * V, V)
            r = jnp.dot(left, rc[:, t * 256:(t + 1) * 256], preferred_element_type=jnp.float32).astype(jnp.bfloat16)
            for lo_col, hi_col, pair, at in columns(t):
                for p in range(2 * n):
                    lanes = pl.ds(p * V + at, hi_col - lo_col)
                    half[(pair - h * hi) * V:(pair - h * hi + 1) * V, lanes] = r[p * V:(p + 1) * V, lo_col:hi_col]
        if h == 0:
            get_par.wait()
        get_raw[h].wait()
        rows = pl.ds(h * HALF, HALF)
        for b0, b1 in ((0, 256), (256, 384)):
            right = [par[r, pl.ds(2 * p, 2)].reshape(V, V)[b0:b1] for r in range(n) for p in range(2)]
            right = jnp.concatenate(right, axis=1)
            r = lax.dot_general(half[...], right, (((1,), (1,)), ((), ())), preferred_element_type=jnp.float32)
            r = r + acc[rows, b0:b1]
            for i in range(hi):
                at = pl.ds((h * hi + i) * V, V)
                acc[at, b0:b1] = jnp.where(live[:, b0:b1], r[i * V:(i + 1) * V], 0.0)
            lanes = pl.ds(b0, b1 - b0)
            puts.append(pltpu.make_async_copy(acc.at[rows, lanes], out.at[rows, lanes], sems.at[4 + NI + len(puts)]))
            puts[-1].start()
    for copy in puts:
        copy.wait()


def shards(irrep_dims, chol_vectors, amplitudes):
    bf, sem = jnp.bfloat16, pltpu.SemaphoreType.DMA
    n = len(REST)
    own, chol, amps = (n, 4, PV, V), chol_vectors.reshape(V, V), amplitudes.reshape(NI, V, V)
    anywhere = pl.BlockSpec(memory_space=pl.ANY)
    raw, rest_own, rest_par = pl.pallas_call(
        kernel,
        out_shape=[
            jax.ShapeDtypeStruct((NI * V, V), jnp.float32),
            jax.ShapeDtypeStruct(own, bf),
            jax.ShapeDtypeStruct(own, bf),
        ],
        in_specs=[pl.BlockSpec(memory_space=pltpu.SMEM), anywhere, anywhere],
        out_specs=[anywhere] * 3,
        scratch_shapes=[
            pltpu.VMEM((SLOTS, PV, V), bf),
            pltpu.VMEM((V, NI * V), bf),
            pltpu.VMEM((8, NI * V, 2 * V), bf),
            pltpu.VMEM((NI * V, V), jnp.float32),
            pltpu.SMEM((MOST_OPS,), jnp.int32),
            pltpu.SMEM((POINTS + 2,), jnp.int32),
            pltpu.SMEM((len(WAYS),), jnp.int32),
            sem((MOST_SENDS,)), sem((FIRST_SENDS,)), sem((SLOTS,)), sem((10 + 2 * n,)),
        ],
        compiler_params=pltpu.CompilerParams(
            collective_id=0, has_side_effects=True, vmem_limit_bytes=63 * 1024 * 1024
        ),
        cost_estimate=pl.CostEstimate(flops=(8 - n) * 3_600_000_000, bytes_accessed=12_000_000, transcendentals=0),
        name="ladder",
    )(irrep_dims, chol, amps)
    total = pl.pallas_call(
        rest_kernel,
        out_shape=jax.ShapeDtypeStruct((NI * V, V), jnp.float32),
        in_specs=[pl.BlockSpec(memory_space=pltpu.SMEM)] + [anywhere] * 4,
        out_specs=anywhere,
        scratch_shapes=[
            pltpu.VMEM(own, bf),
            pltpu.VMEM(own, bf),
            pltpu.VMEM((V, NI * V), bf),
            pltpu.VMEM((HALF, n * 2 * V), bf),
            pltpu.VMEM((NI * V, V), jnp.float32),
            sem((8 + NI,)),
        ],
        compiler_params=pltpu.CompilerParams(vmem_limit_bytes=60 * 1024 * 1024),
        cost_estimate=pl.CostEstimate(flops=n * 3_600_000_000, bytes_accessed=16_000_000, transcendentals=0),
        name="rest",
    )(irrep_dims, rest_own, rest_par, amps, raw)
    return total.reshape(1, NI, V, V)


def solution(mesh):
    return jax.shard_map(
        shards,
        mesh=mesh,
        in_specs=(P(), P(("sym", "occ"), "tile", None), P("sym", "occ", "tile", None)),
        out_specs=P("sym", "occ", "tile", None),
        check_vma=False,
    )
```

```python
import jax
import jax.numpy as jnp
from jax import lax
from jax.experimental import pallas as pl
from jax.experimental.pallas import tpu as pltpu
from jax.sharding import PartitionSpec as P

V = 384
NI = 8
PIECES = 2
PV = V // PIECES
HALF = NI * V // 2
CROSSF, OWN, PASS_Z, FWD_Y, PASS_Y, PAR = range(6)
PARTS = {1: 2, 2: 1}
SEQUENCE = (1, 1, 1, 1, 1, 2, 1, 2, 1, 2, 2, 2, 2, 2)
UNITS = (
    (
        ((0, 0, 0), (0, 0, 0), (0, 0, 0), (0, 0, 0), (0, 0, 0), (0, 0, 0), (0, 0, 0), (0, 0, 0), (0, 0, 0), (0, 0, 0), (0, 0, 0), (0, 0, 0), (0, 0, 0), (0, 0, 0), (0, 0, 0), (0, 0, 0)),
        ((0, 1, 0), (0, 1, 0), (0, 1, 0), (0, 1, 0), (0, 1, 0), (0, 1, 0), (0, 1, 0), (0, 1, 0), (0, 1, 0), (0, 1, 0), (0, 1, 0), (0, 1, 0), (0, 1, 0), (0, 1, 0), (0, 1, 0), (0, 1, 0)),
        ((0, 1, 1), (0, 1, 1), (0, 1, 1), (0, 1, 1), (0, 1, 1), (0, 1, 1), (0, 1, 1), (0, 1, 1), (0, 1, 1), (0, 1, 1), (0, 1, 1), (0, 1, 1), (0, 1, 1), (0, 1, 1), (0, 1, 1), (0, 1, 1)),
        ((1, 0, 0), (1, 0, 0), (1, 0, 0), (1, 0, 0), (0, 2, 0), (0, 2, 0), (1, 0, 0), (1, 0, 0), (1, 0, 0), (1, 0, 0), (1, 0, 0), (1, 0, 0), (1, 0, 0), (1, 0, 0), (1, 0, 0), (1, 0, 0)),
        ((0, 2, 0), (0, 2, 0), (0, 2, 0), (0, 2, 0), (1, 0, 0), (1, 0, 0), (0, 2, 0), (1, 0, 1), (0, 2, 0), (0, 2, 0), (0, 2, 0), (0, 2, 0), (0, 2, 0), (0, 2, 0), (0, 2, 0), (0, 2, 0)),
        ((0, 0, 0), (0, 0, 0), (0, 0, 0), (0, 0, 0), (0, 0, 0), (0, 0, 0), (1, 0, 0), (1, 0, 0), (0, 0, 0), (0, 0, 0), (0, 0, 0), (0, 0, 0), (0, 0, 0), (0, 0, 0), (0, 0, 0), (0, 0, 0)),
        ((1, 1, 0), (1, 1, 0), (1, 1, 0), (1, 1, 0), (1, 3, 0), (1, 1, 0), (1, 1, 0), (1, 1, 0), (1, 3, 0), (1, 3, 0), (1, 1, 0), (1, 1, 0), (1, 1, 0), (1, 1, 0), (1, 1, 0), (1, 1, 0)),
        ((1, 0, 0), (1, 0, 0), (1, 0, 0), (1, 0, 0), (0, 1, 0), (1, 0, 0), (0, 0, 0), (0, 0, 0), (1, 0, 0), (1, 0, 0), (1, 0, 0), (1, 0, 0), (1, 0, 0), (1, 0, 0), (1, 0, 0), (1, 0, 0)),
        ((1, 3, 0), (1, 3, 0), (1, 1, 1), (1, 1, 1), (1, 0, 1), (1, 1, 1), (1, 1, 1), (1, 1, 1), (1, 1, 0), (1, 1, 0), (1, 1, 1), (1, 1, 1), (1, 1, 1), (1, 1, 1), (1, 1, 1), (1, 1, 1)),
        ((0, 1, 0), (0, 1, 0), (0, 1, 0), (0, 1, 0), (1, 0, 0), (0, 1, 0), (0, 1, 0), (0, 1, 0), (0, 1, 0), (0, 1, 0), (0, 1, 0), (0, 1, 0), (0, 1, 0), (0, 1, 0), (0, 1, 0), (0, 1, 0)),
        ((1, 1, 0), (1, 1, 0), (0, 3, 0), (0, 3, 0), (1, 1, 0), (1, 1, 0), (1, 1, 0), (1, 1, 0), (1, 1, 0), (1, 1, 0), (1, 1, 0), (1, 1, 0), (1, 1, 0), (1, 1, 0), (1, 1, 0), (1, 1, 0)),
        ((0, 3, 0), (0, 3, 0), (0, 2, 0), (0, 2, 0), (0, 3, 0), (0, 3, 0), (0, 3, 0), (0, 3, 0), (0, 3, 0), (0, 3, 0), (0, 3, 0), (0, 3, 0), (0, 3, 0), (0, 3, 0), (0, 3, 0), (0, 3, 0)),
        ((1, 3, 0), (1, 3, 0), (1, 3, 0), (1, 1, 0), (1, 3, 0), (1, 3, 0), (1, 3, 0), (1, 3, 0), (1, 3, 0), (1, 3, 0), (1, 3, 0), (1, 3, 0), (1, 3, 0), (1, 3, 0), (1, 3, 0), (1, 3, 0)),
        ((0, 2, 0), (0, 2, 0), (1, 1, 0), (1, 3, 0), (0, 2, 0), (0, 2, 0), (0, 2, 0), (0, 2, 0), (0, 2, 0), (0, 2, 0), (0, 2, 0), (0, 2, 0), (0, 2, 0), (0, 2, 0), (0, 2, 0), (0, 2, 0)),
    ),
    (
        ((0, 0, 1), (0, 0, 1), (0, 0, 1), (0, 0, 1), (0, 0, 1), (0, 0, 1), (0, 0, 1), (0, 0, 1), (0, 0, 1), (0, 0, 1), (0, 0, 1), (0, 0, 1), (0, 0, 1), (0, 0, 1), (0, 0, 1), (0, 0, 1)),
        ((0, 3, 0), (0, 3, 0), (0, 3, 0), (0, 3, 0), (0, 3, 0), (0, 3, 0), (0, 3, 0), (0, 3, 0), (0, 3, 0), (0, 3, 0), (0, 3, 0), (0, 3, 0), (0, 3, 0), (0, 3, 0), (0, 3, 0), (0, 3, 0)),
        ((0, 3, 1), (0, 3, 1), (0, 3, 1), (0, 3, 1), (0, 3, 1), (0, 3, 1), (0, 3, 1), (0, 3, 1), (0, 3, 1), (0, 3, 1), (0, 3, 1), (0, 3, 1), (0, 3, 1), (0, 3, 1), (0, 3, 1), (0, 3, 1)),
        ((1, 0, 1), (1, 0, 1), (1, 0, 1), (1, 0, 1), (0, 2, 1), (0, 2, 1), (1, 0, 1), (0, 2, 0), (1, 0, 1), (1, 0, 1), (1, 0, 1), (1, 0, 1), (1, 0, 1), (1, 0, 1), (1, 0, 1), (1, 0, 1)),
        ((0, 2, 1), (0, 2, 1), (0, 2, 1), (0, 2, 1), (1, 1, 0), (1, 0, 1), (0, 2, 1), (0, 2, 1), (0, 2, 1), (0, 2, 1), (0, 2, 1), (0, 2, 1), (0, 2, 1), (0, 2, 1), (0, 2, 1), (0, 2, 1)),
        ((0, 0, 0), (0, 0, 0), (0, 0, 0), (0, 0, 0), (0, 0, 0), (0, 0, 0), (1, 0, 0), (1, 0, 0), (0, 0, 0), (0, 0, 0), (0, 0, 0), (0, 0, 0), (0, 0, 0), (0, 0, 0), (0, 0, 0), (0, 0, 0)),
        ((1, 1, 1), (1, 1, 1), (1, 3, 0), (1, 3, 0), (1, 1, 1), (1, 3, 0), (1, 3, 0), (1, 3, 0), (1, 3, 1), (1, 3, 1), (1, 3, 0), (1, 3, 0), (1, 3, 0), (1, 3, 0), (1, 3, 0), (1, 3, 0)),
        ((1, 0, 0), (1, 0, 0), (1, 0, 0), (1, 0, 0), (0, 1, 0), (1, 0, 0), (0, 0, 0), (0, 0, 0), (1, 0, 0), (1, 0, 0), (1, 0, 0), (1, 0, 0), (1, 0, 0), (1, 0, 0), (1, 0, 0), (1, 0, 0)),
        ((1, 3, 1), (1, 3, 1), (1, 3, 1), (1, 3, 1), (1, 3, 1), (1, 3, 1), (1, 3, 1), (1, 3, 1), (1, 1, 1), (1, 1, 1), (1, 3, 1), (1, 3, 1), (1, 3, 1), (1, 3, 1), (1, 3, 1), (1, 3, 1)),
        ((0, 1, 0), (0, 1, 0), (0, 1, 0), (0, 1, 0), (1, 0, 0), (0, 1, 0), (0, 1, 0), (0, 1, 0), (0, 1, 0), (0, 1, 0), (0, 1, 0), (0, 1, 0), (0, 1, 0), (0, 1, 0), (0, 1, 0), (0, 1, 0)),
        ((1, 1, 0), (1, 1, 0), (0, 3, 0), (0, 3, 0), (1, 1, 0), (1, 1, 0), (1, 1, 0), (1, 1, 0), (1, 1, 0), (1, 1, 0), (1, 1, 0), (1, 1, 0), (1, 1, 0), (1, 1, 0), (1, 1, 0), (1, 1, 0)),
        ((0, 3, 0), (0, 3, 0), (0, 2, 0), (0, 2, 0), (0, 3, 0), (0, 3, 0), (0, 3, 0), (0, 3, 0), (0, 3, 0), (0, 3, 0), (0, 3, 0), (0, 3, 0), (0, 3, 0), (0, 3, 0), (0, 3, 0), (0, 3, 0)),
        ((1, 3, 0), (1, 3, 0), (1, 3, 0), (1, 1, 0), (1, 3, 0), (1, 3, 0), (1, 3, 0), (1, 3, 0), (1, 3, 0), (1, 3, 0), (1, 3, 0), (1, 3, 0), (1, 3, 0), (1, 3, 0), (1, 3, 0), (1, 3, 0)),
        ((0, 2, 0), (0, 2, 0), (1, 1, 0), (1, 3, 0), (0, 2, 0), (0, 2, 0), (0, 2, 0), (0, 2, 0), (0, 2, 0), (0, 2, 0), (0, 2, 0), (0, 2, 0), (0, 2, 0), (0, 2, 0), (0, 2, 0), (0, 2, 0)),
    ),
)
EVENTS = (
    (
        (2, ((CROSSF, 0), (CROSSF, 1), (OWN, 0, 1, 0), (OWN, 0, 3, 0), (PASS_Z, 0, 0), (PASS_Z, 0, 1),)),
        (3, ((OWN, 0, 1, 1), (OWN, 0, 3, 1),)),
        (4, ((OWN, 1, 0, 0), (OWN, 1, 0, 1), (PASS_Z, 1, 0), (PASS_Z, 3, 0),)),
        (5, ((OWN, 0, 2, 0),)),
        (6, ((OWN, 0, 2, 1), (FWD_Y, 0, 0), (FWD_Y, 0, 1),)),
        (8, ((OWN, 1, 1, 0), (PASS_Z, 1, 1), (PASS_Z, 3, 1),)),
        (9, ((PASS_Y, 0, 1),)),
        (10, ((OWN, 1, 1, 1),)),
        (11, ((OWN, 1, 3, 0), (FWD_Y, 1, 0), (FWD_Y, 3, 0),)),
        (12, ((OWN, 1, 2, 1), (PASS_Z, 2, 0), (PASS_Z, 2, 1),)),
        (13, ((OWN, 1, 2, 0),)),
        (14, ((FWD_Y, 1, 1), (FWD_Y, 3, 1), (PASS_Y, 1, 0), (OWN, 1, 3, 1),)),
        (15, ((FWD_Y, 2, 0), (FWD_Y, 2, 1),)),
        (17, ((PASS_Y, 3, 1),)),
        (18, ((PASS_Y, 2, 0),)),
    ),
    (
        (2, ((CROSSF, 0), (CROSSF, 1), (OWN, 0, 1, 0), (OWN, 0, 3, 0), (PASS_Z, 0, 0), (PASS_Z, 0, 1),)),
        (3, ((OWN, 0, 1, 1), (OWN, 0, 3, 1),)),
        (4, ((OWN, 1, 0, 0), (OWN, 1, 0, 1), (PASS_Z, 1, 0), (PASS_Z, 3, 0),)),
        (5, ((OWN, 0, 2, 0),)),
        (6, ((OWN, 0, 2, 1), (FWD_Y, 0, 0), (FWD_Y, 0, 1),)),
        (8, ((OWN, 1, 1, 0), (PASS_Z, 1, 1), (PASS_Z, 3, 1),)),
        (9, ((PASS_Y, 0, 0),)),
        (10, ((OWN, 1, 1, 1),)),
        (11, ((OWN, 1, 3, 0), (FWD_Y, 1, 0), (FWD_Y, 3, 0),)),
        (12, ((OWN, 1, 2, 1), (PASS_Z, 2, 0), (PASS_Z, 2, 1),)),
        (13, ((OWN, 1, 3, 1),)),
        (14, ((OWN, 1, 2, 0), (FWD_Y, 1, 1), (FWD_Y, 3, 1), (PASS_Y, 3, 0),)),
        (16, ((FWD_Y, 2, 0), (FWD_Y, 2, 1),)),
        (17, ((PASS_Y, 1, 1),)),
        (18, ((PASS_Y, 2, 1),)),
    ),
    (
        (2, ((CROSSF, 0), (CROSSF, 1), (OWN, 0, 1, 0), (OWN, 0, 3, 0), (PASS_Z, 0, 0), (PASS_Z, 0, 1),)),
        (3, ((OWN, 0, 1, 1), (OWN, 0, 3, 1),)),
        (4, ((OWN, 1, 0, 0), (OWN, 1, 0, 1), (PASS_Z, 1, 0), (PASS_Z, 3, 0),)),
        (5, ((OWN, 0, 2, 0),)),
        (6, ((OWN, 0, 2, 1), (PAR, 0, 0, 0), (PAR, 0, 0, 1),)),
        (8, ((OWN, 1, 1, 0), (OWN, 1, 3, 0), (PASS_Z, 1, 1), (PASS_Z, 3, 1),)),
        (9, ((PASS_Y, 0, 0),)),
        (10, ((OWN, 1, 1, 1),)),
        (11, ((OWN, 1, 3, 1), (PAR, 0, 1, 0), (PAR, 0, 3, 0),)),
        (12, ((OWN, 1, 2, 0), (OWN, 1, 2, 1), (PASS_Z, 2, 0), (PASS_Z, 2, 1), (PAR, 1, 0, 0), (PAR, 1, 0, 1),)),
        (13, ((PAR, 0, 3, 1), (PAR, 0, 1, 1),)),
        (14, ((PASS_Y, 3, 0),)),
        (15, ((PAR, 0, 2, 0), (PAR, 0, 2, 1),)),
        (17, ((PASS_Y, 1, 1), (PAR, 1, 1, 0),)),
        (18, ((PAR, 1, 3, 0),)),
        (19, ((PASS_Y, 2, 1), (PAR, 1, 3, 1),)),
        (20, ((PAR, 1, 1, 1), (PAR, 1, 2, 0),)),
        (21, ((PAR, 1, 2, 1),)),
    ),
    (
        (2, ((CROSSF, 0), (CROSSF, 1), (OWN, 0, 1, 0), (OWN, 0, 3, 0), (PASS_Z, 0, 0), (PASS_Z, 0, 1),)),
        (3, ((OWN, 0, 1, 1), (OWN, 0, 3, 1),)),
        (4, ((OWN, 1, 0, 0), (OWN, 1, 0, 1), (PASS_Z, 1, 0), (PASS_Z, 3, 0),)),
        (5, ((OWN, 0, 2, 0),)),
        (6, ((OWN, 0, 2, 1), (PAR, 0, 0, 0), (PAR, 0, 0, 1),)),
        (8, ((OWN, 1, 1, 0), (OWN, 1, 3, 0), (PASS_Z, 1, 1), (PASS_Z, 3, 1),)),
        (9, ((PASS_Y, 0, 1),)),
        (10, ((OWN, 1, 1, 1),)),
        (11, ((OWN, 1, 3, 1), (PAR, 0, 1, 0), (PAR, 0, 3, 0),)),
        (12, ((OWN, 1, 2, 0), (OWN, 1, 2, 1), (PASS_Z, 2, 0), (PASS_Z, 2, 1), (PAR, 1, 0, 0), (PAR, 1, 0, 1),)),
        (13, ((PAR, 0, 3, 1), (PAR, 0, 1, 1),)),
        (14, ((PASS_Y, 1, 0),)),
        (15, ((PAR, 0, 2, 0), (PAR, 0, 2, 1),)),
        (17, ((PASS_Y, 3, 1), (PAR, 1, 3, 0),)),
        (18, ((PAR, 1, 1, 0),)),
        (19, ((PASS_Y, 2, 0), (PAR, 1, 1, 1),)),
        (20, ((PAR, 1, 3, 1), (PAR, 1, 2, 1),)),
        (21, ((PAR, 1, 2, 0),)),
    ),
    (
        (2, ((CROSSF, 0), (OWN, 0, 1, 0), (OWN, 0, 3, 0), (PASS_Z, 0, 0), (PASS_Z, 0, 1), (PAR, 0, 0, 0),)),
        (3, ((CROSSF, 1), (OWN, 0, 1, 1), (OWN, 0, 3, 1), (PAR, 1, 0, 0),)),
        (4, ((PASS_Z, 1, 0), (PASS_Z, 3, 0),)),
        (5, ((OWN, 0, 2, 0), (PAR, 0, 0, 1), (PAR, 1, 0, 1),)),
        (6, ((OWN, 0, 2, 1), (FWD_Y, 0, 0), (FWD_Y, 0, 1),)),
        (7, ((OWN, 1, 0, 0), (OWN, 1, 1, 0), (PAR, 0, 1, 0),)),
        (8, ((OWN, 1, 3, 0), (PASS_Z, 1, 1), (PASS_Z, 3, 1),)),
        (9, ((OWN, 1, 1, 1), (PAR, 0, 3, 0), (PAR, 1, 1, 0),)),
        (10, ((OWN, 1, 3, 1), (FWD_Y, 1, 0), (FWD_Y, 3, 0),)),
        (11, ((OWN, 1, 0, 1), (OWN, 1, 2, 0), (PASS_Z, 2, 0), (PASS_Z, 2, 1), (PAR, 1, 3, 0),)),
        (12, ((OWN, 1, 2, 1), (PAR, 0, 1, 1), (PAR, 1, 1, 1),)),
        (13, ((FWD_Y, 1, 1), (FWD_Y, 3, 1),)),
        (14, ((FWD_Y, 2, 0), (PAR, 0, 3, 1), (PAR, 1, 3, 1),)),
        (15, ((FWD_Y, 2, 1),)),
        (16, ((PAR, 0, 2, 0), (PAR, 1, 2, 0),)),
        (17, ((PAR, 0, 2, 1), (PAR, 1, 2, 1),)),
    ),
    (
        (2, ((CROSSF, 0), (OWN, 0, 1, 0), (OWN, 0, 3, 0), (PASS_Z, 0, 0), (PASS_Z, 0, 1), (PAR, 1, 0, 0),)),
        (3, ((CROSSF, 1), (OWN, 0, 1, 1), (OWN, 0, 3, 1), (PAR, 0, 0, 0),)),
        (4, ((PASS_Z, 1, 0), (PASS_Z, 3, 0),)),
        (5, ((OWN, 0, 2, 0), (PAR, 0, 0, 1), (PAR, 1, 0, 1),)),
        (6, ((OWN, 0, 2, 1), (FWD_Y, 0, 0), (FWD_Y, 0, 1),)),
        (7, ((OWN, 1, 0, 0), (OWN, 1, 0, 1), (OWN, 1, 1, 0),)),
        (8, ((OWN, 1, 3, 0), (PASS_Z, 1, 1), (PASS_Z, 3, 1),)),
        (9, ((OWN, 1, 1, 1), (PAR, 0, 1, 0), (PAR, 1, 1, 0),)),
        (10, ((OWN, 1, 3, 1), (FWD_Y, 1, 0), (FWD_Y, 3, 0),)),
        (11, ((OWN, 1, 2, 0), (OWN, 1, 2, 1), (PASS_Z, 2, 0), (PASS_Z, 2, 1), (PAR, 0, 3, 0), (PAR, 1, 3, 0),)),
        (12, ((PAR, 0, 1, 1), (PAR, 1, 1, 1),)),
        (13, ((FWD_Y, 1, 1), (FWD_Y, 3, 1),)),
        (14, ((FWD_Y, 2, 0), (FWD_Y, 2, 1), (PAR, 0, 3, 1), (PAR, 1, 3, 1),)),
        (16, ((PAR, 0, 2, 0), (PAR, 1, 2, 0),)),
        (17, ((PAR, 0, 2, 1), (PAR, 1, 2, 1),)),
    ),
    (
        (2, ((CROSSF, 0), (CROSSF, 1), (OWN, 0, 1, 0), (OWN, 0, 3, 0), (PASS_Z, 0, 0), (PASS_Z, 0, 1),)),
        (3, ((OWN, 0, 1, 1), (OWN, 0, 3, 1),)),
        (4, ((OWN, 1, 0, 0), (OWN, 1, 0, 1), (PASS_Z, 1, 0), (PASS_Z, 3, 0),)),
        (5, ((OWN, 0, 2, 0),)),
        (6, ((OWN, 0, 2, 1), (FWD_Y, 0, 0), (FWD_Y, 0, 1),)),
        (7, ((OWN, 1, 1, 0),)),
        (8, ((OWN, 1, 3, 0), (PASS_Z, 1, 1), (PASS_Z, 3, 1),)),
        (9, ((OWN, 1, 1, 1), (PAR, 0, 0, 0), (PAR, 1, 0, 0),)),
        (10, ((OWN, 1, 3, 1), (FWD_Y, 1, 0), (FWD_Y, 3, 0), (PAR, 1, 0, 1), (PAR, 0, 0, 1),)),
        (11, ((OWN, 1, 2, 0), (OWN, 1, 2, 1), (PASS_Z, 2, 0), (PASS_Z, 2, 1), (PAR, 0, 1, 0),)),
        (12, ((FWD_Y, 1, 1), (FWD_Y, 3, 1), (PAR, 1, 1, 0),)),
        (13, ((PAR, 0, 3, 0),)),
        (14, ((FWD_Y, 2, 0), (FWD_Y, 2, 1), (PAR, 1, 3, 0),)),
        (15, ((PAR, 0, 1, 1), (PAR, 1, 1, 1),)),
        (17, ((PAR, 0, 3, 1), (PAR, 1, 3, 1),)),
        (18, ((PAR, 0, 2, 0), (PAR, 1, 2, 0),)),
        (19, ((PAR, 0, 2, 1),)),
        (20, ((PAR, 1, 2, 1),)),
    ),
    (
        (2, ((CROSSF, 0), (CROSSF, 1), (OWN, 0, 1, 0), (OWN, 0, 3, 0), (PASS_Z, 0, 0), (PASS_Z, 0, 1),)),
        (3, ((OWN, 0, 1, 1), (OWN, 0, 3, 1),)),
        (4, ((OWN, 1, 0, 0), (PASS_Z, 1, 0), (PASS_Z, 3, 0),)),
        (5, ((OWN, 0, 2, 0),)),
        (6, ((OWN, 0, 2, 1), (OWN, 1, 0, 1), (FWD_Y, 0, 0), (FWD_Y, 0, 1),)),
        (7, ((OWN, 1, 1, 0),)),
        (8, ((OWN, 1, 3, 0), (PASS_Z, 1, 1), (PASS_Z, 3, 1),)),
        (9, ((OWN, 1, 1, 1), (PAR, 0, 0, 0), (PAR, 1, 0, 0),)),
        (10, ((OWN, 1, 3, 1), (FWD_Y, 1, 0), (FWD_Y, 3, 0), (PAR, 1, 0, 1), (PAR, 0, 0, 1),)),
        (11, ((OWN, 1, 2, 0), (OWN, 1, 2, 1), (PASS_Z, 2, 0), (PASS_Z, 2, 1), (PAR, 0, 1, 0),)),
        (12, ((FWD_Y, 1, 1), (FWD_Y, 3, 1), (PAR, 1, 1, 0),)),
        (13, ((PAR, 0, 3, 0),)),
        (14, ((FWD_Y, 2, 0), (FWD_Y, 2, 1), (PAR, 1, 3, 0),)),
        (15, ((PAR, 0, 1, 1), (PAR, 1, 1, 1),)),
        (17, ((PAR, 0, 3, 1), (PAR, 1, 3, 1),)),
        (18, ((PAR, 0, 2, 0), (PAR, 1, 2, 0),)),
        (19, ((PAR, 0, 2, 1),)),
        (20, ((PAR, 1, 2, 1),)),
    ),
    (
        (2, ((CROSSF, 0), (CROSSF, 1), (OWN, 0, 1, 0), (OWN, 0, 3, 0), (FWD_Y, 0, 0), (PAR, 0, 0, 0),)),
        (3, ((OWN, 0, 1, 1), (OWN, 0, 3, 1), (FWD_Y, 0, 1), (PAR, 0, 0, 1),)),
        (4, ((OWN, 1, 0, 0), (OWN, 1, 0, 1),)),
        (5, ((OWN, 0, 2, 0), (FWD_Y, 1, 0), (PAR, 0, 1, 0),)),
        (6, ((OWN, 0, 2, 1), (PASS_Y, 0, 0), (PASS_Y, 0, 1),)),
        (7, ((FWD_Y, 3, 0), (PAR, 0, 3, 0),)),
        (8, ((OWN, 1, 3, 0), (PASS_Y, 1, 0),)),
        (9, ((FWD_Y, 1, 1), (PAR, 0, 1, 1), (PAR, 1, 0, 0),)),
        (10, ((OWN, 1, 3, 1), (PAR, 1, 0, 1),)),
        (11, ((OWN, 1, 1, 0), (FWD_Y, 3, 1), (PASS_Y, 3, 0), (PAR, 0, 3, 1),)),
        (12, ((OWN, 1, 2, 0), (OWN, 1, 2, 1), (PAR, 1, 1, 0),)),
        (13, ((FWD_Y, 2, 0), (PASS_Y, 1, 1), (PAR, 0, 2, 0),)),
        (14, ((OWN, 1, 1, 1), (FWD_Y, 2, 1), (PASS_Y, 3, 1), (PAR, 0, 2, 1), (PAR, 1, 3, 0),)),
        (15, ((PASS_Y, 2, 0),)),
        (16, ((PAR, 1, 1, 1),)),
        (17, ((PASS_Y, 2, 1), (PAR, 1, 3, 1),)),
        (18, ((PAR, 1, 2, 0),)),
        (20, ((PAR, 1, 2, 1),)),
    ),
    (
        (2, ((CROSSF, 0), (CROSSF, 1), (OWN, 0, 1, 0), (OWN, 0, 3, 0), (FWD_Y, 0, 0), (PAR, 0, 0, 0),)),
        (3, ((OWN, 0, 1, 1), (OWN, 0, 3, 1), (FWD_Y, 0, 1), (PAR, 0, 0, 1),)),
        (4, ((OWN, 1, 0, 0), (OWN, 1, 0, 1),)),
        (5, ((OWN, 0, 2, 0), (FWD_Y, 1, 0), (PAR, 0, 1, 0),)),
        (6, ((OWN, 0, 2, 1), (PASS_Y, 0, 0), (PASS_Y, 0, 1),)),
        (7, ((FWD_Y, 3, 0), (PAR, 0, 3, 0),)),
        (8, ((OWN, 1, 3, 0), (PASS_Y, 1, 0),)),
        (9, ((FWD_Y, 1, 1), (PAR, 0, 1, 1), (PAR, 1, 0, 0),)),
        (10, ((OWN, 1, 3, 1), (PAR, 1, 0, 1),)),
        (11, ((OWN, 1, 1, 0), (FWD_Y, 3, 1), (PASS_Y, 3, 0), (PAR, 0, 3, 1),)),
        (12, ((OWN, 1, 1, 1), (OWN, 1, 2, 0), (PAR, 1, 1, 0),)),
        (13, ((FWD_Y, 2, 0), (PASS_Y, 1, 1), (PAR, 0, 2, 0),)),
        (14, ((OWN, 1, 2, 1), (FWD_Y, 2, 1), (PASS_Y, 3, 1), (PAR, 0, 2, 1), (PAR, 1, 3, 0),)),
        (16, ((PASS_Y, 2, 0), (PAR, 1, 1, 1),)),
        (17, ((PAR, 1, 3, 1),)),
        (18, ((PASS_Y, 2, 1),)),
        (19, ((PAR, 1, 2, 0),)),
        (20, ((PAR, 1, 2, 1),)),
    ),
    (
        (2, ((CROSSF, 0), (CROSSF, 1), (OWN, 0, 1, 0), (OWN, 0, 3, 0), (FWD_Y, 0, 0), (PAR, 0, 0, 0),)),
        (3, ((OWN, 0, 1, 1), (OWN, 0, 3, 1), (FWD_Y, 0, 1), (PAR, 0, 0, 1),)),
        (4, ((OWN, 1, 0, 0), (OWN, 1, 0, 1),)),
        (5, ((OWN, 0, 2, 0), (FWD_Y, 1, 0), (PAR, 0, 1, 0),)),
        (6, ((OWN, 0, 2, 1), (PASS_Y, 0, 0), (PASS_Y, 0, 1),)),
        (7, ((OWN, 1, 1, 0), (FWD_Y, 3, 0), (PAR, 0, 3, 0),)),
        (8, ((OWN, 1, 3, 0), (PASS_Y, 1, 0),)),
        (9, ((OWN, 1, 1, 1), (FWD_Y, 1, 1), (PAR, 0, 1, 1), (PAR, 1, 0, 0),)),
        (10, ((OWN, 1, 3, 1), (PAR, 1, 0, 1),)),
        (11, ((OWN, 1, 2, 1), (FWD_Y, 3, 1), (PASS_Y, 3, 0), (PAR, 0, 3, 1),)),
        (12, ((OWN, 1, 2, 0), (PAR, 1, 1, 0),)),
        (13, ((FWD_Y, 2, 0), (PASS_Y, 1, 1), (PAR, 0, 2, 0),)),
        (14, ((FWD_Y, 2, 1), (PASS_Y, 3, 1), (PAR, 0, 2, 1), (PAR, 1, 3, 0),)),
        (16, ((PASS_Y, 2, 0), (PAR, 1, 1, 1),)),
        (17, ((PAR, 1, 3, 1),)),
        (18, ((PASS_Y, 2, 1),)),
        (19, ((PAR, 1, 2, 0),)),
        (20, ((PAR, 1, 2, 1),)),
    ),
    (
        (2, ((CROSSF, 0), (CROSSF, 1), (OWN, 0, 1, 0), (OWN, 0, 3, 0), (FWD_Y, 0, 0), (PAR, 0, 0, 0),)),
        (3, ((OWN, 0, 1, 1), (OWN, 0, 3, 1), (FWD_Y, 0, 1), (PAR, 0, 0, 1),)),
        (4, ((OWN, 1, 0, 0), (OWN, 1, 0, 1),)),
        (5, ((OWN, 0, 2, 0), (FWD_Y, 1, 0), (PAR, 0, 1, 0),)),
        (6, ((OWN, 0, 2, 1), (PASS_Y, 0, 0), (PASS_Y, 0, 1),)),
        (7, ((OWN, 1, 1, 0), (FWD_Y, 3, 0), (PAR, 0, 3, 0),)),
        (8, ((OWN, 1, 3, 0), (PASS_Y, 1, 0),)),
        (9, ((OWN, 1, 1, 1), (FWD_Y, 1, 1), (PAR, 0, 1, 1), (PAR, 1, 0, 0),)),
        (10, ((OWN, 1, 3, 1), (PAR, 1, 0, 1),)),
        (11, ((OWN, 1, 2, 1), (FWD_Y, 3, 1), (PASS_Y, 3, 0), (PAR, 0, 3, 1),)),
        (12, ((OWN, 1, 2, 0), (PAR, 1, 1, 0),)),
        (13, ((FWD_Y, 2, 0), (PASS_Y, 1, 1), (PAR, 0, 2, 0),)),
        (14, ((FWD_Y, 2, 1), (PASS_Y, 3, 1), (PAR, 0, 2, 1), (PAR, 1, 3, 0),)),
        (16, ((PASS_Y, 2, 0), (PAR, 1, 1, 1),)),
        (17, ((PAR, 1, 3, 1),)),
        (18, ((PASS_Y, 2, 1),)),
        (19, ((PAR, 1, 2, 0),)),
        (20, ((PAR, 1, 2, 1),)),
    ),
    (
        (2, ((CROSSF, 0), (CROSSF, 1), (OWN, 0, 1, 0), (OWN, 0, 3, 0), (FWD_Y, 0, 0),)),
        (3, ((OWN, 0, 1, 1), (OWN, 0, 3, 1), (FWD_Y, 0, 1),)),
        (4, ((OWN, 1, 0, 0), (OWN, 1, 0, 1),)),
        (5, ((OWN, 0, 2, 0), (FWD_Y, 1, 0),)),
        (6, ((OWN, 0, 2, 1), (PAR, 0, 0, 0), (PAR, 1, 0, 0),)),
        (7, ((OWN, 1, 1, 0), (FWD_Y, 3, 0),)),
        (8, ((OWN, 1, 3, 0), (PAR, 0, 0, 1), (PAR, 1, 0, 1),)),
        (9, ((OWN, 1, 1, 1), (FWD_Y, 1, 1),)),
        (10, ((OWN, 1, 3, 1), (PAR, 0, 1, 0), (PAR, 1, 1, 0),)),
        (11, ((FWD_Y, 3, 1),)),
        (12, ((PAR, 0, 3, 0), (PAR, 1, 3, 0),)),
        (13, ((FWD_Y, 2, 0),)),
        (14, ((OWN, 1, 2, 0), (FWD_Y, 2, 1), (PAR, 0, 1, 1), (PAR, 1, 1, 1),)),
        (15, ((PAR, 0, 3, 1), (PAR, 1, 3, 1),)),
        (17, ((OWN, 1, 2, 1), (PAR, 0, 2, 0), (PAR, 1, 2, 0),)),
        (18, ((PAR, 0, 2, 1), (PAR, 1, 2, 1),)),
    ),
    (
        (2, ((CROSSF, 0), (CROSSF, 1), (OWN, 0, 1, 0), (OWN, 0, 3, 0), (FWD_Y, 0, 0),)),
        (3, ((OWN, 0, 1, 1), (OWN, 0, 3, 1), (FWD_Y, 0, 1),)),
        (4, ((OWN, 1, 0, 0), (OWN, 1, 0, 1),)),
        (5, ((OWN, 0, 2, 0), (FWD_Y, 1, 0),)),
        (6, ((OWN, 0, 2, 1), (PAR, 0, 0, 0), (PAR, 1, 0, 0),)),
        (7, ((OWN, 1, 1, 0), (FWD_Y, 3, 0),)),
        (8, ((OWN, 1, 3, 0), (PAR, 0, 0, 1), (PAR, 1, 0, 1),)),
        (9, ((OWN, 1, 1, 1), (FWD_Y, 1, 1),)),
        (10, ((OWN, 1, 3, 1), (PAR, 0, 1, 0), (PAR, 1, 1, 0),)),
        (11, ((FWD_Y, 3, 1),)),
        (12, ((PAR, 0, 3, 0), (PAR, 1, 3, 0),)),
        (13, ((FWD_Y, 2, 0),)),
        (14, ((OWN, 1, 2, 0), (FWD_Y, 2, 1), (PAR, 0, 1, 1), (PAR, 1, 1, 1),)),
        (15, ((OWN, 1, 2, 1), (PAR, 0, 3, 1), (PAR, 1, 3, 1),)),
        (17, ((PAR, 0, 2, 0), (PAR, 1, 2, 0),)),
        (18, ((PAR, 0, 2, 1), (PAR, 1, 2, 1),)),
    ),
    (
        (2, ((CROSSF, 0), (CROSSF, 1), (OWN, 0, 1, 0), (OWN, 0, 3, 0), (FWD_Y, 0, 0),)),
        (3, ((OWN, 0, 1, 1), (OWN, 0, 3, 1), (FWD_Y, 0, 1),)),
        (4, ((OWN, 1, 0, 0), (OWN, 1, 0, 1),)),
        (5, ((OWN, 0, 2, 0), (FWD_Y, 1, 0),)),
        (6, ((OWN, 0, 2, 1), (PAR, 0, 0, 0), (PAR, 1, 0, 0),)),
        (7, ((OWN, 1, 1, 0), (FWD_Y, 3, 0),)),
        (8, ((OWN, 1, 3, 0), (PAR, 0, 0, 1), (PAR, 1, 0, 1),)),
        (9, ((OWN, 1, 1, 1), (FWD_Y, 1, 1),)),
        (10, ((OWN, 1, 3, 1), (PAR, 0, 1, 0), (PAR, 1, 1, 0),)),
        (11, ((OWN, 1, 2, 1), (FWD_Y, 3, 1),)),
        (12, ((OWN, 1, 2, 0), (PAR, 0, 3, 0), (PAR, 1, 3, 0),)),
        (13, ((FWD_Y, 2, 0),)),
        (14, ((FWD_Y, 2, 1), (PAR, 0, 1, 1), (PAR, 1, 1, 1),)),
        (15, ((PAR, 0, 3, 1), (PAR, 1, 3, 1),)),
        (17, ((PAR, 0, 2, 0), (PAR, 1, 2, 0),)),
        (18, ((PAR, 0, 2, 1), (PAR, 1, 2, 1),)),
    ),
    (
        (2, ((CROSSF, 0), (CROSSF, 1), (OWN, 0, 1, 0), (OWN, 0, 3, 0), (FWD_Y, 0, 0),)),
        (3, ((OWN, 0, 1, 1), (OWN, 0, 3, 1), (FWD_Y, 0, 1),)),
        (4, ((OWN, 1, 0, 0), (OWN, 1, 0, 1),)),
        (5, ((OWN, 0, 2, 0), (FWD_Y, 1, 0),)),
        (6, ((OWN, 0, 2, 1), (PAR, 0, 0, 0), (PAR, 1, 0, 0),)),
        (7, ((OWN, 1, 1, 0), (FWD_Y, 3, 0),)),
        (8, ((OWN, 1, 3, 0), (PAR, 0, 0, 1), (PAR, 1, 0, 1),)),
        (9, ((OWN, 1, 1, 1), (FWD_Y, 1, 1),)),
        (10, ((OWN, 1, 3, 1), (PAR, 0, 1, 0), (PAR, 1, 1, 0),)),
        (11, ((OWN, 1, 2, 1), (FWD_Y, 3, 1),)),
        (12, ((OWN, 1, 2, 0), (PAR, 0, 3, 0), (PAR, 1, 3, 0),)),
        (13, ((FWD_Y, 2, 0),)),
        (14, ((FWD_Y, 2, 1), (PAR, 0, 1, 1), (PAR, 1, 1, 1),)),
        (15, ((PAR, 0, 3, 1), (PAR, 1, 3, 1),)),
        (17, ((PAR, 0, 2, 0), (PAR, 1, 2, 0),)),
        (18, ((PAR, 0, 2, 1), (PAR, 1, 2, 1),)),
    ),
)

STAGES = len(SEQUENCE)
BASES = [sum(PARTS[stage] for stage in SEQUENCE[:n]) for n in range(STAGES + 1)]
POINTS = BASES[-1] + 1
PAR_AT, T1_AT, T2_AT, T3_AT, TC_AT, SLOTS = 32, 64, 72, 80, 88, 90
WAYS = ("x+", "x-", "y+", "y-", "z+", "z-", "core", "ya", "yb", "za", "zb")
WAIT = 15
CLASSES = [(x, y) for x in range(4) for y in range(4)]


def sign_of(j, k):
    return "+" if (k + (0, 1, 1, 0)[j]) % 2 == 0 else "-"


def name_of(x, y, row, j):
    return (y // 2 + row) % 2 * 4 + (x + 4 - j) % 4


def row_behind(y, sign):
    return (y + 3) % 4 // 2 if sign == "+" else (y + 1) % 4 // 2


def feed(x, y, j, k, src):
    up = y // 2 == 1
    final, via1, via2 = ("par", name_of(x, y, 0, j), k), ("t1", j, k), ("t2", j, k)
    sends = []
    if x in (0, 1):
        sends.append((src, via1, "z" + sign_of(j, k)))
    if x == 1:
        sends.append((src, final, "ya"))
    if x in (2, 3):
        sends.append((src, final if x == 2 and not up else via1, "za"))
        sends.append((src, final if x == 2 and up else via2, "zb"))
    return sends


def expand(x, y, event):
    kind, args = event[0], event[1:]
    up = y // 2 == 1
    ops = []
    if kind == CROSSF:
        (k,) = args
        sign = "+-"[k]
        ops = [("tc", k), (("tc", k), ("own", row_behind(y, sign) * 4 + x, k), "y" + sign)]
    if kind == OWN:
        row, j, k = args
        here = ("own", name_of(x, y, row, j), k)
        ops = [here]
        if (row, j) == (1, 0) or (j == 1 and (k + row) % 2 == 0):
            ops.append((here, here, "x+"))
        if (row, j) == (1, 0) or (j == 3 and (k + row) % 2 == 1):
            ops.append((here, here, "x-"))
        if row == 0:
            ops += feed(x, y, j, k, here)
        ops.append((here, here, "core"))
    if kind == PASS_Z:
        j, k = args
        here = ("t1", j, k)
        there = ("par", name_of(x, y, 0, j), k) if x == 0 and up else ("t2", j, k)
        ops = [here, (here, there, "z" + sign_of(j, k))]
    if kind == FWD_Y:
        j, k = args
        final, there, way = ("par", name_of(x, y, 0, j), k), ("t3", j, k), "y" + sign_of(j, k)
        if x == 3 or (x == 2 and up):
            ops += [("t1", j, k), (("t1", j, k), final, "ya") if x == 3 else (("t1", j, k), there, way)]
        if x in (1, 3) or not up:
            ops += [("t2", j, k), (("t2", j, k), final, "yb") if x in (1, 3) else (("t2", j, k), there, way)]
    if kind == PASS_Y:
        j, k = args
        sign = sign_of(j, k)
        row = row_behind(y, sign)
        if x == 2 or row == 0:
            ops = [("t3", j, k), (("t3", j, k), ("par", row * 4 + (x + 4 - j) % 4, k), "y" + sign)]
    if kind == PAR:
        row, j, k = args
        here = ("par", name_of(x, y, row, j), k)
        ops = [here, (here, here, "core")]
    return ops


def slot(place, c):
    kind, rest = place[0], place[1:]
    if kind in ("own", "par"):
        q, k = rest
        return (PAR_AT if kind == "par" else 0) + q * 4 + c * 2 + k
    if kind == "tc":
        return TC_AT + rest[0]
    return {"t1": T1_AT, "t2": T2_AT, "t3": T3_AT}[kind] + rest[0] * 2 + rest[1]


def tables(x, y):
    per_core = []
    for c in range(2):
        ops, begins, sends, at = [], [], 0, dict(EVENTS[CLASSES.index((x, y))])
        for point in range(POINTS):
            begins.append(len(ops))
            for event in at.get(point, ()):
                for op in expand(x, y, event):
                    if isinstance(op[0], str):
                        ops.append(slot(op, c) + 2097152 * WAIT)
                    else:
                        src, dst, way = op
                        ops.append(slot(src, c) + 128 * slot(dst, c) + 16384 * sends + 2097152 * WAYS.index(way))
                        sends += 1
        per_core.append((ops, begins + [len(ops), sends], sends))
    return per_core


TABLES = {cls: tables(*cls) for cls in CLASSES}
MOST_OPS = max(len(ops) for cores in TABLES.values() for ops, _, _ in cores)
MOST_SENDS = max(sends for cores in TABLES.values() for _, _, sends in cores)
FIRST_SENDS = 12


def columns(t):
    first, last = t * 256, (t + 1) * 256
    cuts = [first] + [cut for cut in range(0, NI * V, V) if first < cut < last] + [last]
    return [(u - first, w - first, u // V, u % V) for u, w in zip(cuts, cuts[1:])]


def kernel(dims, mine, amps, out, out_own, out_par, buf, rc, half, acc, ops, begins, devs,
           ssem, first_sem, rsem, local_sem):
    sym, tile, c = lax.axis_index("sym"), lax.axis_index("tile"), lax.axis_index("occ")
    x, yhi = sym % 4, sym // 4
    x0, x1 = x % 2, x // 2
    z, ylo = tile // 2, tile % 2
    z0, z1 = z % 2, z // 2
    y = 2 * yhi + ylo
    none = sym == 0

    def dev(dx=0, dy=0, dz=0, dc=0):
        xx, yy, zz = (x + 4 + dx) % 4, (y + 4 + dy) % 4, (z + 4 + dz) % 4
        return ((yy // 2) * 4 + xx) * 16 + (zz * 2 + yy % 2) * 2 + (c + dc) % 2

    step_a = 1 - 2 * (yhi + ylo - 2 * yhi * ylo)
    step_z = 1 - 2 * z0
    to = {
        "x+": dev(dx=1), "x-": dev(dx=-1), "y+": dev(dy=1), "y-": dev(dy=-1), "z+": dev(dz=1), "z-": dev(dz=-1),
        "core": dev(dc=1), "ya": dev(dy=step_a), "yb": dev(dy=-step_a), "za": dev(dz=step_z), "zb": dev(dz=-step_z),
    }
    barrier = pltpu.get_barrier_semaphore()
    for way in WAYS[:7]:
        pl.semaphore_signal(barrier, inc=1, device_id=to[way], device_id_type=pl.DeviceIdType.LOGICAL)

    def own_slot(q, core, k):
        return q * 4 + core * 2 + k

    keep = []
    for k in range(PIECES):
        keep.append(pltpu.make_async_copy(mine.at[pl.ds(k * PV, PV)], buf.at[own_slot(sym, c, k)], local_sem.at[8 + k]))
        keep[-1].start()
    loads = [pltpu.make_async_copy(amps.at[i], rc.at[:, pl.ds(i * V, V)], local_sem.at[i]) for i in range(NI)]
    for load in loads:
        load.start()

    pl.semaphore_wait(barrier, 7)

    def remote(src, dst_slot, sem, where):
        return pltpu.make_async_remote_copy(
            src, buf.at[dst_slot], sem, rsem.at[dst_slot], device_id=where, device_id_type=pl.DeviceIdType.LOGICAL
        )

    def arrived(at):
        remote(buf.at[at], at, first_sem.at[0], to["core"]).wait_recv()

    firsts = []

    def first(src, place, where, cond=None):
        index = len(firsts)
        if cond is None:
            remote(src, place, first_sem.at[index], where).start()
        else:
            pl.when(cond)(lambda: remote(src, place, first_sem.at[index], where).start())
        firsts.append((src, place, cond, index))

    step_2 = {k: {"+": to["z+"], "-": to["z-"]}[sign_of(0, k)] for k in range(PIECES)}
    for k in range(PIECES):
        src = mine.at[pl.ds(k * PV, PV)]
        home = own_slot(sym, c, k)
        final, via1, via2 = PAR_AT + home, T1_AT + k, T2_AT + k
        first(src, home, to["core"])
        first(src, home, to["x+"])
        first(src, home, to["x-"])
        first(src, TC_AT + k, to["y" + "+-"[k]])
        direct_b, direct_a = x0 + 2 * (1 - x1) + (1 - yhi) == 0, x0 + 2 * (1 - x1) + yhi == 0
        where_b = x1 * to["zb"] + (1 - x1) * step_2[k]
        place_b = jnp.where(direct_b, final, x1 * via2 + (1 - x1) * via1)
        first(src, place_b, where_b)
        where_a = x1 * to["za"] + (1 - x1) * to["ya"]
        place_a = jnp.where(direct_a | (x1 == 0), final, via1)
        first(src, place_a, where_a, x > 0)

    for (at_x, at_y), cores in TABLES.items():
        @pl.when((x == at_x) & (y == at_y))
        def _():
            (ops0, begins0, _), (ops1, _, _) = cores
            for n, (op0, op1) in enumerate(zip(ops0, ops1)):
                ops[n] = op0 + (op1 - op0) * c if op0 != op1 else op0
            for n, begin in enumerate(begins0):
                begins[n] = begin
    for n, way in enumerate(WAYS):
        devs[n] = to[way]

    n_row = dims[tile]
    n_col = dims[(z1 + yhi - 2 * z1 * yhi) * 4 + (z0 + x1 - 2 * z0 * x1) * 2 + (ylo + x0 - 2 * ylo * x0)]
    live_r = jnp.where(lax.broadcasted_iota(jnp.int32, (V, V), 0) < n_row, 1.0, 0.0)
    live = jnp.where(lax.broadcasted_iota(jnp.int32, (V, V), 1) < n_col, live_r, 0.0).astype(jnp.bfloat16)
    acc[...] = jnp.zeros_like(acc)
    for load in loads:
        load.wait()
    for i in range(NI):
        rc[:, i * V:(i + 1) * V] = rc[:, i * V:(i + 1) * V] * live
    for copy in keep:
        copy.wait()

    def decoded(n):
        op = ops[n]
        src, rest = lax.rem(op, 128), lax.div(op, 128)
        dst, rest = lax.rem(rest, 128), lax.div(rest, 128)
        return src, dst, lax.rem(rest, 128), lax.div(rest, 128)

    def events(point):
        @pl.loop(begins[point], begins[point + 1])
        def _(n):
            src, dst, index, way = decoded(n)

            @pl.when(way == WAIT)
            def _():
                arrived(src)

            @pl.when(way != WAIT)
            def _():
                remote(buf.at[src], dst, ssem.at[index], devs[way]).start()

    digit = (1 + 15 * x0) * (1 + 255 * x1)

    def chosen(groups, n):
        code = 0
        for number, names in enumerate(groups):
            of_y = [0] * 4
            for (at_x, at_y), (row, j, k) in zip(CLASSES, names):
                of_y[at_y] += (row * 8 + j * 2 + k) * 16 ** at_x
            value = of_y[0]
            if len(set(of_y)) > 1:
                value = value + (of_y[1] - of_y[0]) * ylo + (of_y[2] - of_y[0]) * yhi
                value = value + (of_y[3] - of_y[2] - of_y[1] + of_y[0]) * (yhi * ylo)
            code = code + (n == number) * 1 * value
        code = lax.rem(lax.div(code, digit), 16)
        return (yhi + code // 8) % 2 * 4 + (x + 4 - code // 2 % 4) % 4, code % 2

    def base_of(n):
        return sum((n == number) * base for number, base in enumerate(BASES[:-1]) if base)

    par_base = PAR_AT * (1 - (sym == 0) * 1)

    def unit(base, q, core):
        at = base + q * 4 + core * 2
        return buf[pl.ds(at, 2)].reshape(V, V)

    def first_stage(base, halves):
        for q, k in halves:
            arrived(own_slot(q, 1 - c, k))
        for h in range(PARTS[1]):
            if h:
                events(base + h)
            for t in range(h * 12 // PARTS[1], (h + 1) * 12 // PARTS[1]):
                left = jnp.concatenate([buf[q * 4 + 2 * p + k] for q, k in halves for p in range(2)], axis=0)
                r = jnp.dot(left, rc[:, t * 256:(t + 1) * 256], preferred_element_type=jnp.float32).astype(jnp.bfloat16)
                for lo_col, hi_col, pair, at in columns(t):
                    for number, (q, k) in enumerate(halves):
                        rows = pl.ds(pl.multiple_of(pair * V + k * PV, PV), PV)
                        for p in range(2):
                            lanes = pl.ds(p * V + at, hi_col - lo_col)
                            first = (2 * number + p) * PV
                            half[q, rows, lanes] = r[first:first + PV, lo_col:hi_col]

    def second_stage(base, q, last=False):
        @pl.when(jnp.logical_not(none))
        def _():
            for k in range(PIECES):
                arrived(PAR_AT + own_slot(q, 1 - c, k))

        for h in range(2):
            if h and PARTS[2] > 1:
                events(base + h)
            rows = pl.ds(h * HALF, HALF)
            for b0, b1 in ((0, 256), (256, 384)):
                right = jnp.concatenate([unit(par_base, q, p)[b0:b1] for p in range(2)], axis=1)
                acc[rows, b0:b1] += lax.dot_general(
                    half[q, rows, :], right, (((1,), (1,)), ((), ())), preferred_element_type=jnp.float32
                )
            if last:
                pltpu.make_async_copy(acc.at[rows], out.at[rows], local_sem.at[h]).start()

    @pl.loop(0, STAGES - 1)
    def _(n):
        second = sum((n == k) * 1 for k, stage in enumerate(SEQUENCE) if stage == 2)
        halves = [chosen(group, n) for group in UNITS]
        base = base_of(n)
        events(base)
        pl.when(second == 0)(lambda: first_stage(base, halves))
        pl.when(second == 1)(lambda: second_stage(base, halves[0][0]))

    events(BASES[-2])
    second_stage(BASES[-2], chosen(UNITS[0], jnp.int32(STAGES - 1))[0], last=True)
    events(POINTS - 1)

    leaving = []
    for r in range(len(REST)):
        q, _ = chosen(REST, jnp.int32(r))
        for k in range(PIECES):
            arrived(own_slot(q, 1 - c, k))

        @pl.when(jnp.logical_not(none))
        def _():
            for k in range(PIECES):
                arrived(PAR_AT + own_slot(q, 1 - c, k))

        par_at = par_base + q * 4
        for source, target, sem in ((q * 4, out_own.at[r], 18 + 2 * r), (par_at, out_par.at[r], 19 + 2 * r)):
            leaving.append(pltpu.make_async_copy(buf.at[pl.ds(source, 4)], target, local_sem.at[sem - 8]))
            leaving[-1].start()

    for src, place, cond, index in firsts:
        def sent(src=src, place=place, index=index):
            remote(src, place, first_sem.at[index], to["core"]).wait_send()

        if cond is None:
            sent()
        else:
            pl.when(cond)(sent)

    @pl.loop(0, begins[POINTS + 1])
    def _(n):
        remote(buf.at[0], 0, ssem.at[n], to["core"]).wait_send()

    for h in range(2):
        rows = pl.ds(h * HALF, HALF)
        pltpu.make_async_copy(acc.at[rows], out.at[rows], local_sem.at[h]).wait()
    for copy in leaving:
        copy.wait()


ALL = [(row, j) for j in (0, 1, 3, 2) for row in range(2)]


def left_over():
    by_class = []
    for at in range(len(CLASSES)):
        done = [names[at][:2] for group in UNITS for stage, names in zip(SEQUENCE, group) if stage == 1]
        by_class.append([name + (0,) for name in ALL if name not in done])
    return tuple(zip(*by_class))


REST = left_over()


def rest_kernel(dims, own_hbm, par_hbm, amps, raw, out, own, par, rc, half, acc, sems):
    sym, tile = lax.axis_index("sym"), lax.axis_index("tile")
    n, hi = len(REST), NI // 2
    get_own = pltpu.make_async_copy(own_hbm, own, sems.at[0])
    get_par = pltpu.make_async_copy(par_hbm, par, sems.at[1])
    get_amps = [pltpu.make_async_copy(amps.at[i], rc.at[:, pl.ds(i * V, V)], sems.at[2 + i]) for i in range(NI)]
    get_raw = [
        pltpu.make_async_copy(raw.at[pl.ds(h * HALF, HALF)], acc.at[pl.ds(h * HALF, HALF)], sems.at[2 + NI + h])
        for h in range(2)
    ]
    for copy in [get_own] + get_amps[:hi] + [get_par, get_raw[0]] + get_amps[hi:] + [get_raw[1]]:
        copy.start()
    n_row, n_col = dims[tile], dims[jnp.bitwise_xor(tile, sym)]
    live = (lax.broadcasted_iota(jnp.int32, (V, V), 0) < n_row) & (lax.broadcasted_iota(jnp.int32, (V, V), 1) < n_col)
    live_b = jnp.where(live, 1.0, 0.0).astype(jnp.bfloat16)
    puts, masked = [], 0
    for h in range(2):
        if h == 0:
            get_own.wait()
        for t in range(6 * h, 6 * (h + 1)):
            while masked <= columns(t)[-1][2]:
                get_amps[masked].wait()
                rc[:, masked * V:(masked + 1) * V] = rc[:, masked * V:(masked + 1) * V] * live_b
                masked += 1
            left = own[...].reshape(n * 2 * V, V)
            r = jnp.dot(left, rc[:, t * 256:(t + 1) * 256], preferred_element_type=jnp.float32).astype(jnp.bfloat16)
            for lo_col, hi_col, pair, at in columns(t):
                for p in range(2 * n):
                    lanes = pl.ds(p * V + at, hi_col - lo_col)
                    half[(pair - h * hi) * V:(pair - h * hi + 1) * V, lanes] = r[p * V:(p + 1) * V, lo_col:hi_col]
        if h == 0:
            get_par.wait()
        get_raw[h].wait()
        rows = pl.ds(h * HALF, HALF)
        for b0, b1 in ((0, 256), (256, 384)):
            right = [par[r, pl.ds(2 * p, 2)].reshape(V, V)[b0:b1] for r in range(n) for p in range(2)]
            right = jnp.concatenate(right, axis=1)
            r = lax.dot_general(half[...], right, (((1,), (1,)), ((), ())), preferred_element_type=jnp.float32)
            r = r + acc[rows, b0:b1]
            for i in range(hi):
                at = pl.ds((h * hi + i) * V, V)
                acc[at, b0:b1] = jnp.where(live[:, b0:b1], r[i * V:(i + 1) * V], 0.0)
            lanes = pl.ds(b0, b1 - b0)
            puts.append(pltpu.make_async_copy(acc.at[rows, lanes], out.at[rows, lanes], sems.at[4 + NI + len(puts)]))
            puts[-1].start()
    for copy in puts:
        copy.wait()


def shards(irrep_dims, chol_vectors, amplitudes):
    bf, sem = jnp.bfloat16, pltpu.SemaphoreType.DMA
    n = len(REST)
    own, chol, amps = (n, 4, PV, V), chol_vectors.reshape(V, V), amplitudes.reshape(NI, V, V)
    anywhere = pl.BlockSpec(memory_space=pl.ANY)
    raw, rest_own, rest_par = pl.pallas_call(
        kernel,
        out_shape=[
            jax.ShapeDtypeStruct((NI * V, V), jnp.float32),
            jax.ShapeDtypeStruct(own, bf),
            jax.ShapeDtypeStruct(own, bf),
        ],
        in_specs=[pl.BlockSpec(memory_space=pltpu.SMEM), anywhere, anywhere],
        out_specs=[anywhere] * 3,
        scratch_shapes=[
            pltpu.VMEM((SLOTS, PV, V), bf),
            pltpu.VMEM((V, NI * V), bf),
            pltpu.VMEM((8, NI * V, 2 * V), bf),
            pltpu.VMEM((NI * V, V), jnp.float32),
            pltpu.SMEM((MOST_OPS,), jnp.int32),
            pltpu.SMEM((POINTS + 2,), jnp.int32),
            pltpu.SMEM((len(WAYS),), jnp.int32),
            sem((MOST_SENDS,)), sem((FIRST_SENDS,)), sem((SLOTS,)), sem((10 + 2 * n,)),
        ],
        compiler_params=pltpu.CompilerParams(
            collective_id=0, has_side_effects=True, vmem_limit_bytes=63 * 1024 * 1024
        ),
        cost_estimate=pl.CostEstimate(flops=(8 - n) * 3_600_000_000, bytes_accessed=12_000_000, transcendentals=0),
        name="ladder",
    )(irrep_dims, chol, amps)
    total = pl.pallas_call(
        rest_kernel,
        out_shape=jax.ShapeDtypeStruct((NI * V, V), jnp.float32),
        in_specs=[pl.BlockSpec(memory_space=pltpu.SMEM)] + [anywhere] * 4,
        out_specs=anywhere,
        scratch_shapes=[
            pltpu.VMEM(own, bf),
            pltpu.VMEM(own, bf),
            pltpu.VMEM((V, NI * V), bf),
            pltpu.VMEM((HALF, n * 2 * V), bf),
            pltpu.VMEM((NI * V, V), jnp.float32),
            sem((8 + NI,)),
        ],
        compiler_params=pltpu.CompilerParams(vmem_limit_bytes=60 * 1024 * 1024),
        cost_estimate=pl.CostEstimate(flops=n * 3_600_000_000, bytes_accessed=16_000_000, transcendentals=0),
        name="rest",
    )(irrep_dims, rest_own, rest_par, amps, raw)
    return total.reshape(1, NI, V, V)


def solution(mesh):
    return jax.shard_map(
        shards,
        mesh=mesh,
        in_specs=(P(), P(("sym", "occ"), "tile", None), P("sym", "occ", "tile", None)),
        out_specs=P("sym", "occ", "tile", None),
        check_vma=False,
    )
```
